32 devices in a mesh: rep: 4 (over z), fsdp: 8 (over y, x, core).
Axes of the slice: x: 2, y: 2, z: 4, core: 2. Of those that a mesh axis runs over, the one named last changes fastest.
Arguments:
- word_rows: bfloat16 [4096, 768], P(('rep', 'fsdp')), may hold values from -6 to 6
- region_rows: bfloat16 [8192, 768], P(('rep', 'fsdp')), may hold values from -6 to 6
- word_segment: int32 [32, 128], P(('rep', 'fsdp')), may hold values from 0 to 7, never falling along the last dimension, each value on 1 to 20 neighbouring positions
- region_segment: int32 [32, 256], P(('rep', 'fsdp')), may hold values from 0 to 7, never falling along the last dimension, each value on 1 to 36 neighbouring positions
- inward: bfloat16 [3, 768, 2304], P(None, 'fsdp'), may hold values from -0.21875 to 0.21875
- outward: bfloat16 [3, 768, 768], P(None, 'fsdp'), may hold values from -0.875 to 0.875
- biases: bfloat16 [16, 768], P(None, 'fsdp'), may hold values from -3 to 3
- norm_gain: bfloat16 [5, 768], P(None, 'fsdp'), may hold values from 0.5 to 1.5
- expand_weight: bfloat16 [2, 768, 3072], P(None, 'fsdp'), may hold values from -0.21875 to 0.21875
- shrink_weight: bfloat16 [2, 3072, 768], P(None, 'fsdp'), may hold values from -0.109375 to 0.109375
- hidden_bias: bfloat16 [2, 3072], P(None, 'fsdp'), may hold values from -3 to 3
- word_cotangent: bfloat16 [4096, 768], P(('rep', 'fsdp')), may hold values from -6 to 6
- region_cotangent: bfloat16 [8192, 768], P(('rep', 'fsdp')), may hold values from -6 to 6
Outputs:
- word_output: bfloat16 [4096, 768], P(('rep', 'fsdp'))
- region_output: bfloat16 [8192, 768], P(('rep', 'fsdp'))
- word_gradient: float32 [4096, 768], P(('rep', 'fsdp'))
- region_gradient: float32 [8192, 768], P(('rep', 'fsdp'))
- inward_grad: float32 [3, 768, 2304], P(None, 'fsdp')
- outward_grad: float32 [3, 768, 768], P(None, 'fsdp')
- biases_grad: float32 [16, 768], P(None, 'fsdp')
- gain_grad: float32 [5, 768], P(None, 'fsdp')
- expand_grad: float32 [2, 768, 3072], P(None, 'fsdp')
- shrink_grad: float32 [2, 3072, 768], P(None, 'fsdp')
- hidden_grad: float32 [2, 3072], P(None, 'fsdp')
The draws below stay inside these ranges and needn't reach their ends.
Inputs may be any that keep to these rules, and one draw needn't show every extreme that they name: Row g of word_segment gives the ids of the g-th block of 128 word rows: they never fall, every id from 0 to 7 occurs, and an id covers 1 to 20 positions. Equal ids in the same row of word_segment and region_segment name one caption-region pair. Row g of region_segment gives the ids of the g-th block of 256 region rows: they never fall, every id from 0 to 7 occurs, and an id covers 1 to 36 positions.
All inputs are finite; a program needn't handle non-finite values.
Results may differ from the reference program's by a relative error of at most 0.018.
Values may be sent and summed in bfloat16 or wider, within the bound.
A program may use at most 256 MiB of HBM per device.

```python
import math
import jax
import jax.numpy as jnp
import numpy as np
from jax import lax

D = 768
HEADS = 12
HEAD_DIM = 64
FF = 3072
MAX_WORDS = 20
MAX_REGIONS = 36
PAIRS = 8
WORDS_DEV = 128
REGIONS_DEV = 256
DEVS = 32
WORDS = 4096
REGIONS = 8192


def strengthened(drawn, stream_key, source, target, blocks, factor):
    def block_of(position):
        return (jnp.arange(drawn.shape[position]) // (drawn.shape[position] // blocks)).reshape((-1,) + (1,) * (drawn.ndim - 1 - position))

    first = jax.random.permutation(stream_key, blocks)[block_of(target)]
    far = (block_of(target) + blocks // 2) % blocks
    return jnp.where((block_of(source) == first) | (block_of(source) == far), factor * drawn, drawn)


def shard_levels(stream_key, extent, split, least, high):
    level, own = 1.0, jax.random.fold_in(stream_key, 6)
    for axis_at, shards_of in split:
        steps = jnp.exp(jax.random.uniform(jax.random.fold_in(own, axis_at), (shards_of,), jnp.float32, least / len(split), high / len(split)))
        level = level * jnp.repeat(steps, extent[axis_at] // shards_of).reshape([-1 if axis == axis_at else 1 for axis in range(len(extent))])
    return level


def length_profile(amount, total, bound, skew):
    weights = [(1 << 20) // math.isqrt(rank ** skew) + 1 for rank in range(2, amount + 1)]
    spare, holding = total - bound - (amount - 1), [1] * (amount - 1)
    while spare > 0:
        free = [i for i in range(amount - 1) if holding[i] < bound]
        pool, remaining = sum([weights[i] for i in free]), spare
        for i in free:
            addition = min(bound - holding[i], max(1, remaining * weights[i] // pool), spare)
            holding[i] = holding[i] + addition
            spare = spare - addition
    return np.array([bound] + holding)


def uneven_parts(key, amount, total, reach, skew):
    if amount == 2:
        one = jax.random.randint(key, (), max(1, total - reach), min(reach, total - 1) + 1)
        return jnp.stack([one, total - one])
    tallies = jnp.asarray(length_profile(amount, total, reach, skew), jnp.int32)
    pairs = (amount - 1) // 2
    source_of, sink = tallies[1:1 + 2 * pairs:2], tallies[2:2 + 2 * pairs:2]
    margin = jnp.minimum(source_of - 1, reach - sink)
    shifted = jax.random.randint(jax.random.fold_in(key, 1), (pairs,), 0, 1 << 20) % (margin + 1)
    tallies = tallies.at[1:1 + 2 * pairs:2].set(source_of - shifted).at[2:2 + 2 * pairs:2].set(sink + shifted)
    return tallies[jax.random.permutation(jax.random.fold_in(key, 2), amount)]


def normal_values(key, shape, width, reach, shards=(), held_as=jnp.bfloat16):
    array = jax.random.normal(key, shape, jnp.float32) * width
    if len(shards) > 0:
        array = shard_levels(key, shape, shards, -0.22, 0.18) * array
    return jnp.clip(array, min=-reach, max=reach).astype(held_as)


def noise_with(own_key, dims, deviation, limit, shards, heavy, held_as=jnp.bfloat16):
    drawn = deviation * jax.random.normal(own_key, dims, jnp.float32)
    if shards:
        drawn = drawn * shard_levels(own_key, dims, shards, -0.22, 0.18)
    return jnp.clip(strengthened(drawn, jax.random.fold_in(own_key, 3), *heavy), -limit, limit).astype(held_as)


def setup_inputs(seed: int = 0) -> dict:
    keys = jax.random.split(jax.random.key(seed), 14)
    word_rows = noise_with(keys[0], (WORDS, D), 1.0, 6.0, ((0, 32),), (0, 1, 32, 2.75))
    region_rows = noise_with(keys[1], (REGIONS, D), 1.0, 6.0, ((0, 32),), (0, 1, 32, 2.75))
    word_segment = jax.vmap(lambda own: jnp.searchsorted(jnp.cumsum(uneven_parts(own, PAIRS, WORDS_DEV, MAX_WORDS, 1)), jnp.arange(WORDS_DEV), side="right"))(jax.random.split(keys[2], DEVS)).reshape((DEVS, WORDS_DEV)).astype(jnp.int32)
    region_segment = jax.vmap(lambda own: jnp.searchsorted(jnp.cumsum(uneven_parts(own, PAIRS, REGIONS_DEV, MAX_REGIONS, 1)), jnp.arange(REGIONS_DEV), side="right"))(jax.random.split(keys[3], DEVS)).reshape((DEVS, REGIONS_DEV)).astype(jnp.int32)
    inward = normal_values(keys[4], (3, D, 3 * D), D ** -0.5, 0.21875, ((1, 8),))
    outward = normal_values(keys[5], (3, D, D), (D // 16) ** -0.5, 0.875, ((1, 8),))
    biases = normal_values(keys[6], (16, D), 0.5, 3.0, ((1, 8),))
    norm_gain = jnp.clip(1.0 + 0.1 * jax.random.normal(keys[7], (5, D), jnp.float32), 0.5, 1.5).astype(jnp.bfloat16)
    expand_weight = normal_values(keys[8], (2, D, FF), D ** -0.5, 0.21875, ((1, 8),))
    shrink_weight = normal_values(keys[9], (2, FF, D), FF ** -0.5, 0.109375, ((1, 8),))
    hidden_bias = normal_values(keys[10], (2, FF), 0.5, 3.0, ((1, 8),))
    word_cotangent = noise_with(keys[11], (WORDS, D), 1.0, 6.0, ((0, 32),), (0, 1, 32, 2.75))
    region_cotangent = noise_with(keys[12], (REGIONS, D), 1.0, 6.0, ((0, 32),), (0, 1, 32, 2.75))
    return {"word_rows": word_rows, "region_rows": region_rows, "word_segment": word_segment, "region_segment": region_segment, "inward": inward, "outward": outward, "biases": biases, "norm_gain": norm_gain, "expand_weight": expand_weight, "shrink_weight": shrink_weight, "hidden_bias": hidden_bias, "word_cotangent": word_cotangent, "region_cotangent": region_cotangent}


highest_precision = lax.Precision.HIGHEST
norm_epsilon = 1e-12
masked_score = -1e+30

@jax.custom_vjp
def low(v):
    return lax.optimization_barrier(v.astype(jnp.bfloat16)).astype(jnp.float32)

@jax.custom_vjp
def low_back(v):
    return v

def low_keep(v):
    return (low(v), None)

def low_pass(kept, grad):
    return (grad,)

def back_keep(v):
    return (v, None)

def back_low(kept, grad):
    return (low(grad),)
low.defvjp(low_keep, low_pass)
low_back.defvjp(back_keep, back_low)

def matmul(left_op, right_op):
    return jnp.dot(left_op, right_op, precision=highest_precision, preferred_element_type=jnp.float32)

def heads_of(rows_in):
    return rows_in.reshape(rows_in.shape[0], HEADS, HEAD_DIM)

def normalize(summed, gain_row, shift_row):
    center = summed - lax.optimization_barrier(jnp.mean(summed, axis=-1, keepdims=True))
    spread = lax.optimization_barrier(jnp.mean(center * center, axis=-1, keepdims=True))
    return center * lax.rsqrt(spread + norm_epsilon) * gain_row + shift_row

def project(rows_in, weight, bias_query, bias_value):
    bias_all = jnp.concatenate([bias_query, jnp.zeros_like(bias_query), bias_value])
    return low(low_back(matmul(low(rows_in), weight) + bias_all))

def attention(queries, key_rows, value_rows, allowed):
    scores = jnp.einsum('qhd,khd->hqk', heads_of(queries), heads_of(key_rows), precision=highest_precision, preferred_element_type=jnp.float32) * HEAD_DIM ** (-0.5)
    scores = jnp.where(allowed[None], low_back(scores), masked_score)
    top_score = lax.optimization_barrier(jnp.max(scores, axis=-1, keepdims=True))
    lifted = jnp.exp(scores - top_score)
    shares = low(lifted / lax.optimization_barrier(jnp.sum(lifted, axis=-1, keepdims=True)))
    context = jnp.einsum('hqk,khd->qhd', shares, heads_of(value_rows), precision=highest_precision, preferred_element_type=jnp.float32)
    return low(low_back(context.reshape(queries.shape[0], D)))

def self_block(rows_in, allowed, module, params):
    inward, outward, biases, norm_gain = (params[0], params[1], params[2], params[3])
    mixed = project(rows_in, inward[module], biases[3 * module], biases[3 * module + 1])
    context = attention(mixed[:, :D], mixed[:, D:2 * D], mixed[:, 2 * D:], allowed)
    branch = low_back(matmul(context, outward[module]) + biases[3 * module + 2])
    return normalize(rows_in + branch, norm_gain[module], biases[9 + module])

def cross_block(word_x, region_x, allowed, params):
    inward, outward, biases, norm_gain = (params[0], params[1], params[2], params[3])
    word_mix = project(word_x, inward[0], biases[0], biases[1])
    region_mix = project(region_x, inward[0], biases[0], biases[1])
    word_context = attention(word_mix[:, :D], region_mix[:, D:2 * D], region_mix[:, 2 * D:], allowed)
    region_context = attention(region_mix[:, :D], word_mix[:, D:2 * D], word_mix[:, 2 * D:], allowed.T)
    word_branch = low_back(matmul(word_context, outward[0]) + biases[2])
    region_branch = low_back(matmul(region_context, outward[0]) + biases[2])
    word_out = normalize(word_x + word_branch, norm_gain[0], biases[9])
    region_out = normalize(region_x + region_branch, norm_gain[0], biases[9])
    return (word_out, region_out)

def feed_block(rows_in, feed_index, params):
    biases, norm_gain, expand_weight, shrink_weight, hidden_bias = (params[2], params[3], params[4], params[5], params[6])
    before = low_back(matmul(low(rows_in), expand_weight[feed_index]) + hidden_bias[feed_index])
    hidden = low(jax.nn.gelu(before, approximate=False))
    branch = low_back(matmul(hidden, shrink_weight[feed_index]) + biases[14 + feed_index])
    return normalize(rows_in + branch, norm_gain[3 + feed_index], biases[12 + feed_index])

def group_layer(params, word_x, region_x, word_ids, region_ids):
    cross_mask = word_ids[:, None] == region_ids[None, :]
    word_x, region_x = cross_block(word_x, region_x, cross_mask, params)
    word_x = self_block(word_x, word_ids[:, None] == word_ids[None, :], 1, params)
    region_x = self_block(region_x, region_ids[:, None] == region_ids[None, :], 2, params)
    return (feed_block(word_x, 0, params), feed_block(region_x, 1, params))

def reference(word_rows, region_rows, word_segment, region_segment, inward, outward, biases, norm_gain, expand_weight, shrink_weight, hidden_bias, word_cotangent, region_cotangent):
    groups = word_segment.shape[0]
    params = tuple((weight_arg.astype(jnp.float32) for weight_arg in (inward, outward, biases, norm_gain, expand_weight, shrink_weight, hidden_bias)))
    word_in = word_rows.astype(jnp.float32).reshape(groups, -1, D)
    region_in = region_rows.astype(jnp.float32).reshape(groups, -1, D)

    def forward(params, word_in, region_in):

        def one_group(carry_in, group_items):
            return (carry_in, group_layer(params, group_items[0], group_items[1], group_items[2], group_items[3]))
        unused, outputs = lax.scan(jax.checkpoint(one_group), jnp.zeros((), jnp.float32), (word_in, region_in, word_segment, region_segment))
        return outputs
    outputs, pullback = jax.vjp(forward, params, word_in, region_in)
    cotangents = (word_cotangent.astype(jnp.float32).reshape(groups, -1, D), region_cotangent.astype(jnp.float32).reshape(groups, -1, D))
    param_grads, word_grad, region_grad = pullback(cotangents)
    return (outputs[0].reshape(-1, D).astype(jnp.bfloat16), outputs[1].reshape(-1, D).astype(jnp.bfloat16), word_grad.reshape(-1, D), region_grad.reshape(-1, D), param_grads[0], param_grads[1], param_grads[2], param_grads[3], param_grads[4], param_grads[5], param_grads[6])
```

```python
import functools

import jax
import jax.numpy as jnp
from jax import lax
from jax.experimental import pallas as pl
from jax.experimental.pallas import tpu as pltpu
from jax.sharding import PartitionSpec as P

MESH = pl.DeviceIdType.MESH

HEADS = 12
HEAD_DIM = 64


norm_epsilon = 1e-12
masked_score = -1e30


def matmul(left_op, right_op):
    return jnp.dot(left_op, right_op, preferred_element_type=jnp.float32)


def matmul_tn(left_op, right_op):
    return lax.dot_general(
        left_op, right_op, (((0,), (0,)), ((), ())), preferred_element_type=jnp.float32
    )


def matmul_nt(left_op, right_op):
    return lax.dot_general(
        left_op, right_op, (((1,), (1,)), ((), ())), preferred_element_type=jnp.float32
    )


def column_sums(values):
    return jnp.sum(values, axis=0, dtype=jnp.float32)


def heads_of(rows_in):
    return rows_in.reshape(rows_in.shape[0], HEADS, HEAD_DIM)


def merge_heads(head_rows):
    return head_rows.reshape(head_rows.shape[0], -1)


def normalize(summed, gain_row, shift_row):
    center = summed - jnp.mean(summed, axis=-1, keepdims=True)
    inverse = lax.rsqrt(jnp.mean(center * center, axis=-1, keepdims=True) + norm_epsilon)
    normed = center * inverse
    return (normed * gain_row + shift_row, (normed, inverse))


def normalize_back(grad_out, norm_stats, gain_row):
    normed, inverse = norm_stats
    grad_normed = grad_out * gain_row
    grad_sum = inverse * (
        grad_normed
        - jnp.mean(grad_normed, axis=-1, keepdims=True)
        - normed * jnp.mean(grad_normed * normed, axis=-1, keepdims=True)
    )
    return (grad_sum, column_sums(grad_out * normed), column_sums(grad_out))


def score_block(queries, key_rows, allowed):
    scores = jnp.einsum(
        "qhd,khd->hqk", heads_of(queries), heads_of(key_rows), preferred_element_type=jnp.float32
    ) * HEAD_DIM ** (-0.5)
    return jnp.where(allowed[None], scores, masked_score)


def attend(queries, key_rows, value_rows, allowed):
    scores = score_block(queries, key_rows, allowed)
    top_score = jnp.max(scores, axis=-1, keepdims=True)
    log_total = top_score + jnp.log(jnp.sum(jnp.exp(scores - top_score), axis=-1, keepdims=True))
    shares = jnp.exp(scores - log_total).astype(jnp.bfloat16)
    context = jnp.einsum(
        "hqk,khd->qhd", shares, heads_of(value_rows), preferred_element_type=jnp.float32
    )
    return (merge_heads(context).astype(jnp.bfloat16), log_total)


def attend_back(queries, key_rows, value_rows, allowed, log_total, grad_context):
    shares = jnp.exp(score_block(queries, key_rows, allowed) - log_total)
    grad_heads = heads_of(grad_context)
    grad_shares = jnp.einsum(
        "qhd,khd->hqk", grad_heads, heads_of(value_rows), preferred_element_type=jnp.float32
    )
    grad_values = jnp.einsum(
        "hqk,qhd->khd", shares.astype(jnp.bfloat16), grad_heads, preferred_element_type=jnp.float32
    )
    grad_scores = (
        shares * (grad_shares - jnp.sum(shares * grad_shares, axis=-1, keepdims=True))
    ).astype(jnp.bfloat16)
    score_scale = HEAD_DIM ** (-0.5)
    grad_queries = (
        jnp.einsum(
            "hqk,khd->qhd", grad_scores, heads_of(key_rows), preferred_element_type=jnp.float32
        )
        * score_scale
    )
    grad_keys = (
        jnp.einsum(
            "hqk,qhd->khd", grad_scores, heads_of(queries), preferred_element_type=jnp.float32
        )
        * score_scale
    )
    return (merge_heads(grad_queries), merge_heads(grad_keys), merge_heads(grad_values))


def project(rows_low, weight, bias_rows, module):
    width = weight.shape[0]
    bias_all = jnp.concatenate(
        [bias_rows[3 * module], jnp.zeros((width,), jnp.float32), bias_rows[3 * module + 1]]
    )
    return (matmul(rows_low, weight) + bias_all).astype(jnp.bfloat16)


def project_back(grad_sum, grad_parts, rows_low, weight):
    width = weight.shape[0]
    grad_mixed = jnp.concatenate(grad_parts, axis=1).astype(jnp.bfloat16)
    grad_weight = (rows_low, grad_mixed)
    grad_bias = column_sums(grad_mixed)
    grad_rows = grad_sum + matmul_nt(grad_mixed, weight)
    return (grad_rows, grad_weight, grad_bias[:width], grad_bias[2 * width :])


def branch_back(grad_out, context, norm_stats, gain_row, outward_one):
    grad_sum, grad_gain, grad_shift = normalize_back(grad_out, norm_stats, gain_row)
    grad_branch = grad_sum.astype(jnp.bfloat16)
    grad_outward = (context, grad_branch)
    grad_context = matmul_nt(grad_branch, outward_one).astype(jnp.bfloat16)
    return (grad_sum, grad_context, grad_outward, column_sums(grad_branch), grad_gain, grad_shift)


def self_forward(rows_in, weights, module, allowed):
    inward_all, outward_all, bias_rows, gain_rows = weights
    width = rows_in.shape[1]
    rows_low = rows_in.astype(jnp.bfloat16)
    mixed = project(rows_low, inward_all[module], bias_rows, module)
    context, log_total = attend(
        mixed[:, :width], mixed[:, width : 2 * width], mixed[:, 2 * width :], allowed
    )
    summed = rows_in + matmul(context, outward_all[module]) + bias_rows[3 * module + 2]
    result, norm_stats = normalize(summed, gain_rows[module], bias_rows[9 + module])
    return (result, (rows_low, mixed, context, log_total, norm_stats))


def self_backward(grad_out, kept, weights, module, allowed):
    inward_all, outward_all, bias_rows, gain_rows = weights
    rows_low, mixed, context, log_total, norm_stats = kept
    width = rows_low.shape[1]
    grad_sum, grad_context, grad_outward, grad_bias_out, grad_gain, grad_shift = branch_back(
        grad_out, context, norm_stats, gain_rows[module], outward_all[module]
    )
    grad_parts = attend_back(
        mixed[:, :width],
        mixed[:, width : 2 * width],
        mixed[:, 2 * width :],
        allowed,
        log_total,
        grad_context,
    )
    grad_rows, grad_inward, grad_bias_query, grad_bias_value = project_back(
        grad_sum, grad_parts, rows_low, inward_all[module]
    )
    return (
        grad_rows,
        grad_inward,
        grad_outward,
        (grad_bias_query, grad_bias_value, grad_bias_out),
        grad_gain,
        grad_shift,
    )


def cross_forward(word_rows, region_rows, weights, cross_mask):
    inward_all, outward_all, bias_rows, gain_rows = weights
    words_count = word_rows.shape[0]
    width = word_rows.shape[1]
    rows_low = jnp.concatenate([word_rows, region_rows], axis=0)
    mixed = project(rows_low, inward_all[0], bias_rows, 0)
    word_mix = mixed[:words_count]
    region_mix = mixed[words_count:]
    word_context, word_total = attend(
        word_mix[:, :width],
        region_mix[:, width : 2 * width],
        region_mix[:, 2 * width :],
        cross_mask,
    )
    region_context, region_total = attend(
        region_mix[:, :width],
        word_mix[:, width : 2 * width],
        word_mix[:, 2 * width :],
        cross_mask.T,
    )
    context = jnp.concatenate([word_context, region_context], axis=0)
    summed = rows_low.astype(jnp.float32) + matmul(context, outward_all[0]) + bias_rows[2]
    result, norm_stats = normalize(summed, gain_rows[0], bias_rows[9])
    return (result, (rows_low, mixed, context, word_total, region_total, norm_stats))


def cross_backward(grad_out, kept, weights, cross_mask, words_count):
    inward_all, outward_all, bias_rows, gain_rows = weights
    rows_low, mixed, context, word_total, region_total, norm_stats = kept
    width = rows_low.shape[1]
    grad_sum, grad_context, grad_outward, grad_bias_out, grad_gain, grad_shift = branch_back(
        grad_out, context, norm_stats, gain_rows[0], outward_all[0]
    )
    word_mix = mixed[:words_count]
    region_mix = mixed[words_count:]
    word_query_grad, region_key_grad, region_value_grad = attend_back(
        word_mix[:, :width],
        region_mix[:, width : 2 * width],
        region_mix[:, 2 * width :],
        cross_mask,
        word_total,
        grad_context[:words_count],
    )
    region_query_grad, word_key_grad, word_value_grad = attend_back(
        region_mix[:, :width],
        word_mix[:, width : 2 * width],
        word_mix[:, 2 * width :],
        cross_mask.T,
        region_total,
        grad_context[words_count:],
    )
    grad_parts = (
        jnp.concatenate([word_query_grad, region_query_grad], axis=0),
        jnp.concatenate([word_key_grad, region_key_grad], axis=0),
        jnp.concatenate([word_value_grad, region_value_grad], axis=0),
    )
    grad_rows, grad_inward, grad_bias_query, grad_bias_value = project_back(
        grad_sum, grad_parts, rows_low, inward_all[0]
    )
    return (
        grad_rows,
        grad_inward,
        grad_outward,
        (grad_bias_query, grad_bias_value, grad_bias_out),
        grad_gain,
        grad_shift,
    )


def gelu_exact(values):
    return jax.nn.gelu(values, approximate=False)


def feed_forward(rows_in, weights, feed_index, attend_set):
    expand_all, shrink_all, hidden_all = weights
    bias_rows, gain_rows = (attend_set[2], attend_set[3])
    rows_low = rows_in.astype(jnp.bfloat16)
    before = matmul(rows_low, expand_all[feed_index]) + hidden_all[feed_index].astype(jnp.float32)
    hidden = gelu_exact(before).astype(jnp.bfloat16)
    summed = rows_in + matmul(hidden, shrink_all[feed_index]) + bias_rows[14 + feed_index]
    result, norm_stats = normalize(summed, gain_rows[3 + feed_index], bias_rows[12 + feed_index])
    return (result, (rows_low, before, hidden, norm_stats))


def feed_backward(grad_out, kept, weights, feed_index, gain_rows):
    expand_all, shrink_all, hidden_all = weights
    rows_low, before, hidden, norm_stats = kept
    grad_sum, grad_gain, grad_shift = normalize_back(
        grad_out, norm_stats, gain_rows[3 + feed_index]
    )
    grad_branch = grad_sum.astype(jnp.bfloat16)
    grad_shrink = (hidden, grad_branch)
    grad_hidden = matmul_nt(grad_branch, shrink_all[feed_index])
    unused_value, slope_back = jax.vjp(gelu_exact, before)
    grad_before = slope_back(grad_hidden)[0].astype(jnp.bfloat16)
    grad_expand = (rows_low, grad_before)
    grad_rows = grad_sum + matmul_nt(grad_before, expand_all[feed_index])
    return (
        grad_rows,
        grad_expand,
        grad_shrink,
        column_sums(grad_before),
        column_sums(grad_branch),
        grad_gain,
        grad_shift,
    )


UNIT = 96
WIDE = 768
SLOTS = 4
ACC_SLOTS = 6
LAG_A = 2
LAG_B = 2
LAG_Z = 1


def grad_kernel(groups, *refs):
    count = len(groups)
    lefts = refs[:count]
    rights = refs[count : 2 * count]
    small_in = refs[2 * count]
    out, small_out = refs[2 * count + 1 : 2 * count + 3]
    (
        acc,
        core_out,
        core_in,
        half_out,
        half_in,
        full_out,
        full_in,
        plane,
        end_out,
        end_in,
        mid_out,
        mid_in,
        small_in_plane,
        small_planes,
        core_send,
        core_recv,
        half_send,
        half_recv,
        full_send,
        full_recv,
        z_send,
        z_recv,
        small_send,
        small_recv,
        free,
    ) = refs[2 * count + 3 :]
    me = lax.axis_index("fsdp")
    z = lax.axis_index("rep")
    chip = me // 2
    lane = me % 2
    is_end = jnp.logical_or(z == 0, z == 3)
    is_mid = jnp.logical_or(z == 1, z == 2)
    xor = lax.bitwise_xor
    core_peer = {"fsdp": xor(me, 1)}
    links = ({"fsdp": xor(me, 2)}, {"fsdp": xor(me, 4)})
    link_chip = (xor(chip, 1), xor(chip, 2))
    diagonal = xor(chip, 3)
    pair_peer = {"rep": xor(z, 1)}
    mid_peer = {"rep": 3 - z}
    total = sum(group[0] for group in groups)

    barrier = pltpu.get_barrier_semaphore()
    for offset in range(1, 8):
        pl.semaphore_signal(barrier, inc=1, device_id={"fsdp": xor(me, offset)}, device_id_type=MESH)
    for offset in range(1, 4):
        pl.semaphore_signal(barrier, inc=1, device_id={"rep": (z + offset) % 4}, device_id_type=MESH)
    pl.semaphore_wait(barrier, 10)

    def remote(src, dst, send_sem, recv_sem, peer):
        return pltpu.make_async_remote_copy(
            src_ref=src, dst_ref=dst, send_sem=send_sem, recv_sem=recv_sem, device_id=peer, device_id_type=MESH
        )

    def small_copy(offset):
        peer = xor(me, offset)
        return remote(
            small_in.at[peer],
            small_in_plane.at[offset - 1],
            small_send.at[offset - 1],
            small_recv.at[offset - 1],
            {"fsdp": peer},
        )

    def small_plane_copy(offset):
        return remote(
            small_planes.at[z],
            small_planes.at[z],
            small_send.at[6 + offset],
            small_recv.at[6 + offset],
            {"rep": (z + offset) % 4},
        )

    for offset in range(1, 8):
        small_copy(offset).start()

    def core_copy(u):
        slot = u % SLOTS
        return remote(core_out.at[slot], core_in.at[slot], core_send.at[slot], core_recv.at[slot], core_peer)

    def half_copy(u, way):
        slot = u % SLOTS
        return remote(
            half_out.at[slot, way], half_in.at[slot, way], half_send.at[slot, way], half_recv.at[slot, way], links[way]
        )

    def full_copy(u, way):
        slot = u % SLOTS
        return remote(
            full_out.at[slot, way], full_in.at[slot, way], full_send.at[slot, way], full_recv.at[slot, way], links[way]
        )

    def end_copy(u):
        slot = u % SLOTS
        return remote(end_out.at[slot], end_in.at[slot], z_send.at[0, slot], z_recv.at[0, slot], pair_peer)

    def mid_copy(u):
        slot = u % SLOTS
        return remote(mid_out.at[slot], mid_in.at[slot], z_send.at[1, slot], z_recv.at[1, slot], mid_peer)

    def back_copy(u):
        slot = u % SLOTS
        return remote(out.at[u], out.at[u], z_send.at[2, slot], z_recv.at[2, slot], pair_peer)

    def credit(u, channel, peer):
        @pl.when(u + SLOTS < total)
        def _():
            pl.semaphore_signal(free.at[channel], inc=1, device_id=peer, device_id_type=MESH)

    def spend(u, channel):
        @pl.when(u >= SLOTS)
        def _():
            pl.semaphore_wait(free.at[channel], 1)

    def produce(u):
        slot = u % SLOTS
        keep = u % ACC_SLOTS
        spend(u, 0)
        first = 0
        for index, (units, left_step, right_step) in enumerate(groups):
            start = first

            @pl.when(jnp.logical_and(u >= start, u < start + units))
            def _(index=index, start=start, left_step=left_step, right_step=right_step):
                at = u - start
                left_at = at * left_step
                column = pl.multiple_of(at * right_step * WIDE, WIDE)
                right = rights[index][:, pl.ds(column, WIDE)]
                other = jnp.dot(
                    lefts[index][left_at * 2 + 1 - lane], right, preferred_element_type=jnp.float32
                ).astype(jnp.bfloat16)
                for block in range(4):
                    core_out[slot, block] = other[block * UNIT : (block + 1) * UNIT]
                core_copy(u).start()
                own = jnp.dot(lefts[index][left_at * 2 + lane], right, preferred_element_type=jnp.float32)
                for block in range(4):
                    acc[keep, block] = own[block * UNIT : (block + 1) * UNIT]

            first = first + units

    def join_cores(u):
        slot = u % SLOTS
        keep = u % ACC_SLOTS
        core_copy(u).wait()
        for way in range(2):
            spend(u, 1 + way)
        summed = acc[keep, diagonal] + core_in[slot, diagonal].astype(jnp.float32)
        half_out[slot, 0] = summed[: UNIT // 2].astype(jnp.bfloat16)
        half_out[slot, 1] = summed[UNIT // 2 :].astype(jnp.bfloat16)
        for way in range(2):
            half_copy(u, way).start()
        for block in (link_chip[0], link_chip[1], chip):
            acc[keep, block] = acc[keep, block] + core_in[slot, block].astype(jnp.float32)
        credit(u, 0, core_peer)

    def join_diagonal(u):
        slot = u % SLOTS
        keep = u % ACC_SLOTS
        for way in range(2):
            half_copy(u, way).wait()
            spend(u, 3 + way)
        half = UNIT // 2
        full_out[slot, 1, :half] = (acc[keep, link_chip[1], :half] + half_in[slot, 0].astype(jnp.float32)).astype(
            jnp.bfloat16
        )
        full_out[slot, 1, half:] = acc[keep, link_chip[1], half:].astype(jnp.bfloat16)
        full_copy(u, 1).start()
        full_out[slot, 0, half:] = (acc[keep, link_chip[0], half:] + half_in[slot, 1].astype(jnp.float32)).astype(
            jnp.bfloat16
        )
        full_out[slot, 0, :half] = acc[keep, link_chip[0], :half].astype(jnp.bfloat16)
        full_copy(u, 0).start()
        for way in range(2):
            credit(u, 1 + way, links[way])

    def join_plane(u):
        slot = u % SLOTS
        keep = u % ACC_SLOTS
        for way in range(2):
            full_copy(u, way).wait()
        summed = acc[keep, chip] + (full_in[slot, 0].astype(jnp.float32) + full_in[slot, 1].astype(jnp.float32))

        @pl.when(is_end)
        def _():
            spend(u, 5)
            end_out[slot] = summed.astype(jnp.bfloat16)
            end_copy(u).start()

        @pl.when(is_mid)
        def _():
            plane[slot] = summed

        for way in range(2):
            credit(u, 3 + way, links[way])

    def join_pair(u):
        slot = u % SLOTS

        @pl.when(is_end)
        def _():
            end_copy(u).wait_send()

        @pl.when(is_mid)
        def _():
            end_copy(u).wait_recv()
            spend(u, 6)
            mid_out[slot] = (plane[slot] + end_in[slot].astype(jnp.float32)).astype(jnp.bfloat16)
            mid_copy(u).start()
            credit(u, 5, pair_peer)

    def join_middle(u):
        slot = u % SLOTS

        @pl.when(is_mid)
        def _():
            mid_copy(u).wait()
            out[u] = (mid_out[slot].astype(jnp.float32) + mid_in[slot].astype(jnp.float32)).astype(jnp.bfloat16)
            back_copy(u).start()
            credit(u, 6, mid_peer)

    def finish(u):
        @pl.when(is_mid)
        def _():
            back_copy(u).wait_send()

        @pl.when(is_end)
        def _():
            back_copy(u).wait_recv()

    stages = [
        (0, produce),
        (1, join_cores),
        (1 + LAG_A, join_diagonal),
        (1 + LAG_A + LAG_B, join_plane),
        (1 + LAG_A + LAG_B + LAG_Z, join_pair),
        (1 + LAG_A + LAG_B + 2 * LAG_Z, join_middle),
        (1 + LAG_A + LAG_B + 3 * LAG_Z, finish),
    ]

    def step(i, carry):
        for lag, stage in reversed(stages):

            @pl.when(jnp.logical_and(i >= lag, i < total + lag))
            def _(lag=lag, stage=stage):
                stage(i - lag)

        @pl.when(i == 2)
        def _():
            summed = small_in[me]
            for offset in range(1, 8):
                small_copy(offset).wait()
                summed = summed + small_in_plane[offset - 1]
            small_planes[z] = summed
            for offset in range(1, 4):
                small_plane_copy(offset).start()

        @pl.when(i == 4)
        def _():
            for offset in range(1, 4):
                small_plane_copy(offset).wait_send()
            for offset in range(1, 4):
                source = (z + 4 - offset) % 4
                remote(
                    small_planes.at[source],
                    small_planes.at[source],
                    small_send.at[6 + offset],
                    small_recv.at[6 + offset],
                    {"rep": source},
                ).wait_recv()
            small_out[...] = small_planes[0] + small_planes[1] + (small_planes[2] + small_planes[3])

        return carry

    lax.fori_loop(0, total + stages[-1][0], step, 0)


def sum_grads(groups, lefts, rights, small):
    total = sum(group[0] for group in groups)
    block = (UNIT, WIDE)
    low = jnp.bfloat16
    dma = pltpu.SemaphoreType.DMA
    vmem = pl.BlockSpec(memory_space=pltpu.VMEM)
    return pl.pallas_call(
        functools.partial(grad_kernel, groups),
        out_shape=(
            jax.ShapeDtypeStruct((total,) + block, low),
            jax.ShapeDtypeStruct(small.shape[1:], jnp.float32),
        ),
        in_specs=[vmem] * (2 * len(groups) + 1),
        out_specs=(vmem, vmem),
        scratch_shapes=[
            pltpu.VMEM((ACC_SLOTS, 4) + block, jnp.float32),
            pltpu.VMEM((SLOTS, 4) + block, low),
            pltpu.VMEM((SLOTS, 4) + block, low),
            pltpu.VMEM((SLOTS, 2, UNIT // 2, WIDE), low),
            pltpu.VMEM((SLOTS, 2, UNIT // 2, WIDE), low),
            pltpu.VMEM((SLOTS, 2) + block, low),
            pltpu.VMEM((SLOTS, 2) + block, low),
            pltpu.VMEM((SLOTS,) + block, jnp.float32),
            pltpu.VMEM((SLOTS,) + block, low),
            pltpu.VMEM((SLOTS,) + block, low),
            pltpu.VMEM((SLOTS,) + block, low),
            pltpu.VMEM((SLOTS,) + block, low),
            pltpu.VMEM((7,) + small.shape[1:], jnp.float32),
            pltpu.VMEM((4,) + small.shape[1:], jnp.float32),
            dma((SLOTS,)),
            dma((SLOTS,)),
            dma((SLOTS, 2)),
            dma((SLOTS, 2)),
            dma((SLOTS, 2)),
            dma((SLOTS, 2)),
            dma((3, SLOTS)),
            dma((3, SLOTS)),
            dma((10,)),
            dma((10,)),
            pltpu.SemaphoreType.REGULAR((7,)),
        ],
        compiler_params=pltpu.CompilerParams(
            collective_id=0, has_side_effects=True, vmem_limit_bytes=60 * 2**20
        ),
    )(*lefts, *rights, small)


def lanes(rows_low):
    count = rows_low.shape[0]
    return rows_low.reshape(count, 4, 2, UNIT).transpose(2, 1, 3, 0).reshape(2, 4 * UNIT, count)


def hidden_lanes(hidden):
    count = hidden.shape[0]
    return hidden.reshape(count, 4, 2, 4, UNIT).transpose(3, 2, 1, 4, 0).reshape(8, 4 * UNIT, count)


def local(
    devices,
    replicas,
    word_rows,
    region_rows,
    word_segment,
    region_segment,
    inward,
    outward,
    biases,
    norm_gain,
    expand_weight,
    shrink_weight,
    hidden_bias,
    word_cotangent,
    region_cotangent,
):
    words_count = word_rows.shape[0]
    width = word_rows.shape[1]
    word_ids = word_segment[0]
    region_ids = region_segment[0]
    cross_mask = word_ids[:, None] == region_ids[None, :]
    word_mask = word_ids[:, None] == word_ids[None, :]
    region_mask = region_ids[:, None] == region_ids[None, :]
    shard = biases.shape[1]
    per_shard = hidden_bias.shape[1] // shard
    small_shard = jnp.concatenate([biases, norm_gain, hidden_bias.reshape(2 * per_shard, shard)], axis=0)
    small_all = lax.all_gather(small_shard, "fsdp", axis=0)
    bias_count = biases.shape[0]
    gain_count = norm_gain.shape[0]
    row_params = small_all[:, : bias_count + gain_count].transpose(1, 0, 2).reshape(bias_count + gain_count, width)
    hidden_all = (
        small_all[:, bias_count + gain_count :]
        .reshape(devices, 2, per_shard * shard)
        .transpose(1, 0, 2)
        .reshape(2, devices * per_shard * shard)
    )
    inward_all, outward_all = (
        lax.all_gather(inward, "fsdp", axis=1, tiled=True),
        lax.all_gather(outward, "fsdp", axis=1, tiled=True),
    )
    attend_set = (
        inward_all,
        outward_all,
        row_params[:bias_count].astype(jnp.float32),
        row_params[bias_count:].astype(jnp.float32),
    )
    crossed, cross_kept = cross_forward(word_rows, region_rows, attend_set, cross_mask)
    word_one, word_kept = self_forward(crossed[:words_count], attend_set, 1, word_mask)
    region_one, region_kept = self_forward(crossed[words_count:], attend_set, 2, region_mask)
    expand_all, shrink_all = (
        lax.all_gather(expand_weight, "fsdp", axis=1, tiled=True),
        lax.all_gather(shrink_weight, "fsdp", axis=1, tiled=True),
    )
    feed_set = (expand_all, shrink_all, hidden_all)
    word_two, word_feed = feed_forward(word_one, feed_set, 0, attend_set)
    region_two, region_feed = feed_forward(region_one, feed_set, 1, attend_set)
    word_back = feed_backward(word_cotangent.astype(jnp.float32), word_feed, feed_set, 0, attend_set[3])
    region_back = feed_backward(region_cotangent.astype(jnp.float32), region_feed, feed_set, 1, attend_set[3])
    word_self = self_backward(word_back[0], word_kept, attend_set, 1, word_mask)
    region_self = self_backward(region_back[0], region_kept, attend_set, 2, region_mask)
    grad_crossed = jnp.concatenate([word_self[0], region_self[0]], axis=0)
    cross_back = cross_backward(grad_crossed, cross_kept, attend_set, cross_mask, words_count)
    row_grads = jnp.stack(
        [
            cross_back[3][0],
            cross_back[3][1],
            cross_back[3][2],
            word_self[3][0],
            word_self[3][1],
            word_self[3][2],
            region_self[3][0],
            region_self[3][1],
            region_self[3][2],
            cross_back[5],
            word_self[5],
            region_self[5],
            word_back[6],
            region_back[6],
            word_back[4],
            region_back[4],
            cross_back[4],
            word_self[4],
            region_self[4],
            word_back[5],
            region_back[5],
        ]
    )
    hidden_grads = jnp.stack([word_back[3], region_back[3]])
    small_grads = jnp.concatenate(
        [
            row_grads.reshape(bias_count + gain_count, devices, shard).transpose(1, 0, 2),
            hidden_grads.reshape(2, devices, per_shard, shard)
            .transpose(1, 0, 2, 3)
            .reshape(devices, 2 * per_shard, shard),
        ],
        axis=1,
    )
    rows_small = small_grads.shape[1]
    if devices == 8 and replicas == 4:
        groups = ((4, 1, 0), (4, 1, 0), (4, 0, 1), (4, 0, 1), (1, 0, 0), (1, 0, 0), (3, 0, 1), (3, 0, 1), (1, 0, 0), (3, 0, 1))
        pairs = [
            word_back[2],
            region_back[2],
            word_back[1],
            region_back[1],
            word_self[2],
            region_self[2],
            word_self[1],
            region_self[1],
            cross_back[2],
            cross_back[1],
        ]
        lefts = [hidden_lanes(pair[0]) if i < 2 else lanes(pair[0]) for i, pair in enumerate(pairs)]
        rights = [pair[1] for pair in pairs]
        padded = jnp.pad(small_grads, ((0, 0), (0, 32 - rows_small), (0, 128 - shard)))
        units, small_total = sum_grads(groups, lefts, rights, padded)
        units = units.astype(jnp.float32)
        small_total = small_total[:rows_small, :shard]
        shrink_total = units[:8].reshape(2, 4 * UNIT, WIDE)
        expand_total = units[8:16].reshape(2, 4, UNIT, WIDE).transpose(0, 2, 1, 3).reshape(2, UNIT, 4 * WIDE)
        outward_total = jnp.stack([units[24], units[16], units[17]])
        inward_total = (
            jnp.stack([units[25:28], units[18:21], units[21:24]]).transpose(0, 2, 1, 3).reshape(3, UNIT, 3 * WIDE)
        )
    else:

        def reduced(products, axis):
            mine = lax.psum_scatter(jnp.stack(products), "fsdp", scatter_dimension=axis, tiled=True)
            return lax.psum(mine.astype(jnp.bfloat16), "rep").astype(jnp.float32)

        shrink_total = reduced([matmul_tn(*word_back[2]), matmul_tn(*region_back[2])], 1)
        expand_total = reduced([matmul_tn(*word_back[1]), matmul_tn(*region_back[1])], 1)
        outward_total = reduced([matmul_tn(*cross_back[2]), matmul_tn(*word_self[2]), matmul_tn(*region_self[2])], 1)
        inward_total = reduced([matmul_tn(*cross_back[1]), matmul_tn(*word_self[1]), matmul_tn(*region_self[1])], 1)
        small_total = lax.psum(lax.psum_scatter(small_grads, "fsdp", scatter_dimension=0, tiled=False), "rep")
    grad_rows = cross_back[0]
    return (
        word_two.astype(jnp.bfloat16),
        region_two.astype(jnp.bfloat16),
        grad_rows[:words_count],
        grad_rows[words_count:],
        inward_total,
        outward_total,
        small_total[:bias_count],
        small_total[bias_count : bias_count + gain_count],
        expand_total,
        shrink_total,
        small_total[bias_count + gain_count :].reshape(2, per_shard * shard),
    )


def solution(mesh):
    return jax.shard_map(
        functools.partial(local, mesh.shape["fsdp"], mesh.shape["rep"]),
        mesh=mesh,
        in_specs=(
            P(("rep", "fsdp"), None),
            P(("rep", "fsdp"), None),
            P(("rep", "fsdp"), None),
            P(("rep", "fsdp"), None),
            P(None, "fsdp", None),
            P(None, "fsdp", None),
            P(None, "fsdp"),
            P(None, "fsdp"),
            P(None, "fsdp", None),
            P(None, "fsdp", None),
            P(None, "fsdp"),
            P(("rep", "fsdp"), None),
            P(("rep", "fsdp"), None),
        ),
        out_specs=(
            P(("rep", "fsdp"), None),
            P(("rep", "fsdp"), None),
            P(("rep", "fsdp"), None),
            P(("rep", "fsdp"), None),
            P(None, "fsdp", None),
            P(None, "fsdp", None),
            P(None, "fsdp"),
            P(None, "fsdp"),
            P(None, "fsdp", None),
            P(None, "fsdp", None),
            P(None, "fsdp"),
        ),
        check_vma=False,
    )
```

```python
import functools

import jax
import jax.numpy as jnp
from jax import lax
from jax.experimental import pallas as pl
from jax.experimental.pallas import tpu as pltpu
from jax.sharding import PartitionSpec as P

MESH = pl.DeviceIdType.MESH

HEADS = 12
HEAD_DIM = 64


norm_epsilon = 1e-12
masked_score = -1e30


def matmul(left_op, right_op):
    return jnp.dot(left_op, right_op, preferred_element_type=jnp.float32)


def matmul_tn(left_op, right_op):
    return lax.dot_general(
        left_op, right_op, (((0,), (0,)), ((), ())), preferred_element_type=jnp.float32
    )


def matmul_nt(left_op, right_op):
    return lax.dot_general(
        left_op, right_op, (((1,), (1,)), ((), ())), preferred_element_type=jnp.float32
    )


def column_sums(values):
    return jnp.sum(values, axis=0, dtype=jnp.float32)


def heads_of(rows_in):
    return rows_in.reshape(rows_in.shape[0], HEADS, HEAD_DIM)


def merge_heads(head_rows):
    return head_rows.reshape(head_rows.shape[0], -1)


def normalize(summed, gain_row, shift_row):
    center = summed - jnp.mean(summed, axis=-1, keepdims=True)
    inverse = lax.rsqrt(jnp.mean(center * center, axis=-1, keepdims=True) + norm_epsilon)
    normed = center * inverse
    return (normed * gain_row + shift_row, (normed, inverse))


def normalize_back(grad_out, norm_stats, gain_row):
    normed, inverse = norm_stats
    grad_normed = grad_out * gain_row
    grad_sum = inverse * (
        grad_normed
        - jnp.mean(grad_normed, axis=-1, keepdims=True)
        - normed * jnp.mean(grad_normed * normed, axis=-1, keepdims=True)
    )
    return (grad_sum, column_sums(grad_out * normed), column_sums(grad_out))


def score_block(queries, key_rows, allowed):
    scores = jnp.einsum(
        "qhd,khd->hqk", heads_of(queries), heads_of(key_rows), preferred_element_type=jnp.float32
    ) * HEAD_DIM ** (-0.5)
    return jnp.where(allowed[None], scores, masked_score)


def attend(queries, key_rows, value_rows, allowed):
    scores = score_block(queries, key_rows, allowed)
    top_score = jnp.max(scores, axis=-1, keepdims=True)
    log_total = top_score + jnp.log(jnp.sum(jnp.exp(scores - top_score), axis=-1, keepdims=True))
    shares = jnp.exp(scores - log_total).astype(jnp.bfloat16)
    context = jnp.einsum(
        "hqk,khd->qhd", shares, heads_of(value_rows), preferred_element_type=jnp.float32
    )
    return (merge_heads(context).astype(jnp.bfloat16), log_total)


def attend_back(queries, key_rows, value_rows, allowed, log_total, grad_context):
    shares = jnp.exp(score_block(queries, key_rows, allowed) - log_total)
    grad_heads = heads_of(grad_context)
    grad_shares = jnp.einsum(
        "qhd,khd->hqk", grad_heads, heads_of(value_rows), preferred_element_type=jnp.float32
    )
    grad_values = jnp.einsum(
        "hqk,qhd->khd", shares.astype(jnp.bfloat16), grad_heads, preferred_element_type=jnp.float32
    )
    grad_scores = (
        shares * (grad_shares - jnp.sum(shares * grad_shares, axis=-1, keepdims=True))
    ).astype(jnp.bfloat16)
    score_scale = HEAD_DIM ** (-0.5)
    grad_queries = (
        jnp.einsum(
            "hqk,khd->qhd", grad_scores, heads_of(key_rows), preferred_element_type=jnp.float32
        )
        * score_scale
    )
    grad_keys = (
        jnp.einsum(
            "hqk,qhd->khd", grad_scores, heads_of(queries), preferred_element_type=jnp.float32
        )
        * score_scale
    )
    return (merge_heads(grad_queries), merge_heads(grad_keys), merge_heads(grad_values))


def project(rows_low, weight, bias_rows, module):
    width = weight.shape[0]
    bias_all = jnp.concatenate(
        [bias_rows[3 * module], jnp.zeros((width,), jnp.float32), bias_rows[3 * module + 1]]
    )
    return (matmul(rows_low, weight) + bias_all).astype(jnp.bfloat16)


def project_back(grad_sum, grad_parts, rows_low, weight):
    width = weight.shape[0]
    grad_mixed = jnp.concatenate(grad_parts, axis=1).astype(jnp.bfloat16)
    grad_weight = (rows_low, grad_mixed)
    grad_bias = column_sums(grad_mixed)
    grad_rows = grad_sum + matmul_nt(grad_mixed, weight)
    return (grad_rows, grad_weight, grad_bias[:width], grad_bias[2 * width :])


def branch_back(grad_out, context, norm_stats, gain_row, outward_one):
    grad_sum, grad_gain, grad_shift = normalize_back(grad_out, norm_stats, gain_row)
    grad_branch = grad_sum.astype(jnp.bfloat16)
    grad_outward = (context, grad_branch)
    grad_context = matmul_nt(grad_branch, outward_one).astype(jnp.bfloat16)
    return (grad_sum, grad_context, grad_outward, column_sums(grad_branch), grad_gain, grad_shift)


def self_forward(rows_in, weights, module, allowed):
    inward_all, outward_all, bias_rows, gain_rows = weights
    width = rows_in.shape[1]
    rows_low = rows_in.astype(jnp.bfloat16)
    mixed = project(rows_low, inward_all[module], bias_rows, module)
    context, log_total = attend(
        mixed[:, :width], mixed[:, width : 2 * width], mixed[:, 2 * width :], allowed
    )
    summed = rows_in + matmul(context, outward_all[module]) + bias_rows[3 * module + 2]
    result, norm_stats = normalize(summed, gain_rows[module], bias_rows[9 + module])
    return (result, (rows_low, mixed, context, log_total, norm_stats))


def self_backward(grad_out, kept, weights, module, allowed):
    inward_all, outward_all, bias_rows, gain_rows = weights
    rows_low, mixed, context, log_total, norm_stats = kept
    width = rows_low.shape[1]
    grad_sum, grad_context, grad_outward, grad_bias_out, grad_gain, grad_shift = branch_back(
        grad_out, context, norm_stats, gain_rows[module], outward_all[module]
    )
    grad_parts = attend_back(
        mixed[:, :width],
        mixed[:, width : 2 * width],
        mixed[:, 2 * width :],
        allowed,
        log_total,
        grad_context,
    )
    grad_rows, grad_inward, grad_bias_query, grad_bias_value = project_back(
        grad_sum, grad_parts, rows_low, inward_all[module]
    )
    return (
        grad_rows,
        grad_inward,
        grad_outward,
        (grad_bias_query, grad_bias_value, grad_bias_out),
        grad_gain,
        grad_shift,
    )


def cross_forward(word_rows, region_rows, weights, cross_mask):
    inward_all, outward_all, bias_rows, gain_rows = weights
    words_count = word_rows.shape[0]
    width = word_rows.shape[1]
    rows_low = jnp.concatenate([word_rows, region_rows], axis=0)
    mixed = project(rows_low, inward_all[0], bias_rows, 0)
    word_mix = mixed[:words_count]
    region_mix = mixed[words_count:]
    word_context, word_total = attend(
        word_mix[:, :width],
        region_mix[:, width : 2 * width],
        region_mix[:, 2 * width :],
        cross_mask,
    )
    region_context, region_total = attend(
        region_mix[:, :width],
        word_mix[:, width : 2 * width],
        word_mix[:, 2 * width :],
        cross_mask.T,
    )
    context = jnp.concatenate([word_context, region_context], axis=0)
    summed = rows_low.astype(jnp.float32) + matmul(context, outward_all[0]) + bias_rows[2]
    result, norm_stats = normalize(summed, gain_rows[0], bias_rows[9])
    return (result, (rows_low, mixed, context, word_total, region_total, norm_stats))


def cross_backward(grad_out, kept, weights, cross_mask, words_count):
    inward_all, outward_all, bias_rows, gain_rows = weights
    rows_low, mixed, context, word_total, region_total, norm_stats = kept
    width = rows_low.shape[1]
    grad_sum, grad_context, grad_outward, grad_bias_out, grad_gain, grad_shift = branch_back(
        grad_out, context, norm_stats, gain_rows[0], outward_all[0]
    )
    word_mix = mixed[:words_count]
    region_mix = mixed[words_count:]
    word_query_grad, region_key_grad, region_value_grad = attend_back(
        word_mix[:, :width],
        region_mix[:, width : 2 * width],
        region_mix[:, 2 * width :],
        cross_mask,
        word_total,
        grad_context[:words_count],
    )
    region_query_grad, word_key_grad, word_value_grad = attend_back(
        region_mix[:, :width],
        word_mix[:, width : 2 * width],
        word_mix[:, 2 * width :],
        cross_mask.T,
        region_total,
        grad_context[words_count:],
    )
    grad_parts = (
        jnp.concatenate([word_query_grad, region_query_grad], axis=0),
        jnp.concatenate([word_key_grad, region_key_grad], axis=0),
        jnp.concatenate([word_value_grad, region_value_grad], axis=0),
    )
    grad_rows, grad_inward, grad_bias_query, grad_bias_value = project_back(
        grad_sum, grad_parts, rows_low, inward_all[0]
    )
    return (
        grad_rows,
        grad_inward,
        grad_outward,
        (grad_bias_query, grad_bias_value, grad_bias_out),
        grad_gain,
        grad_shift,
    )


def gelu_exact(values):
    return jax.nn.gelu(values, approximate=False)


def feed_forward(rows_in, weights, feed_index, attend_set):
    expand_all, shrink_all, hidden_all = weights
    bias_rows, gain_rows = (attend_set[2], attend_set[3])
    rows_low = rows_in.astype(jnp.bfloat16)
    before = matmul(rows_low, expand_all[feed_index]) + hidden_all[feed_index].astype(jnp.float32)
    hidden = gelu_exact(before).astype(jnp.bfloat16)
    summed = rows_in + matmul(hidden, shrink_all[feed_index]) + bias_rows[14 + feed_index]
    result, norm_stats = normalize(summed, gain_rows[3 + feed_index], bias_rows[12 + feed_index])
    return (result, (rows_low, before, hidden, norm_stats))


def feed_backward(grad_out, kept, weights, feed_index, gain_rows):
    expand_all, shrink_all, hidden_all = weights
    rows_low, before, hidden, norm_stats = kept
    grad_sum, grad_gain, grad_shift = normalize_back(
        grad_out, norm_stats, gain_rows[3 + feed_index]
    )
    grad_branch = grad_sum.astype(jnp.bfloat16)
    grad_shrink = (hidden, grad_branch)
    grad_hidden = matmul_nt(grad_branch, shrink_all[feed_index])
    unused_value, slope_back = jax.vjp(gelu_exact, before)
    grad_before = slope_back(grad_hidden)[0].astype(jnp.bfloat16)
    grad_expand = (rows_low, grad_before)
    grad_rows = grad_sum + matmul_nt(grad_before, expand_all[feed_index])
    return (
        grad_rows,
        grad_expand,
        grad_shrink,
        column_sums(grad_before),
        column_sums(grad_branch),
        grad_gain,
        grad_shift,
    )


UNIT = 96
WIDE = 768
SLOTS = 4
ACC_SLOTS = 6
LAG_A = 2
LAG_B = 2
LAG_Z = 1


WORDS = 128
REGIONS = 256
ROWS = 384
HIDDEN = 3072
PAIRS_OF_HEADS = 6
PAIR_WIDE = 128


def flip(position, bits):
    return lax.bitwise_xor(position, bits)


def dot_nt(left, right):
    return lax.dot_general(left, right, (((1,), (1,)), ((), ())), preferred_element_type=jnp.float32)


def dot_tn(left, right):
    return lax.dot_general(left, right, (((0,), (0,)), ((), ())), preferred_element_type=jnp.float32)


def spread(part):
    source = lax.broadcasted_iota(jnp.int32, (128, WIDE), 0)
    target = lax.broadcasted_iota(jnp.int32, (128, WIDE), 1)
    return jnp.logical_and(source < UNIT, target == source + part * UNIT)


def half_lanes():
    lane = lax.broadcasted_iota(jnp.int32, (1, PAIR_WIDE), 1)
    return (lane < HEAD_DIM, lane >= HEAD_DIM)


def only(values, chosen):
    return jnp.where(chosen, values, jnp.zeros_like(values))


ATTEND_CROSS_WORD = ((0, WORDS), (WORDS, REGIONS))
ATTEND_CROSS_REGION = ((WORDS, REGIONS), (0, WORDS))
ATTEND_WORD = ((0, WORDS), (0, WORDS))
ATTEND_REGION = ((WORDS, REGIONS), (WORDS, REGIONS))


def attend_into(rows_of, mixed, allowed, shares, context):
    (query_at, query_count), (key_at, key_count) = rows_of
    blocked = jnp.where(allowed, 0.0, masked_score)

    def pair(p, carry):
        at = pl.multiple_of(p * PAIR_WIDE, PAIR_WIDE)
        queries = mixed[pl.ds(query_at, query_count), pl.ds(at, PAIR_WIDE)]
        key_rows = mixed[pl.ds(key_at, key_count), pl.ds(WIDE + at, PAIR_WIDE)]
        value_rows = mixed[pl.ds(key_at, key_count), pl.ds(2 * WIDE + at, PAIR_WIDE)]
        total = jnp.zeros((query_count, PAIR_WIDE), jnp.float32)
        for side, chosen in enumerate(half_lanes()):
            scores = dot_nt(only(queries, chosen), key_rows) * HEAD_DIM ** (-0.5) + blocked
            lifted = jnp.exp(scores - jnp.max(scores, axis=-1, keepdims=True))
            share = (lifted / jnp.sum(lifted, axis=-1, keepdims=True)).astype(jnp.bfloat16)
            shares[2 * p + side] = share
            total = total + matmul(share, only(value_rows, chosen))
        context[pl.ds(query_at, query_count), pl.ds(at, PAIR_WIDE)] = total.astype(jnp.bfloat16)
        return carry

    lax.fori_loop(0, PAIRS_OF_HEADS, pair, 0)


def row_norm(summed):
    center = summed - jnp.mean(summed, axis=-1, keepdims=True)
    inverse = lax.rsqrt(jnp.mean(center * center, axis=-1, keepdims=True) + norm_epsilon)
    return (center * inverse, inverse)


def forward_kernel(*refs):
    (
        rows_low,
        word_across,
        region_across,
        word_down,
        region_down,
        small,
        inward,
        outward,
        expand,
        shrink,
        result,
        params,
        hidden_rows,
        mixed_cross,
        mixed_self,
        shares_cw,
        shares_cr,
        shares_w,
        shares_r,
        context_cross_t,
        context_self_t,
        rows_zero_t,
        rows_one_t,
        rows_two_t,
        hidden_t,
        slope,
        normed,
        inverse,
        inward_out,
        outward_out,
        expand_out,
        shrink_out,
        inward_all,
        outward_all,
        expand_all,
        shrink_all,
        small_all,
        stream,
        stream_low,
        context,
        hidden,
        sends,
        recvs,
        small_sends,
        small_recvs,
        local_sems,
    ) = refs
    me = lax.axis_index("fsdp")
    peers = {"x": {"fsdp": flip(me, 2)}, "y": {"fsdp": flip(me, 4)}, "core": {"fsdp": flip(me, 1)}}

    barrier = pltpu.get_barrier_semaphore()
    for offset in range(1, 8):
        pl.semaphore_signal(barrier, inc=1, device_id={"fsdp": flip(me, offset)}, device_id_type=MESH)
    pl.semaphore_wait(barrier, 7)

    def remote(src, dst, send_sem, recv_sem, peer):
        return pltpu.make_async_remote_copy(
            src_ref=src, dst_ref=dst, send_sem=send_sem, recv_sem=recv_sem, device_id=peer, device_id_type=MESH
        )

    def small_copy(offset, owner):
        return remote(
            small_all.at[owner],
            small_all.at[owner],
            small_sends.at[offset - 1],
            small_recvs.at[offset - 1],
            {"fsdp": flip(me, offset)},
        )

    small_all[me] = small[...]
    for offset in range(1, 8):
        small_copy(offset, me).start()

    chunks = [
        (inward, inward_all, 0, 0, UNIT, 0, 3 * WIDE),
        (outward, outward_all, 0, 0, UNIT, 0, WIDE),
        (inward, inward_all, 1, 0, UNIT, 0, 3 * WIDE),
        (inward, inward_all, 2, 0, UNIT, 0, 3 * WIDE),
        (outward, outward_all, 1, 0, UNIT, 0, WIDE),
        (outward, outward_all, 2, 0, UNIT, 0, WIDE),
        (expand, expand_all, 0, 0, UNIT, 0, 2 * WIDE),
        (expand, expand_all, 0, 0, UNIT, 2 * WIDE, 2 * WIDE),
        (expand, expand_all, 1, 0, UNIT, 0, 2 * WIDE),
        (expand, expand_all, 1, 0, UNIT, 2 * WIDE, 2 * WIDE),
        (shrink, shrink_all, 0, 0, 2 * UNIT, 0, WIDE),
        (shrink, shrink_all, 0, 2 * UNIT, 2 * UNIT, 0, WIDE),
        (shrink, shrink_all, 1, 0, 2 * UNIT, 0, WIDE),
        (shrink, shrink_all, 1, 2 * UNIT, 2 * UNIT, 0, WIDE),
    ]

    def own_part(k):
        source, _, matrix, first, count, column, columns = chunks[k]
        return source.at[matrix, pl.ds(first, count), pl.ds(column, columns)]

    def part(k, owner, half=None):
        source, gathered, matrix, first, count, column, columns = chunks[k]
        start = owner * source.shape[1] + first
        if half is not None:
            count = count // 2
            start = start + half * count
        return gathered.at[matrix, pl.ds(pl.multiple_of(start, 16), count), pl.ds(column, columns)]

    X, Y, DIAG_Y, DIAG_X, CORE_OWN, CORE_X, CORE_Y, CORE_DIAG = range(8)

    def copy(k, kind):
        owner, half, peer = {
            X: (me, None, "x"),
            Y: (me, None, "y"),
            DIAG_Y: (flip(me, 2), 0, "y"),
            DIAG_X: (flip(me, 4), 1, "x"),
            CORE_OWN: (me, None, "core"),
            CORE_X: (flip(me, 2), None, "core"),
            CORE_Y: (flip(me, 4), None, "core"),
            CORE_DIAG: (flip(me, 6), None, "core"),
        }[kind]
        source = own_part(k) if kind in (X, Y, CORE_OWN) else part(k, owner, half)
        return remote(source, part(k, owner, half), sends.at[k, kind], recvs.at[k, kind], peers[peer])

    def arrival(k, kind):
        owner, half, peer = {
            X: (flip(me, 2), None, "x"),
            Y: (flip(me, 4), None, "y"),
            DIAG_Y: (flip(me, 6), 0, "y"),
            DIAG_X: (flip(me, 6), 1, "x"),
            CORE_OWN: (flip(me, 1), None, "core"),
            CORE_X: (flip(me, 3), None, "core"),
            CORE_Y: (flip(me, 5), None, "core"),
            CORE_DIAG: (flip(me, 7), None, "core"),
        }[kind]
        here = part(k, owner, half)
        return remote(here, here, sends.at[k, kind], recvs.at[k, kind], peers[peer])

    def own_local(k):
        return pltpu.make_async_copy(own_part(k), part(k, me), local_sems.at[k])

    def start_own(k):
        own_local(k).start()
        for kind in (X, Y, CORE_OWN):
            copy(k, kind).start()

    def forward_first(k):
        arrival(k, X).wait_recv()
        copy(k, DIAG_Y).start()
        copy(k, CORE_X).start()
        arrival(k, Y).wait_recv()
        copy(k, DIAG_X).start()
        copy(k, CORE_Y).start()

    def forward_second(k):
        arrival(k, DIAG_Y).wait_recv()
        arrival(k, DIAG_X).wait_recv()
        copy(k, CORE_DIAG).start()

    def complete(k):
        own_local(k).wait()
        for kind in (CORE_OWN, CORE_X, CORE_Y, CORE_DIAG):
            arrival(k, kind).wait_recv()

    keeps = []

    def keep(source, target):
        saved = pltpu.make_async_copy(source, target, local_sems.at[len(chunks) + len(keeps)])
        saved.start()
        keeps.append(saved)

    def read_small():
        for offset in range(1, 8):
            small_copy(offset, flip(me, offset)).wait_recv()
        totals = jnp.zeros((21, WIDE), jnp.float32)
        hidden_parts = [[jnp.zeros((1, WIDE), jnp.float32) for _ in range(4)] for _ in range(2)]
        for owner in range(8):
            own = small_all[owner]
            totals = totals + matmul(own, spread(owner).astype(jnp.bfloat16))[:21]
            for q in range(4):
                placed = matmul(own, spread((owner % 2) * 4 + q).astype(jnp.bfloat16))
                for f in range(2):
                    row = 21 + 4 * f + q
                    hidden_parts[f][owner // 2] = hidden_parts[f][owner // 2] + placed[row : row + 1]
        params[0:21, :] = totals
        for f in range(2):
            for block in range(4):
                hidden_rows[f : f + 1, block * WIDE : (block + 1) * WIDE] = hidden_parts[f][block]

    def transposed_into(target, values, at, count):
        target[:, pl.ds(at, count)] = values.T

    def project_into(source, at, count, module, mixed):
        for third, bias_row in enumerate((3 * module, None, 3 * module + 1)):
            product = matmul(source[pl.ds(at, count), :], inward_all[module, :, third * WIDE : (third + 1) * WIDE])
            if bias_row is not None:
                product = product + params[bias_row : bias_row + 1, :]
            mixed[pl.ds(at, count), third * WIDE : (third + 1) * WIDE] = product.astype(jnp.bfloat16)

    def join(at, weights, left, residual, bias_row, norm_at, norm_index):
        rows = pl.ds(at, 128)
        summed = residual + matmul(left[rows, :], weights) + params[bias_row : bias_row + 1, :]
        unit, scale = row_norm(summed)
        normed[norm_at, rows, :] = unit
        inverse[norm_at, rows, :] = jnp.broadcast_to(scale, (128, 128))
        return unit * params[16 + norm_index : 17 + norm_index, :] + params[9 + norm_index : 10 + norm_index, :]

    def cross_in():
        project_into(rows_low, 0, ROWS, 0, mixed_cross)
        attend_into(ATTEND_CROSS_WORD, mixed_cross, word_down[...] == region_across[...], shares_cw, context)
        attend_into(ATTEND_CROSS_REGION, mixed_cross, region_down[...] == word_across[...], shares_cr, context)
        for at in range(0, ROWS, 128):
            transposed_into(rows_zero_t, rows_low[at : at + 128, :], at, 128)
            transposed_into(context_cross_t, context[at : at + 128, :], at, 128)

    def cross_out():
        for at in range(0, ROWS, 128):
            one = join(at, outward_all[0], context, rows_low[at : at + 128, :].astype(jnp.float32), 2, 0, 0)
            stream[at : at + 128, :] = one
            one_low = one.astype(jnp.bfloat16)
            stream_low[at : at + 128, :] = one_low
            transposed_into(rows_one_t, one_low, at, 128)

    def word_in():
        project_into(stream_low, 0, WORDS, 1, mixed_self)
        attend_into(ATTEND_WORD, mixed_self, word_down[...] == word_across[...], shares_w, context)
        transposed_into(context_self_t, context[0:WORDS, :], 0, WORDS)

    def region_in():
        project_into(stream_low, WORDS, REGIONS, 2, mixed_self)
        attend_into(ATTEND_REGION, mixed_self, region_down[...] == region_across[...], shares_r, context)
        for at in range(WORDS, ROWS, 128):
            transposed_into(context_self_t, context[at : at + 128, :], at, 128)

    def self_out(module, first, last):
        for at in range(first, last, 128):
            two = join(at, outward_all[module], context, stream[at : at + 128, :], 3 * module + 2, 1, module)
            stream[at : at + 128, :] = two
            two_low = two.astype(jnp.bfloat16)
            stream_low[at : at + 128, :] = two_low
            transposed_into(rows_two_t, two_low, at, 128)

    def feed_in(f, first, last, column, columns):
        step = 256

        def tile(t, carry):
            at = pl.multiple_of(column + t * step, step)
            for row in range(first, last, 128):
                before = (
                    matmul(stream_low[row : row + 128, :], expand_all[f, :, pl.ds(at, step)])
                    + hidden_rows[f : f + 1, pl.ds(at, step)]
                )
                below = 0.5 * (1.0 + lax.erf(before * 0.5**0.5))
                value = (before * below).astype(jnp.bfloat16)
                density = jnp.exp(-0.5 * before * before) * 0.3989422804014327
                hidden[row : row + 128, pl.ds(at, step)] = value
                hidden_t[pl.ds(at, step), row : row + 128] = value.T
                slope[row : row + 128, pl.ds(at, step)] = (below + before * density).astype(jnp.bfloat16)
            return carry

        lax.fori_loop(0, columns // step, tile, 0)

    def feed_out(f, first, last):
        for at in range(first, last, 128):
            last_rows = join(at, shrink_all[f], hidden, stream[at : at + 128, :], 14 + f, 2, 3 + f)
            result[at : at + 128, :] = last_rows.astype(jnp.bfloat16)

    def nothing():
        pass

    pieces = [
        lambda: (cross_in(), keep(inward_all.at[0], inward_out.at[0])),
        lambda: (cross_out(), keep(outward_all.at[0], outward_out.at[0])),
        lambda: (word_in(), keep(inward_all.at[1], inward_out.at[1])),
        lambda: (region_in(), keep(inward_all.at[2], inward_out.at[2])),
        lambda: (self_out(1, 0, WORDS), keep(outward_all.at[1], outward_out.at[1])),
        lambda: (self_out(2, WORDS, ROWS), keep(outward_all.at[2], outward_out.at[2])),
        lambda: feed_in(0, 0, WORDS, 0, 2 * WIDE),
        lambda: (feed_in(0, 0, WORDS, 2 * WIDE, 2 * WIDE), keep(expand_all.at[0], expand_out.at[0])),
        lambda: feed_in(1, WORDS, ROWS, 0, 2 * WIDE),
        lambda: (feed_in(1, WORDS, ROWS, 2 * WIDE, 2 * WIDE), keep(expand_all.at[1], expand_out.at[1])),
        nothing,
        lambda: (keep(shrink_all.at[0], shrink_out.at[0]), feed_out(0, 0, WORDS)),
        nothing,
        lambda: (keep(shrink_all.at[1], shrink_out.at[1]), feed_out(1, WORDS, ROWS)),
    ]
    count = len(chunks)
    start_own(0)
    start_own(1)
    read_small()
    for k in range(count + 2):
        if k + 2 < count:
            start_own(k + 2)
        if k < count:
            forward_first(k)
        if 0 <= k - 1 < count:
            forward_second(k - 1)
        if 0 <= k - 2 < count:
            complete(k - 2)
            pieces[k - 2]()
    for saved in keeps:
        saved.wait()
    for offset in range(1, 8):
        small_copy(offset, me).wait_send()
    for k in range(count):
        for kind in range(8):
            copy(k, kind).wait_send()


def forward(rows_low, word_ids, region_ids, small, inward, outward, expand, shrink):
    low = jnp.bfloat16
    dma = pltpu.SemaphoreType.DMA
    vmem = pl.BlockSpec(memory_space=pltpu.VMEM)
    hbm = pl.BlockSpec(memory_space=pl.ANY)
    shape = jax.ShapeDtypeStruct
    weights = [
        shape((3, WIDE, 3 * WIDE), low),
        shape((3, WIDE, WIDE), low),
        shape((2, WIDE, HIDDEN), low),
        shape((2, HIDDEN, WIDE), low),
    ]
    residuals = [
        shape((24, WIDE), jnp.float32),
        shape((2, HIDDEN), jnp.float32),
        shape((ROWS, 3 * WIDE), low),
        shape((ROWS, 3 * WIDE), low),
        shape((HEADS, WORDS, REGIONS), low),
        shape((HEADS, REGIONS, WORDS), low),
        shape((HEADS, WORDS, WORDS), low),
        shape((HEADS, REGIONS, REGIONS), low),
        shape((WIDE, ROWS), low),
        shape((WIDE, ROWS), low),
        shape((WIDE, ROWS), low),
        shape((WIDE, ROWS), low),
        shape((WIDE, ROWS), low),
        shape((HIDDEN, ROWS), low),
        shape((ROWS, HIDDEN), low),
        shape((3, ROWS, WIDE), jnp.float32),
        shape((3, ROWS, 128), jnp.float32),
    ]
    out_shape = [shape((ROWS, WIDE), low)] + residuals + weights
    outs = pl.pallas_call(
        forward_kernel,
        out_shape=out_shape,
        in_specs=[vmem] * 6 + [hbm] * 4,
        out_specs=[vmem] * (1 + len(residuals)) + [hbm] * 4,
        scratch_shapes=[pltpu.VMEM(w.shape, w.dtype) for w in weights]
        + [
            pltpu.VMEM((8, 32, 128), low),
            pltpu.VMEM((ROWS, WIDE), jnp.float32),
            pltpu.VMEM((ROWS, WIDE), low),
            pltpu.VMEM((ROWS, WIDE), low),
            pltpu.VMEM((ROWS, HIDDEN), low),
            dma((14, 8)),
            dma((14, 8)),
            dma((7,)),
            dma((7,)),
            dma((24,)),
        ],
        compiler_params=pltpu.CompilerParams(
            collective_id=1, has_side_effects=True, vmem_limit_bytes=64 * 2**20 - 2**16
        ),
    )(
        rows_low,
        word_ids,
        region_ids,
        word_ids.reshape(WORDS, 1),
        region_ids.reshape(REGIONS, 1),
        small,
        inward,
        outward,
        expand,
        shrink,
    )
    return outs[0], outs[1 : 1 + len(residuals)], outs[1 + len(residuals) :]


def grad_kernel(groups, *refs):
    lefts = refs[:6]
    rights = refs[6:12]
    small_in = refs[12]
    out, small_out = refs[13:15]
    (
        acc,
        core_out,
        core_in,
        half_out,
        half_in,
        full_out,
        full_in,
        plane,
        end_out,
        end_in,
        mid_out,
        mid_in,
        small_in_plane,
        small_planes,
        core_send,
        core_recv,
        half_send,
        half_recv,
        full_send,
        full_recv,
        z_send,
        z_recv,
        small_send,
        small_recv,
        free,
    ) = refs[15:]
    me = lax.axis_index("fsdp")
    z = lax.axis_index("rep")
    chip = me // 2
    lane = me % 2
    is_end = jnp.logical_or(z == 0, z == 3)
    is_mid = jnp.logical_or(z == 1, z == 2)
    xor = lax.bitwise_xor
    core_peer = {"fsdp": xor(me, 1)}
    links = ({"fsdp": xor(me, 2)}, {"fsdp": xor(me, 4)})
    link_chip = (xor(chip, 1), xor(chip, 2))
    diagonal = xor(chip, 3)
    pair_peer = {"rep": xor(z, 1)}
    mid_peer = {"rep": 3 - z}
    total = sum(group[0] for group in groups)

    barrier = pltpu.get_barrier_semaphore()
    for offset in range(1, 8):
        pl.semaphore_signal(barrier, inc=1, device_id={"fsdp": xor(me, offset)}, device_id_type=MESH)
    for offset in range(1, 4):
        pl.semaphore_signal(barrier, inc=1, device_id={"rep": (z + offset) % 4}, device_id_type=MESH)
    pl.semaphore_wait(barrier, 10)

    def remote(src, dst, send_sem, recv_sem, peer):
        return pltpu.make_async_remote_copy(
            src_ref=src, dst_ref=dst, send_sem=send_sem, recv_sem=recv_sem, device_id=peer, device_id_type=MESH
        )

    def small_copy(offset):
        peer = xor(me, offset)
        return remote(
            small_in.at[peer],
            small_in_plane.at[offset - 1],
            small_send.at[offset - 1],
            small_recv.at[offset - 1],
            {"fsdp": peer},
        )

    def small_plane_copy(offset):
        return remote(
            small_planes.at[z],
            small_planes.at[z],
            small_send.at[6 + offset],
            small_recv.at[6 + offset],
            {"rep": (z + offset) % 4},
        )

    for offset in range(1, 8):
        small_copy(offset).start()

    def core_copy(u):
        slot = u % SLOTS
        return remote(core_out.at[slot], core_in.at[slot], core_send.at[slot], core_recv.at[slot], core_peer)

    def half_copy(u, way):
        slot = u % SLOTS
        return remote(
            half_out.at[slot, way], half_in.at[slot, way], half_send.at[slot, way], half_recv.at[slot, way], links[way]
        )

    def full_copy(u, way):
        slot = u % SLOTS
        return remote(
            full_out.at[slot, way], full_in.at[slot, way], full_send.at[slot, way], full_recv.at[slot, way], links[way]
        )

    def end_copy(u):
        slot = u % SLOTS
        return remote(end_out.at[slot], end_in.at[slot], z_send.at[0, slot], z_recv.at[0, slot], pair_peer)

    def mid_copy(u):
        slot = u % SLOTS
        return remote(mid_out.at[slot], mid_in.at[slot], z_send.at[1, slot], z_recv.at[1, slot], mid_peer)

    def back_copy(u):
        slot = u % SLOTS
        return remote(out.at[u], out.at[u], z_send.at[2, slot], z_recv.at[2, slot], pair_peer)

    def credit(u, channel, peer):
        @pl.when(u + SLOTS < total)
        def _():
            pl.semaphore_signal(free.at[channel], inc=1, device_id=peer, device_id_type=MESH)

    def spend(u, channel):
        @pl.when(u >= SLOTS)
        def _():
            pl.semaphore_wait(free.at[channel], 1)

    def produce(u):
        slot = u % SLOTS
        keep = u % ACC_SLOTS
        spend(u, 0)
        first = 0
        for units, side, first_row, rows, by_row in groups:
            start = first

            @pl.when(jnp.logical_and(u >= start, u < start + units))
            def _(start=start, side=side, rows=pl.ds(first_row, rows), by_row=by_row):
                at = u - start
                column = 0 if by_row else pl.multiple_of(at * WIDE, WIDE)
                right = rights[side][rows, pl.ds(column, WIDE)]

                def product(core):
                    blocks = []
                    for block in range(4):
                        owner = 2 * block + core
                        row = owner * (4 * UNIT) + at * UNIT if by_row else owner * UNIT
                        blocks.append(lefts[side][pl.ds(pl.multiple_of(row, 16), UNIT), rows])
                    return matmul(jnp.concatenate(blocks, axis=0), right)

                other = product(1 - lane).astype(jnp.bfloat16)
                for block in range(4):
                    core_out[slot, block] = other[block * UNIT : (block + 1) * UNIT]
                core_copy(u).start()
                own = product(lane)
                for block in range(4):
                    acc[keep, block] = own[block * UNIT : (block + 1) * UNIT]

            first = first + units

    def join_cores(u):
        slot = u % SLOTS
        keep = u % ACC_SLOTS
        core_copy(u).wait()
        for way in range(2):
            spend(u, 1 + way)
        summed = acc[keep, diagonal] + core_in[slot, diagonal].astype(jnp.float32)
        half_out[slot, 0] = summed[: UNIT // 2].astype(jnp.bfloat16)
        half_out[slot, 1] = summed[UNIT // 2 :].astype(jnp.bfloat16)
        for way in range(2):
            half_copy(u, way).start()
        for block in (link_chip[0], link_chip[1], chip):
            acc[keep, block] = acc[keep, block] + core_in[slot, block].astype(jnp.float32)
        credit(u, 0, core_peer)

    def join_diagonal(u):
        slot = u % SLOTS
        keep = u % ACC_SLOTS
        for way in range(2):
            half_copy(u, way).wait()
            spend(u, 3 + way)
        half = UNIT // 2
        full_out[slot, 1, :half] = (acc[keep, link_chip[1], :half] + half_in[slot, 0].astype(jnp.float32)).astype(
            jnp.bfloat16
        )
        full_out[slot, 1, half:] = acc[keep, link_chip[1], half:].astype(jnp.bfloat16)
        full_copy(u, 1).start()
        full_out[slot, 0, half:] = (acc[keep, link_chip[0], half:] + half_in[slot, 1].astype(jnp.float32)).astype(
            jnp.bfloat16
        )
        full_out[slot, 0, :half] = acc[keep, link_chip[0], :half].astype(jnp.bfloat16)
        full_copy(u, 0).start()
        for way in range(2):
            credit(u, 1 + way, links[way])

    def join_plane(u):
        slot = u % SLOTS
        keep = u % ACC_SLOTS
        for way in range(2):
            full_copy(u, way).wait()
        summed = acc[keep, chip] + (full_in[slot, 0].astype(jnp.float32) + full_in[slot, 1].astype(jnp.float32))

        @pl.when(is_end)
        def _():
            spend(u, 5)
            end_out[slot] = summed.astype(jnp.bfloat16)
            end_copy(u).start()

        @pl.when(is_mid)
        def _():
            plane[slot] = summed

        for way in range(2):
            credit(u, 3 + way, links[way])

    def join_pair(u):
        slot = u % SLOTS

        @pl.when(is_end)
        def _():
            end_copy(u).wait_send()

        @pl.when(is_mid)
        def _():
            end_copy(u).wait_recv()
            spend(u, 6)
            mid_out[slot] = (plane[slot] + end_in[slot].astype(jnp.float32)).astype(jnp.bfloat16)
            mid_copy(u).start()
            credit(u, 5, pair_peer)

    def join_middle(u):
        slot = u % SLOTS

        @pl.when(is_mid)
        def _():
            mid_copy(u).wait()
            out[u] = (mid_out[slot].astype(jnp.float32) + mid_in[slot].astype(jnp.float32)).astype(jnp.bfloat16)
            back_copy(u).start()
            credit(u, 6, mid_peer)

    def finish(u):
        @pl.when(is_mid)
        def _():
            back_copy(u).wait_send()

        @pl.when(is_end)
        def _():
            back_copy(u).wait_recv()

    stages = [
        (0, produce),
        (1, join_cores),
        (1 + LAG_A, join_diagonal),
        (1 + LAG_A + LAG_B, join_plane),
        (1 + LAG_A + LAG_B + LAG_Z, join_pair),
        (1 + LAG_A + LAG_B + 2 * LAG_Z, join_middle),
        (1 + LAG_A + LAG_B + 3 * LAG_Z, finish),
    ]

    def step(i, carry):
        for lag, stage in reversed(stages):

            @pl.when(jnp.logical_and(i >= lag, i < total + lag))
            def _(lag=lag, stage=stage):
                stage(i - lag)

        @pl.when(i == 2)
        def _():
            summed = small_in[me]
            for offset in range(1, 8):
                small_copy(offset).wait()
                summed = summed + small_in_plane[offset - 1]
            small_planes[z] = summed
            for offset in range(1, 4):
                small_plane_copy(offset).start()

        @pl.when(i == 4)
        def _():
            for offset in range(1, 4):
                small_plane_copy(offset).wait_send()
            for offset in range(1, 4):
                source = (z + 4 - offset) % 4
                remote(
                    small_planes.at[source],
                    small_planes.at[source],
                    small_send.at[6 + offset],
                    small_recv.at[6 + offset],
                    {"rep": source},
                ).wait_recv()
            small_out[...] = small_planes[0] + small_planes[1] + (small_planes[2] + small_planes[3])

        return carry

    lax.fori_loop(0, total + stages[-1][0], step, 0)


def sum_grads(groups, lefts, rights, small):
    total = sum(group[0] for group in groups)
    block = (UNIT, WIDE)
    low = jnp.bfloat16
    dma = pltpu.SemaphoreType.DMA
    vmem = pl.BlockSpec(memory_space=pltpu.VMEM)
    return pl.pallas_call(
        functools.partial(grad_kernel, groups),
        out_shape=(
            jax.ShapeDtypeStruct((total,) + block, low),
            jax.ShapeDtypeStruct(small.shape[1:], jnp.float32),
        ),
        in_specs=[vmem] * (len(lefts) + len(rights) + 1),
        out_specs=(vmem, vmem),
        scratch_shapes=[
            pltpu.VMEM((ACC_SLOTS, 4) + block, jnp.float32),
            pltpu.VMEM((SLOTS, 4) + block, low),
            pltpu.VMEM((SLOTS, 4) + block, low),
            pltpu.VMEM((SLOTS, 2, UNIT // 2, WIDE), low),
            pltpu.VMEM((SLOTS, 2, UNIT // 2, WIDE), low),
            pltpu.VMEM((SLOTS, 2) + block, low),
            pltpu.VMEM((SLOTS, 2) + block, low),
            pltpu.VMEM((SLOTS,) + block, jnp.float32),
            pltpu.VMEM((SLOTS,) + block, low),
            pltpu.VMEM((SLOTS,) + block, low),
            pltpu.VMEM((SLOTS,) + block, low),
            pltpu.VMEM((SLOTS,) + block, low),
            pltpu.VMEM((7,) + small.shape[1:], jnp.float32),
            pltpu.VMEM((4,) + small.shape[1:], jnp.float32),
            dma((SLOTS,)),
            dma((SLOTS,)),
            dma((SLOTS, 2)),
            dma((SLOTS, 2)),
            dma((SLOTS, 2)),
            dma((SLOTS, 2)),
            dma((3, SLOTS)),
            dma((3, SLOTS)),
            dma((10,)),
            dma((10,)),
            pltpu.SemaphoreType.REGULAR((7,)),
        ],
        compiler_params=pltpu.CompilerParams(
            collective_id=0, has_side_effects=True, vmem_limit_bytes=60 * 2**20
        ),
    )(*lefts, *rights, small)


GROUPS = (
    (4, 0, 0, WORDS, True),
    (4, 0, WORDS, REGIONS, True),
    (4, 1, 0, WORDS, False),
    (4, 1, WORDS, REGIONS, False),
    (1, 2, 0, WORDS, False),
    (1, 2, WORDS, REGIONS, False),
    (3, 3, 0, WORDS, False),
    (3, 3, WORDS, REGIONS, False),
    (1, 4, 0, ROWS, False),
    (3, 5, 0, ROWS, False),
)


def shares_back(shares, queries, key_rows, value_rows, grad_context):
    grad_heads = heads_of(grad_context)
    grad_shares = jnp.einsum(
        "qhd,khd->hqk", grad_heads, heads_of(value_rows), preferred_element_type=jnp.float32
    )
    grad_values = jnp.einsum("hqk,qhd->khd", shares, grad_heads, preferred_element_type=jnp.float32)
    wide = shares.astype(jnp.float32)
    grad_scores = (wide * (grad_shares - jnp.sum(wide * grad_shares, axis=-1, keepdims=True))).astype(jnp.bfloat16)
    score_scale = HEAD_DIM ** (-0.5)
    grad_queries = score_scale * jnp.einsum(
        "hqk,khd->qhd", grad_scores, heads_of(key_rows), preferred_element_type=jnp.float32
    )
    grad_keys = score_scale * jnp.einsum(
        "hqk,qhd->khd", grad_scores, heads_of(queries), preferred_element_type=jnp.float32
    )
    return (merge_heads(grad_queries), merge_heads(grad_keys), merge_heads(grad_values))


def thirds(mixed):
    return (mixed[:, :WIDE], mixed[:, WIDE : 2 * WIDE], mixed[:, 2 * WIDE :])


def paired(
    word_rows,
    region_rows,
    word_segment,
    region_segment,
    inward,
    outward,
    biases,
    norm_gain,
    expand_weight,
    shrink_weight,
    hidden_bias,
    word_cotangent,
    region_cotangent,
):
    small = jnp.concatenate([biases, norm_gain, hidden_bias.reshape(8, UNIT)], axis=0)
    small = jnp.pad(small, ((0, 3), (0, 128 - UNIT)))
    rows_low = jnp.concatenate([word_rows, region_rows], axis=0)
    result, residuals, weights = forward(
        rows_low, word_segment, region_segment, small, inward, outward, expand_weight, shrink_weight
    )
    (
        params,
        hidden_rows,
        mixed_cross,
        mixed_self,
        shares_cw,
        shares_cr,
        shares_w,
        shares_r,
        context_cross_t,
        context_self_t,
        rows_zero_t,
        rows_one_t,
        rows_two_t,
        hidden_t,
        slope,
        normed,
        inverse,
    ) = residuals
    inward_all, outward_all, expand_all, shrink_all = weights
    gains = params[16:21]
    cut = WORDS
    low = jnp.bfloat16
    f32 = jnp.float32

    def norm_back(grad_out, kind, index, first, last):
        return normalize_back(
            grad_out[first:last], (normed[kind, first:last], inverse[kind, first:last, :1]), gains[index]
        )

    def two(function):
        return (function(0, 0, cut), function(1, cut, ROWS))

    cotangent = jnp.concatenate([word_cotangent, region_cotangent], axis=0).astype(f32)
    feed = two(lambda f, first, last: norm_back(cotangent, 2, 3 + f, first, last))
    grad_sum = jnp.concatenate([feed[0][0], feed[1][0]], axis=0)
    grad_end = grad_sum.astype(low)
    grad_before = jnp.concatenate(
        two(
            lambda f, first, last: (
                matmul_nt(grad_end[first:last], shrink_all[f]) * slope[first:last].astype(f32)
            ).astype(low)
        ),
        axis=0,
    )
    grad_two = grad_sum + jnp.concatenate(
        two(lambda f, first, last: matmul_nt(grad_before[first:last], expand_all[f])), axis=0
    )
    own = two(lambda f, first, last: norm_back(grad_two, 1, 1 + f, first, last))
    grad_sum_one = jnp.concatenate([own[0][0], own[1][0]], axis=0)
    grad_self = grad_sum_one.astype(low)
    grad_context = jnp.concatenate(
        two(lambda f, first, last: matmul_nt(grad_self[first:last], outward_all[1 + f])), axis=0
    ).astype(low)
    self_parts = two(
        lambda f, first, last: jnp.concatenate(
            shares_back((shares_w, shares_r)[f], *thirds(mixed_self[first:last]), grad_context[first:last]), axis=1
        ).astype(low)
    )
    grad_mixed_self = jnp.concatenate(self_parts, axis=0)
    grad_one = grad_sum_one + jnp.concatenate(
        two(lambda f, first, last: matmul_nt(grad_mixed_self[first:last], inward_all[1 + f])), axis=0
    )
    crossed = norm_back(grad_one, 0, 0, 0, ROWS)
    grad_cross = crossed[0].astype(low)
    grad_context_cross = matmul_nt(grad_cross, outward_all[0]).astype(low)
    word_mix, region_mix = thirds(mixed_cross[:cut]), thirds(mixed_cross[cut:])
    from_words = shares_back(shares_cw, word_mix[0], region_mix[1], region_mix[2], grad_context_cross[:cut])
    from_regions = shares_back(shares_cr, region_mix[0], word_mix[1], word_mix[2], grad_context_cross[cut:])
    grad_mixed_cross = jnp.concatenate(
        [
            jnp.concatenate([from_words[0], from_regions[1], from_regions[2]], axis=1),
            jnp.concatenate([from_regions[0], from_words[1], from_words[2]], axis=1),
        ],
        axis=0,
    ).astype(low)
    grad_rows = crossed[0] + matmul_nt(grad_mixed_cross, inward_all[0])

    ends = two(lambda f, first, last: column_sums(grad_end[first:last]))
    hidden_grads = two(lambda f, first, last: column_sums(grad_before[first:last]))
    self_bias = two(lambda f, first, last: column_sums(grad_mixed_self[first:last]))
    self_ends = two(lambda f, first, last: column_sums(grad_self[first:last]))
    cross_bias = column_sums(grad_mixed_cross)
    row_grads = jnp.stack(
        [
            cross_bias[:WIDE],
            cross_bias[2 * WIDE :],
            column_sums(grad_cross),
            self_bias[0][:WIDE],
            self_bias[0][2 * WIDE :],
            self_ends[0],
            self_bias[1][:WIDE],
            self_bias[1][2 * WIDE :],
            self_ends[1],
            crossed[2],
            own[0][2],
            own[1][2],
            feed[0][2],
            feed[1][2],
            ends[0],
            ends[1],
            crossed[1],
            own[0][1],
            own[1][1],
            feed[0][1],
            feed[1][1],
        ]
    )
    small_grads = jnp.concatenate(
        [
            row_grads.reshape(21, 8, UNIT).transpose(1, 0, 2),
            jnp.stack(hidden_grads).reshape(2, 8, 4, UNIT).transpose(1, 0, 2, 3).reshape(8, 8, UNIT),
        ],
        axis=1,
    )
    padded = jnp.pad(small_grads, ((0, 0), (0, 3), (0, 128 - UNIT)))
    lefts = [hidden_t, rows_two_t, context_self_t, rows_one_t, context_cross_t, rows_zero_t]
    rights = [grad_end, grad_before, grad_self, grad_mixed_self, grad_cross, grad_mixed_cross]
    units, small_total = sum_grads(GROUPS, lefts, rights, padded)
    units = units.astype(f32)
    small_total = small_total[:, :UNIT]
    return (
        result[:cut],
        result[cut:],
        grad_rows[:cut],
        grad_rows[cut:],
        jnp.stack([units[25:28], units[18:21], units[21:24]]).transpose(0, 2, 1, 3).reshape(3, UNIT, 3 * WIDE),
        jnp.stack([units[24], units[16], units[17]]),
        small_total[:16],
        small_total[16:21],
        units[8:16].reshape(2, 4, UNIT, WIDE).transpose(0, 2, 1, 3).reshape(2, UNIT, 4 * WIDE),
        units[:8].reshape(2, 4 * UNIT, WIDE),
        small_total[21:29].reshape(2, 4 * UNIT),
    )


def general(
    devices,
    word_rows,
    region_rows,
    word_segment,
    region_segment,
    inward,
    outward,
    biases,
    norm_gain,
    expand_weight,
    shrink_weight,
    hidden_bias,
    word_cotangent,
    region_cotangent,
):
    words_count = word_rows.shape[0]
    width = word_rows.shape[1]
    word_ids = word_segment[0]
    region_ids = region_segment[0]
    cross_mask = word_ids[:, None] == region_ids[None, :]
    word_mask = word_ids[:, None] == word_ids[None, :]
    region_mask = region_ids[:, None] == region_ids[None, :]
    shard = biases.shape[1]
    per_shard = hidden_bias.shape[1] // shard
    small_shard = jnp.concatenate([biases, norm_gain, hidden_bias.reshape(2 * per_shard, shard)], axis=0)
    small_all = lax.all_gather(small_shard, "fsdp", axis=0)
    bias_count = biases.shape[0]
    gain_count = norm_gain.shape[0]
    row_params = small_all[:, : bias_count + gain_count].transpose(1, 0, 2).reshape(bias_count + gain_count, width)
    hidden_all = (
        small_all[:, bias_count + gain_count :]
        .reshape(devices, 2, per_shard * shard)
        .transpose(1, 0, 2)
        .reshape(2, devices * per_shard * shard)
    )
    inward_all, outward_all = (
        lax.all_gather(inward, "fsdp", axis=1, tiled=True),
        lax.all_gather(outward, "fsdp", axis=1, tiled=True),
    )
    attend_set = (
        inward_all,
        outward_all,
        row_params[:bias_count].astype(jnp.float32),
        row_params[bias_count:].astype(jnp.float32),
    )
    crossed, cross_kept = cross_forward(word_rows, region_rows, attend_set, cross_mask)
    word_one, word_kept = self_forward(crossed[:words_count], attend_set, 1, word_mask)
    region_one, region_kept = self_forward(crossed[words_count:], attend_set, 2, region_mask)
    expand_all, shrink_all = (
        lax.all_gather(expand_weight, "fsdp", axis=1, tiled=True),
        lax.all_gather(shrink_weight, "fsdp", axis=1, tiled=True),
    )
    feed_set = (expand_all, shrink_all, hidden_all)
    word_two, word_feed = feed_forward(word_one, feed_set, 0, attend_set)
    region_two, region_feed = feed_forward(region_one, feed_set, 1, attend_set)
    word_back = feed_backward(word_cotangent.astype(jnp.float32), word_feed, feed_set, 0, attend_set[3])
    region_back = feed_backward(region_cotangent.astype(jnp.float32), region_feed, feed_set, 1, attend_set[3])
    word_self = self_backward(word_back[0], word_kept, attend_set, 1, word_mask)
    region_self = self_backward(region_back[0], region_kept, attend_set, 2, region_mask)
    grad_crossed = jnp.concatenate([word_self[0], region_self[0]], axis=0)
    cross_back = cross_backward(grad_crossed, cross_kept, attend_set, cross_mask, words_count)
    row_grads = jnp.stack(
        [
            cross_back[3][0],
            cross_back[3][1],
            cross_back[3][2],
            word_self[3][0],
            word_self[3][1],
            word_self[3][2],
            region_self[3][0],
            region_self[3][1],
            region_self[3][2],
            cross_back[5],
            word_self[5],
            region_self[5],
            word_back[6],
            region_back[6],
            word_back[4],
            region_back[4],
            cross_back[4],
            word_self[4],
            region_self[4],
            word_back[5],
            region_back[5],
        ]
    )
    hidden_grads = jnp.stack([word_back[3], region_back[3]])
    small_grads = jnp.concatenate(
        [
            row_grads.reshape(bias_count + gain_count, devices, shard).transpose(1, 0, 2),
            hidden_grads.reshape(2, devices, per_shard, shard)
            .transpose(1, 0, 2, 3)
            .reshape(devices, 2 * per_shard, shard),
        ],
        axis=1,
    )

    def reduced(products, axis):
        mine = lax.psum_scatter(jnp.stack(products), "fsdp", scatter_dimension=axis, tiled=True)
        return lax.psum(mine.astype(jnp.bfloat16), "rep").astype(jnp.float32)

    shrink_total = reduced([matmul_tn(*word_back[2]), matmul_tn(*region_back[2])], 1)
    expand_total = reduced([matmul_tn(*word_back[1]), matmul_tn(*region_back[1])], 1)
    outward_total = reduced([matmul_tn(*cross_back[2]), matmul_tn(*word_self[2]), matmul_tn(*region_self[2])], 1)
    inward_total = reduced([matmul_tn(*cross_back[1]), matmul_tn(*word_self[1]), matmul_tn(*region_self[1])], 1)
    small_total = lax.psum(lax.psum_scatter(small_grads, "fsdp", scatter_dimension=0, tiled=False), "rep")
    grad_rows = cross_back[0]
    return (
        word_two.astype(jnp.bfloat16),
        region_two.astype(jnp.bfloat16),
        grad_rows[:words_count],
        grad_rows[words_count:],
        inward_total,
        outward_total,
        small_total[:bias_count],
        small_total[bias_count : bias_count + gain_count],
        expand_total,
        shrink_total,
        small_total[bias_count + gain_count :].reshape(2, per_shard * shard),
    )


def solution(mesh):
    sizes = (mesh.shape["rep"], mesh.shape["fsdp"])
    return jax.shard_map(
        paired if sizes == (4, 8) else functools.partial(general, mesh.shape["fsdp"]),
        mesh=mesh,
        in_specs=(
            P(("rep", "fsdp"), None),
            P(("rep", "fsdp"), None),
            P(("rep", "fsdp"), None),
            P(("rep", "fsdp"), None),
            P(None, "fsdp", None),
            P(None, "fsdp", None),
            P(None, "fsdp"),
            P(None, "fsdp"),
            P(None, "fsdp", None),
            P(None, "fsdp", None),
            P(None, "fsdp"),
            P(("rep", "fsdp"), None),
            P(("rep", "fsdp"), None),
        ),
        out_specs=(
            P(("rep", "fsdp"), None),
            P(("rep", "fsdp"), None),
            P(("rep", "fsdp"), None),
            P(("rep", "fsdp"), None),
            P(None, "fsdp", None),
            P(None, "fsdp", None),
            P(None, "fsdp"),
            P(None, "fsdp"),
            P(None, "fsdp", None),
            P(None, "fsdp", None),
            P(None, "fsdp"),
        ),
        check_vma=False,
    )
```

```python
import functools

import jax
import jax.numpy as jnp
from jax import lax
from jax.experimental import pallas as pl
from jax.experimental.pallas import tpu as pltpu
from jax.sharding import PartitionSpec as P

MESH = pl.DeviceIdType.MESH

HEADS = 12
HEAD_DIM = 64


norm_epsilon = 1e-12
masked_score = -1e30


def matmul(left_op, right_op):
    return jnp.dot(left_op, right_op, preferred_element_type=jnp.float32)


def matmul_tn(left_op, right_op):
    return lax.dot_general(
        left_op, right_op, (((0,), (0,)), ((), ())), preferred_element_type=jnp.float32
    )


def matmul_nt(left_op, right_op):
    return lax.dot_general(
        left_op, right_op, (((1,), (1,)), ((), ())), preferred_element_type=jnp.float32
    )


def column_sums(values):
    return jnp.sum(values, axis=0, dtype=jnp.float32)


def heads_of(rows_in):
    return rows_in.reshape(rows_in.shape[0], HEADS, HEAD_DIM)


def merge_heads(head_rows):
    return head_rows.reshape(head_rows.shape[0], -1)


def normalize(summed, gain_row, shift_row):
    center = summed - jnp.mean(summed, axis=-1, keepdims=True)
    inverse = lax.rsqrt(jnp.mean(center * center, axis=-1, keepdims=True) + norm_epsilon)
    normed = center * inverse
    return (normed * gain_row + shift_row, (normed, inverse))


def normalize_back(grad_out, norm_stats, gain_row):
    normed, inverse = norm_stats
    grad_normed = grad_out * gain_row
    grad_sum = inverse * (
        grad_normed
        - jnp.mean(grad_normed, axis=-1, keepdims=True)
        - normed * jnp.mean(grad_normed * normed, axis=-1, keepdims=True)
    )
    return (grad_sum, column_sums(grad_out * normed), column_sums(grad_out))


def score_block(queries, key_rows, allowed):
    scores = jnp.einsum(
        "qhd,khd->hqk", heads_of(queries), heads_of(key_rows), preferred_element_type=jnp.float32
    ) * HEAD_DIM ** (-0.5)
    return jnp.where(allowed[None], scores, masked_score)


def attend(queries, key_rows, value_rows, allowed):
    scores = score_block(queries, key_rows, allowed)
    top_score = jnp.max(scores, axis=-1, keepdims=True)
    log_total = top_score + jnp.log(jnp.sum(jnp.exp(scores - top_score), axis=-1, keepdims=True))
    shares = jnp.exp(scores - log_total).astype(jnp.bfloat16)
    context = jnp.einsum(
        "hqk,khd->qhd", shares, heads_of(value_rows), preferred_element_type=jnp.float32
    )
    return (merge_heads(context).astype(jnp.bfloat16), log_total)


def attend_back(queries, key_rows, value_rows, allowed, log_total, grad_context):
    shares = jnp.exp(score_block(queries, key_rows, allowed) - log_total)
    grad_heads = heads_of(grad_context)
    grad_shares = jnp.einsum(
        "qhd,khd->hqk", grad_heads, heads_of(value_rows), preferred_element_type=jnp.float32
    )
    grad_values = jnp.einsum(
        "hqk,qhd->khd", shares.astype(jnp.bfloat16), grad_heads, preferred_element_type=jnp.float32
    )
    grad_scores = (
        shares * (grad_shares - jnp.sum(shares * grad_shares, axis=-1, keepdims=True))
    ).astype(jnp.bfloat16)
    score_scale = HEAD_DIM ** (-0.5)
    grad_queries = (
        jnp.einsum(
            "hqk,khd->qhd", grad_scores, heads_of(key_rows), preferred_element_type=jnp.float32
        )
        * score_scale
    )
    grad_keys = (
        jnp.einsum(
            "hqk,qhd->khd", grad_scores, heads_of(queries), preferred_element_type=jnp.float32
        )
        * score_scale
    )
    return (merge_heads(grad_queries), merge_heads(grad_keys), merge_heads(grad_values))


def project(rows_low, weight, bias_rows, module):
    width = weight.shape[0]
    bias_all = jnp.concatenate(
        [bias_rows[3 * module], jnp.zeros((width,), jnp.float32), bias_rows[3 * module + 1]]
    )
    return (matmul(rows_low, weight) + bias_all).astype(jnp.bfloat16)


def project_back(grad_sum, grad_parts, rows_low, weight):
    width = weight.shape[0]
    grad_mixed = jnp.concatenate(grad_parts, axis=1).astype(jnp.bfloat16)
    grad_weight = (rows_low, grad_mixed)
    grad_bias = column_sums(grad_mixed)
    grad_rows = grad_sum + matmul_nt(grad_mixed, weight)
    return (grad_rows, grad_weight, grad_bias[:width], grad_bias[2 * width :])


def branch_back(grad_out, context, norm_stats, gain_row, outward_one):
    grad_sum, grad_gain, grad_shift = normalize_back(grad_out, norm_stats, gain_row)
    grad_branch = grad_sum.astype(jnp.bfloat16)
    grad_outward = (context, grad_branch)
    grad_context = matmul_nt(grad_branch, outward_one).astype(jnp.bfloat16)
    return (grad_sum, grad_context, grad_outward, column_sums(grad_branch), grad_gain, grad_shift)


def self_forward(rows_in, weights, module, allowed):
    inward_all, outward_all, bias_rows, gain_rows = weights
    width = rows_in.shape[1]
    rows_low = rows_in.astype(jnp.bfloat16)
    mixed = project(rows_low, inward_all[module], bias_rows, module)
    context, log_total = attend(
        mixed[:, :width], mixed[:, width : 2 * width], mixed[:, 2 * width :], allowed
    )
    summed = rows_in + matmul(context, outward_all[module]) + bias_rows[3 * module + 2]
    result, norm_stats = normalize(summed, gain_rows[module], bias_rows[9 + module])
    return (result, (rows_low, mixed, context, log_total, norm_stats))


def self_backward(grad_out, kept, weights, module, allowed):
    inward_all, outward_all, bias_rows, gain_rows = weights
    rows_low, mixed, context, log_total, norm_stats = kept
    width = rows_low.shape[1]
    grad_sum, grad_context, grad_outward, grad_bias_out, grad_gain, grad_shift = branch_back(
        grad_out, context, norm_stats, gain_rows[module], outward_all[module]
    )
    grad_parts = attend_back(
        mixed[:, :width],
        mixed[:, width : 2 * width],
        mixed[:, 2 * width :],
        allowed,
        log_total,
        grad_context,
    )
    grad_rows, grad_inward, grad_bias_query, grad_bias_value = project_back(
        grad_sum, grad_parts, rows_low, inward_all[module]
    )
    return (
        grad_rows,
        grad_inward,
        grad_outward,
        (grad_bias_query, grad_bias_value, grad_bias_out),
        grad_gain,
        grad_shift,
    )


def cross_forward(word_rows, region_rows, weights, cross_mask):
    inward_all, outward_all, bias_rows, gain_rows = weights
    words_count = word_rows.shape[0]
    width = word_rows.shape[1]
    rows_low = jnp.concatenate([word_rows, region_rows], axis=0)
    mixed = project(rows_low, inward_all[0], bias_rows, 0)
    word_mix = mixed[:words_count]
    region_mix = mixed[words_count:]
    word_context, word_total = attend(
        word_mix[:, :width],
        region_mix[:, width : 2 * width],
        region_mix[:, 2 * width :],
        cross_mask,
    )
    region_context, region_total = attend(
        region_mix[:, :width],
        word_mix[:, width : 2 * width],
        word_mix[:, 2 * width :],
        cross_mask.T,
    )
    context = jnp.concatenate([word_context, region_context], axis=0)
    summed = rows_low.astype(jnp.float32) + matmul(context, outward_all[0]) + bias_rows[2]
    result, norm_stats = normalize(summed, gain_rows[0], bias_rows[9])
    return (result, (rows_low, mixed, context, word_total, region_total, norm_stats))


def cross_backward(grad_out, kept, weights, cross_mask, words_count):
    inward_all, outward_all, bias_rows, gain_rows = weights
    rows_low, mixed, context, word_total, region_total, norm_stats = kept
    width = rows_low.shape[1]
    grad_sum, grad_context, grad_outward, grad_bias_out, grad_gain, grad_shift = branch_back(
        grad_out, context, norm_stats, gain_rows[0], outward_all[0]
    )
    word_mix = mixed[:words_count]
    region_mix = mixed[words_count:]
    word_query_grad, region_key_grad, region_value_grad = attend_back(
        word_mix[:, :width],
        region_mix[:, width : 2 * width],
        region_mix[:, 2 * width :],
        cross_mask,
        word_total,
        grad_context[:words_count],
    )
    region_query_grad, word_key_grad, word_value_grad = attend_back(
        region_mix[:, :width],
        word_mix[:, width : 2 * width],
        word_mix[:, 2 * width :],
        cross_mask.T,
        region_total,
        grad_context[words_count:],
    )
    grad_parts = (
        jnp.concatenate([word_query_grad, region_query_grad], axis=0),
        jnp.concatenate([word_key_grad, region_key_grad], axis=0),
        jnp.concatenate([word_value_grad, region_value_grad], axis=0),
    )
    grad_rows, grad_inward, grad_bias_query, grad_bias_value = project_back(
        grad_sum, grad_parts, rows_low, inward_all[0]
    )
    return (
        grad_rows,
        grad_inward,
        grad_outward,
        (grad_bias_query, grad_bias_value, grad_bias_out),
        grad_gain,
        grad_shift,
    )


def gelu_exact(values):
    return jax.nn.gelu(values, approximate=False)


def feed_forward(rows_in, weights, feed_index, attend_set):
    expand_all, shrink_all, hidden_all = weights
    bias_rows, gain_rows = (attend_set[2], attend_set[3])
    rows_low = rows_in.astype(jnp.bfloat16)
    before = matmul(rows_low, expand_all[feed_index]) + hidden_all[feed_index].astype(jnp.float32)
    hidden = gelu_exact(before).astype(jnp.bfloat16)
    summed = rows_in + matmul(hidden, shrink_all[feed_index]) + bias_rows[14 + feed_index]
    result, norm_stats = normalize(summed, gain_rows[3 + feed_index], bias_rows[12 + feed_index])
    return (result, (rows_low, before, hidden, norm_stats))


def feed_backward(grad_out, kept, weights, feed_index, gain_rows):
    expand_all, shrink_all, hidden_all = weights
    rows_low, before, hidden, norm_stats = kept
    grad_sum, grad_gain, grad_shift = normalize_back(
        grad_out, norm_stats, gain_rows[3 + feed_index]
    )
    grad_branch = grad_sum.astype(jnp.bfloat16)
    grad_shrink = (hidden, grad_branch)
    grad_hidden = matmul_nt(grad_branch, shrink_all[feed_index])
    unused_value, slope_back = jax.vjp(gelu_exact, before)
    grad_before = slope_back(grad_hidden)[0].astype(jnp.bfloat16)
    grad_expand = (rows_low, grad_before)
    grad_rows = grad_sum + matmul_nt(grad_before, expand_all[feed_index])
    return (
        grad_rows,
        grad_expand,
        grad_shrink,
        column_sums(grad_before),
        column_sums(grad_branch),
        grad_gain,
        grad_shift,
    )


UNIT = 96
WIDE = 768
SLOTS = 4
ACC_SLOTS = 6
LAG_A = 2
LAG_B = 2
LAG_Z = 1


WORDS = 128
REGIONS = 256
ROWS = 384
HIDDEN = 3072
PAIRS_OF_HEADS = 6
PAIR_WIDE = 128


def flip(position, bits):
    return lax.bitwise_xor(position, bits)


def dot_nt(left, right):
    return lax.dot_general(left, right, (((1,), (1,)), ((), ())), preferred_element_type=jnp.float32)


def dot_tn(left, right):
    return lax.dot_general(left, right, (((0,), (0,)), ((), ())), preferred_element_type=jnp.float32)


def spread(part):
    source = lax.broadcasted_iota(jnp.int32, (128, WIDE), 0)
    target = lax.broadcasted_iota(jnp.int32, (128, WIDE), 1)
    return jnp.logical_and(source < UNIT, target == source + part * UNIT)


def half_lanes():
    lane = lax.broadcasted_iota(jnp.int32, (1, PAIR_WIDE), 1)
    return (lane < HEAD_DIM, lane >= HEAD_DIM)


def only(values, chosen):
    return jnp.where(chosen, values, jnp.zeros_like(values))


ATTEND_CROSS_WORD = ((0, WORDS), (WORDS, REGIONS))
ATTEND_CROSS_REGION = ((WORDS, REGIONS), (0, WORDS))
ATTEND_WORD = ((0, WORDS), (0, WORDS))
ATTEND_REGION = ((WORDS, REGIONS), (WORDS, REGIONS))


def attend_into(rows_of, mixed, allowed, shares, context):
    (query_at, query_count), (key_at, key_count) = rows_of
    blocked = jnp.where(allowed, 0.0, masked_score)

    def pair(p, carry):
        at = pl.multiple_of(p * PAIR_WIDE, PAIR_WIDE)
        queries = mixed[pl.ds(query_at, query_count), pl.ds(at, PAIR_WIDE)]
        key_rows = mixed[pl.ds(key_at, key_count), pl.ds(WIDE + at, PAIR_WIDE)]
        value_rows = mixed[pl.ds(key_at, key_count), pl.ds(2 * WIDE + at, PAIR_WIDE)]
        total = jnp.zeros((query_count, PAIR_WIDE), jnp.float32)
        for side, chosen in enumerate(half_lanes()):
            scores = dot_nt(only(queries, chosen), key_rows) * HEAD_DIM ** (-0.5) + blocked
            lifted = jnp.exp(scores - jnp.max(scores, axis=-1, keepdims=True))
            share = (lifted / jnp.sum(lifted, axis=-1, keepdims=True)).astype(jnp.bfloat16)
            shares[2 * p + side] = share
            total = total + matmul(share, only(value_rows, chosen))
        context[pl.ds(query_at, query_count), pl.ds(at, PAIR_WIDE)] = total.astype(jnp.bfloat16)
        return carry

    lax.fori_loop(0, PAIRS_OF_HEADS, pair, 0)


def row_norm(summed):
    center = summed - jnp.mean(summed, axis=-1, keepdims=True)
    inverse = lax.rsqrt(jnp.mean(center * center, axis=-1, keepdims=True) + norm_epsilon)
    return (center * inverse, inverse)


def forward_kernel(*refs):
    (
        rows_low,
        word_across,
        region_across,
        word_down,
        region_down,
        small,
        inward,
        outward,
        expand,
        shrink,
        result,
        params,
        hidden_rows,
        mixed_cross,
        mixed_self,
        shares_cw,
        shares_cr,
        shares_w,
        shares_r,
        context_cross_t,
        context_self_t,
        rows_zero_t,
        rows_one_t,
        rows_two_t,
        hidden_t,
        slope,
        normed,
        inverse,
        inward_out,
        outward_out,
        expand_out,
        shrink_out,
        inward_all,
        outward_all,
        expand_all,
        shrink_all,
        small_all,
        stream,
        stream_low,
        context,
        hidden,
        sends,
        recvs,
        small_sends,
        small_recvs,
        local_sems,
    ) = refs
    me = lax.axis_index("fsdp")
    peers = {"x": {"fsdp": flip(me, 2)}, "y": {"fsdp": flip(me, 4)}, "core": {"fsdp": flip(me, 1)}}

    barrier = pltpu.get_barrier_semaphore()
    for offset in range(1, 8):
        pl.semaphore_signal(barrier, inc=1, device_id={"fsdp": flip(me, offset)}, device_id_type=MESH)
    pl.semaphore_wait(barrier, 7)

    def remote(src, dst, send_sem, recv_sem, peer):
        return pltpu.make_async_remote_copy(
            src_ref=src, dst_ref=dst, send_sem=send_sem, recv_sem=recv_sem, device_id=peer, device_id_type=MESH
        )

    def small_copy(offset, owner):
        return remote(
            small_all.at[owner],
            small_all.at[owner],
            small_sends.at[offset - 1],
            small_recvs.at[offset - 1],
            {"fsdp": flip(me, offset)},
        )

    small_all[me] = small[...]
    for offset in range(1, 8):
        small_copy(offset, me).start()

    chunks = [
        (inward, inward_all, 0, 0, UNIT, 0, 3 * WIDE),
        (outward, outward_all, 0, 0, UNIT, 0, WIDE),
        (inward, inward_all, 1, 0, UNIT, 0, 3 * WIDE),
        (inward, inward_all, 2, 0, UNIT, 0, 3 * WIDE),
        (outward, outward_all, 1, 0, UNIT, 0, WIDE),
        (outward, outward_all, 2, 0, UNIT, 0, WIDE),
        (expand, expand_all, 0, 0, UNIT, 0, 2 * WIDE),
        (expand, expand_all, 0, 0, UNIT, 2 * WIDE, 2 * WIDE),
        (expand, expand_all, 1, 0, UNIT, 0, 2 * WIDE),
        (expand, expand_all, 1, 0, UNIT, 2 * WIDE, 2 * WIDE),
        (shrink, shrink_all, 0, 0, 2 * UNIT, 0, WIDE),
        (shrink, shrink_all, 0, 2 * UNIT, 2 * UNIT, 0, WIDE),
        (shrink, shrink_all, 1, 0, 2 * UNIT, 0, WIDE),
        (shrink, shrink_all, 1, 2 * UNIT, 2 * UNIT, 0, WIDE),
    ]

    def own_part(k):
        source, _, matrix, first, count, column, columns = chunks[k]
        return source.at[matrix, pl.ds(first, count), pl.ds(column, columns)]

    def part(k, owner, half=None):
        source, gathered, matrix, first, count, column, columns = chunks[k]
        start = owner * source.shape[1] + first
        if half is not None:
            count = count // 2
            start = start + half * count
        return gathered.at[matrix, pl.ds(pl.multiple_of(start, 16), count), pl.ds(column, columns)]

    X, Y, DIAG_Y, DIAG_X, CORE_OWN, CORE_X, CORE_Y, CORE_DIAG = range(8)

    def copy(k, kind):
        owner, half, peer = {
            X: (me, None, "x"),
            Y: (me, None, "y"),
            DIAG_Y: (flip(me, 2), 0, "y"),
            DIAG_X: (flip(me, 4), 1, "x"),
            CORE_OWN: (me, None, "core"),
            CORE_X: (flip(me, 2), None, "core"),
            CORE_Y: (flip(me, 4), None, "core"),
            CORE_DIAG: (flip(me, 6), None, "core"),
        }[kind]
        source = own_part(k) if kind in (X, Y, CORE_OWN) else part(k, owner, half)
        return remote(source, part(k, owner, half), sends.at[k, kind], recvs.at[k, kind], peers[peer])

    def arrival(k, kind):
        owner, half, peer = {
            X: (flip(me, 2), None, "x"),
            Y: (flip(me, 4), None, "y"),
            DIAG_Y: (flip(me, 6), 0, "y"),
            DIAG_X: (flip(me, 6), 1, "x"),
            CORE_OWN: (flip(me, 1), None, "core"),
            CORE_X: (flip(me, 3), None, "core"),
            CORE_Y: (flip(me, 5), None, "core"),
            CORE_DIAG: (flip(me, 7), None, "core"),
        }[kind]
        here = part(k, owner, half)
        return remote(here, here, sends.at[k, kind], recvs.at[k, kind], peers[peer])

    def own_local(k):
        return pltpu.make_async_copy(own_part(k), part(k, me), local_sems.at[k])

    def start_own(k):
        own_local(k).start()
        for kind in (X, Y, CORE_OWN):
            copy(k, kind).start()

    def forward_first(k):
        arrival(k, X).wait_recv()
        copy(k, DIAG_Y).start()
        copy(k, CORE_X).start()
        arrival(k, Y).wait_recv()
        copy(k, DIAG_X).start()
        copy(k, CORE_Y).start()

    def forward_second(k):
        arrival(k, DIAG_Y).wait_recv()
        arrival(k, DIAG_X).wait_recv()
        copy(k, CORE_DIAG).start()

    def complete(k):
        own_local(k).wait()
        for kind in (CORE_OWN, CORE_X, CORE_Y, CORE_DIAG):
            arrival(k, kind).wait_recv()

    keeps = []

    def keep(source, target):
        saved = pltpu.make_async_copy(source, target, local_sems.at[len(chunks) + len(keeps)])
        saved.start()
        keeps.append(saved)

    def read_small():
        for offset in range(1, 8):
            small_copy(offset, flip(me, offset)).wait_recv()
        totals = jnp.zeros((21, WIDE), jnp.float32)
        hidden_parts = [[jnp.zeros((1, WIDE), jnp.float32) for _ in range(4)] for _ in range(2)]
        for owner in range(8):
            own = small_all[owner]
            totals = totals + matmul(own, spread(owner).astype(jnp.bfloat16))[:21]
            for q in range(4):
                placed = matmul(own, spread((owner % 2) * 4 + q).astype(jnp.bfloat16))
                for f in range(2):
                    row = 21 + 4 * f + q
                    hidden_parts[f][owner // 2] = hidden_parts[f][owner // 2] + placed[row : row + 1]
        params[0:21, :] = totals
        for f in range(2):
            for block in range(4):
                hidden_rows[f : f + 1, block * WIDE : (block + 1) * WIDE] = hidden_parts[f][block]

    def transposed_into(target, values, at, count):
        target[:, pl.ds(at, count)] = values.T

    def project_into(source, at, count, module, mixed):
        for third, bias_row in enumerate((3 * module, None, 3 * module + 1)):
            product = matmul(source[pl.ds(at, count), :], inward_all[module, :, third * WIDE : (third + 1) * WIDE])
            if bias_row is not None:
                product = product + params[bias_row : bias_row + 1, :]
            mixed[pl.ds(at, count), third * WIDE : (third + 1) * WIDE] = product.astype(jnp.bfloat16)

    def join(at, weights, left, residual, bias_row, norm_at, norm_index):
        rows = pl.ds(at, 128)
        summed = residual + matmul(left[rows, :], weights) + params[bias_row : bias_row + 1, :]
        unit, scale = row_norm(summed)
        normed[norm_at, rows, :] = unit
        inverse[norm_at, rows, :] = jnp.broadcast_to(scale, (128, 128))
        return unit * params[16 + norm_index : 17 + norm_index, :] + params[9 + norm_index : 10 + norm_index, :]

    def cross_in():
        project_into(rows_low, 0, ROWS, 0, mixed_cross)
        attend_into(ATTEND_CROSS_WORD, mixed_cross, word_down[...] == region_across[...], shares_cw, context)
        attend_into(ATTEND_CROSS_REGION, mixed_cross, region_down[...] == word_across[...], shares_cr, context)
        for at in range(0, ROWS, 128):
            transposed_into(rows_zero_t, rows_low[at : at + 128, :], at, 128)
            transposed_into(context_cross_t, context[at : at + 128, :], at, 128)

    def cross_out():
        for at in range(0, ROWS, 128):
            one = join(at, outward_all[0], context, rows_low[at : at + 128, :].astype(jnp.float32), 2, 0, 0)
            stream[at : at + 128, :] = one
            one_low = one.astype(jnp.bfloat16)
            stream_low[at : at + 128, :] = one_low
            transposed_into(rows_one_t, one_low, at, 128)

    def word_in():
        project_into(stream_low, 0, WORDS, 1, mixed_self)
        attend_into(ATTEND_WORD, mixed_self, word_down[...] == word_across[...], shares_w, context)
        transposed_into(context_self_t, context[0:WORDS, :], 0, WORDS)

    def region_in():
        project_into(stream_low, WORDS, REGIONS, 2, mixed_self)
        attend_into(ATTEND_REGION, mixed_self, region_down[...] == region_across[...], shares_r, context)
        for at in range(WORDS, ROWS, 128):
            transposed_into(context_self_t, context[at : at + 128, :], at, 128)

    def self_out(module, first, last):
        for at in range(first, last, 128):
            two = join(at, outward_all[module], context, stream[at : at + 128, :], 3 * module + 2, 1, module)
            stream[at : at + 128, :] = two
            two_low = two.astype(jnp.bfloat16)
            stream_low[at : at + 128, :] = two_low
            transposed_into(rows_two_t, two_low, at, 128)

    def feed_in(f, first, last, column, columns):
        step = 256

        def tile(t, carry):
            at = pl.multiple_of(column + t * step, step)
            for row in range(first, last, 128):
                before = (
                    matmul(stream_low[row : row + 128, :], expand_all[f, :, pl.ds(at, step)])
                    + hidden_rows[f : f + 1, pl.ds(at, step)]
                )
                below = 0.5 * (1.0 + lax.erf(before * 0.5**0.5))
                value = (before * below).astype(jnp.bfloat16)
                density = jnp.exp(-0.5 * before * before) * 0.3989422804014327
                hidden[row : row + 128, pl.ds(at, step)] = value
                hidden_t[pl.ds(at, step), row : row + 128] = value.T
                slope[row : row + 128, pl.ds(at, step)] = (below + before * density).astype(jnp.bfloat16)
            return carry

        lax.fori_loop(0, columns // step, tile, 0)

    def feed_out(f, first, last):
        for at in range(first, last, 128):
            last_rows = join(at, shrink_all[f], hidden, stream[at : at + 128, :], 14 + f, 2, 3 + f)
            result[at : at + 128, :] = last_rows.astype(jnp.bfloat16)

    def nothing():
        pass

    pieces = [
        lambda: (cross_in(), keep(inward_all.at[0], inward_out.at[0])),
        lambda: (cross_out(), keep(outward_all.at[0], outward_out.at[0])),
        lambda: (word_in(), keep(inward_all.at[1], inward_out.at[1])),
        lambda: (region_in(), keep(inward_all.at[2], inward_out.at[2])),
        lambda: (self_out(1, 0, WORDS), keep(outward_all.at[1], outward_out.at[1])),
        lambda: (self_out(2, WORDS, ROWS), keep(outward_all.at[2], outward_out.at[2])),
        lambda: feed_in(0, 0, WORDS, 0, 2 * WIDE),
        lambda: (feed_in(0, 0, WORDS, 2 * WIDE, 2 * WIDE), keep(expand_all.at[0], expand_out.at[0])),
        lambda: feed_in(1, WORDS, ROWS, 0, 2 * WIDE),
        lambda: (feed_in(1, WORDS, ROWS, 2 * WIDE, 2 * WIDE), keep(expand_all.at[1], expand_out.at[1])),
        nothing,
        lambda: (keep(shrink_all.at[0], shrink_out.at[0]), feed_out(0, 0, WORDS)),
        nothing,
        lambda: (keep(shrink_all.at[1], shrink_out.at[1]), feed_out(1, WORDS, ROWS)),
    ]
    count = len(chunks)
    start_own(0)
    start_own(1)
    read_small()
    for k in range(count + 2):
        if k + 2 < count:
            start_own(k + 2)
        if k < count:
            forward_first(k)
        if 0 <= k - 1 < count:
            forward_second(k - 1)
        if 0 <= k - 2 < count:
            complete(k - 2)
            pieces[k - 2]()
    for saved in keeps:
        saved.wait()
    for offset in range(1, 8):
        small_copy(offset, me).wait_send()
    for k in range(count):
        for kind in range(8):
            copy(k, kind).wait_send()


def forward(rows_low, word_ids, region_ids, small, inward, outward, expand, shrink):
    low = jnp.bfloat16
    dma = pltpu.SemaphoreType.DMA
    vmem = pl.BlockSpec(memory_space=pltpu.VMEM)
    hbm = pl.BlockSpec(memory_space=pl.ANY)
    shape = jax.ShapeDtypeStruct
    weights = [
        shape((3, WIDE, 3 * WIDE), low),
        shape((3, WIDE, WIDE), low),
        shape((2, WIDE, HIDDEN), low),
        shape((2, HIDDEN, WIDE), low),
    ]
    residuals = [
        shape((24, WIDE), jnp.float32),
        shape((2, HIDDEN), jnp.float32),
        shape((ROWS, 3 * WIDE), low),
        shape((ROWS, 3 * WIDE), low),
        shape((HEADS, WORDS, REGIONS), low),
        shape((HEADS, REGIONS, WORDS), low),
        shape((HEADS, WORDS, WORDS), low),
        shape((HEADS, REGIONS, REGIONS), low),
        shape((WIDE, ROWS), low),
        shape((WIDE, ROWS), low),
        shape((WIDE, ROWS), low),
        shape((WIDE, ROWS), low),
        shape((WIDE, ROWS), low),
        shape((HIDDEN, ROWS), low),
        shape((ROWS, HIDDEN), low),
        shape((3, ROWS, WIDE), jnp.float32),
        shape((3, ROWS, 128), jnp.float32),
    ]
    out_shape = [shape((ROWS, WIDE), low)] + residuals + weights
    outs = pl.pallas_call(
        forward_kernel,
        out_shape=out_shape,
        in_specs=[vmem] * 6 + [hbm] * 4,
        out_specs=[vmem] * (1 + len(residuals)) + [hbm] * 4,
        scratch_shapes=[pltpu.VMEM(w.shape, w.dtype) for w in weights]
        + [
            pltpu.VMEM((8, 32, 128), low),
            pltpu.VMEM((ROWS, WIDE), jnp.float32),
            pltpu.VMEM((ROWS, WIDE), low),
            pltpu.VMEM((ROWS, WIDE), low),
            pltpu.VMEM((ROWS, HIDDEN), low),
            dma((14, 8)),
            dma((14, 8)),
            dma((7,)),
            dma((7,)),
            dma((24,)),
        ],
        compiler_params=pltpu.CompilerParams(
            collective_id=1, has_side_effects=True, vmem_limit_bytes=64 * 2**20 - 2**16
        ),
    )(
        rows_low,
        word_ids,
        region_ids,
        word_ids.reshape(WORDS, 1),
        region_ids.reshape(REGIONS, 1),
        small,
        inward,
        outward,
        expand,
        shrink,
    )
    return outs[0], outs[1 : 1 + len(residuals)], outs[1 + len(residuals) :]


WINDOW = 6

GROUPS = (
    (4, 0, 0, WORDS, True, (3, 0)),
    (4, 0, WORDS, REGIONS, True, (3, 1)),
    (4, 1, 0, WORDS, False, (2, 0)),
    (4, 1, WORDS, REGIONS, False, (2, 1)),
    (1, 2, 0, WORDS, False, (1, 1)),
    (1, 2, WORDS, REGIONS, False, (1, 2)),
    (3, 3, 0, WORDS, False, (0, 1)),
    (3, 3, WORDS, REGIONS, False, (0, 2)),
    (1, 4, 0, ROWS, False, (1, 0)),
    (3, 5, 0, ROWS, False, (0, 0)),
)
UNITS = sum(group[0] for group in GROUPS)

BLOCKS = (
    [(kind, f, c) for f in range(2) for c in range(4) for kind in (3, 2)]
    + [(1, 1, 0), (1, 2, 0)]
    + [(0, m, c) for m in (1, 2) for c in range(3)]
    + [(1, 0, 0)]
    + [(0, 0, c) for c in range(3)]
)


def attend_back_into(rows_of, mixed, shares, grad_context, grad_mixed, first_pair, last_pair):
    (query_at, query_count), (key_at, key_count) = rows_of
    query_rows, key_rows = pl.ds(query_at, query_count), pl.ds(key_at, key_count)

    def pair(p, carry):
        at = pl.multiple_of(p * PAIR_WIDE, PAIR_WIDE)
        at_query, at_key, at_value = (pl.ds(third * WIDE + at, PAIR_WIDE) for third in range(3))
        queries = mixed[query_rows, at_query]
        keys = mixed[key_rows, at_key]
        values = mixed[key_rows, at_value]
        grads = grad_context[query_rows, at_query]
        grad_queries = jnp.zeros((query_count, PAIR_WIDE), jnp.float32)
        grad_keys = jnp.zeros((key_count, PAIR_WIDE), jnp.float32)
        grad_values = jnp.zeros((key_count, PAIR_WIDE), jnp.float32)
        for side, chosen in enumerate(half_lanes()):
            share = shares[2 * p + side]
            grad_head = only(grads, chosen)
            wide = share.astype(jnp.float32)
            weighted = wide * dot_nt(grad_head, values)
            grad_scores = (weighted - wide * jnp.sum(weighted, axis=-1, keepdims=True)).astype(jnp.bfloat16)
            grad_values = grad_values + dot_tn(share, grad_head)
            grad_queries = grad_queries + matmul(grad_scores, only(keys, chosen))
            grad_keys = grad_keys + dot_tn(grad_scores, only(queries, chosen))
        score_scale = HEAD_DIM ** (-0.5)
        grad_mixed[query_rows, at_query] = (grad_queries * score_scale).astype(jnp.bfloat16)
        grad_mixed[key_rows, at_key] = (grad_keys * score_scale).astype(jnp.bfloat16)
        grad_mixed[key_rows, at_value] = grad_values.astype(jnp.bfloat16)
        return carry

    lax.fori_loop(first_pair, last_pair, pair, 0)


def backward_kernel(*refs):
    saved_hbm, weights = refs[:18], refs[18:22]
    word_gradient, region_gradient, small_out, *totals = refs[22:29]
    (
        params,
        word_cotangent,
        region_cotangent,
        normed,
        inverse,
        hidden_t,
        slope,
        rows_two_t,
        context_self_t,
        mixed_self,
        shares_w,
        shares_r,
        rows_one_t,
        context_cross_t,
        mixed_cross,
        shares_cw,
        shares_cr,
        rows_zero_t,
    ) = saved = refs[29:47]
    (
        window,
        end_feed,
        grad_before,
        end_self,
        grad_mixed_self,
        end_cross,
        grad_mixed_cross,
        stream,
        grad_context,
        row_sums,
        hidden_sums,
        out,
        acc,
        core_out,
        core_in,
        half_out,
        half_in,
        full_out,
        full_in,
        plane,
        end_out,
        end_in,
        mid_out,
        mid_in,
        small_in,
        small_in_plane,
        small_planes,
        saved_sems,
        window_sems,
        total_sems,
        core_send,
        core_recv,
        half_send,
        half_recv,
        full_send,
        full_recv,
        z_send,
        z_recv,
        small_send,
        small_recv,
        free,
    ) = refs[47:]
    lefts = (hidden_t, rows_two_t, context_self_t, rows_one_t, context_cross_t, rows_zero_t)
    rights = (end_feed, grad_before, end_self, grad_mixed_self, end_cross, grad_mixed_cross)
    me = lax.axis_index("fsdp")
    z = lax.axis_index("rep")
    chip = me // 2
    lane = me % 2
    is_end = jnp.logical_or(z == 0, z == 3)
    is_mid = jnp.logical_or(z == 1, z == 2)
    core_peer = {"fsdp": flip(me, 1)}
    links = ({"fsdp": flip(me, 2)}, {"fsdp": flip(me, 4)})
    link_chip = (flip(chip, 1), flip(chip, 2))
    diagonal = flip(chip, 3)
    pair_peer = {"rep": flip(z, 1)}
    mid_peer = {"rep": 3 - z}
    low = jnp.bfloat16

    def load_saved(index):
        return pltpu.make_async_copy(saved_hbm[index], saved[index], saved_sems.at[index])

    def load_block(n):
        kind, index, c = BLOCKS[n]
        part = slice(c * WIDE, (c + 1) * WIDE)
        source = weights[kind].at[index, part, :] if kind == 3 else weights[kind].at[index, :, part]
        return pltpu.make_async_copy(source, window.at[n % WINDOW], window_sems.at[n % WINDOW])

    def wait_saved(*names):
        for name in names:
            load_saved([ref is name for ref in saved].index(True)).wait()

    for index in range(7):
        load_saved(index).start()
    for n in range(WINDOW):
        load_block(n).start()
    for index in range(7, 18):
        load_saved(index).start()

    barrier = pltpu.get_barrier_semaphore()
    for offset in range(1, 8):
        pl.semaphore_signal(barrier, inc=1, device_id={"fsdp": flip(me, offset)}, device_id_type=MESH)
    for offset in range(1, 4):
        pl.semaphore_signal(barrier, inc=1, device_id={"rep": (z + offset) % 4}, device_id_type=MESH)
    pl.semaphore_wait(barrier, 10)

    def remote(src, dst, send_sem, recv_sem, peer):
        return pltpu.make_async_remote_copy(
            src_ref=src, dst_ref=dst, send_sem=send_sem, recv_sem=recv_sem, device_id=peer, device_id_type=MESH
        )

    def small_copy(offset):
        peer = flip(me, offset)
        return remote(
            small_in.at[peer],
            small_in_plane.at[offset - 1],
            small_send.at[offset - 1],
            small_recv.at[offset - 1],
            {"fsdp": peer},
        )

    def small_plane_copy(offset, source):
        peer = (z + offset) % 4 if source is z else source
        return remote(
            small_planes.at[source],
            small_planes.at[source],
            small_send.at[6 + offset],
            small_recv.at[6 + offset],
            {"rep": peer},
        )

    def core_copy(u):
        slot = u % SLOTS
        return remote(core_out.at[slot], core_in.at[slot], core_send.at[slot], core_recv.at[slot], core_peer)

    def half_copy(u, way):
        slot = u % SLOTS
        return remote(
            half_out.at[slot, way], half_in.at[slot, way], half_send.at[slot, way], half_recv.at[slot, way], links[way]
        )

    def full_copy(u, way):
        slot = u % SLOTS
        return remote(
            full_out.at[slot, way], full_in.at[slot, way], full_send.at[slot, way], full_recv.at[slot, way], links[way]
        )

    def end_copy(u):
        slot = u % SLOTS
        return remote(end_out.at[slot], end_in.at[slot], z_send.at[0, slot], z_recv.at[0, slot], pair_peer)

    def mid_copy(u):
        slot = u % SLOTS
        return remote(mid_out.at[slot], mid_in.at[slot], z_send.at[1, slot], z_recv.at[1, slot], mid_peer)

    def back_copy(u):
        slot = u % SLOTS
        return remote(out.at[u], out.at[u], z_send.at[2, slot], z_recv.at[2, slot], pair_peer)

    def credit(u, channel, peer):
        @pl.when(u + SLOTS < UNITS)
        def _():
            pl.semaphore_signal(free.at[channel], inc=1, device_id=peer, device_id_type=MESH)

    def spend(u, channel):
        @pl.when(u >= SLOTS)
        def _():
            pl.semaphore_wait(free.at[channel], 1)

    def per_group(u, function):
        first = 0
        for group in GROUPS:
            start, units = first, group[0]

            @pl.when(jnp.logical_and(u >= start, u < start + units))
            def _(start=start, group=group):
                function(u - start, *group[1:])

            first = first + units

    def produce(u):
        slot = u % SLOTS
        keep = u % ACC_SLOTS
        spend(u, 0)

        def products(at, side, first_row, count, by_row, matrix):
            rows = pl.ds(first_row, count)
            column = 0 if by_row else pl.multiple_of(at * WIDE, WIDE)
            right = rights[side][rows, pl.ds(column, WIDE)]

            def product(core):
                blocks = []
                for block in range(4):
                    owner = 2 * block + core
                    row = owner * (4 * UNIT) + at * UNIT if by_row else owner * UNIT
                    blocks.append(lefts[side][pl.ds(pl.multiple_of(row, 16), UNIT), rows])
                return matmul(jnp.concatenate(blocks, axis=0), right)

            other = product(1 - lane).astype(low)
            for block in range(4):
                core_out[slot, block] = other[block * UNIT : (block + 1) * UNIT]
            core_copy(u).start()
            own = product(lane)
            for block in range(4):
                acc[keep, block] = own[block * UNIT : (block + 1) * UNIT]

        per_group(u, products)

    def join_cores(u):
        slot = u % SLOTS
        keep = u % ACC_SLOTS
        core_copy(u).wait()
        for way in range(2):
            spend(u, 1 + way)
        summed = acc[keep, diagonal] + core_in[slot, diagonal].astype(jnp.float32)
        half_out[slot, 0] = summed[: UNIT // 2].astype(low)
        half_out[slot, 1] = summed[UNIT // 2 :].astype(low)
        for way in range(2):
            half_copy(u, way).start()
        for block in (link_chip[0], link_chip[1], chip):
            acc[keep, block] = acc[keep, block] + core_in[slot, block].astype(jnp.float32)
        credit(u, 0, core_peer)

    def join_diagonal(u):
        slot = u % SLOTS
        keep = u % ACC_SLOTS
        for way in range(2):
            half_copy(u, way).wait()
            spend(u, 3 + way)
        half = UNIT // 2
        full_out[slot, 1, :half] = (acc[keep, link_chip[1], :half] + half_in[slot, 0].astype(jnp.float32)).astype(low)
        full_out[slot, 1, half:] = acc[keep, link_chip[1], half:].astype(low)
        full_copy(u, 1).start()
        full_out[slot, 0, half:] = (acc[keep, link_chip[0], half:] + half_in[slot, 1].astype(jnp.float32)).astype(low)
        full_out[slot, 0, :half] = acc[keep, link_chip[0], :half].astype(low)
        full_copy(u, 0).start()
        for way in range(2):
            credit(u, 1 + way, links[way])

    def join_plane(u):
        slot = u % SLOTS
        keep = u % ACC_SLOTS
        for way in range(2):
            full_copy(u, way).wait()
        summed = acc[keep, chip] + (full_in[slot, 0].astype(jnp.float32) + full_in[slot, 1].astype(jnp.float32))

        @pl.when(is_end)
        def _():
            spend(u, 5)
            end_out[slot] = summed.astype(low)
            end_copy(u).start()

        @pl.when(is_mid)
        def _():
            plane[slot] = summed

        for way in range(2):
            credit(u, 3 + way, links[way])

    def join_pair(u):
        slot = u % SLOTS

        @pl.when(is_end)
        def _():
            end_copy(u).wait_send()

        @pl.when(is_mid)
        def _():
            end_copy(u).wait_recv()
            spend(u, 6)
            mid_out[slot] = (plane[slot] + end_in[slot].astype(jnp.float32)).astype(low)
            mid_copy(u).start()
            credit(u, 5, pair_peer)

    def join_middle(u):
        slot = u % SLOTS

        @pl.when(is_mid)
        def _():
            mid_copy(u).wait()
            out[u] = (mid_out[slot].astype(jnp.float32) + mid_in[slot].astype(jnp.float32)).astype(low)
            back_copy(u).start()
            credit(u, 6, mid_peer)

    def total_copy(u, at, by_row, matrix):
        kind, index = matrix
        if by_row:
            place = totals[kind].at[index, pl.ds(pl.multiple_of(at * UNIT, UNIT), UNIT), :]
        else:
            place = totals[kind].at[index, :, pl.ds(pl.multiple_of(at * WIDE, WIDE), WIDE)]
        return pltpu.make_async_copy(out.at[u], place, total_sems.at[u])

    def finish(u):
        @pl.when(is_mid)
        def _():
            back_copy(u).wait_send()

        @pl.when(is_end)
        def _():
            back_copy(u).wait_recv()

        per_group(u, lambda at, side, first_row, count, by_row, matrix: total_copy(u, at, by_row, matrix).start())

    stages = [
        (0, produce),
        (1, join_cores),
        (1 + LAG_A, join_diagonal),
        (1 + LAG_A + LAG_B, join_plane),
        (1 + LAG_A + LAG_B + LAG_Z, join_pair),
        (1 + LAG_A + LAG_B + 2 * LAG_Z, join_middle),
        (1 + LAG_A + LAG_B + 3 * LAG_Z, finish),
    ]

    row_tiles = ((0, 0), (1, 128), (1, 256))

    def add_row(index, values):
        row_sums[index : index + 1, :] += jnp.sum(values, axis=0, keepdims=True)

    def norm_back(grad, kind, norm_index, at, ends, end_bias):
        rows = slice(at, at + 128)
        unit = normed[kind, rows, :]
        grad_unit = grad * params[16 + norm_index : 17 + norm_index, :]
        summed = inverse[kind, rows, :1] * (
            grad_unit
            - jnp.mean(grad_unit, axis=-1, keepdims=True)
            - unit * jnp.mean(grad_unit * unit, axis=-1, keepdims=True)
        )
        add_row(16 + norm_index, grad * unit)
        add_row(9 + norm_index, grad)
        stream[rows, :] = summed
        summed_low = summed.astype(low)
        ends[rows, :] = summed_low
        add_row(end_bias, summed_low.astype(jnp.float32))

    def feed_norm():
        wait_saved(params, word_cotangent, region_cotangent, normed, inverse)
        row_sums[...] = jnp.zeros_like(row_sums)
        hidden_sums[...] = jnp.zeros_like(hidden_sums)
        for f, at in row_tiles:
            cotangent = word_cotangent if f == 0 else region_cotangent
            first = at if f == 0 else at - WORDS
            norm_back(cotangent[first : first + 128, :].astype(jnp.float32), 2, 3 + f, at, end_feed, 14 + f)

    def next_block(n):
        if n + WINDOW < len(BLOCKS):
            load_block(n + WINDOW).start()

    def feed_back(f, c):
        n = 2 * (4 * f + c)
        load_block(n).wait()
        load_block(n + 1).wait()
        columns = slice(c * WIDE, (c + 1) * WIDE)
        for which, at in row_tiles:
            if which == f:
                rows = slice(at, at + 128)
                grad_hidden = dot_nt(end_feed[rows, :], window[n % WINDOW])
                before = (grad_hidden * slope[rows, columns].astype(jnp.float32)).astype(low)
                grad_before[rows, columns] = before
                row = 4 * f + c
                hidden_sums[row : row + 1, :] += jnp.sum(before.astype(jnp.float32), axis=0, keepdims=True)
                stream[rows, :] += dot_nt(before, window[(n + 1) % WINDOW])
        next_block(n)
        next_block(n + 1)

    def self_norm():
        for f, at in row_tiles:
            norm_back(stream[at : at + 128, :], 1, 1 + f, at, end_self, 5 + 3 * f)

    def self_context():
        for f in range(2):
            n = 16 + f
            load_block(n).wait()
            for which, at in row_tiles:
                if which == f:
                    grad_context[at : at + 128, :] = dot_nt(end_self[at : at + 128, :], window[n % WINDOW]).astype(low)
            next_block(n)

    def project_back(n, module, grad_mixed, tiles):
        for c in range(3):
            load_block(n + c).wait()
            columns = slice(c * WIDE, (c + 1) * WIDE)
            for at in tiles:
                part = grad_mixed[at : at + 128, columns]
                if c != 1:
                    add_row(3 * module + c // 2, part.astype(jnp.float32))
                stream[at : at + 128, :] += dot_nt(part, window[(n + c) % WINDOW])
            next_block(n + c)

    def cross_norm():
        for _, at in row_tiles:
            norm_back(stream[at : at + 128, :], 0, 0, at, end_cross, 2)

    def cross_context():
        n = 24
        load_block(n).wait()
        for _, at in row_tiles:
            grad_context[at : at + 128, :] = dot_nt(end_cross[at : at + 128, :], window[n % WINDOW]).astype(low)
        next_block(n)

    def give_rows():
        word_gradient[...] = stream[0:WORDS, :]
        region_gradient[...] = stream[WORDS:ROWS, :]

    def exact_nt(left, right):
        return lax.dot_general(
            left,
            right.astype(jnp.float32),
            (((1,), (1,)), ((), ())),
            precision=lax.Precision.HIGHEST,
            preferred_element_type=jnp.float32,
        )

    def give_small():
        small_in[...] = jnp.zeros_like(small_in)
        for owner in range(8):
            small_in[owner, 0:21, :] = exact_nt(row_sums[...], spread(owner))[:21]
        for place in range(8):
            placed = exact_nt(hidden_sums[...], spread(place))
            for f in range(2):
                for c in range(4):
                    row = 21 + 4 * f + place % 4
                    small_in[2 * c + place // 4, row : row + 1, :] = placed[4 * f + c : 4 * f + c + 1]
        for offset in range(1, 8):
            small_copy(offset).start()

    def join_small():
        summed = small_in[me]
        for offset in range(1, 8):
            small_copy(offset).wait()
            summed = summed + small_in_plane[offset - 1]
        small_planes[z] = summed
        for offset in range(1, 4):
            small_plane_copy(offset, z).start()

    def finish_small():
        for offset in range(1, 4):
            small_plane_copy(offset, z).wait_send()
            small_plane_copy(offset, (z + 4 - offset) % 4).wait_recv()
        small_out[...] = small_planes[0] + small_planes[1] + (small_planes[2] + small_planes[3])

    def self_back(rows_of, shares, first, last):
        attend_back_into(rows_of, mixed_self, shares, grad_context, grad_mixed_self, first, last)

    def cross_back(rows_of, shares, first, last):
        attend_back_into(rows_of, mixed_cross, shares, grad_context, grad_mixed_cross, first, last)

    pieces = {
        0: lambda: (wait_saved(slope), feed_back(0, 0)),
        1: lambda: feed_back(0, 1),
        2: lambda: feed_back(0, 2),
        3: lambda: feed_back(0, 3),
        4: lambda: feed_back(1, 0),
        5: lambda: feed_back(1, 1),
        6: lambda: feed_back(1, 2),
        7: lambda: (feed_back(1, 3), wait_saved(rows_two_t)),
        8: self_norm,
        9: lambda: (self_context(), wait_saved(context_self_t, mixed_self, shares_w)),
        10: lambda: (self_back(ATTEND_WORD, shares_w, 0, 6), wait_saved(shares_r, rows_one_t)),
        11: lambda: self_back(ATTEND_REGION, shares_r, 0, 2),
        12: lambda: self_back(ATTEND_REGION, shares_r, 2, 4),
        13: lambda: self_back(ATTEND_REGION, shares_r, 4, 6),
        14: lambda: project_back(18, 1, grad_mixed_self, (0,)),
        15: lambda: project_back(21, 2, grad_mixed_self, (128, 256)),
        16: lambda: (cross_norm(), wait_saved(context_cross_t, mixed_cross, shares_cw, shares_cr, rows_zero_t)),
        17: cross_context,
        18: lambda: cross_back(ATTEND_CROSS_WORD, shares_cw, 0, 3),
        19: lambda: cross_back(ATTEND_CROSS_WORD, shares_cw, 3, 6),
        20: lambda: cross_back(ATTEND_CROSS_REGION, shares_cr, 0, 3),
        21: lambda: cross_back(ATTEND_CROSS_REGION, shares_cr, 3, 6),
        22: lambda: (project_back(25, 0, grad_mixed_cross, (0, 128, 256)), give_rows()),
        23: give_small,
        25: join_small,
        27: finish_small,
    }

    feed_norm()

    def step(i, carry):
        for lag, stage in reversed(stages):
            if stage is produce:

                @pl.when(i == 0)
                def _():
                    wait_saved(hidden_t)

            @pl.when(jnp.logical_and(i >= lag, i < UNITS + lag))
            def _(lag=lag, stage=stage):
                stage(i - lag)

        for at, piece in pieces.items():

            @pl.when(i == at)
            def _(piece=piece):
                piece()

        return carry

    lax.fori_loop(0, UNITS + stages[-1][0], step, 0)

    def settle(u, carry):
        per_group(u, lambda at, side, first_row, count, by_row, matrix: total_copy(u, at, by_row, matrix).wait())
        return carry

    lax.fori_loop(0, UNITS, settle, 0)


def backward(saved, weights):
    block = (UNIT, WIDE)
    low, f32 = jnp.bfloat16, jnp.float32
    dma = pltpu.SemaphoreType.DMA
    vmem = pl.BlockSpec(memory_space=pltpu.VMEM)
    hbm = pl.BlockSpec(memory_space=pl.ANY)
    shape = jax.ShapeDtypeStruct
    small = (32, 128)
    return pl.pallas_call(
        backward_kernel,
        out_shape=(
            shape((WORDS, WIDE), f32),
            shape((REGIONS, WIDE), f32),
            shape(small, f32),
            shape((3, UNIT, 3 * WIDE), low),
            shape((3, UNIT, WIDE), low),
            shape((2, UNIT, HIDDEN), low),
            shape((2, 4 * UNIT, WIDE), low),
        ),
        in_specs=[hbm] * (len(saved) + len(weights)),
        out_specs=[vmem] * 3 + [hbm] * 4,
        scratch_shapes=[pltpu.VMEM(array.shape, array.dtype) for array in saved]
        + [
            pltpu.VMEM((WINDOW, WIDE, WIDE), low),
            pltpu.VMEM((ROWS, WIDE), low),
            pltpu.VMEM((ROWS, HIDDEN), low),
            pltpu.VMEM((ROWS, WIDE), low),
            pltpu.VMEM((ROWS, 3 * WIDE), low),
            pltpu.VMEM((ROWS, WIDE), low),
            pltpu.VMEM((ROWS, 3 * WIDE), low),
            pltpu.VMEM((ROWS, WIDE), f32),
            pltpu.VMEM((ROWS, WIDE), low),
            pltpu.VMEM((24, WIDE), f32),
            pltpu.VMEM((8, WIDE), f32),
            pltpu.VMEM((UNITS,) + block, low),
            pltpu.VMEM((ACC_SLOTS, 4) + block, f32),
            pltpu.VMEM((SLOTS, 4) + block, low),
            pltpu.VMEM((SLOTS, 4) + block, low),
            pltpu.VMEM((SLOTS, 2, UNIT // 2, WIDE), low),
            pltpu.VMEM((SLOTS, 2, UNIT // 2, WIDE), low),
            pltpu.VMEM((SLOTS, 2) + block, low),
            pltpu.VMEM((SLOTS, 2) + block, low),
            pltpu.VMEM((SLOTS,) + block, f32),
            pltpu.VMEM((SLOTS,) + block, low),
            pltpu.VMEM((SLOTS,) + block, low),
            pltpu.VMEM((SLOTS,) + block, low),
            pltpu.VMEM((SLOTS,) + block, low),
            pltpu.VMEM((8,) + small, f32),
            pltpu.VMEM((7,) + small, f32),
            pltpu.VMEM((4,) + small, f32),
            dma((18,)),
            dma((WINDOW,)),
            dma((UNITS,)),
            dma((SLOTS,)),
            dma((SLOTS,)),
            dma((SLOTS, 2)),
            dma((SLOTS, 2)),
            dma((SLOTS, 2)),
            dma((SLOTS, 2)),
            dma((3, SLOTS)),
            dma((3, SLOTS)),
            dma((10,)),
            dma((10,)),
            pltpu.SemaphoreType.REGULAR((7,)),
        ],
        compiler_params=pltpu.CompilerParams(
            collective_id=0, has_side_effects=True, vmem_limit_bytes=64 * 2**20 - 2**16
        ),
    )(*saved, *weights)


def paired(
    word_rows,
    region_rows,
    word_segment,
    region_segment,
    inward,
    outward,
    biases,
    norm_gain,
    expand_weight,
    shrink_weight,
    hidden_bias,
    word_cotangent,
    region_cotangent,
):
    small = jnp.concatenate([biases, norm_gain, hidden_bias.reshape(8, UNIT)], axis=0)
    small = jnp.pad(small, ((0, 3), (0, 128 - UNIT)))
    rows_low = jnp.concatenate([word_rows, region_rows], axis=0)
    result, residuals, weights = forward(
        rows_low, word_segment, region_segment, small, inward, outward, expand_weight, shrink_weight
    )
    (
        params,
        hidden_rows,
        mixed_cross,
        mixed_self,
        shares_cw,
        shares_cr,
        shares_w,
        shares_r,
        context_cross_t,
        context_self_t,
        rows_zero_t,
        rows_one_t,
        rows_two_t,
        hidden_t,
        slope,
        normed,
        inverse,
    ) = residuals
    saved = (
        params,
        word_cotangent,
        region_cotangent,
        normed,
        inverse,
        hidden_t,
        slope,
        rows_two_t,
        context_self_t,
        mixed_self,
        shares_w,
        shares_r,
        rows_one_t,
        context_cross_t,
        mixed_cross,
        shares_cw,
        shares_cr,
        rows_zero_t,
    )
    word_gradient, region_gradient, small_total, *totals = backward(saved, weights)
    inward_total, outward_total, expand_total, shrink_total = (total.astype(jnp.float32) for total in totals)
    small_total = small_total[:, :UNIT]
    return (
        result[:WORDS],
        result[WORDS:],
        word_gradient,
        region_gradient,
        inward_total,
        outward_total,
        small_total[:16],
        small_total[16:21],
        expand_total,
        shrink_total,
        small_total[21:29].reshape(2, 4 * UNIT),
    )


def general(
    devices,
    word_rows,
    region_rows,
    word_segment,
    region_segment,
    inward,
    outward,
    biases,
    norm_gain,
    expand_weight,
    shrink_weight,
    hidden_bias,
    word_cotangent,
    region_cotangent,
):
    words_count = word_rows.shape[0]
    width = word_rows.shape[1]
    word_ids = word_segment[0]
    region_ids = region_segment[0]
    cross_mask = word_ids[:, None] == region_ids[None, :]
    word_mask = word_ids[:, None] == word_ids[None, :]
    region_mask = region_ids[:, None] == region_ids[None, :]
    shard = biases.shape[1]
    per_shard = hidden_bias.shape[1] // shard
    small_shard = jnp.concatenate([biases, norm_gain, hidden_bias.reshape(2 * per_shard, shard)], axis=0)
    small_all = lax.all_gather(small_shard, "fsdp", axis=0)
    bias_count = biases.shape[0]
    gain_count = norm_gain.shape[0]
    row_params = small_all[:, : bias_count + gain_count].transpose(1, 0, 2).reshape(bias_count + gain_count, width)
    hidden_all = (
        small_all[:, bias_count + gain_count :]
        .reshape(devices, 2, per_shard * shard)
        .transpose(1, 0, 2)
        .reshape(2, devices * per_shard * shard)
    )
    inward_all, outward_all = (
        lax.all_gather(inward, "fsdp", axis=1, tiled=True),
        lax.all_gather(outward, "fsdp", axis=1, tiled=True),
    )
    attend_set = (
        inward_all,
        outward_all,
        row_params[:bias_count].astype(jnp.float32),
        row_params[bias_count:].astype(jnp.float32),
    )
    crossed, cross_kept = cross_forward(word_rows, region_rows, attend_set, cross_mask)
    word_one, word_kept = self_forward(crossed[:words_count], attend_set, 1, word_mask)
    region_one, region_kept = self_forward(crossed[words_count:], attend_set, 2, region_mask)
    expand_all, shrink_all = (
        lax.all_gather(expand_weight, "fsdp", axis=1, tiled=True),
        lax.all_gather(shrink_weight, "fsdp", axis=1, tiled=True),
    )
    feed_set = (expand_all, shrink_all, hidden_all)
    word_two, word_feed = feed_forward(word_one, feed_set, 0, attend_set)
    region_two, region_feed = feed_forward(region_one, feed_set, 1, attend_set)
    word_back = feed_backward(word_cotangent.astype(jnp.float32), word_feed, feed_set, 0, attend_set[3])
    region_back = feed_backward(region_cotangent.astype(jnp.float32), region_feed, feed_set, 1, attend_set[3])
    word_self = self_backward(word_back[0], word_kept, attend_set, 1, word_mask)
    region_self = self_backward(region_back[0], region_kept, attend_set, 2, region_mask)
    grad_crossed = jnp.concatenate([word_self[0], region_self[0]], axis=0)
    cross_back = cross_backward(grad_crossed, cross_kept, attend_set, cross_mask, words_count)
    row_grads = jnp.stack(
        [
            cross_back[3][0],
            cross_back[3][1],
            cross_back[3][2],
            word_self[3][0],
            word_self[3][1],
            word_self[3][2],
            region_self[3][0],
            region_self[3][1],
            region_self[3][2],
            cross_back[5],
            word_self[5],
            region_self[5],
            word_back[6],
            region_back[6],
            word_back[4],
            region_back[4],
            cross_back[4],
            word_self[4],
            region_self[4],
            word_back[5],
            region_back[5],
        ]
    )
    hidden_grads = jnp.stack([word_back[3], region_back[3]])
    small_grads = jnp.concatenate(
        [
            row_grads.reshape(bias_count + gain_count, devices, shard).transpose(1, 0, 2),
            hidden_grads.reshape(2, devices, per_shard, shard)
            .transpose(1, 0, 2, 3)
            .reshape(devices, 2 * per_shard, shard),
        ],
        axis=1,
    )

    def reduced(products, axis):
        mine = lax.psum_scatter(jnp.stack(products), "fsdp", scatter_dimension=axis, tiled=True)
        return lax.psum(mine.astype(jnp.bfloat16), "rep").astype(jnp.float32)

    shrink_total = reduced([matmul_tn(*word_back[2]), matmul_tn(*region_back[2])], 1)
    expand_total = reduced([matmul_tn(*word_back[1]), matmul_tn(*region_back[1])], 1)
    outward_total = reduced([matmul_tn(*cross_back[2]), matmul_tn(*word_self[2]), matmul_tn(*region_self[2])], 1)
    inward_total = reduced([matmul_tn(*cross_back[1]), matmul_tn(*word_self[1]), matmul_tn(*region_self[1])], 1)
    small_total = lax.psum(lax.psum_scatter(small_grads, "fsdp", scatter_dimension=0, tiled=False), "rep")
    grad_rows = cross_back[0]
    return (
        word_two.astype(jnp.bfloat16),
        region_two.astype(jnp.bfloat16),
        grad_rows[:words_count],
        grad_rows[words_count:],
        inward_total,
        outward_total,
        small_total[:bias_count],
        small_total[bias_count : bias_count + gain_count],
        expand_total,
        shrink_total,
        small_total[bias_count + gain_count :].reshape(2, per_shard * shard),
    )


def solution(mesh):
    sizes = (mesh.shape["rep"], mesh.shape["fsdp"])
    return jax.shard_map(
        paired if sizes == (4, 8) else functools.partial(general, mesh.shape["fsdp"]),
        mesh=mesh,
        in_specs=(
            P(("rep", "fsdp"), None),
            P(("rep", "fsdp"), None),
            P(("rep", "fsdp"), None),
            P(("rep", "fsdp"), None),
            P(None, "fsdp", None),
            P(None, "fsdp", None),
            P(None, "fsdp"),
            P(None, "fsdp"),
            P(None, "fsdp", None),
            P(None, "fsdp", None),
            P(None, "fsdp"),
            P(("rep", "fsdp"), None),
            P(("rep", "fsdp"), None),
        ),
        out_specs=(
            P(("rep", "fsdp"), None),
            P(("rep", "fsdp"), None),
            P(("rep", "fsdp"), None),
            P(("rep", "fsdp"), None),
            P(None, "fsdp", None),
            P(None, "fsdp", None),
            P(None, "fsdp"),
            P(None, "fsdp"),
            P(None, "fsdp", None),
            P(None, "fsdp", None),
            P(None, "fsdp"),
        ),
        check_vma=False,
    )
```

```python
import functools

import jax
import jax.numpy as jnp
from jax import lax
from jax.experimental import pallas as pl
from jax.experimental.pallas import tpu as pltpu
from jax.sharding import PartitionSpec as P

MESH = pl.DeviceIdType.MESH

HEADS = 12
HEAD_DIM = 64


norm_epsilon = 1e-12
masked_score = -1e30


def matmul(left_op, right_op):
    return jnp.dot(left_op, right_op, preferred_element_type=jnp.float32)


def matmul_tn(left_op, right_op):
    return lax.dot_general(
        left_op, right_op, (((0,), (0,)), ((), ())), preferred_element_type=jnp.float32
    )


def matmul_nt(left_op, right_op):
    return lax.dot_general(
        left_op, right_op, (((1,), (1,)), ((), ())), preferred_element_type=jnp.float32
    )


def column_sums(values):
    return jnp.sum(values, axis=0, dtype=jnp.float32)


def heads_of(rows_in):
    return rows_in.reshape(rows_in.shape[0], HEADS, HEAD_DIM)


def merge_heads(head_rows):
    return head_rows.reshape(head_rows.shape[0], -1)


def normalize(summed, gain_row, shift_row):
    center = summed - jnp.mean(summed, axis=-1, keepdims=True)
    inverse = lax.rsqrt(jnp.mean(center * center, axis=-1, keepdims=True) + norm_epsilon)
    normed = center * inverse
    return (normed * gain_row + shift_row, (normed, inverse))


def normalize_back(grad_out, norm_stats, gain_row):
    normed, inverse = norm_stats
    grad_normed = grad_out * gain_row
    grad_sum = inverse * (
        grad_normed
        - jnp.mean(grad_normed, axis=-1, keepdims=True)
        - normed * jnp.mean(grad_normed * normed, axis=-1, keepdims=True)
    )
    return (grad_sum, column_sums(grad_out * normed), column_sums(grad_out))


def score_block(queries, key_rows, allowed):
    scores = jnp.einsum(
        "qhd,khd->hqk", heads_of(queries), heads_of(key_rows), preferred_element_type=jnp.float32
    ) * HEAD_DIM ** (-0.5)
    return jnp.where(allowed[None], scores, masked_score)


def attend(queries, key_rows, value_rows, allowed):
    scores = score_block(queries, key_rows, allowed)
    top_score = jnp.max(scores, axis=-1, keepdims=True)
    log_total = top_score + jnp.log(jnp.sum(jnp.exp(scores - top_score), axis=-1, keepdims=True))
    shares = jnp.exp(scores - log_total).astype(jnp.bfloat16)
    context = jnp.einsum(
        "hqk,khd->qhd", shares, heads_of(value_rows), preferred_element_type=jnp.float32
    )
    return (merge_heads(context).astype(jnp.bfloat16), log_total)


def attend_back(queries, key_rows, value_rows, allowed, log_total, grad_context):
    shares = jnp.exp(score_block(queries, key_rows, allowed) - log_total)
    grad_heads = heads_of(grad_context)
    grad_shares = jnp.einsum(
        "qhd,khd->hqk", grad_heads, heads_of(value_rows), preferred_element_type=jnp.float32
    )
    grad_values = jnp.einsum(
        "hqk,qhd->khd", shares.astype(jnp.bfloat16), grad_heads, preferred_element_type=jnp.float32
    )
    grad_scores = (
        shares * (grad_shares - jnp.sum(shares * grad_shares, axis=-1, keepdims=True))
    ).astype(jnp.bfloat16)
    score_scale = HEAD_DIM ** (-0.5)
    grad_queries = (
        jnp.einsum(
            "hqk,khd->qhd", grad_scores, heads_of(key_rows), preferred_element_type=jnp.float32
        )
        * score_scale
    )
    grad_keys = (
        jnp.einsum(
            "hqk,qhd->khd", grad_scores, heads_of(queries), preferred_element_type=jnp.float32
        )
        * score_scale
    )
    return (merge_heads(grad_queries), merge_heads(grad_keys), merge_heads(grad_values))


def project(rows_low, weight, bias_rows, module):
    width = weight.shape[0]
    bias_all = jnp.concatenate(
        [bias_rows[3 * module], jnp.zeros((width,), jnp.float32), bias_rows[3 * module + 1]]
    )
    return (matmul(rows_low, weight) + bias_all).astype(jnp.bfloat16)


def project_back(grad_sum, grad_parts, rows_low, weight):
    width = weight.shape[0]
    grad_mixed = jnp.concatenate(grad_parts, axis=1).astype(jnp.bfloat16)
    grad_weight = (rows_low, grad_mixed)
    grad_bias = column_sums(grad_mixed)
    grad_rows = grad_sum + matmul_nt(grad_mixed, weight)
    return (grad_rows, grad_weight, grad_bias[:width], grad_bias[2 * width :])


def branch_back(grad_out, context, norm_stats, gain_row, outward_one):
    grad_sum, grad_gain, grad_shift = normalize_back(grad_out, norm_stats, gain_row)
    grad_branch = grad_sum.astype(jnp.bfloat16)
    grad_outward = (context, grad_branch)
    grad_context = matmul_nt(grad_branch, outward_one).astype(jnp.bfloat16)
    return (grad_sum, grad_context, grad_outward, column_sums(grad_branch), grad_gain, grad_shift)


def self_forward(rows_in, weights, module, allowed):
    inward_all, outward_all, bias_rows, gain_rows = weights
    width = rows_in.shape[1]
    rows_low = rows_in.astype(jnp.bfloat16)
    mixed = project(rows_low, inward_all[module], bias_rows, module)
    context, log_total = attend(
        mixed[:, :width], mixed[:, width : 2 * width], mixed[:, 2 * width :], allowed
    )
    summed = rows_in + matmul(context, outward_all[module]) + bias_rows[3 * module + 2]
    result, norm_stats = normalize(summed, gain_rows[module], bias_rows[9 + module])
    return (result, (rows_low, mixed, context, log_total, norm_stats))


def self_backward(grad_out, kept, weights, module, allowed):
    inward_all, outward_all, bias_rows, gain_rows = weights
    rows_low, mixed, context, log_total, norm_stats = kept
    width = rows_low.shape[1]
    grad_sum, grad_context, grad_outward, grad_bias_out, grad_gain, grad_shift = branch_back(
        grad_out, context, norm_stats, gain_rows[module], outward_all[module]
    )
    grad_parts = attend_back(
        mixed[:, :width],
        mixed[:, width : 2 * width],
        mixed[:, 2 * width :],
        allowed,
        log_total,
        grad_context,
    )
    grad_rows, grad_inward, grad_bias_query, grad_bias_value = project_back(
        grad_sum, grad_parts, rows_low, inward_all[module]
    )
    return (
        grad_rows,
        grad_inward,
        grad_outward,
        (grad_bias_query, grad_bias_value, grad_bias_out),
        grad_gain,
        grad_shift,
    )


def cross_forward(word_rows, region_rows, weights, cross_mask):
    inward_all, outward_all, bias_rows, gain_rows = weights
    words_count = word_rows.shape[0]
    width = word_rows.shape[1]
    rows_low = jnp.concatenate([word_rows, region_rows], axis=0)
    mixed = project(rows_low, inward_all[0], bias_rows, 0)
    word_mix = mixed[:words_count]
    region_mix = mixed[words_count:]
    word_context, word_total = attend(
        word_mix[:, :width],
        region_mix[:, width : 2 * width],
        region_mix[:, 2 * width :],
        cross_mask,
    )
    region_context, region_total = attend(
        region_mix[:, :width],
        word_mix[:, width : 2 * width],
        word_mix[:, 2 * width :],
        cross_mask.T,
    )
    context = jnp.concatenate([word_context, region_context], axis=0)
    summed = rows_low.astype(jnp.float32) + matmul(context, outward_all[0]) + bias_rows[2]
    result, norm_stats = normalize(summed, gain_rows[0], bias_rows[9])
    return (result, (rows_low, mixed, context, word_total, region_total, norm_stats))


def cross_backward(grad_out, kept, weights, cross_mask, words_count):
    inward_all, outward_all, bias_rows, gain_rows = weights
    rows_low, mixed, context, word_total, region_total, norm_stats = kept
    width = rows_low.shape[1]
    grad_sum, grad_context, grad_outward, grad_bias_out, grad_gain, grad_shift = branch_back(
        grad_out, context, norm_stats, gain_rows[0], outward_all[0]
    )
    word_mix = mixed[:words_count]
    region_mix = mixed[words_count:]
    word_query_grad, region_key_grad, region_value_grad = attend_back(
        word_mix[:, :width],
        region_mix[:, width : 2 * width],
        region_mix[:, 2 * width :],
        cross_mask,
        word_total,
        grad_context[:words_count],
    )
    region_query_grad, word_key_grad, word_value_grad = attend_back(
        region_mix[:, :width],
        word_mix[:, width : 2 * width],
        word_mix[:, 2 * width :],
        cross_mask.T,
        region_total,
        grad_context[words_count:],
    )
    grad_parts = (
        jnp.concatenate([word_query_grad, region_query_grad], axis=0),
        jnp.concatenate([word_key_grad, region_key_grad], axis=0),
        jnp.concatenate([word_value_grad, region_value_grad], axis=0),
    )
    grad_rows, grad_inward, grad_bias_query, grad_bias_value = project_back(
        grad_sum, grad_parts, rows_low, inward_all[0]
    )
    return (
        grad_rows,
        grad_inward,
        grad_outward,
        (grad_bias_query, grad_bias_value, grad_bias_out),
        grad_gain,
        grad_shift,
    )


def gelu_exact(values):
    return jax.nn.gelu(values, approximate=False)


def feed_forward(rows_in, weights, feed_index, attend_set):
    expand_all, shrink_all, hidden_all = weights
    bias_rows, gain_rows = (attend_set[2], attend_set[3])
    rows_low = rows_in.astype(jnp.bfloat16)
    before = matmul(rows_low, expand_all[feed_index]) + hidden_all[feed_index].astype(jnp.float32)
    hidden = gelu_exact(before).astype(jnp.bfloat16)
    summed = rows_in + matmul(hidden, shrink_all[feed_index]) + bias_rows[14 + feed_index]
    result, norm_stats = normalize(summed, gain_rows[3 + feed_index], bias_rows[12 + feed_index])
    return (result, (rows_low, before, hidden, norm_stats))


def feed_backward(grad_out, kept, weights, feed_index, gain_rows):
    expand_all, shrink_all, hidden_all = weights
    rows_low, before, hidden, norm_stats = kept
    grad_sum, grad_gain, grad_shift = normalize_back(
        grad_out, norm_stats, gain_rows[3 + feed_index]
    )
    grad_branch = grad_sum.astype(jnp.bfloat16)
    grad_shrink = (hidden, grad_branch)
    grad_hidden = matmul_nt(grad_branch, shrink_all[feed_index])
    unused_value, slope_back = jax.vjp(gelu_exact, before)
    grad_before = slope_back(grad_hidden)[0].astype(jnp.bfloat16)
    grad_expand = (rows_low, grad_before)
    grad_rows = grad_sum + matmul_nt(grad_before, expand_all[feed_index])
    return (
        grad_rows,
        grad_expand,
        grad_shrink,
        column_sums(grad_before),
        column_sums(grad_branch),
        grad_gain,
        grad_shift,
    )


UNIT = 96
WIDE = 768
SLOTS = 4
ACC_SLOTS = 6
LAG_A = 2
LAG_B = 2
LAG_Z = 1


WORDS = 128
REGIONS = 256
ROWS = 384
HIDDEN = 3072
PAIRS_OF_HEADS = 6
PAIR_WIDE = 128


def flip(position, bits):
    return lax.bitwise_xor(position, bits)


def dot_nt(left, right):
    return lax.dot_general(left, right, (((1,), (1,)), ((), ())), preferred_element_type=jnp.float32)


def dot_tn(left, right):
    return lax.dot_general(left, right, (((0,), (0,)), ((), ())), preferred_element_type=jnp.float32)


def spread(part):
    source = lax.broadcasted_iota(jnp.int32, (128, WIDE), 0)
    target = lax.broadcasted_iota(jnp.int32, (128, WIDE), 1)
    return jnp.logical_and(source < UNIT, target == source + part * UNIT)


def half_lanes():
    lane = lax.broadcasted_iota(jnp.int32, (1, PAIR_WIDE), 1)
    return (lane < HEAD_DIM, lane >= HEAD_DIM)


def only(values, chosen):
    return jnp.where(chosen, values, jnp.zeros_like(values))


ATTEND_CROSS_WORD = ((0, WORDS), (WORDS, REGIONS))
ATTEND_CROSS_REGION = ((WORDS, REGIONS), (0, WORDS))
ATTEND_WORD = ((0, WORDS), (0, WORDS))
ATTEND_REGION = ((WORDS, REGIONS), (WORDS, REGIONS))


def attend_into(rows_of, mixed, allowed, shares, context):
    (query_at, query_count), (key_at, key_count) = rows_of
    blocked = jnp.where(allowed, 0.0, masked_score)

    def pair(p, carry):
        at = pl.multiple_of(p * PAIR_WIDE, PAIR_WIDE)
        queries = mixed[pl.ds(query_at, query_count), pl.ds(at, PAIR_WIDE)]
        key_rows = mixed[pl.ds(key_at, key_count), pl.ds(WIDE + at, PAIR_WIDE)]
        value_rows = mixed[pl.ds(key_at, key_count), pl.ds(2 * WIDE + at, PAIR_WIDE)]
        total = jnp.zeros((query_count, PAIR_WIDE), jnp.float32)
        for side, chosen in enumerate(half_lanes()):
            scores = dot_nt(only(queries, chosen), key_rows) * HEAD_DIM ** (-0.5) + blocked
            lifted = jnp.exp(scores - jnp.max(scores, axis=-1, keepdims=True))
            share = (lifted / jnp.sum(lifted, axis=-1, keepdims=True)).astype(jnp.bfloat16)
            shares[2 * p + side] = share
            total = total + matmul(share, only(value_rows, chosen))
        context[pl.ds(query_at, query_count), pl.ds(at, PAIR_WIDE)] = total.astype(jnp.bfloat16)
        return carry

    lax.fori_loop(0, PAIRS_OF_HEADS, pair, 0)


def row_norm(summed):
    center = summed - jnp.mean(summed, axis=-1, keepdims=True)
    inverse = lax.rsqrt(jnp.mean(center * center, axis=-1, keepdims=True) + norm_epsilon)
    return (center * inverse, inverse)


def down(across):
    wide = jnp.broadcast_to(across.astype(jnp.float32), (128, across.shape[1]))
    return jnp.concatenate([wide[:, at : at + 128].T[:, :1] for at in range(0, across.shape[1], 128)], axis=0)


LOW, F32 = jnp.bfloat16, jnp.float32
SAVED = (
    ((24, WIDE), F32),
    ((3, ROWS, WIDE), F32),
    ((3, ROWS, 128), F32),
    ((HIDDEN, ROWS), LOW),
    ((ROWS, HIDDEN), LOW),
    ((WIDE, ROWS), LOW),
    ((WIDE, ROWS), LOW),
    ((ROWS, 3 * WIDE), LOW),
    ((HEADS, WORDS, WORDS), LOW),
    ((HEADS, REGIONS, REGIONS), LOW),
    ((WIDE, ROWS), LOW),
    ((WIDE, ROWS), LOW),
    ((ROWS, 3 * WIDE), LOW),
    ((HEADS, WORDS, REGIONS), LOW),
    ((HEADS, REGIONS, WORDS), LOW),
    ((WIDE, ROWS), LOW),
)
WEIGHTS = (
    (3, WIDE, 3 * WIDE),
    (3, WIDE, WIDE),
    (2, WIDE, HIDDEN),
    (2, HIDDEN, WIDE),
)

CHUNKS = (
    (2, 0, None),
    (0, 0, (0, UNIT)),
    (1, 0, (0, UNIT)),
    (2, 1, None),
    (0, 2, (0, UNIT)),
    (1, 2, (0, UNIT)),
    (3, 1, None),
    (0, 1, (0, UNIT)),
    (1, 1, (0, UNIT)),
    (3, 0, (0, 2 * UNIT)),
    (3, 0, (2 * UNIT, 2 * UNIT)),
)
EXPAND_0, INWARD_0, OUTWARD_0, EXPAND_1, INWARD_2, OUTWARD_2, SHRINK_1, INWARD_1, OUTWARD_1, SHRINK_0A, SHRINK_0B = range(
    len(CHUNKS)
)


def forward_kernel(*refs):
    word_rows, region_rows, word_ids, region_ids, biases, gains, hidden_bias, *shards = refs[:11]
    word_result, region_result, *kept = refs[11:29]
    weights_kept = refs[29:33]
    (
        params,
        normed,
        inverse,
        hidden_t,
        slope,
        rows_two_t,
        context_self_t,
        mixed_self,
        shares_w,
        shares_r,
        rows_one_t,
        context_cross_t,
        mixed_cross,
        shares_cw,
        shares_cr,
        rows_zero_t,
    ) = saved = refs[33:49]
    inward_all, outward_all, expand_all, shrink_all = gathered = refs[49:53]
    (
        small_own,
        small_all,
        hidden_rows,
        rows_low,
        stream,
        stream_low,
        context,
        hidden,
        sends,
        recvs,
        z_sends,
        z_recvs,
        foreign_sends,
        foreign_recvs,
        small_sends,
        small_recvs,
        local_sems,
        keep_sems,
    ) = refs[53:]
    me = lax.axis_index("fsdp")
    z = lax.axis_index("rep")
    peers = {"x": {"fsdp": flip(me, 2)}, "y": {"fsdp": flip(me, 4)}, "core": {"fsdp": flip(me, 1)}}
    above, below = {"rep": (z + 1) % 4}, {"rep": (z + 3) % 4}

    barrier = pltpu.get_barrier_semaphore()
    for offset in range(1, 8):
        pl.semaphore_signal(barrier, inc=1, device_id={"fsdp": flip(me, offset)}, device_id_type=MESH)
    for offset in range(1, 4):
        pl.semaphore_signal(barrier, inc=1, device_id={"rep": (z + offset) % 4}, device_id_type=MESH)
    pl.semaphore_wait(barrier, 10)

    def remote(src, dst, send_sem, recv_sem, peer):
        return pltpu.make_async_remote_copy(
            src_ref=src, dst_ref=dst, send_sem=send_sem, recv_sem=recv_sem, device_id=peer, device_id_type=MESH
        )

    def small_copy(offset, owner):
        return remote(
            small_all.at[owner],
            small_all.at[owner],
            small_sends.at[offset - 1],
            small_recvs.at[offset - 1],
            {"fsdp": flip(me, offset)},
        )

    X, Y, DIAG_Y, DIAG_X, CORE_OWN, CORE_X, CORE_Y, CORE_DIAG = range(8)

    def place(k, owner, half=None, quarter=None):
        kind, _, rows = CHUNKS[k]
        shard_rows, columns = shards[kind].shape[1:]
        first, count, column = 0, shard_rows, 0
        if rows is not None:
            first, count = rows
        elif quarter is not None and kind == 3:
            first, count = quarter * UNIT, UNIT
        elif quarter is not None:
            column, columns = quarter * WIDE, WIDE
        if half is not None:
            count = count // 2
            first = first + half * count
        if not isinstance(column, int):
            column = pl.multiple_of(column, WIDE)
        if not isinstance(first, int):
            first = pl.multiple_of(first, 16)
        whole = pl.multiple_of(owner * shard_rows + first, 16)
        return pl.ds(whole, count), pl.ds(first, count), pl.ds(column, columns)

    def own_part(k, quarter=None):
        kind, index, _ = CHUNKS[k]
        _, rows, columns = place(k, me, None, quarter)
        return shards[kind].at[index, rows, columns]

    def part(k, owner, half=None, quarter=None):
        kind, index, _ = CHUNKS[k]
        rows, _, columns = place(k, owner, half, quarter)
        return gathered[kind].at[index, rows, columns]

    def mine(k):
        return z if CHUNKS[k][2] is None else None

    def copy(k, kind, arriving=False):
        owner, half, peer = {
            X: (flip(me, 2) if arriving else me, None, "x"),
            Y: (flip(me, 4) if arriving else me, None, "y"),
            DIAG_Y: (flip(me, 6 if arriving else 2), 0, "y"),
            DIAG_X: (flip(me, 6 if arriving else 4), 1, "x"),
            CORE_OWN: (flip(me, 1) if arriving else me, None, "core"),
            CORE_X: (flip(me, 3 if arriving else 2), None, "core"),
            CORE_Y: (flip(me, 5 if arriving else 4), None, "core"),
            CORE_DIAG: (flip(me, 7 if arriving else 6), None, "core"),
        }[kind]
        quarter = None if kind == CORE_OWN else mine(k)
        target = part(k, owner, half, quarter)
        source = own_part(k, quarter) if kind in (X, Y, CORE_OWN) and not arriving else target
        return remote(source, target, sends.at[k, kind], recvs.at[k, kind], peers[peer])

    z_chunks = [k for k in range(len(CHUNKS)) if CHUNKS[k][2] is None]
    owners = (flip(me, 2), flip(me, 4), flip(me, 6))
    core_owners = (flip(me, 3), flip(me, 5), flip(me, 7))

    def z_copy(k, way, hop, which, arriving=False):
        steps = hop + 1 if arriving else hop
        quarter = z - steps if way == 0 else z + steps
        here = part(k, owners[which], None, quarter)
        at = (z_chunks.index(k), way, hop, which)
        return remote(here, here, z_sends.at[at], z_recvs.at[at], (above, below)[way])

    def foreign_copy(k, way, hop, which, arriving=False):
        quarter = z - hop - 1 if way == 0 else z + hop + 1
        here = part(k, (core_owners if arriving else owners)[which], None, quarter)
        at = (z_chunks.index(k), way, hop, which)
        return remote(here, here, foreign_sends.at[at], foreign_recvs.at[at], peers["core"])

    def goes(way, hop):
        return jnp.logical_and(z >= hop, z < 3) if way == 0 else jnp.logical_and(z <= 3 - hop, z > 0)

    def comes(way, hop):
        return z >= hop + 1 if way == 0 else z <= 2 - hop

    def send_z(k, hop, which):
        for way in range(2):

            @pl.when(goes(way, hop))
            def _(way=way):
                for one in which:
                    z_copy(k, way, hop, one).start()

    def own_local(k):
        return pltpu.make_async_copy(own_part(k), part(k, me), local_sems.at[k])

    def own(k):
        for kind in (X, Y):
            copy(k, kind).start()
        own_local(k).start()
        copy(k, CORE_OWN).start()

    def pass_first(k):
        copy(k, X, True).wait_recv()
        copy(k, DIAG_Y).start()
        copy(k, Y, True).wait_recv()
        copy(k, DIAG_X).start()
        if k in z_chunks:
            send_z(k, 0, (0, 1))
        copy(k, CORE_X).start()
        copy(k, CORE_Y).start()

    def pass_second(k):
        copy(k, DIAG_Y, True).wait_recv()
        copy(k, DIAG_X, True).wait_recv()
        if k in z_chunks:
            send_z(k, 0, (2,))
        copy(k, CORE_DIAG).start()

    def pass_quarter(k, hop):
        for way in range(2):

            @pl.when(comes(way, hop))
            def _(way=way):
                for which in range(3):
                    z_copy(k, way, hop, which, True).wait_recv()

        if hop < 2:
            send_z(k, hop + 1, (0, 1, 2))
        for way in range(2):

            @pl.when(comes(way, hop))
            def _(way=way):
                for which in range(3):
                    foreign_copy(k, way, hop, which).start()

    def complete(k):
        own_local(k).wait()
        for kind in (CORE_OWN, CORE_X, CORE_Y, CORE_DIAG):
            copy(k, kind, True).wait_recv()
        if k in z_chunks:
            for hop in range(3):
                for way in range(2):

                    @pl.when(comes(way, hop))
                    def _(way=way, hop=hop):
                        for which in range(3):
                            foreign_copy(k, way, hop, which, True).wait_recv()

    keeps = []

    def keep(source, target):
        copied = pltpu.make_async_copy(source, target, keep_sems.at[len(keeps)])
        copied.start()
        keeps.append(copied)

    def keep_weights(kind, index):
        keep(gathered[kind].at[index], weights_kept[kind].at[index])

    def keep_saved(*refs_done):
        for done in refs_done:
            index = [ref is done for ref in saved].index(True)
            keep(saved[index], kept[index])

    def give_small():
        small_own[...] = jnp.zeros_like(small_own)
        small_own[0:16, 0:UNIT] = biases[...].astype(F32)
        small_own[16:21, 0:UNIT] = gains[...].astype(F32)
        source = lax.broadcasted_iota(jnp.int32, (4 * UNIT, 128), 0)
        target = lax.broadcasted_iota(jnp.int32, (4 * UNIT, 128), 1)
        for q in range(4):
            chosen = jnp.logical_and(target < UNIT, source == target + q * UNIT).astype(LOW)
            placed = matmul(hidden_bias[...], chosen)
            for f in range(2):
                row = 21 + 4 * f + q
                small_own[row : row + 1, :] = placed[f : f + 1]
        small_all[me] = small_own[...].astype(LOW)
        for offset in range(1, 8):
            small_copy(offset, me).start()

    def read_small():
        for offset in range(1, 8):
            small_copy(offset, flip(me, offset)).wait_recv()
        totals = jnp.zeros((21, WIDE), jnp.float32)
        hidden_parts = [[jnp.zeros((1, WIDE), jnp.float32) for _ in range(4)] for _ in range(2)]
        for owner in range(8):
            one = small_all[owner]
            totals = totals + matmul(one, spread(owner).astype(LOW))[:21]
            for q in range(4):
                placed = matmul(one, spread((owner % 2) * 4 + q).astype(LOW))
                for f in range(2):
                    row = 21 + 4 * f + q
                    hidden_parts[f][owner // 2] = hidden_parts[f][owner // 2] + placed[row : row + 1]
        params[...] = jnp.zeros_like(params)
        params[0:21, :] = totals
        for f in range(2):
            for block in range(4):
                hidden_rows[f : f + 1, block * WIDE : (block + 1) * WIDE] = hidden_parts[f][block]
        keep_saved(params)

    def read_rows():
        rows_low[0:WORDS, :] = word_rows[...]
        rows_low[WORDS:ROWS, :] = region_rows[...]
        for at in range(0, ROWS, 128):
            transposed_into(rows_zero_t, rows_low[at : at + 128, :], at, 128)
        keep_saved(rows_zero_t)

    def transposed_into(target, values, at, count):
        target[:, pl.ds(at, count)] = values.T

    def project_into(source, at, count, module, mixed):
        for third, bias_row in enumerate((3 * module, None, 3 * module + 1)):
            product = matmul(source[pl.ds(at, count), :], inward_all[module, :, third * WIDE : (third + 1) * WIDE])
            if bias_row is not None:
                product = product + params[bias_row : bias_row + 1, :]
            mixed[pl.ds(at, count), third * WIDE : (third + 1) * WIDE] = product.astype(jnp.bfloat16)

    def join(at, weights, left, residual, bias_row, norm_at, norm_index):
        rows = pl.ds(at, 128)
        summed = residual + matmul(left[rows, :], weights) + params[bias_row : bias_row + 1, :]
        unit, scale = row_norm(summed)
        normed[norm_at, rows, :] = unit
        inverse[norm_at, rows, :] = jnp.broadcast_to(scale, (128, 128))
        return unit * params[16 + norm_index : 17 + norm_index, :] + params[9 + norm_index : 10 + norm_index, :]

    def cross_in():
        project_into(rows_low, 0, ROWS, 0, mixed_cross)
        keep_saved(mixed_cross)
        keep_weights(0, 0)

    def cross_words():
        allowed = down(word_ids[...]) == region_ids[...].astype(F32)
        attend_into(ATTEND_CROSS_WORD, mixed_cross, allowed, shares_cw, context)
        keep_saved(shares_cw)

    def cross_regions():
        allowed = down(region_ids[...]) == word_ids[...].astype(F32)
        attend_into(ATTEND_CROSS_REGION, mixed_cross, allowed, shares_cr, context)
        keep_saved(shares_cr)

    def cross_out():
        for at in range(0, ROWS, 128):
            one = join(at, outward_all[0], context, rows_low[at : at + 128, :].astype(F32), 2, 0, 0)
            stream[at : at + 128, :] = one
            one_low = one.astype(LOW)
            stream_low[at : at + 128, :] = one_low
            transposed_into(rows_one_t, one_low, at, 128)
            transposed_into(context_cross_t, context[at : at + 128, :], at, 128)
        keep_saved(rows_one_t, context_cross_t)
        keep_weights(1, 0)

    def word_in():
        project_into(stream_low, 0, WORDS, 1, mixed_self)
        keep_weights(0, 1)
        allowed = down(word_ids[...]) == word_ids[...].astype(F32)
        attend_into(ATTEND_WORD, mixed_self, allowed, shares_w, context)
        transposed_into(context_self_t, context[0:WORDS, :], 0, WORDS)
        keep_saved(shares_w)

    def region_in():
        project_into(stream_low, WORDS, REGIONS, 2, mixed_self)
        keep_weights(0, 2)

    def region_attend():
        allowed = down(region_ids[...]) == region_ids[...].astype(F32)
        attend_into(ATTEND_REGION, mixed_self, allowed, shares_r, context)
        for at in range(WORDS, ROWS, 128):
            transposed_into(context_self_t, context[at : at + 128, :], at, 128)
        keep_saved(shares_r)

    def self_out(module, first, last):
        for at in range(first, last, 128):
            two = join(at, outward_all[module], context, stream[at : at + 128, :], 3 * module + 2, 1, module)
            stream[at : at + 128, :] = two
            two_low = two.astype(LOW)
            stream_low[at : at + 128, :] = two_low
            transposed_into(rows_two_t, two_low, at, 128)
        keep_weights(1, module)

    def feed_in(f, first, last, column, columns):
        step = 256

        def tile(t, carry):
            at = pl.multiple_of(column + t * step, step)
            for row in range(first, last, 128):
                before = (
                    matmul(stream_low[row : row + 128, :], expand_all[f, :, pl.ds(at, step)])
                    + hidden_rows[f : f + 1, pl.ds(at, step)]
                )
                below = 0.5 * (1.0 + lax.erf(before * 0.5**0.5))
                value = (before * below).astype(jnp.bfloat16)
                density = jnp.exp(-0.5 * before * before) * 0.3989422804014327
                hidden[row : row + 128, pl.ds(at, step)] = value
                hidden_t[pl.ds(at, step), row : row + 128] = value.T
                slope[row : row + 128, pl.ds(at, step)] = (below + before * density).astype(jnp.bfloat16)
            return carry

        lax.fori_loop(0, columns // step, tile, 0)

    def feed_out(f, first, last):
        for at in range(first, last, 128):
            last_rows = join(at, shrink_all[f], hidden, stream[at : at + 128, :], 14 + f, 2, 3 + f)
            target, row = (word_result, at) if f == 0 else (region_result, at - WORDS)
            target[row : row + 128, :] = last_rows.astype(LOW)

    give_small()
    own(EXPAND_0)
    read_rows()
    pass_first(EXPAND_0)
    own(INWARD_0)
    own(OUTWARD_0)
    read_small()
    pass_second(EXPAND_0)
    pass_first(INWARD_0)
    own(EXPAND_1)
    pass_quarter(EXPAND_0, 0)
    pass_first(OUTWARD_0)
    own(INWARD_2)
    pass_second(INWARD_0)
    pass_quarter(EXPAND_0, 1)
    complete(INWARD_0)
    cross_in()
    pass_second(OUTWARD_0)
    cross_words()
    pass_first(EXPAND_1)
    own(OUTWARD_2)
    cross_regions()
    pass_second(EXPAND_1)
    complete(OUTWARD_0)
    pass_quarter(EXPAND_0, 2)
    cross_out()
    pass_first(INWARD_2)
    own(SHRINK_1)
    complete(EXPAND_0)
    keep_weights(2, 0)
    pass_quarter(EXPAND_1, 0)
    pass_first(OUTWARD_2)
    own(INWARD_1)
    pass_second(INWARD_2)
    complete(INWARD_2)
    region_in()
    pass_second(OUTWARD_2)
    pass_first(SHRINK_1)
    own(OUTWARD_1)
    region_attend()
    pass_quarter(EXPAND_1, 1)
    complete(OUTWARD_2)
    pass_second(SHRINK_1)
    self_out(2, WORDS, ROWS)
    pass_first(INWARD_1)
    own(SHRINK_0A)
    pass_quarter(EXPAND_1, 2)
    pass_first(OUTWARD_1)
    own(SHRINK_0B)
    pass_second(INWARD_1)
    complete(EXPAND_1)
    keep_weights(2, 1)
    complete(INWARD_1)
    word_in()
    keep_saved(mixed_self, context_self_t)
    pass_quarter(SHRINK_1, 0)
    pass_second(OUTWARD_1)
    feed_in(1, WORDS, ROWS, 0, 2 * WIDE)
    pass_first(SHRINK_0A)
    complete(OUTWARD_1)
    self_out(1, 0, WORDS)
    keep_saved(rows_two_t)
    feed_in(1, WORDS, ROWS, 2 * WIDE, 2 * WIDE)
    pass_quarter(SHRINK_1, 1)
    pass_second(SHRINK_0A)
    feed_in(0, 0, WORDS, 0, 2 * WIDE)
    pass_first(SHRINK_0B)
    feed_in(0, 0, WORDS, 2 * WIDE, 2 * WIDE)
    keep_saved(hidden_t, slope)
    pass_second(SHRINK_0B)
    complete(SHRINK_0A)
    pass_quarter(SHRINK_1, 2)
    complete(SHRINK_0B)
    keep_weights(3, 0)
    feed_out(0, 0, WORDS)
    complete(SHRINK_1)
    keep_weights(3, 1)
    feed_out(1, WORDS, ROWS)
    keep_saved(normed, inverse)
    for copied in keeps:
        copied.wait()
    for offset in range(1, 8):
        small_copy(offset, me).wait_send()
    for k in range(len(CHUNKS)):
        for kind in range(8):
            copy(k, kind).wait_send()
    for k in z_chunks:
        for way in range(2):
            for hop in range(3):

                @pl.when(goes(way, hop))
                def _(k=k, way=way, hop=hop):
                    for which in range(3):
                        z_copy(k, way, hop, which).wait_send()

                @pl.when(comes(way, hop))
                def _(k=k, way=way, hop=hop):
                    for which in range(3):
                        foreign_copy(k, way, hop, which).wait_send()


def forward(word_rows, region_rows, word_ids, region_ids, biases, gains, hidden_bias, shards):
    dma = pltpu.SemaphoreType.DMA
    vmem = pl.BlockSpec(memory_space=pltpu.VMEM)
    hbm = pl.BlockSpec(memory_space=pl.ANY)
    saved = [jax.ShapeDtypeStruct(*one) for one in SAVED]
    weights = [jax.ShapeDtypeStruct(one, LOW) for one in WEIGHTS]
    quarters = (sum(chunk[2] is None for chunk in CHUNKS), 2, 3, 3)
    outs = pl.pallas_call(
        forward_kernel,
        out_shape=[jax.ShapeDtypeStruct((WORDS, WIDE), LOW), jax.ShapeDtypeStruct((REGIONS, WIDE), LOW)] + saved + weights,
        in_specs=[vmem] * 7 + [hbm] * 4,
        out_specs=[vmem] * 2 + [hbm] * (len(saved) + len(weights)),
        scratch_shapes=[pltpu.VMEM(one.shape, one.dtype) for one in saved + weights]
        + [
            pltpu.VMEM((32, 128), F32),
            pltpu.VMEM((8, 32, 128), LOW),
            pltpu.VMEM((2, HIDDEN), F32),
            pltpu.VMEM((ROWS, WIDE), LOW),
            pltpu.VMEM((ROWS, WIDE), F32),
            pltpu.VMEM((ROWS, WIDE), LOW),
            pltpu.VMEM((ROWS, WIDE), LOW),
            pltpu.VMEM((ROWS, HIDDEN), LOW),
            dma((len(CHUNKS), 8)),
            dma((len(CHUNKS), 8)),
            dma(quarters),
            dma(quarters),
            dma(quarters),
            dma(quarters),
            dma((7,)),
            dma((7,)),
            dma((len(CHUNKS),)),
            dma((len(saved) + 10,)),
        ],
        compiler_params=pltpu.CompilerParams(
            collective_id=1, has_side_effects=True, vmem_limit_bytes=64 * 2**20 - 2**16
        ),
    )(word_rows, region_rows, word_ids, region_ids, biases, gains, hidden_bias, *shards)
    return outs[:2], outs[2 : 2 + len(saved)], outs[2 + len(saved) :]


WINDOW = 6

GROUPS = (
    (4, 0, 0, WORDS, True, (3, 0)),
    (4, 0, WORDS, REGIONS, True, (3, 1)),
    (4, 1, 0, WORDS, False, (2, 0)),
    (4, 1, WORDS, REGIONS, False, (2, 1)),
    (1, 2, 0, WORDS, False, (1, 1)),
    (1, 2, WORDS, REGIONS, False, (1, 2)),
    (3, 3, 0, WORDS, False, (0, 1)),
    (3, 3, WORDS, REGIONS, False, (0, 2)),
    (1, 4, 0, ROWS, False, (1, 0)),
    (3, 5, 0, ROWS, False, (0, 0)),
)
UNITS = sum(group[0] for group in GROUPS)

BLOCKS = (
    [(kind, f, c) for f in range(2) for c in range(4) for kind in (3, 2)]
    + [(1, 1, 0), (1, 2, 0)]
    + [(0, m, c) for m in (1, 2) for c in range(3)]
    + [(1, 0, 0)]
    + [(0, 0, c) for c in range(3)]
)


def attend_back_into(rows_of, mixed, shares, grad_context, grad_mixed, first_pair, last_pair):
    (query_at, query_count), (key_at, key_count) = rows_of
    query_rows, key_rows = pl.ds(query_at, query_count), pl.ds(key_at, key_count)

    def pair(p, carry):
        at = pl.multiple_of(p * PAIR_WIDE, PAIR_WIDE)
        at_query, at_key, at_value = (pl.ds(third * WIDE + at, PAIR_WIDE) for third in range(3))
        queries = mixed[query_rows, at_query]
        keys = mixed[key_rows, at_key]
        values = mixed[key_rows, at_value]
        grads = grad_context[query_rows, at_query]
        grad_queries = jnp.zeros((query_count, PAIR_WIDE), jnp.float32)
        grad_keys = jnp.zeros((key_count, PAIR_WIDE), jnp.float32)
        grad_values = jnp.zeros((key_count, PAIR_WIDE), jnp.float32)
        for side, chosen in enumerate(half_lanes()):
            share = shares[2 * p + side]
            grad_head = only(grads, chosen)
            wide = share.astype(jnp.float32)
            weighted = wide * dot_nt(grad_head, values)
            grad_scores = (weighted - wide * jnp.sum(weighted, axis=-1, keepdims=True)).astype(jnp.bfloat16)
            grad_values = grad_values + dot_tn(share, grad_head)
            grad_queries = grad_queries + matmul(grad_scores, only(keys, chosen))
            grad_keys = grad_keys + dot_tn(grad_scores, only(queries, chosen))
        score_scale = HEAD_DIM ** (-0.5)
        grad_mixed[query_rows, at_query] = (grad_queries * score_scale).astype(jnp.bfloat16)
        grad_mixed[key_rows, at_key] = (grad_keys * score_scale).astype(jnp.bfloat16)
        grad_mixed[key_rows, at_value] = grad_values.astype(jnp.bfloat16)
        return carry

    lax.fori_loop(first_pair, last_pair, pair, 0)


def backward_kernel(*refs):
    saved_hbm, weights = refs[:18], refs[18:22]
    word_gradient, region_gradient, small_out, *totals = refs[22:29]
    (
        params,
        word_cotangent,
        region_cotangent,
        normed,
        inverse,
        hidden_t,
        slope,
        rows_two_t,
        context_self_t,
        mixed_self,
        shares_w,
        shares_r,
        rows_one_t,
        context_cross_t,
        mixed_cross,
        shares_cw,
        shares_cr,
        rows_zero_t,
    ) = saved = refs[29:47]
    (
        window,
        end_feed,
        grad_before,
        end_self,
        grad_mixed_self,
        end_cross,
        grad_mixed_cross,
        stream,
        grad_context,
        row_sums,
        hidden_sums,
        out,
        acc,
        core_out,
        core_in,
        half_out,
        half_in,
        full_out,
        full_in,
        plane,
        end_out,
        end_in,
        mid_out,
        mid_in,
        small_in,
        small_in_plane,
        small_planes,
        saved_sems,
        window_sems,
        total_sems,
        core_send,
        core_recv,
        half_send,
        half_recv,
        full_send,
        full_recv,
        z_send,
        z_recv,
        small_send,
        small_recv,
        free,
    ) = refs[47:]
    lefts = (hidden_t, rows_two_t, context_self_t, rows_one_t, context_cross_t, rows_zero_t)
    rights = (end_feed, grad_before, end_self, grad_mixed_self, end_cross, grad_mixed_cross)
    me = lax.axis_index("fsdp")
    z = lax.axis_index("rep")
    chip = me // 2
    lane = me % 2
    is_end = jnp.logical_or(z == 0, z == 3)
    is_mid = jnp.logical_or(z == 1, z == 2)
    core_peer = {"fsdp": flip(me, 1)}
    links = ({"fsdp": flip(me, 2)}, {"fsdp": flip(me, 4)})
    link_chip = (flip(chip, 1), flip(chip, 2))
    diagonal = flip(chip, 3)
    pair_peer = {"rep": flip(z, 1)}
    mid_peer = {"rep": 3 - z}
    low = jnp.bfloat16

    def load_saved(index):
        return pltpu.make_async_copy(saved_hbm[index], saved[index], saved_sems.at[index])

    def load_block(n):
        kind, index, c = BLOCKS[n]
        part = slice(c * WIDE, (c + 1) * WIDE)
        source = weights[kind].at[index, part, :] if kind == 3 else weights[kind].at[index, :, part]
        return pltpu.make_async_copy(source, window.at[n % WINDOW], window_sems.at[n % WINDOW])

    def wait_saved(*names):
        for name in names:
            load_saved([ref is name for ref in saved].index(True)).wait()

    for index in range(7):
        load_saved(index).start()
    for n in range(WINDOW):
        load_block(n).start()
    for index in range(7, 18):
        load_saved(index).start()

    barrier = pltpu.get_barrier_semaphore()
    for offset in range(1, 8):
        pl.semaphore_signal(barrier, inc=1, device_id={"fsdp": flip(me, offset)}, device_id_type=MESH)
    for offset in range(1, 4):
        pl.semaphore_signal(barrier, inc=1, device_id={"rep": (z + offset) % 4}, device_id_type=MESH)
    pl.semaphore_wait(barrier, 10)

    def remote(src, dst, send_sem, recv_sem, peer):
        return pltpu.make_async_remote_copy(
            src_ref=src, dst_ref=dst, send_sem=send_sem, recv_sem=recv_sem, device_id=peer, device_id_type=MESH
        )

    def small_copy(offset):
        peer = flip(me, offset)
        return remote(
            small_in.at[peer],
            small_in_plane.at[offset - 1],
            small_send.at[offset - 1],
            small_recv.at[offset - 1],
            {"fsdp": peer},
        )

    def small_plane_copy(offset, source):
        peer = (z + offset) % 4 if source is z else source
        return remote(
            small_planes.at[source],
            small_planes.at[source],
            small_send.at[6 + offset],
            small_recv.at[6 + offset],
            {"rep": peer},
        )

    def core_copy(u):
        slot = u % SLOTS
        return remote(core_out.at[slot], core_in.at[slot], core_send.at[slot], core_recv.at[slot], core_peer)

    def half_copy(u, way):
        slot = u % SLOTS
        return remote(
            half_out.at[slot, way], half_in.at[slot, way], half_send.at[slot, way], half_recv.at[slot, way], links[way]
        )

    def full_copy(u, way):
        slot = u % SLOTS
        return remote(
            full_out.at[slot, way], full_in.at[slot, way], full_send.at[slot, way], full_recv.at[slot, way], links[way]
        )

    def end_copy(u):
        slot = u % SLOTS
        return remote(end_out.at[slot], end_in.at[slot], z_send.at[0, slot], z_recv.at[0, slot], pair_peer)

    def mid_copy(u):
        slot = u % SLOTS
        return remote(mid_out.at[slot], mid_in.at[slot], z_send.at[1, slot], z_recv.at[1, slot], mid_peer)

    def back_copy(u):
        slot = u % SLOTS
        return remote(out.at[u], out.at[u], z_send.at[2, slot], z_recv.at[2, slot], pair_peer)

    def credit(u, channel, peer):
        @pl.when(u + SLOTS < UNITS)
        def _():
            pl.semaphore_signal(free.at[channel], inc=1, device_id=peer, device_id_type=MESH)

    def spend(u, channel):
        @pl.when(u >= SLOTS)
        def _():
            pl.semaphore_wait(free.at[channel], 1)

    def per_group(u, function):
        first = 0
        for group in GROUPS:
            start, units = first, group[0]

            @pl.when(jnp.logical_and(u >= start, u < start + units))
            def _(start=start, group=group):
                function(u - start, *group[1:])

            first = first + units

    def produce(u):
        slot = u % SLOTS
        keep = u % ACC_SLOTS
        spend(u, 0)

        def products(at, side, first_row, count, by_row, matrix):
            rows = pl.ds(first_row, count)
            column = 0 if by_row else pl.multiple_of(at * WIDE, WIDE)
            right = rights[side][rows, pl.ds(column, WIDE)]

            def product(core):
                blocks = []
                for block in range(4):
                    owner = 2 * block + core
                    row = owner * (4 * UNIT) + at * UNIT if by_row else owner * UNIT
                    blocks.append(lefts[side][pl.ds(pl.multiple_of(row, 16), UNIT), rows])
                return matmul(jnp.concatenate(blocks, axis=0), right)

            other = product(1 - lane).astype(low)
            for block in range(4):
                core_out[slot, block] = other[block * UNIT : (block + 1) * UNIT]
            core_copy(u).start()
            own = product(lane)
            for block in range(4):
                acc[keep, block] = own[block * UNIT : (block + 1) * UNIT]

        per_group(u, products)

    def join_cores(u):
        slot = u % SLOTS
        keep = u % ACC_SLOTS
        core_copy(u).wait()
        for way in range(2):
            spend(u, 1 + way)
        summed = acc[keep, diagonal] + core_in[slot, diagonal].astype(jnp.float32)
        half_out[slot, 0] = summed[: UNIT // 2].astype(low)
        half_out[slot, 1] = summed[UNIT // 2 :].astype(low)
        for way in range(2):
            half_copy(u, way).start()
        for block in (link_chip[0], link_chip[1], chip):
            acc[keep, block] = acc[keep, block] + core_in[slot, block].astype(jnp.float32)
        credit(u, 0, core_peer)

    def join_diagonal(u):
        slot = u % SLOTS
        keep = u % ACC_SLOTS
        for way in range(2):
            half_copy(u, way).wait()
            spend(u, 3 + way)
        half = UNIT // 2
        full_out[slot, 1, :half] = (acc[keep, link_chip[1], :half] + half_in[slot, 0].astype(jnp.float32)).astype(low)
        full_out[slot, 1, half:] = acc[keep, link_chip[1], half:].astype(low)
        full_copy(u, 1).start()
        full_out[slot, 0, half:] = (acc[keep, link_chip[0], half:] + half_in[slot, 1].astype(jnp.float32)).astype(low)
        full_out[slot, 0, :half] = acc[keep, link_chip[0], :half].astype(low)
        full_copy(u, 0).start()
        for way in range(2):
            credit(u, 1 + way, links[way])

    def join_plane(u):
        slot = u % SLOTS
        keep = u % ACC_SLOTS
        for way in range(2):
            full_copy(u, way).wait()
        summed = acc[keep, chip] + (full_in[slot, 0].astype(jnp.float32) + full_in[slot, 1].astype(jnp.float32))

        @pl.when(is_end)
        def _():
            spend(u, 5)
            end_out[slot] = summed.astype(low)
            end_copy(u).start()

        @pl.when(is_mid)
        def _():
            plane[slot] = summed

        for way in range(2):
            credit(u, 3 + way, links[way])

    def join_pair(u):
        slot = u % SLOTS

        @pl.when(is_end)
        def _():
            end_copy(u).wait_send()

        @pl.when(is_mid)
        def _():
            end_copy(u).wait_recv()
            spend(u, 6)
            mid_out[slot] = (plane[slot] + end_in[slot].astype(jnp.float32)).astype(low)
            mid_copy(u).start()
            credit(u, 5, pair_peer)

    def join_middle(u):
        slot = u % SLOTS

        @pl.when(is_mid)
        def _():
            mid_copy(u).wait()
            out[u] = (mid_out[slot].astype(jnp.float32) + mid_in[slot].astype(jnp.float32)).astype(low)
            back_copy(u).start()
            credit(u, 6, mid_peer)

    def total_copy(u, at, by_row, matrix):
        kind, index = matrix
        if by_row:
            place = totals[kind].at[index, pl.ds(pl.multiple_of(at * UNIT, UNIT), UNIT), :]
        else:
            place = totals[kind].at[index, :, pl.ds(pl.multiple_of(at * WIDE, WIDE), WIDE)]
        return pltpu.make_async_copy(out.at[u], place, total_sems.at[u])

    def finish(u):
        @pl.when(is_mid)
        def _():
            back_copy(u).wait_send()

        @pl.when(is_end)
        def _():
            back_copy(u).wait_recv()

        per_group(u, lambda at, side, first_row, count, by_row, matrix: total_copy(u, at, by_row, matrix).start())

    stages = [
        (0, produce),
        (1, join_cores),
        (1 + LAG_A, join_diagonal),
        (1 + LAG_A + LAG_B, join_plane),
        (1 + LAG_A + LAG_B + LAG_Z, join_pair),
        (1 + LAG_A + LAG_B + 2 * LAG_Z, join_middle),
        (1 + LAG_A + LAG_B + 3 * LAG_Z, finish),
    ]

    row_tiles = ((0, 0), (1, 128), (1, 256))

    def add_row(index, values):
        row_sums[index : index + 1, :] += jnp.sum(values, axis=0, keepdims=True)

    def norm_back(grad, kind, norm_index, at, ends, end_bias):
        rows = slice(at, at + 128)
        unit = normed[kind, rows, :]
        grad_unit = grad * params[16 + norm_index : 17 + norm_index, :]
        summed = inverse[kind, rows, :1] * (
            grad_unit
            - jnp.mean(grad_unit, axis=-1, keepdims=True)
            - unit * jnp.mean(grad_unit * unit, axis=-1, keepdims=True)
        )
        add_row(16 + norm_index, grad * unit)
        add_row(9 + norm_index, grad)
        stream[rows, :] = summed
        summed_low = summed.astype(low)
        ends[rows, :] = summed_low
        add_row(end_bias, summed_low.astype(jnp.float32))

    def feed_norm():
        wait_saved(params, word_cotangent, region_cotangent, normed, inverse)
        row_sums[...] = jnp.zeros_like(row_sums)
        hidden_sums[...] = jnp.zeros_like(hidden_sums)
        for f, at in row_tiles:
            cotangent = word_cotangent if f == 0 else region_cotangent
            first = at if f == 0 else at - WORDS
            norm_back(cotangent[first : first + 128, :].astype(jnp.float32), 2, 3 + f, at, end_feed, 14 + f)

    def next_block(n):
        if n + WINDOW < len(BLOCKS):
            load_block(n + WINDOW).start()

    def feed_back(f, c):
        n = 2 * (4 * f + c)
        load_block(n).wait()
        load_block(n + 1).wait()
        columns = slice(c * WIDE, (c + 1) * WIDE)
        for which, at in row_tiles:
            if which == f:
                rows = slice(at, at + 128)
                grad_hidden = dot_nt(end_feed[rows, :], window[n % WINDOW])
                before = (grad_hidden * slope[rows, columns].astype(jnp.float32)).astype(low)
                grad_before[rows, columns] = before
                row = 4 * f + c
                hidden_sums[row : row + 1, :] += jnp.sum(before.astype(jnp.float32), axis=0, keepdims=True)
                stream[rows, :] += dot_nt(before, window[(n + 1) % WINDOW])
        next_block(n)
        next_block(n + 1)

    def self_norm():
        for f, at in row_tiles:
            norm_back(stream[at : at + 128, :], 1, 1 + f, at, end_self, 5 + 3 * f)

    def self_context():
        for f in range(2):
            n = 16 + f
            load_block(n).wait()
            for which, at in row_tiles:
                if which == f:
                    grad_context[at : at + 128, :] = dot_nt(end_self[at : at + 128, :], window[n % WINDOW]).astype(low)
            next_block(n)

    def project_back(n, module, grad_mixed, tiles):
        for c in range(3):
            load_block(n + c).wait()
            columns = slice(c * WIDE, (c + 1) * WIDE)
            for at in tiles:
                part = grad_mixed[at : at + 128, columns]
                if c != 1:
                    add_row(3 * module + c // 2, part.astype(jnp.float32))
                stream[at : at + 128, :] += dot_nt(part, window[(n + c) % WINDOW])
            next_block(n + c)

    def cross_norm():
        for _, at in row_tiles:
            norm_back(stream[at : at + 128, :], 0, 0, at, end_cross, 2)

    def cross_context():
        n = 24
        load_block(n).wait()
        for _, at in row_tiles:
            grad_context[at : at + 128, :] = dot_nt(end_cross[at : at + 128, :], window[n % WINDOW]).astype(low)
        next_block(n)

    def give_rows():
        word_gradient[...] = stream[0:WORDS, :]
        region_gradient[...] = stream[WORDS:ROWS, :]

    def exact_nt(left, right):
        return lax.dot_general(
            left,
            right.astype(jnp.float32),
            (((1,), (1,)), ((), ())),
            precision=lax.Precision.HIGHEST,
            preferred_element_type=jnp.float32,
        )

    def give_small():
        small_in[...] = jnp.zeros_like(small_in)
        for owner in range(8):
            small_in[owner, 0:21, :] = exact_nt(row_sums[...], spread(owner))[:21]
        for place in range(8):
            placed = exact_nt(hidden_sums[...], spread(place))
            for f in range(2):
                for c in range(4):
                    row = 21 + 4 * f + place % 4
                    small_in[2 * c + place // 4, row : row + 1, :] = placed[4 * f + c : 4 * f + c + 1]
        for offset in range(1, 8):
            small_copy(offset).start()

    def join_small():
        summed = small_in[me]
        for offset in range(1, 8):
            small_copy(offset).wait()
            summed = summed + small_in_plane[offset - 1]
        small_planes[z] = summed
        for offset in range(1, 4):
            small_plane_copy(offset, z).start()

    def finish_small():
        for offset in range(1, 4):
            small_plane_copy(offset, z).wait_send()
            small_plane_copy(offset, (z + 4 - offset) % 4).wait_recv()
        small_out[...] = small_planes[0] + small_planes[1] + (small_planes[2] + small_planes[3])

    def self_back(rows_of, shares, first, last):
        attend_back_into(rows_of, mixed_self, shares, grad_context, grad_mixed_self, first, last)

    def cross_back(rows_of, shares, first, last):
        attend_back_into(rows_of, mixed_cross, shares, grad_context, grad_mixed_cross, first, last)

    pieces = {
        0: lambda: (wait_saved(slope), feed_back(0, 0)),
        1: lambda: feed_back(0, 1),
        2: lambda: feed_back(0, 2),
        3: lambda: feed_back(0, 3),
        4: lambda: feed_back(1, 0),
        5: lambda: feed_back(1, 1),
        6: lambda: feed_back(1, 2),
        7: lambda: (feed_back(1, 3), wait_saved(rows_two_t)),
        8: self_norm,
        9: lambda: (self_context(), wait_saved(context_self_t, mixed_self, shares_w)),
        10: lambda: (self_back(ATTEND_WORD, shares_w, 0, 6), wait_saved(shares_r, rows_one_t)),
        11: lambda: self_back(ATTEND_REGION, shares_r, 0, 2),
        12: lambda: self_back(ATTEND_REGION, shares_r, 2, 4),
        13: lambda: self_back(ATTEND_REGION, shares_r, 4, 6),
        14: lambda: project_back(18, 1, grad_mixed_self, (0,)),
        15: lambda: project_back(21, 2, grad_mixed_self, (128, 256)),
        16: lambda: (cross_norm(), wait_saved(context_cross_t, mixed_cross, shares_cw, shares_cr, rows_zero_t)),
        17: cross_context,
        18: lambda: cross_back(ATTEND_CROSS_WORD, shares_cw, 0, 3),
        19: lambda: cross_back(ATTEND_CROSS_WORD, shares_cw, 3, 6),
        20: lambda: cross_back(ATTEND_CROSS_REGION, shares_cr, 0, 3),
        21: lambda: cross_back(ATTEND_CROSS_REGION, shares_cr, 3, 6),
        22: lambda: (project_back(25, 0, grad_mixed_cross, (0, 128, 256)), give_rows()),
        23: give_small,
        25: join_small,
        27: finish_small,
    }

    feed_norm()

    def step(i, carry):
        for lag, stage in reversed(stages):
            if stage is produce:

                @pl.when(i == 0)
                def _():
                    wait_saved(hidden_t)

            @pl.when(jnp.logical_and(i >= lag, i < UNITS + lag))
            def _(lag=lag, stage=stage):
                stage(i - lag)

        for at, piece in pieces.items():

            @pl.when(i == at)
            def _(piece=piece):
                piece()

        return carry

    lax.fori_loop(0, UNITS + stages[-1][0], step, 0)

    def settle(u, carry):
        per_group(u, lambda at, side, first_row, count, by_row, matrix: total_copy(u, at, by_row, matrix).wait())
        return carry

    lax.fori_loop(0, UNITS, settle, 0)


def backward(saved, weights):
    block = (UNIT, WIDE)
    low, f32 = jnp.bfloat16, jnp.float32
    dma = pltpu.SemaphoreType.DMA
    vmem = pl.BlockSpec(memory_space=pltpu.VMEM)
    hbm = pl.BlockSpec(memory_space=pl.ANY)
    shape = jax.ShapeDtypeStruct
    small = (32, 128)
    return pl.pallas_call(
        backward_kernel,
        out_shape=(
            shape((WORDS, WIDE), f32),
            shape((REGIONS, WIDE), f32),
            shape(small, f32),
            shape((3, UNIT, 3 * WIDE), low),
            shape((3, UNIT, WIDE), low),
            shape((2, UNIT, HIDDEN), low),
            shape((2, 4 * UNIT, WIDE), low),
        ),
        in_specs=[hbm] * (len(saved) + len(weights)),
        out_specs=[vmem] * 3 + [hbm] * 4,
        scratch_shapes=[pltpu.VMEM(array.shape, array.dtype) for array in saved]
        + [
            pltpu.VMEM((WINDOW, WIDE, WIDE), low),
            pltpu.VMEM((ROWS, WIDE), low),
            pltpu.VMEM((ROWS, HIDDEN), low),
            pltpu.VMEM((ROWS, WIDE), low),
            pltpu.VMEM((ROWS, 3 * WIDE), low),
            pltpu.VMEM((ROWS, WIDE), low),
            pltpu.VMEM((ROWS, 3 * WIDE), low),
            pltpu.VMEM((ROWS, WIDE), f32),
            pltpu.VMEM((ROWS, WIDE), low),
            pltpu.VMEM((24, WIDE), f32),
            pltpu.VMEM((8, WIDE), f32),
            pltpu.VMEM((UNITS,) + block, low),
            pltpu.VMEM((ACC_SLOTS, 4) + block, f32),
            pltpu.VMEM((SLOTS, 4) + block, low),
            pltpu.VMEM((SLOTS, 4) + block, low),
            pltpu.VMEM((SLOTS, 2, UNIT // 2, WIDE), low),
            pltpu.VMEM((SLOTS, 2, UNIT // 2, WIDE), low),
            pltpu.VMEM((SLOTS, 2) + block, low),
            pltpu.VMEM((SLOTS, 2) + block, low),
            pltpu.VMEM((SLOTS,) + block, f32),
            pltpu.VMEM((SLOTS,) + block, low),
            pltpu.VMEM((SLOTS,) + block, low),
            pltpu.VMEM((SLOTS,) + block, low),
            pltpu.VMEM((SLOTS,) + block, low),
            pltpu.VMEM((8,) + small, f32),
            pltpu.VMEM((7,) + small, f32),
            pltpu.VMEM((4,) + small, f32),
            dma((18,)),
            dma((WINDOW,)),
            dma((UNITS,)),
            dma((SLOTS,)),
            dma((SLOTS,)),
            dma((SLOTS, 2)),
            dma((SLOTS, 2)),
            dma((SLOTS, 2)),
            dma((SLOTS, 2)),
            dma((3, SLOTS)),
            dma((3, SLOTS)),
            dma((10,)),
            dma((10,)),
            pltpu.SemaphoreType.REGULAR((7,)),
        ],
        compiler_params=pltpu.CompilerParams(
            collective_id=0, has_side_effects=True, vmem_limit_bytes=64 * 2**20 - 2**16
        ),
    )(*saved, *weights)


def deliver_kernel(*refs):
    moved, small, totals = refs[:4], refs[4], refs[5:9]
    moved_out, bias_out, gain_out, hidden_out, totals_out = refs[9:13], refs[13], refs[14], refs[15], refs[16:20]
    narrow, wide = refs[20:24], refs[24:28]
    move_sems, load_sems, store_sems = refs[28:]
    moves = [pltpu.make_async_copy(moved[i], moved_out[i], move_sems.at[i]) for i in range(4)]
    loads = [pltpu.make_async_copy(totals[i], narrow[i], load_sems.at[i]) for i in range(4)]
    stores = [pltpu.make_async_copy(wide[i], totals_out[i], store_sems.at[i]) for i in range(4)]
    for one in loads + moves:
        one.start()
    bias_out[...] = small[0:16, 0:UNIT]
    gain_out[...] = small[16:21, 0:UNIT]
    source = lax.broadcasted_iota(jnp.int32, (128, 4 * UNIT), 0)
    target = lax.broadcasted_iota(jnp.int32, (128, 4 * UNIT), 1)
    for f in range(2):
        row = jnp.zeros((1, 4 * UNIT), F32)
        for q in range(4):
            chosen = jnp.logical_and(source < UNIT, target == source + q * UNIT).astype(F32)
            line = 21 + 4 * f + q
            row = row + jnp.dot(
                small[line : line + 1, :], chosen, precision=lax.Precision.HIGHEST, preferred_element_type=F32
            )
        hidden_out[f : f + 1, :] = row
    for i in range(4):
        loads[i].wait()
        wide[i][...] = narrow[i][...].astype(F32)
        stores[i].start()
    for one in moves + stores:
        one.wait()


def deliver(moved, small, totals):
    vmem = pl.BlockSpec(memory_space=pltpu.VMEM)
    hbm = pl.BlockSpec(memory_space=pl.ANY)
    shape = jax.ShapeDtypeStruct
    widened = [shape(total.shape, F32) for total in totals]
    sem = pltpu.SemaphoreType.DMA((4,))
    return pl.pallas_call(
        deliver_kernel,
        out_shape=[shape(one.shape, one.dtype) for one in moved]
        + [shape((16, UNIT), F32), shape((5, UNIT), F32), shape((2, 4 * UNIT), F32)]
        + widened,
        in_specs=[hbm] * 4 + [vmem] + [hbm] * 4,
        out_specs=[hbm] * 4 + [vmem] * 3 + [hbm] * 4,
        scratch_shapes=[pltpu.VMEM(one.shape, one.dtype) for one in totals]
        + [pltpu.VMEM(one.shape, F32) for one in totals]
        + [sem, sem, sem],
        compiler_params=pltpu.CompilerParams(vmem_limit_bytes=64 * 2**20 - 2**16),
    )(*moved, small, *totals)


def paired(
    word_rows,
    region_rows,
    word_segment,
    region_segment,
    inward,
    outward,
    biases,
    norm_gain,
    expand_weight,
    shrink_weight,
    hidden_bias,
    word_cotangent,
    region_cotangent,
):
    results, saved, weights = forward(
        word_rows,
        region_rows,
        word_segment,
        region_segment,
        biases,
        norm_gain,
        hidden_bias,
        (inward, outward, expand_weight, shrink_weight),
    )
    word_gradient, region_gradient, small, *totals = backward(
        (saved[0], word_cotangent, region_cotangent, *saved[1:]), weights
    )
    word_out, region_out, word_gradient, region_gradient, bias, gain, hidden, *totals = deliver(
        (*results, word_gradient, region_gradient), small, totals
    )
    inward_total, outward_total, expand_total, shrink_total = totals
    return (
        word_out,
        region_out,
        word_gradient,
        region_gradient,
        inward_total,
        outward_total,
        bias,
        gain,
        expand_total,
        shrink_total,
        hidden,
    )


def general(
    devices,
    word_rows,
    region_rows,
    word_segment,
    region_segment,
    inward,
    outward,
    biases,
    norm_gain,
    expand_weight,
    shrink_weight,
    hidden_bias,
    word_cotangent,
    region_cotangent,
):
    words_count = word_rows.shape[0]
    width = word_rows.shape[1]
    word_ids = word_segment[0]
    region_ids = region_segment[0]
    cross_mask = word_ids[:, None] == region_ids[None, :]
    word_mask = word_ids[:, None] == word_ids[None, :]
    region_mask = region_ids[:, None] == region_ids[None, :]
    shard = biases.shape[1]
    per_shard = hidden_bias.shape[1] // shard
    small_shard = jnp.concatenate([biases, norm_gain, hidden_bias.reshape(2 * per_shard, shard)], axis=0)
    small_all = lax.all_gather(small_shard, "fsdp", axis=0)
    bias_count = biases.shape[0]
    gain_count = norm_gain.shape[0]
    row_params = small_all[:, : bias_count + gain_count].transpose(1, 0, 2).reshape(bias_count + gain_count, width)
    hidden_all = (
        small_all[:, bias_count + gain_count :]
        .reshape(devices, 2, per_shard * shard)
        .transpose(1, 0, 2)
        .reshape(2, devices * per_shard * shard)
    )
    inward_all, outward_all = (
        lax.all_gather(inward, "fsdp", axis=1, tiled=True),
        lax.all_gather(outward, "fsdp", axis=1, tiled=True),
    )
    attend_set = (
        inward_all,
        outward_all,
        row_params[:bias_count].astype(jnp.float32),
        row_params[bias_count:].astype(jnp.float32),
    )
    crossed, cross_kept = cross_forward(word_rows, region_rows, attend_set, cross_mask)
    word_one, word_kept = self_forward(crossed[:words_count], attend_set, 1, word_mask)
    region_one, region_kept = self_forward(crossed[words_count:], attend_set, 2, region_mask)
    expand_all, shrink_all = (
        lax.all_gather(expand_weight, "fsdp", axis=1, tiled=True),
        lax.all_gather(shrink_weight, "fsdp", axis=1, tiled=True),
    )
    feed_set = (expand_all, shrink_all, hidden_all)
    word_two, word_feed = feed_forward(word_one, feed_set, 0, attend_set)
    region_two, region_feed = feed_forward(region_one, feed_set, 1, attend_set)
    word_back = feed_backward(word_cotangent.astype(jnp.float32), word_feed, feed_set, 0, attend_set[3])
    region_back = feed_backward(region_cotangent.astype(jnp.float32), region_feed, feed_set, 1, attend_set[3])
    word_self = self_backward(word_back[0], word_kept, attend_set, 1, word_mask)
    region_self = self_backward(region_back[0], region_kept, attend_set, 2, region_mask)
    grad_crossed = jnp.concatenate([word_self[0], region_self[0]], axis=0)
    cross_back = cross_backward(grad_crossed, cross_kept, attend_set, cross_mask, words_count)
    row_grads = jnp.stack(
        [
            cross_back[3][0],
            cross_back[3][1],
            cross_back[3][2],
            word_self[3][0],
            word_self[3][1],
            word_self[3][2],
            region_self[3][0],
            region_self[3][1],
            region_self[3][2],
            cross_back[5],
            word_self[5],
            region_self[5],
            word_back[6],
            region_back[6],
            word_back[4],
            region_back[4],
            cross_back[4],
            word_self[4],
            region_self[4],
            word_back[5],
            region_back[5],
        ]
    )
    hidden_grads = jnp.stack([word_back[3], region_back[3]])
    small_grads = jnp.concatenate(
        [
            row_grads.reshape(bias_count + gain_count, devices, shard).transpose(1, 0, 2),
            hidden_grads.reshape(2, devices, per_shard, shard)
            .transpose(1, 0, 2, 3)
            .reshape(devices, 2 * per_shard, shard),
        ],
        axis=1,
    )

    def reduced(products, axis):
        mine = lax.psum_scatter(jnp.stack(products), "fsdp", scatter_dimension=axis, tiled=True)
        return lax.psum(mine.astype(jnp.bfloat16), "rep").astype(jnp.float32)

    shrink_total = reduced([matmul_tn(*word_back[2]), matmul_tn(*region_back[2])], 1)
    expand_total = reduced([matmul_tn(*word_back[1]), matmul_tn(*region_back[1])], 1)
    outward_total = reduced([matmul_tn(*cross_back[2]), matmul_tn(*word_self[2]), matmul_tn(*region_self[2])], 1)
    inward_total = reduced([matmul_tn(*cross_back[1]), matmul_tn(*word_self[1]), matmul_tn(*region_self[1])], 1)
    small_total = lax.psum(lax.psum_scatter(small_grads, "fsdp", scatter_dimension=0, tiled=False), "rep")
    grad_rows = cross_back[0]
    return (
        word_two.astype(jnp.bfloat16),
        region_two.astype(jnp.bfloat16),
        grad_rows[:words_count],
        grad_rows[words_count:],
        inward_total,
        outward_total,
        small_total[:bias_count],
        small_total[bias_count : bias_count + gain_count],
        expand_total,
        shrink_total,
        small_total[bias_count + gain_count :].reshape(2, per_shard * shard),
    )


def solution(mesh):
    sizes = (mesh.shape["rep"], mesh.shape["fsdp"])
    return jax.shard_map(
        paired if sizes == (4, 8) else functools.partial(general, mesh.shape["fsdp"]),
        mesh=mesh,
        in_specs=(
            P(("rep", "fsdp"), None),
            P(("rep", "fsdp"), None),
            P(("rep", "fsdp"), None),
            P(("rep", "fsdp"), None),
            P(None, "fsdp", None),
            P(None, "fsdp", None),
            P(None, "fsdp"),
            P(None, "fsdp"),
            P(None, "fsdp", None),
            P(None, "fsdp", None),
            P(None, "fsdp"),
            P(("rep", "fsdp"), None),
            P(("rep", "fsdp"), None),
        ),
        out_specs=(
            P(("rep", "fsdp"), None),
            P(("rep", "fsdp"), None),
            P(("rep", "fsdp"), None),
            P(("rep", "fsdp"), None),
            P(None, "fsdp", None),
            P(None, "fsdp", None),
            P(None, "fsdp"),
            P(None, "fsdp"),
            P(None, "fsdp", None),
            P(None, "fsdp", None),
            P(None, "fsdp"),
        ),
        check_vma=False,
    )
```

```python
import functools

import jax
import jax.numpy as jnp
from jax import lax
from jax.experimental import pallas as pl
from jax.experimental.pallas import tpu as pltpu
from jax.sharding import PartitionSpec as P

MESH = pl.DeviceIdType.MESH

HEADS = 12
HEAD_DIM = 64


norm_epsilon = 1e-12
masked_score = -1e30


def matmul(left_op, right_op):
    return jnp.dot(left_op, right_op, preferred_element_type=jnp.float32)


def matmul_tn(left_op, right_op):
    return lax.dot_general(
        left_op, right_op, (((0,), (0,)), ((), ())), preferred_element_type=jnp.float32
    )


def matmul_nt(left_op, right_op):
    return lax.dot_general(
        left_op, right_op, (((1,), (1,)), ((), ())), preferred_element_type=jnp.float32
    )


def column_sums(values):
    return jnp.sum(values, axis=0, dtype=jnp.float32)


def heads_of(rows_in):
    return rows_in.reshape(rows_in.shape[0], HEADS, HEAD_DIM)


def merge_heads(head_rows):
    return head_rows.reshape(head_rows.shape[0], -1)


def normalize(summed, gain_row, shift_row):
    center = summed - jnp.mean(summed, axis=-1, keepdims=True)
    inverse = lax.rsqrt(jnp.mean(center * center, axis=-1, keepdims=True) + norm_epsilon)
    normed = center * inverse
    return (normed * gain_row + shift_row, (normed, inverse))


def normalize_back(grad_out, norm_stats, gain_row):
    normed, inverse = norm_stats
    grad_normed = grad_out * gain_row
    grad_sum = inverse * (
        grad_normed
        - jnp.mean(grad_normed, axis=-1, keepdims=True)
        - normed * jnp.mean(grad_normed * normed, axis=-1, keepdims=True)
    )
    return (grad_sum, column_sums(grad_out * normed), column_sums(grad_out))


def score_block(queries, key_rows, allowed):
    scores = jnp.einsum(
        "qhd,khd->hqk", heads_of(queries), heads_of(key_rows), preferred_element_type=jnp.float32
    ) * HEAD_DIM ** (-0.5)
    return jnp.where(allowed[None], scores, masked_score)


def attend(queries, key_rows, value_rows, allowed):
    scores = score_block(queries, key_rows, allowed)
    top_score = jnp.max(scores, axis=-1, keepdims=True)
    log_total = top_score + jnp.log(jnp.sum(jnp.exp(scores - top_score), axis=-1, keepdims=True))
    shares = jnp.exp(scores - log_total).astype(jnp.bfloat16)
    context = jnp.einsum(
        "hqk,khd->qhd", shares, heads_of(value_rows), preferred_element_type=jnp.float32
    )
    return (merge_heads(context).astype(jnp.bfloat16), log_total)


def attend_back(queries, key_rows, value_rows, allowed, log_total, grad_context):
    shares = jnp.exp(score_block(queries, key_rows, allowed) - log_total)
    grad_heads = heads_of(grad_context)
    grad_shares = jnp.einsum(
        "qhd,khd->hqk", grad_heads, heads_of(value_rows), preferred_element_type=jnp.float32
    )
    grad_values = jnp.einsum(
        "hqk,qhd->khd", shares.astype(jnp.bfloat16), grad_heads, preferred_element_type=jnp.float32
    )
    grad_scores = (
        shares * (grad_shares - jnp.sum(shares * grad_shares, axis=-1, keepdims=True))
    ).astype(jnp.bfloat16)
    score_scale = HEAD_DIM ** (-0.5)
    grad_queries = (
        jnp.einsum(
            "hqk,khd->qhd", grad_scores, heads_of(key_rows), preferred_element_type=jnp.float32
        )
        * score_scale
    )
    grad_keys = (
        jnp.einsum(
            "hqk,qhd->khd", grad_scores, heads_of(queries), preferred_element_type=jnp.float32
        )
        * score_scale
    )
    return (merge_heads(grad_queries), merge_heads(grad_keys), merge_heads(grad_values))


def project(rows_low, weight, bias_rows, module):
    width = weight.shape[0]
    bias_all = jnp.concatenate(
        [bias_rows[3 * module], jnp.zeros((width,), jnp.float32), bias_rows[3 * module + 1]]
    )
    return (matmul(rows_low, weight) + bias_all).astype(jnp.bfloat16)


def project_back(grad_sum, grad_parts, rows_low, weight):
    width = weight.shape[0]
    grad_mixed = jnp.concatenate(grad_parts, axis=1).astype(jnp.bfloat16)
    grad_weight = (rows_low, grad_mixed)
    grad_bias = column_sums(grad_mixed)
    grad_rows = grad_sum + matmul_nt(grad_mixed, weight)
    return (grad_rows, grad_weight, grad_bias[:width], grad_bias[2 * width :])


def branch_back(grad_out, context, norm_stats, gain_row, outward_one):
    grad_sum, grad_gain, grad_shift = normalize_back(grad_out, norm_stats, gain_row)
    grad_branch = grad_sum.astype(jnp.bfloat16)
    grad_outward = (context, grad_branch)
    grad_context = matmul_nt(grad_branch, outward_one).astype(jnp.bfloat16)
    return (grad_sum, grad_context, grad_outward, column_sums(grad_branch), grad_gain, grad_shift)


def self_forward(rows_in, weights, module, allowed):
    inward_all, outward_all, bias_rows, gain_rows = weights
    width = rows_in.shape[1]
    rows_low = rows_in.astype(jnp.bfloat16)
    mixed = project(rows_low, inward_all[module], bias_rows, module)
    context, log_total = attend(
        mixed[:, :width], mixed[:, width : 2 * width], mixed[:, 2 * width :], allowed
    )
    summed = rows_in + matmul(context, outward_all[module]) + bias_rows[3 * module + 2]
    result, norm_stats = normalize(summed, gain_rows[module], bias_rows[9 + module])
    return (result, (rows_low, mixed, context, log_total, norm_stats))


def self_backward(grad_out, kept, weights, module, allowed):
    inward_all, outward_all, bias_rows, gain_rows = weights
    rows_low, mixed, context, log_total, norm_stats = kept
    width = rows_low.shape[1]
    grad_sum, grad_context, grad_outward, grad_bias_out, grad_gain, grad_shift = branch_back(
        grad_out, context, norm_stats, gain_rows[module], outward_all[module]
    )
    grad_parts = attend_back(
        mixed[:, :width],
        mixed[:, width : 2 * width],
        mixed[:, 2 * width :],
        allowed,
        log_total,
        grad_context,
    )
    grad_rows, grad_inward, grad_bias_query, grad_bias_value = project_back(
        grad_sum, grad_parts, rows_low, inward_all[module]
    )
    return (
        grad_rows,
        grad_inward,
        grad_outward,
        (grad_bias_query, grad_bias_value, grad_bias_out),
        grad_gain,
        grad_shift,
    )


def cross_forward(word_rows, region_rows, weights, cross_mask):
    inward_all, outward_all, bias_rows, gain_rows = weights
    words_count = word_rows.shape[0]
    width = word_rows.shape[1]
    rows_low = jnp.concatenate([word_rows, region_rows], axis=0)
    mixed = project(rows_low, inward_all[0], bias_rows, 0)
    word_mix = mixed[:words_count]
    region_mix = mixed[words_count:]
    word_context, word_total = attend(
        word_mix[:, :width],
        region_mix[:, width : 2 * width],
        region_mix[:, 2 * width :],
        cross_mask,
    )
    region_context, region_total = attend(
        region_mix[:, :width],
        word_mix[:, width : 2 * width],
        word_mix[:, 2 * width :],
        cross_mask.T,
    )
    context = jnp.concatenate([word_context, region_context], axis=0)
    summed = rows_low.astype(jnp.float32) + matmul(context, outward_all[0]) + bias_rows[2]
    result, norm_stats = normalize(summed, gain_rows[0], bias_rows[9])
    return (result, (rows_low, mixed, context, word_total, region_total, norm_stats))


def cross_backward(grad_out, kept, weights, cross_mask, words_count):
    inward_all, outward_all, bias_rows, gain_rows = weights
    rows_low, mixed, context, word_total, region_total, norm_stats = kept
    width = rows_low.shape[1]
    grad_sum, grad_context, grad_outward, grad_bias_out, grad_gain, grad_shift = branch_back(
        grad_out, context, norm_stats, gain_rows[0], outward_all[0]
    )
    word_mix = mixed[:words_count]
    region_mix = mixed[words_count:]
    word_query_grad, region_key_grad, region_value_grad = attend_back(
        word_mix[:, :width],
        region_mix[:, width : 2 * width],
        region_mix[:, 2 * width :],
        cross_mask,
        word_total,
        grad_context[:words_count],
    )
    region_query_grad, word_key_grad, word_value_grad = attend_back(
        region_mix[:, :width],
        word_mix[:, width : 2 * width],
        word_mix[:, 2 * width :],
        cross_mask.T,
        region_total,
        grad_context[words_count:],
    )
    grad_parts = (
        jnp.concatenate([word_query_grad, region_query_grad], axis=0),
        jnp.concatenate([word_key_grad, region_key_grad], axis=0),
        jnp.concatenate([word_value_grad, region_value_grad], axis=0),
    )
    grad_rows, grad_inward, grad_bias_query, grad_bias_value = project_back(
        grad_sum, grad_parts, rows_low, inward_all[0]
    )
    return (
        grad_rows,
        grad_inward,
        grad_outward,
        (grad_bias_query, grad_bias_value, grad_bias_out),
        grad_gain,
        grad_shift,
    )


def gelu_exact(values):
    return jax.nn.gelu(values, approximate=False)


def feed_forward(rows_in, weights, feed_index, attend_set):
    expand_all, shrink_all, hidden_all = weights
    bias_rows, gain_rows = (attend_set[2], attend_set[3])
    rows_low = rows_in.astype(jnp.bfloat16)
    before = matmul(rows_low, expand_all[feed_index]) + hidden_all[feed_index].astype(jnp.float32)
    hidden = gelu_exact(before).astype(jnp.bfloat16)
    summed = rows_in + matmul(hidden, shrink_all[feed_index]) + bias_rows[14 + feed_index]
    result, norm_stats = normalize(summed, gain_rows[3 + feed_index], bias_rows[12 + feed_index])
    return (result, (rows_low, before, hidden, norm_stats))


def feed_backward(grad_out, kept, weights, feed_index, gain_rows):
    expand_all, shrink_all, hidden_all = weights
    rows_low, before, hidden, norm_stats = kept
    grad_sum, grad_gain, grad_shift = normalize_back(
        grad_out, norm_stats, gain_rows[3 + feed_index]
    )
    grad_branch = grad_sum.astype(jnp.bfloat16)
    grad_shrink = (hidden, grad_branch)
    grad_hidden = matmul_nt(grad_branch, shrink_all[feed_index])
    unused_value, slope_back = jax.vjp(gelu_exact, before)
    grad_before = slope_back(grad_hidden)[0].astype(jnp.bfloat16)
    grad_expand = (rows_low, grad_before)
    grad_rows = grad_sum + matmul_nt(grad_before, expand_all[feed_index])
    return (
        grad_rows,
        grad_expand,
        grad_shrink,
        column_sums(grad_before),
        column_sums(grad_branch),
        grad_gain,
        grad_shift,
    )


UNIT = 96
WIDE = 768
SLOTS = 4
ACC_SLOTS = 6
LAG_A = 2
LAG_B = 2
LAG_Z = 1


WORDS = 128
REGIONS = 256
ROWS = 384
HIDDEN = 3072
PAIRS_OF_HEADS = 6
PAIR_WIDE = 128


def flip(position, bits):
    return lax.bitwise_xor(position, bits)


def dot_nt(left, right):
    return lax.dot_general(left, right, (((1,), (1,)), ((), ())), preferred_element_type=jnp.float32)


def dot_tn(left, right):
    return lax.dot_general(left, right, (((0,), (0,)), ((), ())), preferred_element_type=jnp.float32)


def spread(part):
    source = lax.broadcasted_iota(jnp.int32, (128, WIDE), 0)
    target = lax.broadcasted_iota(jnp.int32, (128, WIDE), 1)
    return jnp.logical_and(source < UNIT, target == source + part * UNIT)


def half_lanes():
    lane = lax.broadcasted_iota(jnp.int32, (1, PAIR_WIDE), 1)
    return (lane < HEAD_DIM, lane >= HEAD_DIM)


def only(values, chosen):
    return jnp.where(chosen, values, jnp.zeros_like(values))


ATTEND_CROSS_WORD = ((0, WORDS), (WORDS, REGIONS))
ATTEND_CROSS_REGION = ((WORDS, REGIONS), (0, WORDS))
ATTEND_WORD = ((0, WORDS), (0, WORDS))
ATTEND_REGION = ((WORDS, REGIONS), (WORDS, REGIONS))


def attend_into(rows_of, mixed, allowed, shares, context):
    (query_at, query_count), (key_at, key_count) = rows_of
    blocked = jnp.where(allowed, 0.0, masked_score)

    def pair(p, carry):
        at = pl.multiple_of(p * PAIR_WIDE, PAIR_WIDE)
        queries = mixed[pl.ds(query_at, query_count), pl.ds(at, PAIR_WIDE)]
        key_rows = mixed[pl.ds(key_at, key_count), pl.ds(WIDE + at, PAIR_WIDE)]
        value_rows = mixed[pl.ds(key_at, key_count), pl.ds(2 * WIDE + at, PAIR_WIDE)]
        total = jnp.zeros((query_count, PAIR_WIDE), jnp.float32)
        for side, chosen in enumerate(half_lanes()):
            scores = dot_nt(only(queries, chosen), key_rows) * HEAD_DIM ** (-0.5) + blocked
            lifted = jnp.exp(scores - jnp.max(scores, axis=-1, keepdims=True))
            share = (lifted / jnp.sum(lifted, axis=-1, keepdims=True)).astype(jnp.bfloat16)
            shares[2 * p + side] = share
            total = total + matmul(share, only(value_rows, chosen))
        context[pl.ds(query_at, query_count), pl.ds(at, PAIR_WIDE)] = total.astype(jnp.bfloat16)
        return carry

    lax.fori_loop(0, PAIRS_OF_HEADS, pair, 0)


def row_norm(summed):
    center = summed - jnp.mean(summed, axis=-1, keepdims=True)
    inverse = lax.rsqrt(jnp.mean(center * center, axis=-1, keepdims=True) + norm_epsilon)
    return (center * inverse, inverse)


def down(across):
    wide = jnp.broadcast_to(across.astype(jnp.float32), (128, across.shape[1]))
    return jnp.concatenate([wide[:, at : at + 128].T[:, :1] for at in range(0, across.shape[1], 128)], axis=0)


LOW, F32 = jnp.bfloat16, jnp.float32
SAVED = (
    ((24, WIDE), F32),
    ((3, ROWS, WIDE), F32),
    ((3, ROWS, 128), F32),
    ((HIDDEN, ROWS), LOW),
    ((ROWS, HIDDEN), LOW),
    ((WIDE, ROWS), LOW),
    ((WIDE, ROWS), LOW),
    ((ROWS, 3 * WIDE), LOW),
    ((HEADS, WORDS, WORDS), LOW),
    ((HEADS, REGIONS, REGIONS), LOW),
    ((WIDE, ROWS), LOW),
    ((WIDE, ROWS), LOW),
    ((ROWS, 3 * WIDE), LOW),
    ((HEADS, WORDS, REGIONS), LOW),
    ((HEADS, REGIONS, WORDS), LOW),
    ((WIDE, ROWS), LOW),
)
WEIGHTS = (
    (3, WIDE, 3 * WIDE),
    (3, WIDE, WIDE),
    (2, WIDE, HIDDEN),
    (2, HIDDEN, WIDE),
)

CHUNKS = (
    (2, 0, None),
    (0, 0, (0, UNIT)),
    (1, 0, (0, UNIT)),
    (2, 1, None),
    (0, 2, (0, UNIT)),
    (1, 2, (0, UNIT)),
    (3, 1, None),
    (0, 1, (0, UNIT)),
    (1, 1, (0, UNIT)),
    (3, 0, (0, 2 * UNIT)),
    (3, 0, (2 * UNIT, 2 * UNIT)),
)
EXPAND_0, INWARD_0, OUTWARD_0, EXPAND_1, INWARD_2, OUTWARD_2, SHRINK_1, INWARD_1, OUTWARD_1, SHRINK_0A, SHRINK_0B = range(
    len(CHUNKS)
)


def forward_kernel(*refs):
    word_rows, region_rows, word_ids, region_ids, biases, gains, hidden_bias, *shards = refs[:11]
    word_result, region_result, *kept = refs[11:29]
    weights_kept = refs[29:33]
    (
        params,
        normed,
        inverse,
        hidden_t,
        slope,
        rows_two_t,
        context_self_t,
        mixed_self,
        shares_w,
        shares_r,
        rows_one_t,
        context_cross_t,
        mixed_cross,
        shares_cw,
        shares_cr,
        rows_zero_t,
    ) = saved = refs[33:49]
    inward_all, outward_all, expand_all, shrink_all = gathered = refs[49:53]
    (
        small_own,
        small_all,
        hidden_rows,
        rows_low,
        stream,
        stream_low,
        context,
        hidden,
        sends,
        recvs,
        z_sends,
        z_recvs,
        foreign_sends,
        foreign_recvs,
        small_sends,
        small_recvs,
        local_sems,
        keep_sems,
    ) = refs[53:]
    me = lax.axis_index("fsdp")
    z = lax.axis_index("rep")
    peers = {"x": {"fsdp": flip(me, 2)}, "y": {"fsdp": flip(me, 4)}, "core": {"fsdp": flip(me, 1)}}
    above, below = {"rep": (z + 1) % 4}, {"rep": (z + 3) % 4}

    barrier = pltpu.get_barrier_semaphore()
    for offset in range(1, 8):
        pl.semaphore_signal(barrier, inc=1, device_id={"fsdp": flip(me, offset)}, device_id_type=MESH)
    for offset in range(1, 4):
        pl.semaphore_signal(barrier, inc=1, device_id={"rep": (z + offset) % 4}, device_id_type=MESH)
    pl.semaphore_wait(barrier, 10)

    def remote(src, dst, send_sem, recv_sem, peer):
        return pltpu.make_async_remote_copy(
            src_ref=src, dst_ref=dst, send_sem=send_sem, recv_sem=recv_sem, device_id=peer, device_id_type=MESH
        )

    def small_copy(offset, owner):
        return remote(
            small_all.at[owner],
            small_all.at[owner],
            small_sends.at[offset - 1],
            small_recvs.at[offset - 1],
            {"fsdp": flip(me, offset)},
        )

    X, Y, DIAG_Y, DIAG_X, CORE_OWN, CORE_X, CORE_Y, CORE_DIAG = range(8)

    def place(k, owner, half=None, quarter=None):
        kind, _, rows = CHUNKS[k]
        shard_rows, columns = shards[kind].shape[1:]
        first, count, column = 0, shard_rows, 0
        if rows is not None:
            first, count = rows
        elif quarter is not None and kind == 3:
            first, count = quarter * UNIT, UNIT
        elif quarter is not None:
            column, columns = quarter * WIDE, WIDE
        if half is not None:
            count = count // 2
            first = first + half * count
        if not isinstance(column, int):
            column = pl.multiple_of(column, WIDE)
        if not isinstance(first, int):
            first = pl.multiple_of(first, 16)
        whole = pl.multiple_of(owner * shard_rows + first, 16)
        return pl.ds(whole, count), pl.ds(first, count), pl.ds(column, columns)

    def own_part(k, quarter=None):
        kind, index, _ = CHUNKS[k]
        _, rows, columns = place(k, me, None, quarter)
        return shards[kind].at[index, rows, columns]

    def part(k, owner, half=None, quarter=None):
        kind, index, _ = CHUNKS[k]
        rows, _, columns = place(k, owner, half, quarter)
        return gathered[kind].at[index, rows, columns]

    def mine(k):
        return z if CHUNKS[k][2] is None else None

    def copy(k, kind, arriving=False):
        owner, half, peer = {
            X: (flip(me, 2) if arriving else me, None, "x"),
            Y: (flip(me, 4) if arriving else me, None, "y"),
            DIAG_Y: (flip(me, 6 if arriving else 2), 0, "y"),
            DIAG_X: (flip(me, 6 if arriving else 4), 1, "x"),
            CORE_OWN: (flip(me, 1) if arriving else me, None, "core"),
            CORE_X: (flip(me, 3 if arriving else 2), None, "core"),
            CORE_Y: (flip(me, 5 if arriving else 4), None, "core"),
            CORE_DIAG: (flip(me, 7 if arriving else 6), None, "core"),
        }[kind]
        quarter = None if kind == CORE_OWN else mine(k)
        target = part(k, owner, half, quarter)
        source = own_part(k, quarter) if kind in (X, Y, CORE_OWN) and not arriving else target
        return remote(source, target, sends.at[k, kind], recvs.at[k, kind], peers[peer])

    z_chunks = [k for k in range(len(CHUNKS)) if CHUNKS[k][2] is None]
    owners = (flip(me, 2), flip(me, 4), flip(me, 6))
    core_owners = (flip(me, 3), flip(me, 5), flip(me, 7))

    def z_copy(k, way, hop, which, arriving=False):
        steps = hop + 1 if arriving else hop
        quarter = z - steps if way == 0 else z + steps
        here = part(k, owners[which], None, quarter)
        at = (z_chunks.index(k), way, hop, which)
        return remote(here, here, z_sends.at[at], z_recvs.at[at], (above, below)[way])

    def foreign_copy(k, way, hop, which, arriving=False):
        quarter = z - hop - 1 if way == 0 else z + hop + 1
        here = part(k, (core_owners if arriving else owners)[which], None, quarter)
        at = (z_chunks.index(k), way, hop, which)
        return remote(here, here, foreign_sends.at[at], foreign_recvs.at[at], peers["core"])

    def goes(way, hop):
        return jnp.logical_and(z >= hop, z < 3) if way == 0 else jnp.logical_and(z <= 3 - hop, z > 0)

    def comes(way, hop):
        return z >= hop + 1 if way == 0 else z <= 2 - hop

    def send_z(k, hop, which):
        for way in range(2):

            @pl.when(goes(way, hop))
            def _(way=way):
                for one in which:
                    z_copy(k, way, hop, one).start()

    def own_local(k):
        return pltpu.make_async_copy(own_part(k), part(k, me), local_sems.at[k])

    def own(k):
        for kind in (X, Y):
            copy(k, kind).start()
        own_local(k).start()
        copy(k, CORE_OWN).start()

    def pass_first(k):
        copy(k, X, True).wait_recv()
        copy(k, DIAG_Y).start()
        copy(k, Y, True).wait_recv()
        copy(k, DIAG_X).start()
        if k in z_chunks:
            send_z(k, 0, (0, 1))
        copy(k, CORE_X).start()
        copy(k, CORE_Y).start()

    def pass_second(k):
        copy(k, DIAG_Y, True).wait_recv()
        copy(k, DIAG_X, True).wait_recv()
        if k in z_chunks:
            send_z(k, 0, (2,))
        copy(k, CORE_DIAG).start()

    def pass_quarter(k, hop):
        for way in range(2):

            @pl.when(comes(way, hop))
            def _(way=way):
                for which in range(3):
                    z_copy(k, way, hop, which, True).wait_recv()

        if hop < 2:
            send_z(k, hop + 1, (0, 1, 2))
        for way in range(2):

            @pl.when(comes(way, hop))
            def _(way=way):
                for which in range(3):
                    foreign_copy(k, way, hop, which).start()

    def complete(k):
        own_local(k).wait()
        for kind in (CORE_OWN, CORE_X, CORE_Y, CORE_DIAG):
            copy(k, kind, True).wait_recv()
        if k in z_chunks:
            for hop in range(3):
                for way in range(2):

                    @pl.when(comes(way, hop))
                    def _(way=way, hop=hop):
                        for which in range(3):
                            foreign_copy(k, way, hop, which, True).wait_recv()

    keeps = []

    def keep(source, target):
        copied = pltpu.make_async_copy(source, target, keep_sems.at[len(keeps)])
        copied.start()
        keeps.append(copied)

    def keep_weights(kind, index):
        keep(gathered[kind].at[index], weights_kept[kind].at[index])

    def keep_saved(*refs_done):
        for done in refs_done:
            index = [ref is done for ref in saved].index(True)
            keep(saved[index], kept[index])

    def give_small():
        small_own[...] = jnp.zeros_like(small_own)
        small_own[0:16, 0:UNIT] = biases[...].astype(F32)
        small_own[16:21, 0:UNIT] = gains[...].astype(F32)
        source = lax.broadcasted_iota(jnp.int32, (4 * UNIT, 128), 0)
        target = lax.broadcasted_iota(jnp.int32, (4 * UNIT, 128), 1)
        for q in range(4):
            chosen = jnp.logical_and(target < UNIT, source == target + q * UNIT).astype(LOW)
            placed = matmul(hidden_bias[...], chosen)
            for f in range(2):
                row = 21 + 4 * f + q
                small_own[row : row + 1, :] = placed[f : f + 1]
        small_all[me] = small_own[...].astype(LOW)
        for offset in range(1, 8):
            small_copy(offset, me).start()

    def read_small():
        for offset in range(1, 8):
            small_copy(offset, flip(me, offset)).wait_recv()
        totals = jnp.zeros((21, WIDE), jnp.float32)
        hidden_parts = [[jnp.zeros((1, WIDE), jnp.float32) for _ in range(4)] for _ in range(2)]
        for owner in range(8):
            one = small_all[owner]
            totals = totals + matmul(one, spread(owner).astype(LOW))[:21]
            for q in range(4):
                placed = matmul(one, spread((owner % 2) * 4 + q).astype(LOW))
                for f in range(2):
                    row = 21 + 4 * f + q
                    hidden_parts[f][owner // 2] = hidden_parts[f][owner // 2] + placed[row : row + 1]
        params[...] = jnp.zeros_like(params)
        params[0:21, :] = totals
        for f in range(2):
            for block in range(4):
                hidden_rows[f : f + 1, block * WIDE : (block + 1) * WIDE] = hidden_parts[f][block]
        keep_saved(params)

    def read_rows():
        rows_low[0:WORDS, :] = word_rows[...]
        rows_low[WORDS:ROWS, :] = region_rows[...]
        for at in range(0, ROWS, 128):
            transposed_into(rows_zero_t, rows_low[at : at + 128, :], at, 128)
        keep_saved(rows_zero_t)

    def transposed_into(target, values, at, count):
        target[:, pl.ds(at, count)] = values.T

    def project_into(source, at, count, module, mixed):
        for third, bias_row in enumerate((3 * module, None, 3 * module + 1)):
            product = matmul(source[pl.ds(at, count), :], inward_all[module, :, third * WIDE : (third + 1) * WIDE])
            if bias_row is not None:
                product = product + params[bias_row : bias_row + 1, :]
            mixed[pl.ds(at, count), third * WIDE : (third + 1) * WIDE] = product.astype(jnp.bfloat16)

    def join(at, weights, left, residual, bias_row, norm_at, norm_index):
        rows = pl.ds(at, 128)
        summed = residual + matmul(left[rows, :], weights) + params[bias_row : bias_row + 1, :]
        unit, scale = row_norm(summed)
        normed[norm_at, rows, :] = unit
        inverse[norm_at, rows, :] = jnp.broadcast_to(scale, (128, 128))
        return unit * params[16 + norm_index : 17 + norm_index, :] + params[9 + norm_index : 10 + norm_index, :]

    def cross_in():
        project_into(rows_low, 0, ROWS, 0, mixed_cross)
        keep_saved(mixed_cross)
        keep_weights(0, 0)

    def cross_words():
        allowed = down(word_ids[...]) == region_ids[...].astype(F32)
        attend_into(ATTEND_CROSS_WORD, mixed_cross, allowed, shares_cw, context)
        keep_saved(shares_cw)

    def cross_regions():
        allowed = down(region_ids[...]) == word_ids[...].astype(F32)
        attend_into(ATTEND_CROSS_REGION, mixed_cross, allowed, shares_cr, context)
        keep_saved(shares_cr)

    def cross_out():
        for at in range(0, ROWS, 128):
            one = join(at, outward_all[0], context, rows_low[at : at + 128, :].astype(F32), 2, 0, 0)
            stream[at : at + 128, :] = one
            one_low = one.astype(LOW)
            stream_low[at : at + 128, :] = one_low
            transposed_into(rows_one_t, one_low, at, 128)
            transposed_into(context_cross_t, context[at : at + 128, :], at, 128)
        keep_saved(rows_one_t, context_cross_t)
        keep_weights(1, 0)

    def word_in():
        project_into(stream_low, 0, WORDS, 1, mixed_self)
        keep_weights(0, 1)
        allowed = down(word_ids[...]) == word_ids[...].astype(F32)
        attend_into(ATTEND_WORD, mixed_self, allowed, shares_w, context)
        transposed_into(context_self_t, context[0:WORDS, :], 0, WORDS)
        keep_saved(shares_w)

    def region_in():
        project_into(stream_low, WORDS, REGIONS, 2, mixed_self)
        keep_weights(0, 2)

    def region_attend():
        allowed = down(region_ids[...]) == region_ids[...].astype(F32)
        attend_into(ATTEND_REGION, mixed_self, allowed, shares_r, context)
        for at in range(WORDS, ROWS, 128):
            transposed_into(context_self_t, context[at : at + 128, :], at, 128)
        keep_saved(shares_r)

    def self_out(module, first, last):
        for at in range(first, last, 128):
            two = join(at, outward_all[module], context, stream[at : at + 128, :], 3 * module + 2, 1, module)
            stream[at : at + 128, :] = two
            two_low = two.astype(LOW)
            stream_low[at : at + 128, :] = two_low
            transposed_into(rows_two_t, two_low, at, 128)
        keep_weights(1, module)

    def feed_in(f, first, last, column, columns):
        step = 256

        def tile(t, carry):
            at = pl.multiple_of(column + t * step, step)
            for row in range(first, last, 128):
                before = (
                    matmul(stream_low[row : row + 128, :], expand_all[f, :, pl.ds(at, step)])
                    + hidden_rows[f : f + 1, pl.ds(at, step)]
                )
                below = 0.5 * (1.0 + lax.erf(before * 0.5**0.5))
                value = (before * below).astype(jnp.bfloat16)
                density = jnp.exp(-0.5 * before * before) * 0.3989422804014327
                hidden[row : row + 128, pl.ds(at, step)] = value
                hidden_t[pl.ds(at, step), row : row + 128] = value.T
                slope[row : row + 128, pl.ds(at, step)] = (below + before * density).astype(jnp.bfloat16)
            return carry

        lax.fori_loop(0, columns // step, tile, 0)

    def feed_out(f, first, last):
        for at in range(first, last, 128):
            last_rows = join(at, shrink_all[f], hidden, stream[at : at + 128, :], 14 + f, 2, 3 + f)
            target, row = (word_result, at) if f == 0 else (region_result, at - WORDS)
            target[row : row + 128, :] = last_rows.astype(LOW)

    give_small()
    own(EXPAND_0)
    read_rows()
    pass_first(EXPAND_0)
    own(INWARD_0)
    own(OUTWARD_0)
    read_small()
    pass_second(EXPAND_0)
    pass_first(INWARD_0)
    own(EXPAND_1)
    pass_quarter(EXPAND_0, 0)
    pass_first(OUTWARD_0)
    own(INWARD_2)
    pass_second(INWARD_0)
    pass_quarter(EXPAND_0, 1)
    complete(INWARD_0)
    cross_in()
    pass_second(OUTWARD_0)
    cross_words()
    pass_first(EXPAND_1)
    own(OUTWARD_2)
    cross_regions()
    pass_second(EXPAND_1)
    complete(OUTWARD_0)
    pass_quarter(EXPAND_0, 2)
    cross_out()
    pass_first(INWARD_2)
    own(SHRINK_1)
    complete(EXPAND_0)
    keep_weights(2, 0)
    pass_quarter(EXPAND_1, 0)
    pass_first(OUTWARD_2)
    own(INWARD_1)
    pass_second(INWARD_2)
    complete(INWARD_2)
    region_in()
    pass_second(OUTWARD_2)
    pass_first(SHRINK_1)
    own(OUTWARD_1)
    region_attend()
    pass_quarter(EXPAND_1, 1)
    complete(OUTWARD_2)
    pass_second(SHRINK_1)
    self_out(2, WORDS, ROWS)
    pass_first(INWARD_1)
    own(SHRINK_0A)
    pass_quarter(EXPAND_1, 2)
    pass_first(OUTWARD_1)
    own(SHRINK_0B)
    pass_second(INWARD_1)
    complete(EXPAND_1)
    keep_weights(2, 1)
    complete(INWARD_1)
    word_in()
    keep_saved(mixed_self, context_self_t)
    pass_quarter(SHRINK_1, 0)
    pass_second(OUTWARD_1)
    feed_in(1, WORDS, ROWS, 0, 2 * WIDE)
    pass_first(SHRINK_0A)
    complete(OUTWARD_1)
    self_out(1, 0, WORDS)
    keep_saved(rows_two_t)
    feed_in(1, WORDS, ROWS, 2 * WIDE, 2 * WIDE)
    pass_quarter(SHRINK_1, 1)
    pass_second(SHRINK_0A)
    feed_in(0, 0, WORDS, 0, 2 * WIDE)
    pass_first(SHRINK_0B)
    feed_in(0, 0, WORDS, 2 * WIDE, 2 * WIDE)
    keep_saved(hidden_t, slope)
    pass_second(SHRINK_0B)
    complete(SHRINK_0A)
    pass_quarter(SHRINK_1, 2)
    complete(SHRINK_0B)
    keep_weights(3, 0)
    feed_out(0, 0, WORDS)
    complete(SHRINK_1)
    keep_weights(3, 1)
    feed_out(1, WORDS, ROWS)
    keep_saved(normed, inverse)
    for copied in keeps:
        copied.wait()
    for offset in range(1, 8):
        small_copy(offset, me).wait_send()
    for k in range(len(CHUNKS)):
        for kind in range(8):
            copy(k, kind).wait_send()
    for k in z_chunks:
        for way in range(2):
            for hop in range(3):

                @pl.when(goes(way, hop))
                def _(k=k, way=way, hop=hop):
                    for which in range(3):
                        z_copy(k, way, hop, which).wait_send()

                @pl.when(comes(way, hop))
                def _(k=k, way=way, hop=hop):
                    for which in range(3):
                        foreign_copy(k, way, hop, which).wait_send()


def forward(word_rows, region_rows, word_ids, region_ids, biases, gains, hidden_bias, shards):
    dma = pltpu.SemaphoreType.DMA
    vmem = pl.BlockSpec(memory_space=pltpu.VMEM)
    hbm = pl.BlockSpec(memory_space=pl.ANY)
    saved = [jax.ShapeDtypeStruct(*one) for one in SAVED]
    weights = [jax.ShapeDtypeStruct(one, LOW) for one in WEIGHTS]
    quarters = (sum(chunk[2] is None for chunk in CHUNKS), 2, 3, 3)
    outs = pl.pallas_call(
        forward_kernel,
        out_shape=[jax.ShapeDtypeStruct((WORDS, WIDE), LOW), jax.ShapeDtypeStruct((REGIONS, WIDE), LOW)] + saved + weights,
        in_specs=[vmem] * 7 + [hbm] * 4,
        out_specs=[vmem] * 2 + [hbm] * (len(saved) + len(weights)),
        scratch_shapes=[pltpu.VMEM(one.shape, one.dtype) for one in saved + weights]
        + [
            pltpu.VMEM((32, 128), F32),
            pltpu.VMEM((8, 32, 128), LOW),
            pltpu.VMEM((2, HIDDEN), F32),
            pltpu.VMEM((ROWS, WIDE), LOW),
            pltpu.VMEM((ROWS, WIDE), F32),
            pltpu.VMEM((ROWS, WIDE), LOW),
            pltpu.VMEM((ROWS, WIDE), LOW),
            pltpu.VMEM((ROWS, HIDDEN), LOW),
            dma((len(CHUNKS), 8)),
            dma((len(CHUNKS), 8)),
            dma(quarters),
            dma(quarters),
            dma(quarters),
            dma(quarters),
            dma((7,)),
            dma((7,)),
            dma((len(CHUNKS),)),
            dma((len(saved) + 10,)),
        ],
        compiler_params=pltpu.CompilerParams(
            collective_id=1, has_side_effects=True, vmem_limit_bytes=64 * 2**20 - 2**16
        ),
    )(word_rows, region_rows, word_ids, region_ids, biases, gains, hidden_bias, *shards)
    return outs[:2], outs[2 : 2 + len(saved)], outs[2 + len(saved) :]


WINDOW = 6

GROUPS = (
    (4, 0, 0, WORDS, True, (3, 0)),
    (4, 0, WORDS, REGIONS, True, (3, 1)),
    (4, 1, 0, WORDS, False, (2, 0)),
    (4, 1, WORDS, REGIONS, False, (2, 1)),
    (1, 2, 0, WORDS, False, (1, 1)),
    (1, 2, WORDS, REGIONS, False, (1, 2)),
    (3, 3, 0, WORDS, False, (0, 1)),
    (3, 3, WORDS, REGIONS, False, (0, 2)),
    (1, 4, 0, ROWS, False, (1, 0)),
    (3, 5, 0, ROWS, False, (0, 0)),
)
UNITS = sum(group[0] for group in GROUPS)

BLOCKS = (
    [(kind, f, c) for f in range(2) for c in range(4) for kind in (3, 2)]
    + [(1, 1, 0), (1, 2, 0)]
    + [(0, m, c) for m in (1, 2) for c in range(3)]
    + [(1, 0, 0)]
    + [(0, 0, c) for c in range(3)]
)


def attend_back_into(rows_of, mixed, shares, grad_context, grad_mixed, first_pair, last_pair):
    (query_at, query_count), (key_at, key_count) = rows_of
    query_rows, key_rows = pl.ds(query_at, query_count), pl.ds(key_at, key_count)

    def pair(p, carry):
        at = pl.multiple_of(p * PAIR_WIDE, PAIR_WIDE)
        at_query, at_key, at_value = (pl.ds(third * WIDE + at, PAIR_WIDE) for third in range(3))
        queries = mixed[query_rows, at_query]
        keys = mixed[key_rows, at_key]
        values = mixed[key_rows, at_value]
        grads = grad_context[query_rows, at_query]
        grad_queries = jnp.zeros((query_count, PAIR_WIDE), jnp.float32)
        grad_keys = jnp.zeros((key_count, PAIR_WIDE), jnp.float32)
        grad_values = jnp.zeros((key_count, PAIR_WIDE), jnp.float32)
        for side, chosen in enumerate(half_lanes()):
            share = shares[2 * p + side]
            grad_head = only(grads, chosen)
            wide = share.astype(jnp.float32)
            weighted = wide * dot_nt(grad_head, values)
            grad_scores = (weighted - wide * jnp.sum(weighted, axis=-1, keepdims=True)).astype(jnp.bfloat16)
            grad_values = grad_values + dot_tn(share, grad_head)
            grad_queries = grad_queries + matmul(grad_scores, only(keys, chosen))
            grad_keys = grad_keys + dot_tn(grad_scores, only(queries, chosen))
        score_scale = HEAD_DIM ** (-0.5)
        grad_mixed[query_rows, at_query] = (grad_queries * score_scale).astype(jnp.bfloat16)
        grad_mixed[key_rows, at_key] = (grad_keys * score_scale).astype(jnp.bfloat16)
        grad_mixed[key_rows, at_value] = grad_values.astype(jnp.bfloat16)
        return carry

    lax.fori_loop(first_pair, last_pair, pair, 0)


def backward_kernel(*refs):
    saved_hbm, weights = refs[:18], refs[18:22]
    word_gradient, region_gradient, small_out, *totals = refs[22:29]
    (
        params,
        word_cotangent,
        region_cotangent,
        normed,
        inverse,
        hidden_t,
        slope,
        rows_two_t,
        context_self_t,
        mixed_self,
        shares_w,
        shares_r,
        rows_one_t,
        context_cross_t,
        mixed_cross,
        shares_cw,
        shares_cr,
        rows_zero_t,
    ) = saved = refs[29:47]
    (
        window,
        end_feed,
        grad_before,
        end_self,
        grad_mixed_self,
        end_cross,
        grad_mixed_cross,
        stream,
        grad_context,
        row_sums,
        hidden_sums,
        out,
        acc,
        core_out,
        core_in,
        half_out,
        half_in,
        full_out,
        full_in,
        plane,
        end_out,
        end_in,
        mid_out,
        mid_in,
        small_in,
        small_in_plane,
        small_planes,
        saved_sems,
        window_sems,
        total_sems,
        core_send,
        core_recv,
        half_send,
        half_recv,
        full_send,
        full_recv,
        z_send,
        z_recv,
        small_send,
        small_recv,
        free,
    ) = refs[47:]
    lefts = (hidden_t, rows_two_t, context_self_t, rows_one_t, context_cross_t, rows_zero_t)
    rights = (end_feed, grad_before, end_self, grad_mixed_self, end_cross, grad_mixed_cross)
    me = lax.axis_index("fsdp")
    z = lax.axis_index("rep")
    chip = me // 2
    lane = me % 2
    is_end = jnp.logical_or(z == 0, z == 3)
    is_mid = jnp.logical_or(z == 1, z == 2)
    core_peer = {"fsdp": flip(me, 1)}
    links = ({"fsdp": flip(me, 2)}, {"fsdp": flip(me, 4)})
    link_chip = (flip(chip, 1), flip(chip, 2))
    diagonal = flip(chip, 3)
    pair_peer = {"rep": flip(z, 1)}
    mid_peer = {"rep": 3 - z}
    low = jnp.bfloat16

    def load_saved(index):
        return pltpu.make_async_copy(saved_hbm[index], saved[index], saved_sems.at[index])

    def load_block(n):
        kind, index, c = BLOCKS[n]
        part = slice(c * WIDE, (c + 1) * WIDE)
        source = weights[kind].at[index, part, :] if kind == 3 else weights[kind].at[index, :, part]
        return pltpu.make_async_copy(source, window.at[n % WINDOW], window_sems.at[n % WINDOW])

    def wait_saved(*names):
        for name in names:
            load_saved([ref is name for ref in saved].index(True)).wait()

    for index in range(7):
        load_saved(index).start()
    for n in range(WINDOW):
        load_block(n).start()
    for index in range(7, 18):
        load_saved(index).start()

    barrier = pltpu.get_barrier_semaphore()
    for offset in range(1, 8):
        pl.semaphore_signal(barrier, inc=1, device_id={"fsdp": flip(me, offset)}, device_id_type=MESH)
    for offset in range(1, 4):
        pl.semaphore_signal(barrier, inc=1, device_id={"rep": (z + offset) % 4}, device_id_type=MESH)
    pl.semaphore_wait(barrier, 10)

    def remote(src, dst, send_sem, recv_sem, peer):
        return pltpu.make_async_remote_copy(
            src_ref=src, dst_ref=dst, send_sem=send_sem, recv_sem=recv_sem, device_id=peer, device_id_type=MESH
        )

    def small_copy(offset):
        peer = flip(me, offset)
        return remote(
            small_in.at[peer],
            small_in_plane.at[offset - 1],
            small_send.at[offset - 1],
            small_recv.at[offset - 1],
            {"fsdp": peer},
        )

    def small_plane_copy(offset, source):
        peer = (z + offset) % 4 if source is z else source
        return remote(
            small_planes.at[source],
            small_planes.at[source],
            small_send.at[6 + offset],
            small_recv.at[6 + offset],
            {"rep": peer},
        )

    def core_copy(u):
        slot = u % SLOTS
        return remote(core_out.at[slot], core_in.at[slot], core_send.at[slot], core_recv.at[slot], core_peer)

    def half_copy(u, way):
        slot = u % SLOTS
        return remote(
            half_out.at[slot, way], half_in.at[slot, way], half_send.at[slot, way], half_recv.at[slot, way], links[way]
        )

    def full_copy(u, way):
        slot = u % SLOTS
        return remote(
            full_out.at[slot, way], full_in.at[slot, way], full_send.at[slot, way], full_recv.at[slot, way], links[way]
        )

    def end_copy(u):
        slot = u % SLOTS
        return remote(end_out.at[slot], end_in.at[slot], z_send.at[0, slot], z_recv.at[0, slot], pair_peer)

    def mid_copy(u):
        slot = u % SLOTS
        return remote(mid_out.at[slot], mid_in.at[slot], z_send.at[1, slot], z_recv.at[1, slot], mid_peer)

    def back_copy(u):
        slot = u % SLOTS
        return remote(out.at[u], out.at[u], z_send.at[2, slot], z_recv.at[2, slot], pair_peer)

    def credit(u, channel, peer):
        @pl.when(u + SLOTS < UNITS)
        def _():
            pl.semaphore_signal(free.at[channel], inc=1, device_id=peer, device_id_type=MESH)

    def spend(u, channel):
        @pl.when(u >= SLOTS)
        def _():
            pl.semaphore_wait(free.at[channel], 1)

    def per_group(u, function):
        first = 0
        for group in GROUPS:
            start, units = first, group[0]

            @pl.when(jnp.logical_and(u >= start, u < start + units))
            def _(start=start, group=group):
                function(u - start, *group[1:])

            first = first + units

    def produce(u):
        slot = u % SLOTS
        keep = u % ACC_SLOTS
        spend(u, 0)

        def products(at, side, first_row, count, by_row, matrix):
            rows = pl.ds(first_row, count)
            column = 0 if by_row else pl.multiple_of(at * WIDE, WIDE)
            right = rights[side][rows, pl.ds(column, WIDE)]

            def product(core):
                blocks = []
                for block in range(4):
                    owner = 2 * block + core
                    row = owner * (4 * UNIT) + at * UNIT if by_row else owner * UNIT
                    blocks.append(lefts[side][pl.ds(pl.multiple_of(row, 16), UNIT), rows])
                return matmul(jnp.concatenate(blocks, axis=0), right)

            other = product(1 - lane).astype(low)
            for block in range(4):
                core_out[slot, block] = other[block * UNIT : (block + 1) * UNIT]
            core_copy(u).start()
            own = product(lane)
            for block in range(4):
                acc[keep, block] = own[block * UNIT : (block + 1) * UNIT]

        per_group(u, products)

    def join_cores(u):
        slot = u % SLOTS
        keep = u % ACC_SLOTS
        core_copy(u).wait()
        for way in range(2):
            spend(u, 1 + way)
        summed = acc[keep, diagonal] + core_in[slot, diagonal].astype(jnp.float32)
        half_out[slot, 0] = summed[: UNIT // 2].astype(low)
        half_out[slot, 1] = summed[UNIT // 2 :].astype(low)
        for way in range(2):
            half_copy(u, way).start()
        for block in (link_chip[0], link_chip[1], chip):
            acc[keep, block] = acc[keep, block] + core_in[slot, block].astype(jnp.float32)
        credit(u, 0, core_peer)

    def join_diagonal(u):
        slot = u % SLOTS
        keep = u % ACC_SLOTS
        for way in range(2):
            half_copy(u, way).wait()
            spend(u, 3 + way)
        half = UNIT // 2
        full_out[slot, 1, :half] = (acc[keep, link_chip[1], :half] + half_in[slot, 0].astype(jnp.float32)).astype(low)
        full_out[slot, 1, half:] = acc[keep, link_chip[1], half:].astype(low)
        full_copy(u, 1).start()
        full_out[slot, 0, half:] = (acc[keep, link_chip[0], half:] + half_in[slot, 1].astype(jnp.float32)).astype(low)
        full_out[slot, 0, :half] = acc[keep, link_chip[0], :half].astype(low)
        full_copy(u, 0).start()
        for way in range(2):
            credit(u, 1 + way, links[way])

    def join_plane(u):
        slot = u % SLOTS
        keep = u % ACC_SLOTS
        for way in range(2):
            full_copy(u, way).wait()
        summed = acc[keep, chip] + (full_in[slot, 0].astype(jnp.float32) + full_in[slot, 1].astype(jnp.float32))

        @pl.when(is_end)
        def _():
            spend(u, 5)
            end_out[slot] = summed.astype(low)
            end_copy(u).start()

        @pl.when(is_mid)
        def _():
            plane[slot] = summed

        for way in range(2):
            credit(u, 3 + way, links[way])

    def join_pair(u):
        slot = u % SLOTS

        @pl.when(is_end)
        def _():
            end_copy(u).wait_send()

        @pl.when(is_mid)
        def _():
            end_copy(u).wait_recv()
            spend(u, 6)
            mid_out[slot] = (plane[slot] + end_in[slot].astype(jnp.float32)).astype(low)
            mid_copy(u).start()
            credit(u, 5, pair_peer)

    def join_middle(u):
        slot = u % SLOTS

        @pl.when(is_mid)
        def _():
            mid_copy(u).wait()
            out[u] = (mid_out[slot].astype(jnp.float32) + mid_in[slot].astype(jnp.float32)).astype(low)
            back_copy(u).start()
            credit(u, 6, mid_peer)

    def total_copy(u, at, by_row, matrix):
        kind, index = matrix
        if by_row:
            place = totals[kind].at[index, pl.ds(pl.multiple_of(at * UNIT, UNIT), UNIT), :]
        else:
            place = totals[kind].at[index, :, pl.ds(pl.multiple_of(at * WIDE, WIDE), WIDE)]
        return pltpu.make_async_copy(out.at[u], place, total_sems.at[u])

    def finish(u):
        @pl.when(is_mid)
        def _():
            back_copy(u).wait_send()

        @pl.when(is_end)
        def _():
            back_copy(u).wait_recv()

        per_group(u, lambda at, side, first_row, count, by_row, matrix: total_copy(u, at, by_row, matrix).start())

    stages = [
        (0, produce),
        (1, join_cores),
        (1 + LAG_A, join_diagonal),
        (1 + LAG_A + LAG_B, join_plane),
        (1 + LAG_A + LAG_B + LAG_Z, join_pair),
        (1 + LAG_A + LAG_B + 2 * LAG_Z, join_middle),
        (1 + LAG_A + LAG_B + 3 * LAG_Z, finish),
    ]

    row_tiles = ((0, 0), (1, 128), (1, 256))

    def add_row(index, values):
        row_sums[index : index + 1, :] += jnp.sum(values, axis=0, keepdims=True)

    def norm_back(grad, kind, norm_index, at, ends, end_bias):
        rows = slice(at, at + 128)
        unit = normed[kind, rows, :]
        grad_unit = grad * params[16 + norm_index : 17 + norm_index, :]
        summed = inverse[kind, rows, :1] * (
            grad_unit
            - jnp.mean(grad_unit, axis=-1, keepdims=True)
            - unit * jnp.mean(grad_unit * unit, axis=-1, keepdims=True)
        )
        add_row(16 + norm_index, grad * unit)
        add_row(9 + norm_index, grad)
        stream[rows, :] = summed
        summed_low = summed.astype(low)
        ends[rows, :] = summed_low
        add_row(end_bias, summed_low.astype(jnp.float32))

    def feed_norm():
        wait_saved(params, word_cotangent, region_cotangent, normed, inverse)
        row_sums[...] = jnp.zeros_like(row_sums)
        hidden_sums[...] = jnp.zeros_like(hidden_sums)
        for f, at in row_tiles:
            cotangent = word_cotangent if f == 0 else region_cotangent
            first = at if f == 0 else at - WORDS
            norm_back(cotangent[first : first + 128, :].astype(jnp.float32), 2, 3 + f, at, end_feed, 14 + f)

    def next_block(n):
        if n + WINDOW < len(BLOCKS):
            load_block(n + WINDOW).start()

    def feed_back(f, c):
        n = 2 * (4 * f + c)
        load_block(n).wait()
        load_block(n + 1).wait()
        columns = slice(c * WIDE, (c + 1) * WIDE)
        for which, at in row_tiles:
            if which == f:
                rows = slice(at, at + 128)
                grad_hidden = dot_nt(end_feed[rows, :], window[n % WINDOW])
                before = (grad_hidden * slope[rows, columns].astype(jnp.float32)).astype(low)
                grad_before[rows, columns] = before
                row = 4 * f + c
                hidden_sums[row : row + 1, :] += jnp.sum(before.astype(jnp.float32), axis=0, keepdims=True)
                stream[rows, :] += dot_nt(before, window[(n + 1) % WINDOW])
        next_block(n)
        next_block(n + 1)

    def self_norm():
        for f, at in row_tiles:
            norm_back(stream[at : at + 128, :], 1, 1 + f, at, end_self, 5 + 3 * f)

    def self_context():
        for f in range(2):
            n = 16 + f
            load_block(n).wait()
            for which, at in row_tiles:
                if which == f:
                    grad_context[at : at + 128, :] = dot_nt(end_self[at : at + 128, :], window[n % WINDOW]).astype(low)
            next_block(n)

    def project_back(n, module, grad_mixed, tiles):
        for c in range(3):
            load_block(n + c).wait()
            columns = slice(c * WIDE, (c + 1) * WIDE)
            for at in tiles:
                part = grad_mixed[at : at + 128, columns]
                if c != 1:
                    add_row(3 * module + c // 2, part.astype(jnp.float32))
                stream[at : at + 128, :] += dot_nt(part, window[(n + c) % WINDOW])
            next_block(n + c)

    def cross_norm():
        for _, at in row_tiles:
            norm_back(stream[at : at + 128, :], 0, 0, at, end_cross, 2)

    def cross_context():
        n = 24
        load_block(n).wait()
        for _, at in row_tiles:
            grad_context[at : at + 128, :] = dot_nt(end_cross[at : at + 128, :], window[n % WINDOW]).astype(low)
        next_block(n)

    def give_rows():
        word_gradient[...] = stream[0:WORDS, :]
        region_gradient[...] = stream[WORDS:ROWS, :]

    def exact_nt(left, right):
        return lax.dot_general(
            left,
            right.astype(jnp.float32),
            (((1,), (1,)), ((), ())),
            precision=lax.Precision.HIGHEST,
            preferred_element_type=jnp.float32,
        )

    def give_small():
        small_in[...] = jnp.zeros_like(small_in)
        for owner in range(8):
            small_in[owner, 0:21, :] = exact_nt(row_sums[...], spread(owner))[:21]
        for place in range(8):
            placed = exact_nt(hidden_sums[...], spread(place))
            for f in range(2):
                for c in range(4):
                    row = 21 + 4 * f + place % 4
                    small_in[2 * c + place // 4, row : row + 1, :] = placed[4 * f + c : 4 * f + c + 1]
        for offset in range(1, 8):
            small_copy(offset).start()

    def join_small():
        summed = small_in[me]
        for offset in range(1, 8):
            small_copy(offset).wait()
            summed = summed + small_in_plane[offset - 1]
        small_planes[z] = summed
        for offset in range(1, 4):
            small_plane_copy(offset, z).start()

    def finish_small():
        for offset in range(1, 4):
            small_plane_copy(offset, z).wait_send()
            small_plane_copy(offset, (z + 4 - offset) % 4).wait_recv()
        small_out[...] = small_planes[0] + small_planes[1] + (small_planes[2] + small_planes[3])

    def self_back(rows_of, shares, first, last):
        attend_back_into(rows_of, mixed_self, shares, grad_context, grad_mixed_self, first, last)

    def cross_back(rows_of, shares, first, last):
        attend_back_into(rows_of, mixed_cross, shares, grad_context, grad_mixed_cross, first, last)

    pieces = {
        0: lambda: (wait_saved(slope), feed_back(0, 0)),
        1: lambda: feed_back(0, 1),
        2: lambda: feed_back(0, 2),
        3: lambda: feed_back(0, 3),
        4: lambda: feed_back(1, 0),
        5: lambda: feed_back(1, 1),
        6: lambda: feed_back(1, 2),
        7: lambda: (feed_back(1, 3), wait_saved(rows_two_t)),
        8: self_norm,
        9: lambda: (self_context(), wait_saved(context_self_t, mixed_self, shares_w)),
        10: lambda: (self_back(ATTEND_WORD, shares_w, 0, 6), wait_saved(shares_r, rows_one_t)),
        11: lambda: self_back(ATTEND_REGION, shares_r, 0, 2),
        12: lambda: self_back(ATTEND_REGION, shares_r, 2, 4),
        13: lambda: self_back(ATTEND_REGION, shares_r, 4, 6),
        14: lambda: project_back(18, 1, grad_mixed_self, (0,)),
        15: lambda: project_back(21, 2, grad_mixed_self, (128, 256)),
        16: lambda: (cross_norm(), wait_saved(context_cross_t, mixed_cross, shares_cw, shares_cr, rows_zero_t)),
        17: cross_context,
        18: lambda: cross_back(ATTEND_CROSS_WORD, shares_cw, 0, 3),
        19: lambda: cross_back(ATTEND_CROSS_WORD, shares_cw, 3, 6),
        20: lambda: cross_back(ATTEND_CROSS_REGION, shares_cr, 0, 3),
        21: lambda: cross_back(ATTEND_CROSS_REGION, shares_cr, 3, 6),
        22: lambda: (project_back(25, 0, grad_mixed_cross, (0, 128, 256)), give_rows()),
        23: give_small,
        25: join_small,
        27: finish_small,
    }

    feed_norm()

    def step(i, carry):
        for lag, stage in reversed(stages):
            if stage is produce:

                @pl.when(i == 0)
                def _():
                    wait_saved(hidden_t)

            @pl.when(jnp.logical_and(i >= lag, i < UNITS + lag))
            def _(lag=lag, stage=stage):
                stage(i - lag)

        for at, piece in pieces.items():

            @pl.when(i == at)
            def _(piece=piece):
                piece()

        return carry

    lax.fori_loop(0, UNITS + stages[-1][0], step, 0)

    def settle(u, carry):
        per_group(u, lambda at, side, first_row, count, by_row, matrix: total_copy(u, at, by_row, matrix).wait())
        return carry

    lax.fori_loop(0, UNITS, settle, 0)


def backward(saved, weights):
    block = (UNIT, WIDE)
    low, f32 = jnp.bfloat16, jnp.float32
    dma = pltpu.SemaphoreType.DMA
    vmem = pl.BlockSpec(memory_space=pltpu.VMEM)
    hbm = pl.BlockSpec(memory_space=pl.ANY)
    shape = jax.ShapeDtypeStruct
    small = (32, 128)
    return pl.pallas_call(
        backward_kernel,
        out_shape=(
            shape((WORDS, WIDE), f32),
            shape((REGIONS, WIDE), f32),
            shape(small, f32),
            shape((3, UNIT, 3 * WIDE), low),
            shape((3, UNIT, WIDE), low),
            shape((2, UNIT, HIDDEN), low),
            shape((2, 4 * UNIT, WIDE), low),
        ),
        in_specs=[hbm] * (len(saved) + len(weights)),
        out_specs=[vmem] * 3 + [hbm] * 4,
        scratch_shapes=[pltpu.VMEM(array.shape, array.dtype) for array in saved]
        + [
            pltpu.VMEM((WINDOW, WIDE, WIDE), low),
            pltpu.VMEM((ROWS, WIDE), low),
            pltpu.VMEM((ROWS, HIDDEN), low),
            pltpu.VMEM((ROWS, WIDE), low),
            pltpu.VMEM((ROWS, 3 * WIDE), low),
            pltpu.VMEM((ROWS, WIDE), low),
            pltpu.VMEM((ROWS, 3 * WIDE), low),
            pltpu.VMEM((ROWS, WIDE), f32),
            pltpu.VMEM((ROWS, WIDE), low),
            pltpu.VMEM((24, WIDE), f32),
            pltpu.VMEM((8, WIDE), f32),
            pltpu.VMEM((UNITS,) + block, low),
            pltpu.VMEM((ACC_SLOTS, 4) + block, f32),
            pltpu.VMEM((SLOTS, 4) + block, low),
            pltpu.VMEM((SLOTS, 4) + block, low),
            pltpu.VMEM((SLOTS, 2, UNIT // 2, WIDE), low),
            pltpu.VMEM((SLOTS, 2, UNIT // 2, WIDE), low),
            pltpu.VMEM((SLOTS, 2) + block, low),
            pltpu.VMEM((SLOTS, 2) + block, low),
            pltpu.VMEM((SLOTS,) + block, f32),
            pltpu.VMEM((SLOTS,) + block, low),
            pltpu.VMEM((SLOTS,) + block, low),
            pltpu.VMEM((SLOTS,) + block, low),
            pltpu.VMEM((SLOTS,) + block, low),
            pltpu.VMEM((8,) + small, f32),
            pltpu.VMEM((7,) + small, f32),
            pltpu.VMEM((4,) + small, f32),
            dma((18,)),
            dma((WINDOW,)),
            dma((UNITS,)),
            dma((SLOTS,)),
            dma((SLOTS,)),
            dma((SLOTS, 2)),
            dma((SLOTS, 2)),
            dma((SLOTS, 2)),
            dma((SLOTS, 2)),
            dma((3, SLOTS)),
            dma((3, SLOTS)),
            dma((10,)),
            dma((10,)),
            pltpu.SemaphoreType.REGULAR((7,)),
        ],
        compiler_params=pltpu.CompilerParams(
            collective_id=0, has_side_effects=True, vmem_limit_bytes=64 * 2**20 - 2**16
        ),
    )(*saved, *weights)


def deliver_kernel(*refs):
    moved, small, totals = refs[:4], refs[4], refs[5:9]
    moved_out, bias_out, gain_out, hidden_out, totals_out = refs[9:13], refs[13], refs[14], refs[15], refs[16:20]
    narrow, wide, held = refs[20:24], refs[24:28], refs[28:32]
    take_sems, give_sems, load_sems, store_sems = refs[32:]
    takes = [pltpu.make_async_copy(moved[i], held[i], take_sems.at[i]) for i in range(4)]
    gives = [pltpu.make_async_copy(held[i], moved_out[i], give_sems.at[i]) for i in range(4)]
    loads = [pltpu.make_async_copy(totals[i], narrow[i], load_sems.at[i]) for i in range(4)]
    stores = [pltpu.make_async_copy(wide[i], totals_out[i], store_sems.at[i]) for i in range(4)]
    for one in loads + takes:
        one.start()
    bias_out[...] = small[0:16, 0:UNIT]
    gain_out[...] = small[16:21, 0:UNIT]
    source = lax.broadcasted_iota(jnp.int32, (128, 4 * UNIT), 0)
    target = lax.broadcasted_iota(jnp.int32, (128, 4 * UNIT), 1)
    for f in range(2):
        row = jnp.zeros((1, 4 * UNIT), F32)
        for q in range(4):
            chosen = jnp.logical_and(source < UNIT, target == source + q * UNIT).astype(F32)
            line = 21 + 4 * f + q
            row = row + jnp.dot(
                small[line : line + 1, :], chosen, precision=lax.Precision.HIGHEST, preferred_element_type=F32
            )
        hidden_out[f : f + 1, :] = row
    for i in range(4):
        loads[i].wait()
        wide[i][...] = narrow[i][...].astype(F32)
        stores[i].start()
        takes[i].wait()
        gives[i].start()
    for one in gives + stores:
        one.wait()


def deliver(moved, small, totals):
    vmem = pl.BlockSpec(memory_space=pltpu.VMEM)
    hbm = pl.BlockSpec(memory_space=pl.ANY)
    shape = jax.ShapeDtypeStruct
    widened = [shape(total.shape, F32) for total in totals]
    sem = pltpu.SemaphoreType.DMA((4,))
    return pl.pallas_call(
        deliver_kernel,
        out_shape=[shape(one.shape, one.dtype) for one in moved]
        + [shape((16, UNIT), F32), shape((5, UNIT), F32), shape((2, 4 * UNIT), F32)]
        + widened,
        in_specs=[hbm] * 4 + [vmem] + [hbm] * 4,
        out_specs=[hbm] * 4 + [vmem] * 3 + [hbm] * 4,
        scratch_shapes=[pltpu.VMEM(one.shape, one.dtype) for one in totals]
        + [pltpu.VMEM(one.shape, F32) for one in totals]
        + [pltpu.VMEM(one.shape, one.dtype) for one in moved]
        + [sem, sem, sem, sem],
        compiler_params=pltpu.CompilerParams(vmem_limit_bytes=64 * 2**20 - 2**16),
    )(*moved, small, *totals)


def paired(
    word_rows,
    region_rows,
    word_segment,
    region_segment,
    inward,
    outward,
    biases,
    norm_gain,
    expand_weight,
    shrink_weight,
    hidden_bias,
    word_cotangent,
    region_cotangent,
):
    results, saved, weights = forward(
        word_rows,
        region_rows,
        word_segment,
        region_segment,
        biases,
        norm_gain,
        hidden_bias,
        (inward, outward, expand_weight, shrink_weight),
    )
    word_gradient, region_gradient, small, *totals = backward(
        (saved[0], word_cotangent, region_cotangent, *saved[1:]), weights
    )
    word_out, region_out, word_gradient, region_gradient, bias, gain, hidden, *totals = deliver(
        (*results, word_gradient, region_gradient), small, totals
    )
    inward_total, outward_total, expand_total, shrink_total = totals
    return (
        word_out,
        region_out,
        word_gradient,
        region_gradient,
        inward_total,
        outward_total,
        bias,
        gain,
        expand_total,
        shrink_total,
        hidden,
    )


def general(
    devices,
    word_rows,
    region_rows,
    word_segment,
    region_segment,
    inward,
    outward,
    biases,
    norm_gain,
    expand_weight,
    shrink_weight,
    hidden_bias,
    word_cotangent,
    region_cotangent,
):
    words_count = word_rows.shape[0]
    width = word_rows.shape[1]
    word_ids = word_segment[0]
    region_ids = region_segment[0]
    cross_mask = word_ids[:, None] == region_ids[None, :]
    word_mask = word_ids[:, None] == word_ids[None, :]
    region_mask = region_ids[:, None] == region_ids[None, :]
    shard = biases.shape[1]
    per_shard = hidden_bias.shape[1] // shard
    small_shard = jnp.concatenate([biases, norm_gain, hidden_bias.reshape(2 * per_shard, shard)], axis=0)
    small_all = lax.all_gather(small_shard, "fsdp", axis=0)
    bias_count = biases.shape[0]
    gain_count = norm_gain.shape[0]
    row_params = small_all[:, : bias_count + gain_count].transpose(1, 0, 2).reshape(bias_count + gain_count, width)
    hidden_all = (
        small_all[:, bias_count + gain_count :]
        .reshape(devices, 2, per_shard * shard)
        .transpose(1, 0, 2)
        .reshape(2, devices * per_shard * shard)
    )
    inward_all, outward_all = (
        lax.all_gather(inward, "fsdp", axis=1, tiled=True),
        lax.all_gather(outward, "fsdp", axis=1, tiled=True),
    )
    attend_set = (
        inward_all,
        outward_all,
        row_params[:bias_count].astype(jnp.float32),
        row_params[bias_count:].astype(jnp.float32),
    )
    crossed, cross_kept = cross_forward(word_rows, region_rows, attend_set, cross_mask)
    word_one, word_kept = self_forward(crossed[:words_count], attend_set, 1, word_mask)
    region_one, region_kept = self_forward(crossed[words_count:], attend_set, 2, region_mask)
    expand_all, shrink_all = (
        lax.all_gather(expand_weight, "fsdp", axis=1, tiled=True),
        lax.all_gather(shrink_weight, "fsdp", axis=1, tiled=True),
    )
    feed_set = (expand_all, shrink_all, hidden_all)
    word_two, word_feed = feed_forward(word_one, feed_set, 0, attend_set)
    region_two, region_feed = feed_forward(region_one, feed_set, 1, attend_set)
    word_back = feed_backward(word_cotangent.astype(jnp.float32), word_feed, feed_set, 0, attend_set[3])
    region_back = feed_backward(region_cotangent.astype(jnp.float32), region_feed, feed_set, 1, attend_set[3])
    word_self = self_backward(word_back[0], word_kept, attend_set, 1, word_mask)
    region_self = self_backward(region_back[0], region_kept, attend_set, 2, region_mask)
    grad_crossed = jnp.concatenate([word_self[0], region_self[0]], axis=0)
    cross_back = cross_backward(grad_crossed, cross_kept, attend_set, cross_mask, words_count)
    row_grads = jnp.stack(
        [
            cross_back[3][0],
            cross_back[3][1],
            cross_back[3][2],
            word_self[3][0],
            word_self[3][1],
            word_self[3][2],
            region_self[3][0],
            region_self[3][1],
            region_self[3][2],
            cross_back[5],
            word_self[5],
            region_self[5],
            word_back[6],
            region_back[6],
            word_back[4],
            region_back[4],
            cross_back[4],
            word_self[4],
            region_self[4],
            word_back[5],
            region_back[5],
        ]
    )
    hidden_grads = jnp.stack([word_back[3], region_back[3]])
    small_grads = jnp.concatenate(
        [
            row_grads.reshape(bias_count + gain_count, devices, shard).transpose(1, 0, 2),
            hidden_grads.reshape(2, devices, per_shard, shard)
            .transpose(1, 0, 2, 3)
            .reshape(devices, 2 * per_shard, shard),
        ],
        axis=1,
    )

    def reduced(products, axis):
        mine = lax.psum_scatter(jnp.stack(products), "fsdp", scatter_dimension=axis, tiled=True)
        return lax.psum(mine.astype(jnp.bfloat16), "rep").astype(jnp.float32)

    shrink_total = reduced([matmul_tn(*word_back[2]), matmul_tn(*region_back[2])], 1)
    expand_total = reduced([matmul_tn(*word_back[1]), matmul_tn(*region_back[1])], 1)
    outward_total = reduced([matmul_tn(*cross_back[2]), matmul_tn(*word_self[2]), matmul_tn(*region_self[2])], 1)
    inward_total = reduced([matmul_tn(*cross_back[1]), matmul_tn(*word_self[1]), matmul_tn(*region_self[1])], 1)
    small_total = lax.psum(lax.psum_scatter(small_grads, "fsdp", scatter_dimension=0, tiled=False), "rep")
    grad_rows = cross_back[0]
    return (
        word_two.astype(jnp.bfloat16),
        region_two.astype(jnp.bfloat16),
        grad_rows[:words_count],
        grad_rows[words_count:],
        inward_total,
        outward_total,
        small_total[:bias_count],
        small_total[bias_count : bias_count + gain_count],
        expand_total,
        shrink_total,
        small_total[bias_count + gain_count :].reshape(2, per_shard * shard),
    )


def solution(mesh):
    sizes = (mesh.shape["rep"], mesh.shape["fsdp"])
    return jax.shard_map(
        paired if sizes == (4, 8) else functools.partial(general, mesh.shape["fsdp"]),
        mesh=mesh,
        in_specs=(
            P(("rep", "fsdp"), None),
            P(("rep", "fsdp"), None),
            P(("rep", "fsdp"), None),
            P(("rep", "fsdp"), None),
            P(None, "fsdp", None),
            P(None, "fsdp", None),
            P(None, "fsdp"),
            P(None, "fsdp"),
            P(None, "fsdp", None),
            P(None, "fsdp", None),
            P(None, "fsdp"),
            P(("rep", "fsdp"), None),
            P(("rep", "fsdp"), None),
        ),
        out_specs=(
            P(("rep", "fsdp"), None),
            P(("rep", "fsdp"), None),
            P(("rep", "fsdp"), None),
            P(("rep", "fsdp"), None),
            P(None, "fsdp", None),
            P(None, "fsdp", None),
            P(None, "fsdp"),
            P(None, "fsdp"),
            P(None, "fsdp", None),
            P(None, "fsdp", None),
            P(None, "fsdp"),
        ),
        check_vma=False,
    )
```

```python
import functools

import jax
import jax.numpy as jnp
from jax import lax
from jax.experimental import pallas as pl
from jax.experimental.pallas import tpu as pltpu
from jax.sharding import PartitionSpec as P

MESH = pl.DeviceIdType.MESH

HEADS = 12
HEAD_DIM = 64


norm_epsilon = 1e-12
masked_score = -1e30


def matmul(left_op, right_op):
    return jnp.dot(left_op, right_op, preferred_element_type=jnp.float32)


def matmul_tn(left_op, right_op):
    return lax.dot_general(
        left_op, right_op, (((0,), (0,)), ((), ())), preferred_element_type=jnp.float32
    )


def matmul_nt(left_op, right_op):
    return lax.dot_general(
        left_op, right_op, (((1,), (1,)), ((), ())), preferred_element_type=jnp.float32
    )


def column_sums(values):
    return jnp.sum(values, axis=0, dtype=jnp.float32)


def heads_of(rows_in):
    return rows_in.reshape(rows_in.shape[0], HEADS, HEAD_DIM)


def merge_heads(head_rows):
    return head_rows.reshape(head_rows.shape[0], -1)


def normalize(summed, gain_row, shift_row):
    center = summed - jnp.mean(summed, axis=-1, keepdims=True)
    inverse = lax.rsqrt(jnp.mean(center * center, axis=-1, keepdims=True) + norm_epsilon)
    normed = center * inverse
    return (normed * gain_row + shift_row, (normed, inverse))


def normalize_back(grad_out, norm_stats, gain_row):
    normed, inverse = norm_stats
    grad_normed = grad_out * gain_row
    grad_sum = inverse * (
        grad_normed
        - jnp.mean(grad_normed, axis=-1, keepdims=True)
        - normed * jnp.mean(grad_normed * normed, axis=-1, keepdims=True)
    )
    return (grad_sum, column_sums(grad_out * normed), column_sums(grad_out))


def score_block(queries, key_rows, allowed):
    scores = jnp.einsum(
        "qhd,khd->hqk", heads_of(queries), heads_of(key_rows), preferred_element_type=jnp.float32
    ) * HEAD_DIM ** (-0.5)
    return jnp.where(allowed[None], scores, masked_score)


def attend(queries, key_rows, value_rows, allowed):
    scores = score_block(queries, key_rows, allowed)
    top_score = jnp.max(scores, axis=-1, keepdims=True)
    log_total = top_score + jnp.log(jnp.sum(jnp.exp(scores - top_score), axis=-1, keepdims=True))
    shares = jnp.exp(scores - log_total).astype(jnp.bfloat16)
    context = jnp.einsum(
        "hqk,khd->qhd", shares, heads_of(value_rows), preferred_element_type=jnp.float32
    )
    return (merge_heads(context).astype(jnp.bfloat16), log_total)


def attend_back(queries, key_rows, value_rows, allowed, log_total, grad_context):
    shares = jnp.exp(score_block(queries, key_rows, allowed) - log_total)
    grad_heads = heads_of(grad_context)
    grad_shares = jnp.einsum(
        "qhd,khd->hqk", grad_heads, heads_of(value_rows), preferred_element_type=jnp.float32
    )
    grad_values = jnp.einsum(
        "hqk,qhd->khd", shares.astype(jnp.bfloat16), grad_heads, preferred_element_type=jnp.float32
    )
    grad_scores = (
        shares * (grad_shares - jnp.sum(shares * grad_shares, axis=-1, keepdims=True))
    ).astype(jnp.bfloat16)
    score_scale = HEAD_DIM ** (-0.5)
    grad_queries = (
        jnp.einsum(
            "hqk,khd->qhd", grad_scores, heads_of(key_rows), preferred_element_type=jnp.float32
        )
        * score_scale
    )
    grad_keys = (
        jnp.einsum(
            "hqk,qhd->khd", grad_scores, heads_of(queries), preferred_element_type=jnp.float32
        )
        * score_scale
    )
    return (merge_heads(grad_queries), merge_heads(grad_keys), merge_heads(grad_values))


def project(rows_low, weight, bias_rows, module):
    width = weight.shape[0]
    bias_all = jnp.concatenate(
        [bias_rows[3 * module], jnp.zeros((width,), jnp.float32), bias_rows[3 * module + 1]]
    )
    return (matmul(rows_low, weight) + bias_all).astype(jnp.bfloat16)


def project_back(grad_sum, grad_parts, rows_low, weight):
    width = weight.shape[0]
    grad_mixed = jnp.concatenate(grad_parts, axis=1).astype(jnp.bfloat16)
    grad_weight = (rows_low, grad_mixed)
    grad_bias = column_sums(grad_mixed)
    grad_rows = grad_sum + matmul_nt(grad_mixed, weight)
    return (grad_rows, grad_weight, grad_bias[:width], grad_bias[2 * width :])


def branch_back(grad_out, context, norm_stats, gain_row, outward_one):
    grad_sum, grad_gain, grad_shift = normalize_back(grad_out, norm_stats, gain_row)
    grad_branch = grad_sum.astype(jnp.bfloat16)
    grad_outward = (context, grad_branch)
    grad_context = matmul_nt(grad_branch, outward_one).astype(jnp.bfloat16)
    return (grad_sum, grad_context, grad_outward, column_sums(grad_branch), grad_gain, grad_shift)


def self_forward(rows_in, weights, module, allowed):
    inward_all, outward_all, bias_rows, gain_rows = weights
    width = rows_in.shape[1]
    rows_low = rows_in.astype(jnp.bfloat16)
    mixed = project(rows_low, inward_all[module], bias_rows, module)
    context, log_total = attend(
        mixed[:, :width], mixed[:, width : 2 * width], mixed[:, 2 * width :], allowed
    )
    summed = rows_in + matmul(context, outward_all[module]) + bias_rows[3 * module + 2]
    result, norm_stats = normalize(summed, gain_rows[module], bias_rows[9 + module])
    return (result, (rows_low, mixed, context, log_total, norm_stats))


def self_backward(grad_out, kept, weights, module, allowed):
    inward_all, outward_all, bias_rows, gain_rows = weights
    rows_low, mixed, context, log_total, norm_stats = kept
    width = rows_low.shape[1]
    grad_sum, grad_context, grad_outward, grad_bias_out, grad_gain, grad_shift = branch_back(
        grad_out, context, norm_stats, gain_rows[module], outward_all[module]
    )
    grad_parts = attend_back(
        mixed[:, :width],
        mixed[:, width : 2 * width],
        mixed[:, 2 * width :],
        allowed,
        log_total,
        grad_context,
    )
    grad_rows, grad_inward, grad_bias_query, grad_bias_value = project_back(
        grad_sum, grad_parts, rows_low, inward_all[module]
    )
    return (
        grad_rows,
        grad_inward,
        grad_outward,
        (grad_bias_query, grad_bias_value, grad_bias_out),
        grad_gain,
        grad_shift,
    )


def cross_forward(word_rows, region_rows, weights, cross_mask):
    inward_all, outward_all, bias_rows, gain_rows = weights
    words_count = word_rows.shape[0]
    width = word_rows.shape[1]
    rows_low = jnp.concatenate([word_rows, region_rows], axis=0)
    mixed = project(rows_low, inward_all[0], bias_rows, 0)
    word_mix = mixed[:words_count]
    region_mix = mixed[words_count:]
    word_context, word_total = attend(
        word_mix[:, :width],
        region_mix[:, width : 2 * width],
        region_mix[:, 2 * width :],
        cross_mask,
    )
    region_context, region_total = attend(
        region_mix[:, :width],
        word_mix[:, width : 2 * width],
        word_mix[:, 2 * width :],
        cross_mask.T,
    )
    context = jnp.concatenate([word_context, region_context], axis=0)
    summed = rows_low.astype(jnp.float32) + matmul(context, outward_all[0]) + bias_rows[2]
    result, norm_stats = normalize(summed, gain_rows[0], bias_rows[9])
    return (result, (rows_low, mixed, context, word_total, region_total, norm_stats))


def cross_backward(grad_out, kept, weights, cross_mask, words_count):
    inward_all, outward_all, bias_rows, gain_rows = weights
    rows_low, mixed, context, word_total, region_total, norm_stats = kept
    width = rows_low.shape[1]
    grad_sum, grad_context, grad_outward, grad_bias_out, grad_gain, grad_shift = branch_back(
        grad_out, context, norm_stats, gain_rows[0], outward_all[0]
    )
    word_mix = mixed[:words_count]
    region_mix = mixed[words_count:]
    word_query_grad, region_key_grad, region_value_grad = attend_back(
        word_mix[:, :width],
        region_mix[:, width : 2 * width],
        region_mix[:, 2 * width :],
        cross_mask,
        word_total,
        grad_context[:words_count],
    )
    region_query_grad, word_key_grad, word_value_grad = attend_back(
        region_mix[:, :width],
        word_mix[:, width : 2 * width],
        word_mix[:, 2 * width :],
        cross_mask.T,
        region_total,
        grad_context[words_count:],
    )
    grad_parts = (
        jnp.concatenate([word_query_grad, region_query_grad], axis=0),
        jnp.concatenate([word_key_grad, region_key_grad], axis=0),
        jnp.concatenate([word_value_grad, region_value_grad], axis=0),
    )
    grad_rows, grad_inward, grad_bias_query, grad_bias_value = project_back(
        grad_sum, grad_parts, rows_low, inward_all[0]
    )
    return (
        grad_rows,
        grad_inward,
        grad_outward,
        (grad_bias_query, grad_bias_value, grad_bias_out),
        grad_gain,
        grad_shift,
    )


def gelu_exact(values):
    return jax.nn.gelu(values, approximate=False)


def feed_forward(rows_in, weights, feed_index, attend_set):
    expand_all, shrink_all, hidden_all = weights
    bias_rows, gain_rows = (attend_set[2], attend_set[3])
    rows_low = rows_in.astype(jnp.bfloat16)
    before = matmul(rows_low, expand_all[feed_index]) + hidden_all[feed_index].astype(jnp.float32)
    hidden = gelu_exact(before).astype(jnp.bfloat16)
    summed = rows_in + matmul(hidden, shrink_all[feed_index]) + bias_rows[14 + feed_index]
    result, norm_stats = normalize(summed, gain_rows[3 + feed_index], bias_rows[12 + feed_index])
    return (result, (rows_low, before, hidden, norm_stats))


def feed_backward(grad_out, kept, weights, feed_index, gain_rows):
    expand_all, shrink_all, hidden_all = weights
    rows_low, before, hidden, norm_stats = kept
    grad_sum, grad_gain, grad_shift = normalize_back(
        grad_out, norm_stats, gain_rows[3 + feed_index]
    )
    grad_branch = grad_sum.astype(jnp.bfloat16)
    grad_shrink = (hidden, grad_branch)
    grad_hidden = matmul_nt(grad_branch, shrink_all[feed_index])
    unused_value, slope_back = jax.vjp(gelu_exact, before)
    grad_before = slope_back(grad_hidden)[0].astype(jnp.bfloat16)
    grad_expand = (rows_low, grad_before)
    grad_rows = grad_sum + matmul_nt(grad_before, expand_all[feed_index])
    return (
        grad_rows,
        grad_expand,
        grad_shrink,
        column_sums(grad_before),
        column_sums(grad_branch),
        grad_gain,
        grad_shift,
    )


UNIT = 96
WIDE = 768
SLOTS = 6
ACC_SLOTS = 9
LAG_CORE = 2
LAG_A = 3
LAG_B = 3
LAG_Z = 3
OWNED_SHRINK_AT = 5
OWNED_EXPAND_AT = 10
WORDS = 128
REGIONS = 256
ROWS = 384
HIDDEN = 3072
SLICE = HIDDEN // 8
PLANE_WORDS = 8 * WORDS
PAIRS_OF_HEADS = 6
PAIR_WIDE = 128
LOW, F32 = jnp.bfloat16, jnp.float32

X, Y, DIAG_Y, DIAG_X, CORE_OWN, CORE_X, CORE_Y, CORE_DIAG = range(8)


def flip(position, bits):
    return lax.bitwise_xor(position, bits)


def remote(src, dst, send_sem, recv_sem, peer):
    return pltpu.make_async_remote_copy(
        src_ref=src, dst_ref=dst, send_sem=send_sem, recv_sem=recv_sem, device_id=peer, device_id_type=MESH
    )


def greet(me, z):
    barrier = pltpu.get_barrier_semaphore()
    for offset in range(1, 8):
        pl.semaphore_signal(barrier, inc=1, device_id={"fsdp": flip(me, offset)}, device_id_type=MESH)
    for offset in range(1, 4):
        pl.semaphore_signal(barrier, inc=1, device_id={"rep": (z + offset) % 4}, device_id_type=MESH)
    pl.semaphore_wait(barrier, 10)


def route(me, kind, arriving):
    owner, half, step = {
        X: (2 if arriving else 0, None, 2),
        Y: (4 if arriving else 0, None, 4),
        DIAG_Y: (6 if arriving else 2, 0, 4),
        DIAG_X: (6 if arriving else 4, 1, 2),
        CORE_OWN: (1 if arriving else 0, None, 1),
        CORE_X: (3 if arriving else 2, None, 1),
        CORE_Y: (5 if arriving else 4, None, 1),
        CORE_DIAG: (7 if arriving else 6, None, 1),
    }[kind]
    return flip(me, owner), half, {"fsdp": flip(me, step)}


class RowGather:
    def __init__(self, me, rows, sends, recvs):
        self.me, self.rows, self.sends, self.recvs = me, rows, sends, recvs

    def copy(self, kind, arriving=False):
        owner, half, peer = route(self.me, kind, arriving)
        first, count = (owner * WORDS, WORDS) if half is None else (owner * WORDS + half * (WORDS // 2), WORDS // 2)
        here = self.rows.at[pl.ds(pl.multiple_of(first, 16), count), :]
        return remote(here, here, self.sends.at[kind], self.recvs.at[kind], peer)

    def start(self):
        for kind in (X, Y, CORE_OWN):
            self.copy(kind).start()

    def first(self):
        self.copy(X, True).wait_recv()
        self.copy(DIAG_Y).start()
        self.copy(CORE_X).start()
        self.copy(Y, True).wait_recv()
        self.copy(DIAG_X).start()
        self.copy(CORE_Y).start()

    def second(self):
        self.copy(DIAG_Y, True).wait_recv()
        self.copy(DIAG_X, True).wait_recv()
        self.copy(CORE_DIAG).start()

    def complete(self):
        for kind in (CORE_OWN, CORE_X, CORE_Y, CORE_DIAG):
            self.copy(kind, True).wait_recv()

    def settle(self):
        for kind in range(8):
            self.copy(kind).wait_send()


class RowSum:
    def __init__(self, me, partial, core_out, core_in, half_out, half_in, full_out, full_in, sends, recvs):
        self.me, self.partial, self.sends, self.recvs = me, partial, sends, recvs
        self.core_out, self.core_in = core_out, core_in
        self.half_out, self.half_in, self.full_out, self.full_in = half_out, half_in, full_out, full_in
        self.chip, self.lane = me // 2, me % 2

    def copy(self, at):
        if at == 0:
            source, target, peer = self.core_out, self.core_in, 1
        elif at < 3:
            source, target, peer = self.half_out.at[at - 1], self.half_in.at[at - 1], (2, 4)[at - 1]
        else:
            source, target, peer = self.full_out.at[at - 3], self.full_in.at[at - 3], (2, 4)[at - 3]
        return remote(source, target, self.sends.at[at], self.recvs.at[at], {"fsdp": flip(self.me, peer)})

    def start(self):
        for block in range(4):
            self.core_out[block] = self.partial[2 * block + 1 - self.lane].astype(LOW)
        self.copy(0).start()

    def joined(self, block):
        return self.partial[2 * block + self.lane] + self.core_in[block].astype(F32)

    def cores(self):
        self.copy(0).wait()
        half = WORDS // 2
        summed = self.joined(flip(self.chip, 3))
        self.half_out[0] = summed[:half].astype(LOW)
        self.half_out[1] = summed[half:].astype(LOW)
        for way in range(2):
            self.copy(1 + way).start()

    def diagonal(self):
        half = WORDS // 2
        for way in range(2):
            self.copy(1 + way).wait()
        for way, side in ((1, 0), (0, 1)):
            summed = self.joined(flip(self.chip, 1 + way))
            at, other = (slice(0, half), slice(half, WORDS)) if side == 0 else (slice(half, WORDS), slice(0, half))
            self.full_out[way, at] = (summed[at] + self.half_in[side].astype(F32)).astype(LOW)
            self.full_out[way, other] = summed[other].astype(LOW)
            self.copy(3 + way).start()

    def total(self):
        for way in range(2):
            self.copy(3 + way).wait()
        return self.joined(self.chip) + (self.full_in[0].astype(F32) + self.full_in[1].astype(F32))


def row_sum_scratch():
    half, whole = (2, WORDS // 2, WIDE), (2, WORDS, WIDE)
    return [
        pltpu.VMEM((8, WORDS, WIDE), F32),
        pltpu.VMEM((4, WORDS, WIDE), LOW),
        pltpu.VMEM((4, WORDS, WIDE), LOW),
        pltpu.VMEM(half, LOW),
        pltpu.VMEM(half, LOW),
        pltpu.VMEM(whole, LOW),
        pltpu.VMEM(whole, LOW),
        pltpu.SemaphoreType.DMA((5,)),
        pltpu.SemaphoreType.DMA((5,)),
    ]


def dot_nt(left, right):
    return lax.dot_general(left, right, (((1,), (1,)), ((), ())), preferred_element_type=jnp.float32)


def dot_tn(left, right):
    return lax.dot_general(left, right, (((0,), (0,)), ((), ())), preferred_element_type=jnp.float32)


def spread(part):
    source = lax.broadcasted_iota(jnp.int32, (128, WIDE), 0)
    target = lax.broadcasted_iota(jnp.int32, (128, WIDE), 1)
    return jnp.logical_and(source < UNIT, target == source + part * UNIT)


def half_lanes():
    lane = lax.broadcasted_iota(jnp.int32, (1, PAIR_WIDE), 1)
    return (lane < HEAD_DIM, lane >= HEAD_DIM)


def only(values, chosen):
    return jnp.where(chosen, values, jnp.zeros_like(values))


ATTEND_CROSS_WORD = ((0, WORDS), (WORDS, REGIONS))
ATTEND_CROSS_REGION = ((WORDS, REGIONS), (0, WORDS))
ATTEND_WORD = ((0, WORDS), (0, WORDS))
ATTEND_REGION = ((WORDS, REGIONS), (WORDS, REGIONS))


def attend_into(rows_of, mixed, allowed, shares, context):
    (query_at, query_count), (key_at, key_count) = rows_of
    blocked = jnp.where(allowed, 0.0, masked_score)

    def pair(p, carry):
        at = pl.multiple_of(p * PAIR_WIDE, PAIR_WIDE)
        queries = mixed[pl.ds(query_at, query_count), pl.ds(at, PAIR_WIDE)]
        key_rows = mixed[pl.ds(key_at, key_count), pl.ds(WIDE + at, PAIR_WIDE)]
        value_rows = mixed[pl.ds(key_at, key_count), pl.ds(2 * WIDE + at, PAIR_WIDE)]
        total = jnp.zeros((query_count, PAIR_WIDE), jnp.float32)
        for side, chosen in enumerate(half_lanes()):
            scores = dot_nt(only(queries, chosen), key_rows) * HEAD_DIM ** (-0.5) + blocked
            lifted = jnp.exp(scores - jnp.max(scores, axis=-1, keepdims=True))
            share = (lifted / jnp.sum(lifted, axis=-1, keepdims=True)).astype(jnp.bfloat16)
            shares[2 * p + side] = share
            total = total + matmul(share, only(value_rows, chosen))
        context[pl.ds(query_at, query_count), pl.ds(at, PAIR_WIDE)] = total.astype(jnp.bfloat16)
        return carry

    lax.fori_loop(0, PAIRS_OF_HEADS, pair, 0)


def row_norm(summed):
    center = summed - jnp.mean(summed, axis=-1, keepdims=True)
    inverse = lax.rsqrt(jnp.mean(center * center, axis=-1, keepdims=True) + norm_epsilon)
    return (center * inverse, inverse)


def down(across):
    wide = jnp.broadcast_to(across.astype(jnp.float32), (128, across.shape[1]))
    return jnp.concatenate([wide[:, at : at + 128].T[:, :1] for at in range(0, across.shape[1], 128)], axis=0)


SAVED = (
    ((24, WIDE), F32),
    ((3, ROWS, WIDE), F32),
    ((3, ROWS, 128), F32),
    ((HIDDEN, REGIONS), LOW),
    ((REGIONS, HIDDEN), LOW),
    ((WIDE, REGIONS), LOW),
    ((PLANE_WORDS, SLICE), LOW),
    ((WIDE, SLICE), LOW),
    ((SLICE, PLANE_WORDS), LOW),
    ((WIDE, PLANE_WORDS), LOW),
    ((WIDE, ROWS), LOW),
    ((ROWS, 3 * WIDE), LOW),
    ((HEADS, WORDS, WORDS), LOW),
    ((HEADS, REGIONS, REGIONS), LOW),
    ((WIDE, ROWS), LOW),
    ((WIDE, ROWS), LOW),
    ((ROWS, 3 * WIDE), LOW),
    ((HEADS, WORDS, REGIONS), LOW),
    ((HEADS, REGIONS, WORDS), LOW),
    ((WIDE, ROWS), LOW),
)
WEIGHTS = (
    (3, WIDE, 3 * WIDE),
    (3, WIDE, WIDE),
    (1, WIDE, HIDDEN),
    (1, HIDDEN, WIDE),
)

CHUNKS = (
    (2, 0, None),
    (0, 0, (0, UNIT)),
    (1, 0, (0, UNIT)),
    (0, 1, (0, UNIT)),
    (3, 0, None),
    (1, 1, (0, UNIT)),
    (0, 2, (0, UNIT)),
    (1, 2, (0, UNIT)),
)
EXPAND, INWARD_0, OUTWARD_0, INWARD_1, SHRINK, OUTWARD_1, INWARD_2, OUTWARD_2 = range(len(CHUNKS))


def forward_kernel(*refs):
    word_rows, region_rows, word_ids, region_ids, biases, gains, hidden_bias, *shards = refs[:11]
    word_result, region_result, *kept = refs[11:33]
    weights_kept = refs[33:37]
    (
        params,
        normed,
        inverse,
        hidden_t,
        slope,
        rows_two_t,
        slope_words,
        expand_words,
        hidden_words_t,
        rows_two_words_t,
        context_self_t,
        mixed_self,
        shares_w,
        shares_r,
        rows_one_t,
        context_cross_t,
        mixed_cross,
        shares_cw,
        shares_cr,
        rows_zero_t,
    ) = saved = refs[37:57]
    inward_all, outward_all, expand_all, shrink_all = gathered = refs[57:61]
    (
        small_own,
        small_all,
        hidden_rows,
        rows_low,
        stream,
        stream_low,
        context,
        hidden,
        words_two,
        hidden_words,
        shrink_words,
        partial,
        core_out,
        core_in,
        half_out,
        half_in,
        full_out,
        full_in,
        sum_sends,
        sum_recvs,
        gather_sends,
        gather_recvs,
        slice_sends,
        slice_recvs,
        sends,
        recvs,
        z_sends,
        z_recvs,
        foreign_sends,
        foreign_recvs,
        small_sends,
        small_recvs,
        local_sems,
        keep_sems,
    ) = refs[61:]
    me = lax.axis_index("fsdp")
    z = lax.axis_index("rep")
    above, below = {"rep": (z + 1) % 4}, {"rep": (z + 3) % 4}
    gather_words = RowGather(me, words_two, gather_sends, gather_recvs)
    sum_words = RowSum(
        me, partial, core_out, core_in, half_out, half_in, full_out, full_in, sum_sends, sum_recvs
    )
    greet(me, z)

    def small_copy(offset, owner):
        return remote(
            small_all.at[owner],
            small_all.at[owner],
            small_sends.at[offset - 1],
            small_recvs.at[offset - 1],
            {"fsdp": flip(me, offset)},
        )

    def place(k, owner, half=None, quarter=None):
        kind, _, rows = CHUNKS[k]
        shard_rows, columns = shards[kind].shape[1:]
        first, count, column = 0, shard_rows, 0
        if rows is not None:
            first, count = rows
        elif quarter is not None and kind == 3:
            first, count = quarter * UNIT, UNIT
        elif quarter is not None:
            column, columns = quarter * WIDE, WIDE
        if half is not None:
            count = count // 2
            first = first + half * count
        if not isinstance(column, int):
            column = pl.multiple_of(column, WIDE)
        if not isinstance(first, int):
            first = pl.multiple_of(first, 16)
        whole = pl.multiple_of(owner * shard_rows + first, 16)
        return pl.ds(whole, count), pl.ds(first, count), pl.ds(column, columns)

    def own_part(k, quarter=None):
        kind, index, _ = CHUNKS[k]
        _, rows, columns = place(k, me, None, quarter)
        return shards[kind].at[index + (1 if kind > 1 else 0), rows, columns]

    def part(k, owner, half=None, quarter=None):
        kind, index, _ = CHUNKS[k]
        rows, _, columns = place(k, owner, half, quarter)
        return gathered[kind].at[index, rows, columns]

    def mine(k):
        return z if CHUNKS[k][2] is None else None

    def copy(k, kind, arriving=False):
        owner, half, peer = route(me, kind, arriving)
        quarter = None if kind == CORE_OWN else mine(k)
        target = part(k, owner, half, quarter)
        source = own_part(k, quarter) if kind in (X, Y, CORE_OWN) and not arriving else target
        return remote(source, target, sends.at[k, kind], recvs.at[k, kind], peer)

    z_chunks = [k for k in range(len(CHUNKS)) if CHUNKS[k][2] is None]
    owners = (flip(me, 2), flip(me, 4), flip(me, 6))
    core_owners = (flip(me, 3), flip(me, 5), flip(me, 7))

    def z_copy(k, way, hop, which, arriving=False):
        steps = hop + 1 if arriving else hop
        quarter = z - steps if way == 0 else z + steps
        here = part(k, owners[which], None, quarter)
        at = (z_chunks.index(k), way, hop, which)
        return remote(here, here, z_sends.at[at], z_recvs.at[at], (above, below)[way])

    def foreign_copy(k, way, hop, which, arriving=False):
        quarter = z - hop - 1 if way == 0 else z + hop + 1
        here = part(k, (core_owners if arriving else owners)[which], None, quarter)
        at = (z_chunks.index(k), way, hop, which)
        return remote(here, here, foreign_sends.at[at], foreign_recvs.at[at], {"fsdp": flip(me, 1)})

    def goes(way, hop):
        return jnp.logical_and(z >= hop, z < 3) if way == 0 else jnp.logical_and(z <= 3 - hop, z > 0)

    def comes(way, hop):
        return z >= hop + 1 if way == 0 else z <= 2 - hop

    def send_z(k, hop, which):
        for way in range(2):

            @pl.when(goes(way, hop))
            def _(way=way):
                for one in which:
                    z_copy(k, way, hop, one).start()

    def own_local(k):
        return pltpu.make_async_copy(own_part(k), part(k, me), local_sems.at[k])

    def own(k):
        for kind in (X, Y):
            copy(k, kind).start()
        own_local(k).start()
        copy(k, CORE_OWN).start()

    def pass_first(k):
        copy(k, X, True).wait_recv()
        copy(k, DIAG_Y).start()
        copy(k, Y, True).wait_recv()
        copy(k, DIAG_X).start()
        if k in z_chunks:
            send_z(k, 0, (0, 1))
        copy(k, CORE_X).start()
        copy(k, CORE_Y).start()

    def pass_second(k):
        copy(k, DIAG_Y, True).wait_recv()
        copy(k, DIAG_X, True).wait_recv()
        if k in z_chunks:
            send_z(k, 0, (2,))
        copy(k, CORE_DIAG).start()

    def pass_quarter(k, hop):
        for way in range(2):

            @pl.when(comes(way, hop))
            def _(way=way):
                for which in range(3):
                    z_copy(k, way, hop, which, True).wait_recv()

        if hop < 2:
            send_z(k, hop + 1, (0, 1, 2))
        for way in range(2):

            @pl.when(comes(way, hop))
            def _(way=way):
                for which in range(3):
                    foreign_copy(k, way, hop, which).start()

    def complete(k):
        own_local(k).wait()
        for kind in (CORE_OWN, CORE_X, CORE_Y, CORE_DIAG):
            copy(k, kind, True).wait_recv()
        if k in z_chunks:
            for hop in range(3):
                for way in range(2):

                    @pl.when(comes(way, hop))
                    def _(way=way, hop=hop):
                        for which in range(3):
                            foreign_copy(k, way, hop, which, True).wait_recv()

    def slice_copy(offset, arriving=False):
        peer = flip(me, offset)
        rows = pl.ds(pl.multiple_of((peer if arriving else me) * UNIT, UNIT), UNIT)
        target = expand_words.at[rows, :]
        source = shards[2].at[0, :, pl.ds(pl.multiple_of(peer * SLICE, SLICE), SLICE)]
        return remote(source, target, slice_sends.at[offset - 1], slice_recvs.at[offset - 1], {"fsdp": peer})

    own_slice = pltpu.make_async_copy(
        shards[2].at[0, :, pl.ds(pl.multiple_of(me * SLICE, SLICE), SLICE)],
        expand_words.at[pl.ds(pl.multiple_of(me * UNIT, UNIT), UNIT), :],
        local_sems.at[len(CHUNKS)],
    )
    own_shrink = pltpu.make_async_copy(shards[3].at[0], shrink_words, local_sems.at[len(CHUNKS) + 1])

    def start_slices():
        own_slice.start()
        own_shrink.start()
        for offset in range(1, 8):
            slice_copy(offset).start()

    def wait_slices():
        own_slice.wait()
        own_shrink.wait()
        for offset in range(1, 8):
            slice_copy(offset, True).wait_recv()

    keeps = []

    def keep(source, target):
        copied = pltpu.make_async_copy(source, target, keep_sems.at[len(keeps)])
        copied.start()
        keeps.append(copied)

    def keep_weights(kind, index):
        keep(gathered[kind].at[index], weights_kept[kind].at[index])

    def keep_saved(*refs_done):
        for done in refs_done:
            index = [ref is done for ref in saved].index(True)
            keep(saved[index], kept[index])

    def give_small():
        small_own[...] = jnp.zeros_like(small_own)
        small_own[0:16, 0:UNIT] = biases[...].astype(F32)
        small_own[16:21, 0:UNIT] = gains[...].astype(F32)
        source = lax.broadcasted_iota(jnp.int32, (4 * UNIT, 128), 0)
        target = lax.broadcasted_iota(jnp.int32, (4 * UNIT, 128), 1)
        for q in range(4):
            chosen = jnp.logical_and(target < UNIT, source == target + q * UNIT).astype(LOW)
            placed = matmul(hidden_bias[...], chosen)
            for f in range(2):
                row = 21 + 4 * f + q
                small_own[row : row + 1, :] = placed[f : f + 1]
        small_all[me] = small_own[...].astype(LOW)
        for offset in range(1, 8):
            small_copy(offset, me).start()

    def read_small():
        for offset in range(1, 8):
            small_copy(offset, flip(me, offset)).wait_recv()
        totals = jnp.zeros((21, WIDE), jnp.float32)
        hidden_parts = [jnp.zeros((1, WIDE), jnp.float32) for _ in range(4)]
        for owner in range(8):
            one = small_all[owner]
            totals = totals + matmul(one, spread(owner).astype(LOW))[:21]
            for q in range(4):
                placed = matmul(one, spread((owner % 2) * 4 + q).astype(LOW))
                row = 25 + q
                hidden_parts[owner // 2] = hidden_parts[owner // 2] + placed[row : row + 1]
        params[...] = jnp.zeros_like(params)
        params[0:21, :] = totals
        for block in range(4):
            hidden_rows[:, block * WIDE : (block + 1) * WIDE] = hidden_parts[block]
        keep_saved(params)

    def read_rows():
        rows_low[0:WORDS, :] = word_rows[...]
        rows_low[WORDS:ROWS, :] = region_rows[...]
        for at in range(0, ROWS, 128):
            transposed_into(rows_zero_t, rows_low[at : at + 128, :], at, 128)
        keep_saved(rows_zero_t)

    def transposed_into(target, values, at, count):
        target[:, pl.ds(at, count)] = values.T

    def project_into(source, at, count, module, mixed):
        for third, bias_row in enumerate((3 * module, None, 3 * module + 1)):
            product = matmul(source[pl.ds(at, count), :], inward_all[module, :, third * WIDE : (third + 1) * WIDE])
            if bias_row is not None:
                product = product + params[bias_row : bias_row + 1, :]
            mixed[pl.ds(at, count), third * WIDE : (third + 1) * WIDE] = product.astype(jnp.bfloat16)

    def join(at, product, residual, bias_row, norm_at, norm_index):
        rows = pl.ds(at, 128)
        unit, scale = row_norm(residual + product + params[bias_row : bias_row + 1, :])
        normed[norm_at, rows, :] = unit
        inverse[norm_at, rows, :] = jnp.broadcast_to(scale, (128, 128))
        return unit * params[16 + norm_index : 17 + norm_index, :] + params[9 + norm_index : 10 + norm_index, :]

    def cross_in():
        project_into(rows_low, 0, ROWS, 0, mixed_cross)
        keep_saved(mixed_cross)
        keep_weights(0, 0)

    def cross_words():
        allowed = down(word_ids[...]) == region_ids[...].astype(F32)
        attend_into(ATTEND_CROSS_WORD, mixed_cross, allowed, shares_cw, context)
        keep_saved(shares_cw)

    def cross_regions():
        allowed = down(region_ids[...]) == word_ids[...].astype(F32)
        attend_into(ATTEND_CROSS_REGION, mixed_cross, allowed, shares_cr, context)
        keep_saved(shares_cr)

    def cross_out():
        for at in range(0, ROWS, 128):
            product = matmul(context[at : at + 128, :], outward_all[0])
            one = join(at, product, rows_low[at : at + 128, :].astype(F32), 2, 0, 0)
            stream[at : at + 128, :] = one
            one_low = one.astype(LOW)
            stream_low[at : at + 128, :] = one_low
            transposed_into(rows_one_t, one_low, at, 128)
            transposed_into(context_cross_t, context[at : at + 128, :], at, 128)
        keep_saved(rows_one_t, context_cross_t)
        keep_weights(1, 0)

    def word_in():
        project_into(stream_low, 0, WORDS, 1, mixed_self)
        keep_weights(0, 1)
        allowed = down(word_ids[...]) == word_ids[...].astype(F32)
        attend_into(ATTEND_WORD, mixed_self, allowed, shares_w, context)
        transposed_into(context_self_t, context[0:WORDS, :], 0, WORDS)
        keep_saved(shares_w)

    def region_in():
        project_into(stream_low, WORDS, REGIONS, 2, mixed_self)
        keep_weights(0, 2)

    def region_attend():
        allowed = down(region_ids[...]) == region_ids[...].astype(F32)
        attend_into(ATTEND_REGION, mixed_self, allowed, shares_r, context)
        for at in range(WORDS, ROWS, 128):
            transposed_into(context_self_t, context[at : at + 128, :], at, 128)
        keep_saved(shares_r)

    def self_out(module, first, last):
        for at in range(first, last, 128):
            product = matmul(context[at : at + 128, :], outward_all[module])
            two = join(at, product, stream[at : at + 128, :], 3 * module + 2, 1, module)
            stream[at : at + 128, :] = two
            two_low = two.astype(LOW)
            stream_low[at : at + 128, :] = two_low
            if module == 1:
                words_two[pl.ds(pl.multiple_of(me * WORDS, WORDS), WORDS), :] = two_low
            else:
                transposed_into(rows_two_t, two_low, at - WORDS, 128)
        keep_weights(1, module)

    def activate(before, hidden_to, hidden_t_to, slope_to):
        below = 0.5 * (1.0 + lax.erf(before * 0.5**0.5))
        density = jnp.exp(-0.5 * before * before) * 0.3989422804014327
        value = (before * below).astype(LOW)
        hidden_to[...] = value
        hidden_t_to[...] = value.T
        slope_to[...] = (below + before * density).astype(LOW)

    def feed_in(column, columns):
        step = 256

        def tile(t, carry):
            at = pl.ds(pl.multiple_of(column + t * step, step), step)
            for row in range(0, REGIONS, 128):
                rows = slice(row, row + 128)
                before = matmul(stream_low[WORDS + row : WORDS + row + 128, :], expand_all[0, :, at])
                activate(before + hidden_rows[:, at], hidden.at[rows, at], hidden_t.at[at, rows], slope.at[rows, at])
            return carry

        lax.fori_loop(0, columns // step, tile, 0)

    def feed_out():
        for at in range(WORDS, ROWS, 128):
            product = matmul(hidden[at - WORDS : at - WORDS + 128, :], shrink_all[0])
            last_rows = join(at, product, stream[at : at + 128, :], 15, 2, 4)
            region_result[at - WORDS : at - WORDS + 128, :] = last_rows.astype(LOW)

    def words_in():
        for at in range(0, PLANE_WORDS, 128):
            rows = slice(at, at + 128)
            before = matmul(words_two[rows, :], expand_words[...]) + hidden_bias[0:1, :].astype(F32)
            activate(before, hidden_words.at[rows, :], hidden_words_t.at[:, rows], slope_words.at[rows, :])
            rows_two_words_t[:, rows] = words_two[rows, :].T
        keep_saved(slope_words, expand_words, hidden_words_t, rows_two_words_t)

    def words_out():
        for at in range(0, PLANE_WORDS, 128):
            partial[at // 128] = matmul(hidden_words[at : at + 128, :], shrink_words[...])
        sum_words.start()

    def words_last():
        last_rows = join(0, sum_words.total(), stream[0:WORDS, :], 14, 2, 3)
        word_result[...] = last_rows.astype(LOW)

    give_small()
    own(EXPAND)
    read_rows()
    pass_first(EXPAND)
    own(INWARD_0)
    own(OUTWARD_0)
    read_small()
    pass_second(EXPAND)
    pass_first(INWARD_0)
    own(INWARD_1)
    pass_quarter(EXPAND, 0)
    pass_first(OUTWARD_0)
    own(SHRINK)
    pass_second(INWARD_0)
    complete(INWARD_0)
    pass_quarter(EXPAND, 1)
    cross_in()
    pass_second(OUTWARD_0)
    cross_words()
    cross_regions()
    complete(OUTWARD_0)
    cross_out()
    pass_first(INWARD_1)
    own(OUTWARD_1)
    pass_quarter(EXPAND, 2)
    pass_first(SHRINK)
    own(INWARD_2)
    pass_second(INWARD_1)
    pass_second(SHRINK)
    complete(INWARD_1)
    complete(EXPAND)
    keep_weights(2, 0)
    word_in()
    pass_first(OUTWARD_1)
    start_slices()
    pass_quarter(SHRINK, 0)
    pass_second(OUTWARD_1)
    complete(OUTWARD_1)
    self_out(1, 0, WORDS)
    gather_words.start()
    pass_first(INWARD_2)
    own(OUTWARD_2)
    gather_words.first()
    pass_quarter(SHRINK, 1)
    gather_words.second()
    wait_slices()
    gather_words.complete()
    words_in()
    words_out()
    pass_second(INWARD_2)
    complete(INWARD_2)
    pass_first(OUTWARD_2)
    sum_words.cores()
    region_in()
    pass_quarter(SHRINK, 2)
    region_attend()
    keep_saved(mixed_self, context_self_t)
    sum_words.diagonal()
    pass_second(OUTWARD_2)
    complete(OUTWARD_2)
    self_out(2, WORDS, ROWS)
    keep_saved(rows_two_t)
    feed_in(0, HIDDEN)
    keep_saved(hidden_t, slope)
    complete(SHRINK)
    keep_weights(3, 0)
    words_last()
    feed_out()
    keep_saved(normed, inverse)
    for copied in keeps:
        copied.wait()
    for offset in range(1, 8):
        small_copy(offset, me).wait_send()
        slice_copy(offset).wait_send()
    gather_words.settle()
    for k in range(len(CHUNKS)):
        for kind in range(8):
            copy(k, kind).wait_send()
    for k in z_chunks:
        for way in range(2):
            for hop in range(3):

                @pl.when(goes(way, hop))
                def _(k=k, way=way, hop=hop):
                    for which in range(3):
                        z_copy(k, way, hop, which).wait_send()

                @pl.when(comes(way, hop))
                def _(k=k, way=way, hop=hop):
                    for which in range(3):
                        foreign_copy(k, way, hop, which).wait_send()


def forward(word_rows, region_rows, word_ids, region_ids, biases, gains, hidden_bias, shards):
    dma = pltpu.SemaphoreType.DMA
    vmem = pl.BlockSpec(memory_space=pltpu.VMEM)
    hbm = pl.BlockSpec(memory_space=pl.ANY)
    saved = [jax.ShapeDtypeStruct(*one) for one in SAVED]
    weights = [jax.ShapeDtypeStruct(one, LOW) for one in WEIGHTS]
    quarters = (sum(chunk[2] is None for chunk in CHUNKS), 2, 3, 3)
    outs = pl.pallas_call(
        forward_kernel,
        out_shape=[jax.ShapeDtypeStruct((WORDS, WIDE), LOW), jax.ShapeDtypeStruct((REGIONS, WIDE), LOW)] + saved + weights,
        in_specs=[vmem] * 7 + [hbm] * 4,
        out_specs=[vmem] * 2 + [hbm] * (len(saved) + len(weights)),
        scratch_shapes=[pltpu.VMEM(one.shape, one.dtype) for one in saved + weights]
        + [
            pltpu.VMEM((32, 128), F32),
            pltpu.VMEM((8, 32, 128), LOW),
            pltpu.VMEM((1, HIDDEN), F32),
            pltpu.VMEM((ROWS, WIDE), LOW),
            pltpu.VMEM((ROWS, WIDE), F32),
            pltpu.VMEM((ROWS, WIDE), LOW),
            pltpu.VMEM((ROWS, WIDE), LOW),
            pltpu.VMEM((REGIONS, HIDDEN), LOW),
            pltpu.VMEM((PLANE_WORDS, WIDE), LOW),
            pltpu.VMEM((PLANE_WORDS, SLICE), LOW),
            pltpu.VMEM((SLICE, WIDE), LOW),
            *row_sum_scratch(),
            dma((8,)),
            dma((8,)),
            dma((7,)),
            dma((7,)),
            dma((len(CHUNKS), 8)),
            dma((len(CHUNKS), 8)),
            dma(quarters),
            dma(quarters),
            dma(quarters),
            dma(quarters),
            dma((7,)),
            dma((7,)),
            dma((len(CHUNKS) + 2,)),
            dma((len(saved) + 8,)),
        ],
        compiler_params=pltpu.CompilerParams(
            collective_id=1, has_side_effects=True, vmem_limit_bytes=64 * 2**20 - 2**16
        ),
    )(word_rows, region_rows, word_ids, region_ids, biases, gains, hidden_bias, *shards)
    return outs[:2], outs[2 : 2 + len(saved)], outs[2 + len(saved) :]


WINDOW = 6
SPAN = WIDE // 2
Z_SLOTS = 10

GROUPS = (
    (8, None, 0, 0, True, (3, 0)),
    (8, None, 0, 0, False, (2, 0)),
    (8, 0, 0, REGIONS, True, (3, 1)),
    (8, 1, 0, REGIONS, False, (2, 1)),
    (2, 2, 0, WORDS, False, (1, 1)),
    (2, 2, WORDS, REGIONS, False, (1, 2)),
    (6, 3, 0, WORDS, False, (0, 1)),
    (6, 3, WORDS, REGIONS, False, (0, 2)),
    (2, 4, 0, ROWS, False, (1, 0)),
    (6, 5, 0, ROWS, False, (0, 0)),
)
UNITS = sum(group[0] for group in GROUPS)
OWNED = sum(group[0] for group in GROUPS if group[1] is None)
CROSSING = UNITS - OWNED

BLOCKS = (
    [(kind, 0, c) for c in range(4) for kind in (3, 2)]
    + [(1, 1, 0), (1, 2, 0)]
    + [(0, m, c) for m in (1, 2) for c in range(3)]
    + [(1, 0, 0)]
    + [(0, 0, c) for c in range(3)]
)


def attend_back_into(rows_of, mixed, shares, grad_context, grad_mixed, first_pair, last_pair):
    (query_at, query_count), (key_at, key_count) = rows_of
    query_rows, key_rows = pl.ds(query_at, query_count), pl.ds(key_at, key_count)

    def pair(p, carry):
        at = pl.multiple_of(p * PAIR_WIDE, PAIR_WIDE)
        at_query, at_key, at_value = (pl.ds(third * WIDE + at, PAIR_WIDE) for third in range(3))
        queries = mixed[query_rows, at_query]
        keys = mixed[key_rows, at_key]
        values = mixed[key_rows, at_value]
        grads = grad_context[query_rows, at_query]
        grad_queries = jnp.zeros((query_count, PAIR_WIDE), jnp.float32)
        grad_keys = jnp.zeros((key_count, PAIR_WIDE), jnp.float32)
        grad_values = jnp.zeros((key_count, PAIR_WIDE), jnp.float32)
        for side, chosen in enumerate(half_lanes()):
            share = shares[2 * p + side]
            grad_head = only(grads, chosen)
            wide = share.astype(jnp.float32)
            weighted = wide * dot_nt(grad_head, values)
            grad_scores = (weighted - wide * jnp.sum(weighted, axis=-1, keepdims=True)).astype(jnp.bfloat16)
            grad_values = grad_values + dot_tn(share, grad_head)
            grad_queries = grad_queries + matmul(grad_scores, only(keys, chosen))
            grad_keys = grad_keys + dot_tn(grad_scores, only(queries, chosen))
        score_scale = HEAD_DIM ** (-0.5)
        grad_mixed[query_rows, at_query] = (grad_queries * score_scale).astype(jnp.bfloat16)
        grad_mixed[key_rows, at_key] = (grad_keys * score_scale).astype(jnp.bfloat16)
        grad_mixed[key_rows, at_value] = grad_values.astype(jnp.bfloat16)
        return carry

    lax.fori_loop(first_pair, last_pair, pair, 0)


def backward_kernel(*refs):
    saved_hbm, weights = refs[:23], refs[23:27]
    word_gradient, region_gradient, small_out, *totals = refs[27:34]
    (
        params,
        word_cotangent,
        region_cotangent,
        normed,
        inverse,
        hidden_t,
        slope,
        rows_two_t,
        slope_words,
        expand_words,
        hidden_words_t,
        rows_two_words_t,
        context_self_t,
        mixed_self,
        shares_w,
        shares_r,
        rows_one_t,
        context_cross_t,
        mixed_cross,
        shares_cw,
        shares_cr,
        rows_zero_t,
        shrink_words,
    ) = saved = refs[34:57]
    (
        window,
        end_feed,
        end_self,
        end_cross,
        stream,
        grad_context,
        row_sums,
        hidden_sums,
        end_words,
        hidden_sums_words,
        owned_shrink,
        owned_out,
        owned_expand,
        partial,
        sum_core_out,
        sum_core_in,
        sum_half_out,
        sum_half_in,
        sum_full_out,
        sum_full_in,
        sum_sends,
        sum_recvs,
        gather_sends,
        gather_recvs,
        slice_sends,
        slice_recvs,
        out,
        acc,
        core_out,
        core_in,
        half_out,
        half_in,
        full_out,
        full_in,
        plane,
        end_out,
        end_in,
        mid_out,
        mid_in,
        small_in,
        small_in_plane,
        small_planes,
        saved_sems,
        window_sems,
        total_sems,
        core_send,
        core_recv,
        half_send,
        half_recv,
        full_send,
        full_recv,
        z_send,
        z_recv,
        back_send,
        back_recv,
        small_send,
        small_recv,
        free,
    ) = refs[57:]
    grad_before, before_words, grad_mixed_self, grad_mixed_cross = slope, slope_words, mixed_self, mixed_cross
    lefts = (hidden_t, rows_two_t, context_self_t, rows_one_t, context_cross_t, rows_zero_t)
    rights = (end_feed, grad_before, end_self, grad_mixed_self, end_cross, grad_mixed_cross)
    me = lax.axis_index("fsdp")
    z = lax.axis_index("rep")
    chip = me // 2
    lane = me % 2
    is_end = jnp.logical_or(z == 0, z == 3)
    is_mid = jnp.logical_or(z == 1, z == 2)
    core_peer = {"fsdp": flip(me, 1)}
    links = ({"fsdp": flip(me, 2)}, {"fsdp": flip(me, 4)})
    link_chip = (flip(chip, 1), flip(chip, 2))
    diagonal = flip(chip, 3)
    pair_peer = {"rep": flip(z, 1)}
    mid_peer = {"rep": 3 - z}
    low = LOW
    gather_words = RowGather(me, end_words, gather_sends, gather_recvs)
    sum_words = RowSum(
        me,
        partial,
        sum_core_out,
        sum_core_in,
        sum_half_out,
        sum_half_in,
        sum_full_out,
        sum_full_in,
        sum_sends,
        sum_recvs,
    )

    def load_saved(index):
        source = saved_hbm[index].at[0] if saved[index] is shrink_words else saved_hbm[index]
        return pltpu.make_async_copy(source, saved[index], saved_sems.at[index])

    def load_block(n):
        kind, index, c = BLOCKS[n]
        part = slice(c * WIDE, (c + 1) * WIDE)
        source = weights[kind].at[index, part, :] if kind == 3 else weights[kind].at[index, :, part]
        return pltpu.make_async_copy(source, window.at[n % WINDOW], window_sems.at[n % WINDOW])

    def wait_saved(*names):
        for name in names:
            load_saved([ref is name for ref in saved].index(True)).wait()

    first_saved = [0, 1, 2, 3, 4, 5]
    for index in first_saved:
        load_saved(index).start()
    for n in range(WINDOW):
        load_block(n).start()
    for index in [22, 8, 9, 10, 11, 6, 7] + list(range(12, 22)):
        load_saved(index).start()
    greet(me, z)

    def small_copy(offset):
        peer = flip(me, offset)
        return remote(
            small_in.at[peer],
            small_in_plane.at[offset - 1],
            small_send.at[offset - 1],
            small_recv.at[offset - 1],
            {"fsdp": peer},
        )

    def small_plane_copy(offset, source):
        peer = (z + offset) % 4 if source is z else source
        return remote(
            small_planes.at[source],
            small_planes.at[source],
            small_send.at[6 + offset],
            small_recv.at[6 + offset],
            {"rep": peer},
        )

    def core_copy(u):
        slot = u % SLOTS
        return remote(core_out.at[slot], core_in.at[slot], core_send.at[slot], core_recv.at[slot], core_peer)

    def half_copy(u, way):
        slot = u % SLOTS
        return remote(
            half_out.at[slot, way], half_in.at[slot, way], half_send.at[slot, way], half_recv.at[slot, way], links[way]
        )

    def full_copy(u, way):
        slot = u % SLOTS
        return remote(
            full_out.at[slot, way], full_in.at[slot, way], full_send.at[slot, way], full_recv.at[slot, way], links[way]
        )

    def end_copy(n):
        slot = n % Z_SLOTS
        return remote(end_out.at[slot], end_in.at[slot], z_send.at[0, slot], z_recv.at[0, slot], pair_peer)

    def mid_copy(n):
        slot = n % Z_SLOTS
        return remote(mid_out.at[slot], mid_in.at[slot], z_send.at[1, slot], z_recv.at[1, slot], mid_peer)

    def back_copy(n):
        u = z_order[n]
        return remote(out.at[u], out.at[u], back_send.at[u], back_recv.at[u], pair_peer)

    def credit(u, channel, peer, slots=SLOTS, count=CROSSING):
        if u + slots < count:
            pl.semaphore_signal(free.at[channel], inc=1, device_id=peer, device_id_type=MESH)

    def spend(u, channel, slots=SLOTS):
        if u >= slots:
            pl.semaphore_wait(free.at[channel], 1)

    def per_group(u, function):
        for group in GROUPS:
            if u < group[0]:
                return function(u, *group[1:])
            u = u - group[0]

    def produce(u):
        slot = u % SLOTS
        keep = u % ACC_SLOTS
        spend(u, 0)

        def products(at, side, first_row, count, by_row, matrix):
            rows = pl.ds(first_row, count)
            column = (at % 2 if by_row else at) * SPAN
            right = rights[side][rows, pl.ds(column, SPAN)]

            def product(core):
                blocks = []
                for block in range(4):
                    owner = 2 * block + core
                    row = owner * (4 * UNIT) + (at // 2) * UNIT if by_row else owner * UNIT
                    blocks.append(lefts[side][pl.ds(pl.multiple_of(row, 16), UNIT), rows])
                return matmul(jnp.concatenate(blocks, axis=0), right)

            other = product(1 - lane).astype(low)
            for block in range(4):
                core_out[slot, block] = other[block * UNIT : (block + 1) * UNIT]
            core_copy(u).start()
            own = product(lane)
            for block in range(4):
                acc[keep, block] = own[block * UNIT : (block + 1) * UNIT]

        per_group(crossing[u], products)

    def join_cores(u):
        slot = u % SLOTS
        keep = u % ACC_SLOTS
        core_copy(u).wait()
        for way in range(2):
            spend(u, 1 + way)
        summed = acc[keep, diagonal] + core_in[slot, diagonal].astype(jnp.float32)
        half_out[slot, 0] = summed[: UNIT // 2].astype(low)
        half_out[slot, 1] = summed[UNIT // 2 :].astype(low)
        for way in range(2):
            half_copy(u, way).start()
        for block in (link_chip[0], link_chip[1], chip):
            acc[keep, block] = acc[keep, block] + core_in[slot, block].astype(jnp.float32)
        credit(u, 0, core_peer)

    def join_diagonal(u):
        slot = u % SLOTS
        keep = u % ACC_SLOTS
        for way in range(2):
            half_copy(u, way).wait()
            spend(u, 3 + way)
        half = UNIT // 2
        full_out[slot, 1, :half] = (acc[keep, link_chip[1], :half] + half_in[slot, 0].astype(jnp.float32)).astype(low)
        full_out[slot, 1, half:] = acc[keep, link_chip[1], half:].astype(low)
        full_copy(u, 1).start()
        full_out[slot, 0, half:] = (acc[keep, link_chip[0], half:] + half_in[slot, 1].astype(jnp.float32)).astype(low)
        full_out[slot, 0, :half] = acc[keep, link_chip[0], :half].astype(low)
        full_copy(u, 0).start()
        for way in range(2):
            credit(u, 1 + way, links[way])

    def join_plane(u):
        slot = u % SLOTS
        keep = u % ACC_SLOTS
        for way in range(2):
            full_copy(u, way).wait()
        summed = acc[keep, chip] + (full_in[slot, 0].astype(F32) + full_in[slot, 1].astype(F32))
        for way in range(2):
            credit(u, 3 + way, links[way])
        enter(z_order.index(crossing[u]), summed)

    def join_owned(u):
        half = slice(u % 2 * SPAN, u % 2 * SPAN + SPAN)
        if u < 8:
            summed = owned_shrink[u // 2 * UNIT : (u // 2 + 1) * UNIT, half]
        else:
            summed = owned_expand[u - 8].astype(F32)
        enter(z_order.index(u), summed)

    def enter(n, summed):
        slot = n % Z_SLOTS

        @pl.when(is_end)
        def _():
            spend(n, 5, Z_SLOTS)
            end_out[slot] = summed.astype(low)
            end_copy(n).start()

        @pl.when(is_mid)
        def _():
            plane[slot] = summed

    def join_pair(n):
        slot = n % Z_SLOTS

        @pl.when(is_end)
        def _():
            end_copy(n).wait_send()

        @pl.when(is_mid)
        def _():
            end_copy(n).wait_recv()
            spend(n, 6, Z_SLOTS)
            mid_out[slot] = (plane[slot] + end_in[slot].astype(F32)).astype(low)
            mid_copy(n).start()
            credit(n, 5, pair_peer, Z_SLOTS, UNITS)

    def join_middle(n):
        slot = n % Z_SLOTS

        @pl.when(is_mid)
        def _():
            mid_copy(n).wait()
            out[z_order[n]] = (mid_out[slot].astype(F32) + mid_in[slot].astype(F32)).astype(low)
            back_copy(n).start()
            credit(n, 6, mid_peer, Z_SLOTS, UNITS)

    def total_copy(u, at, by_row, matrix):
        kind, index = matrix
        if by_row:
            row, column = (at // 2) * UNIT, (at % 2) * SPAN
        else:
            row, column = 0, at * SPAN
        place = totals[kind].at[index, pl.ds(row, UNIT), pl.ds(column, SPAN)]
        return pltpu.make_async_copy(out.at[u], place, total_sems.at[u])

    def finish(n):
        @pl.when(is_mid)
        def _():
            back_copy(n).wait_send()

        @pl.when(is_end)
        def _():
            back_copy(n).wait_recv()

        u = z_order[n]
        per_group(u, lambda at, side, first_row, count, by_row, matrix: total_copy(u, at, by_row, matrix).start())

    crossing = [u for u in range(UNITS) if u >= OWNED]
    to_plane = LAG_CORE + LAG_A + LAG_B
    entries = [(i + to_plane, 1, u) for i, u in enumerate(crossing)]
    entries += [(OWNED_SHRINK_AT + u * 3 // 8, 0, u) for u in range(8)]
    entries += [(OWNED_EXPAND_AT + 2 * (u - 8), 0, u) for u in range(8, OWNED)]
    entries.sort()
    z_order = [u for _, _, u in entries]
    for n in range(UNITS - Z_SLOTS):
        assert entries[n + Z_SLOTS][0] >= entries[n][0] + LAG_Z
    last = entries[-1][0] + 3 * LAG_Z

    row_tiles = ((0, 0), (1, 128), (1, 256))

    def add_row(index, values):
        row_sums[index : index + 1, :] += jnp.sum(values, axis=0, keepdims=True)

    def norm_back(grad, kind, norm_index, at, ends, end_bias, end_at=None):
        rows = slice(at, at + 128)
        unit = normed[kind, rows, :]
        grad_unit = grad * params[16 + norm_index : 17 + norm_index, :]
        summed = inverse[kind, rows, :1] * (
            grad_unit
            - jnp.mean(grad_unit, axis=-1, keepdims=True)
            - unit * jnp.mean(grad_unit * unit, axis=-1, keepdims=True)
        )
        add_row(16 + norm_index, grad * unit)
        add_row(9 + norm_index, grad)
        stream[rows, :] = summed
        summed_low = summed.astype(low)
        if end_at is None:
            ends[rows, :] = summed_low
        else:
            ends[pl.ds(end_at, 128), :] = summed_low
        add_row(end_bias, summed_low.astype(jnp.float32))

    def feed_norm():
        wait_saved(params, word_cotangent, region_cotangent, normed, inverse)
        row_sums[...] = jnp.zeros_like(row_sums)
        hidden_sums[...] = jnp.zeros_like(hidden_sums)
        hidden_sums_words[...] = jnp.zeros_like(hidden_sums_words)
        own_rows = pl.multiple_of(me * WORDS, WORDS)
        norm_back(word_cotangent[...].astype(F32), 2, 3, 0, end_words, 14, own_rows)
        gather_words.start()
        for at in range(0, REGIONS, 128):
            cotangent = region_cotangent[at : at + 128, :].astype(F32)
            norm_back(cotangent, 2, 4, WORDS + at, end_feed, 15, at)

    def slice_copy(offset, arriving=False):
        peer = flip(me, offset)
        rows = pl.ds(pl.multiple_of(peer * UNIT, UNIT), UNIT)
        target = owned_expand.at[peer if arriving else me]
        return remote(
            owned_out.at[rows, :], target, slice_sends.at[offset - 1], slice_recvs.at[offset - 1], {"fsdp": peer}
        )

    def words_back():
        wait_saved(shrink_words, slope_words, expand_words)
        for at in range(0, PLANE_WORDS, 128):
            rows = slice(at, at + 128)
            before = (dot_nt(end_words[rows, :], shrink_words[...]) * slope_words[rows, :].astype(F32)).astype(low)
            before_words[rows, :] = before
            hidden_sums_words[0:1, :] += jnp.sum(before.astype(F32), axis=0, keepdims=True)
            partial[at // 128] = dot_nt(before, expand_words[...])
        sum_words.start()

    def words_shrink():
        wait_saved(hidden_words_t)
        owned_shrink[...] = matmul(hidden_words_t[...], end_words[...])

    def words_expand():
        wait_saved(rows_two_words_t)
        owned_out[...] = matmul(rows_two_words_t[...], before_words[...]).astype(low)
        for offset in range(1, 8):
            slice_copy(offset).start()
        owned_expand[me] = owned_out[pl.ds(pl.multiple_of(me * UNIT, UNIT), UNIT), :]

    def words_expanded():
        for offset in range(1, 8):
            slice_copy(offset).wait_send()
            slice_copy(offset, True).wait_recv()

    def words_rows():
        stream[0:WORDS, :] += sum_words.total()

    def next_block(n):
        if n + WINDOW < len(BLOCKS):
            load_block(n + WINDOW).start()

    def feed_back(c):
        n = 2 * c
        load_block(n).wait()
        load_block(n + 1).wait()
        columns = slice(c * WIDE, (c + 1) * WIDE)
        for at in range(0, REGIONS, 128):
            rows = slice(at, at + 128)
            grad_hidden = dot_nt(end_feed[rows, :], window[n % WINDOW])
            before = (grad_hidden * slope[rows, columns].astype(F32)).astype(low)
            grad_before[rows, columns] = before
            hidden_sums[c : c + 1, :] += jnp.sum(before.astype(F32), axis=0, keepdims=True)
            stream[WORDS + at : WORDS + at + 128, :] += dot_nt(before, window[(n + 1) % WINDOW])
        next_block(n)
        next_block(n + 1)

    def self_norm():
        for f, at in row_tiles:
            norm_back(stream[at : at + 128, :], 1, 1 + f, at, end_self, 5 + 3 * f)

    def self_context():
        for f in range(2):
            n = 8 + f
            load_block(n).wait()
            for which, at in row_tiles:
                if which == f:
                    grad_context[at : at + 128, :] = dot_nt(end_self[at : at + 128, :], window[n % WINDOW]).astype(low)
            next_block(n)

    def project_back(n, module, grad_mixed, tiles):
        for c in range(3):
            load_block(n + c).wait()
            columns = slice(c * WIDE, (c + 1) * WIDE)
            for at in tiles:
                part = grad_mixed[at : at + 128, columns]
                if c != 1:
                    add_row(3 * module + c // 2, part.astype(jnp.float32))
                stream[at : at + 128, :] += dot_nt(part, window[(n + c) % WINDOW])
            next_block(n + c)

    def cross_norm():
        for _, at in row_tiles:
            norm_back(stream[at : at + 128, :], 0, 0, at, end_cross, 2)

    def cross_context():
        n = 16
        load_block(n).wait()
        for _, at in row_tiles:
            grad_context[at : at + 128, :] = dot_nt(end_cross[at : at + 128, :], window[n % WINDOW]).astype(low)
        next_block(n)

    def give_rows():
        word_gradient[...] = stream[0:WORDS, :]
        region_gradient[...] = stream[WORDS:ROWS, :]

    def exact_nt(left, right):
        return lax.dot_general(
            left,
            right.astype(jnp.float32),
            (((1,), (1,)), ((), ())),
            precision=lax.Precision.HIGHEST,
            preferred_element_type=jnp.float32,
        )

    def give_small():
        small_in[...] = jnp.zeros_like(small_in)
        for owner in range(8):
            small_in[owner, 0:21, :] = exact_nt(row_sums[...], spread(owner))[:21]
        for place in range(8):
            placed = exact_nt(hidden_sums[...], spread(place))
            for c in range(4):
                row = 25 + place % 4
                small_in[2 * c + place // 4, row : row + 1, :] = placed[c : c + 1]
        source = lax.broadcasted_iota(jnp.int32, (128, SLICE), 0)
        target = lax.broadcasted_iota(jnp.int32, (128, SLICE), 1)
        for q in range(4):
            chosen = jnp.logical_and(source < UNIT, target == source + q * UNIT)
            small_in[me, 21 + q : 22 + q, :] = exact_nt(hidden_sums_words[...], chosen)[0:1]
        for offset in range(1, 8):
            small_copy(offset).start()

    def join_small():
        summed = small_in[me]
        for offset in range(1, 8):
            small_copy(offset).wait()
            summed = summed + small_in_plane[offset - 1]
        small_planes[z] = summed
        for offset in range(1, 4):
            small_plane_copy(offset, z).start()

    def finish_small():
        for offset in range(1, 4):
            small_plane_copy(offset, z).wait_send()
            small_plane_copy(offset, (z + 4 - offset) % 4).wait_recv()
        small_out[...] = small_planes[0] + small_planes[1] + (small_planes[2] + small_planes[3])

    def self_back(rows_of, shares, first, last):
        attend_back_into(rows_of, mixed_self, shares, grad_context, grad_mixed_self, first, last)

    def cross_back(rows_of, shares, first, last):
        attend_back_into(rows_of, mixed_cross, shares, grad_context, grad_mixed_cross, first, last)

    pieces = {
        0: (gather_words.first, lambda: wait_saved(slope)),
        1: (gather_words.second, functools.partial(feed_back, 0)),
        2: (gather_words.complete, words_back),
        3: (functools.partial(feed_back, 1),),
        4: (sum_words.cores, words_shrink),
        5: (functools.partial(feed_back, 2), words_expand),
        6: (sum_words.diagonal,),
        7: (functools.partial(feed_back, 3), lambda: wait_saved(rows_two_t)),
        8: (words_rows, gather_words.settle),
        9: (words_expanded,),
        10: (self_norm,),
        11: (self_context, lambda: wait_saved(context_self_t, mixed_self, shares_w)),
        12: (lambda: self_back(ATTEND_WORD, shares_w, 0, 3),),
        13: (lambda: self_back(ATTEND_WORD, shares_w, 3, 6), lambda: wait_saved(shares_r, rows_one_t)),
        **{14 + p: (functools.partial(self_back, ATTEND_REGION, shares_r, p, p + 1),) for p in range(6)},
        20: (lambda: project_back(10, 1, grad_mixed_self, (0,)),),
        21: (lambda: project_back(13, 2, grad_mixed_self, (128, 256)),),
        23: (cross_norm, lambda: wait_saved(context_cross_t, mixed_cross, shares_cw, shares_cr, rows_zero_t)),
        24: (cross_context,),
        **{25 + p: (functools.partial(cross_back, ATTEND_CROSS_WORD, shares_cw, 2 * p, 2 * p + 2),) for p in range(3)},
        **{28 + p: (functools.partial(cross_back, ATTEND_CROSS_REGION, shares_cr, 2 * p, 2 * p + 2),) for p in range(3)},
        32: (lambda: project_back(17, 0, grad_mixed_cross, (0, 128, 256)),),
        33: (give_rows,),
        34: (give_small,),
        37: (join_small,),
        40: (finish_small,),
    }

    feed_norm()
    wait_saved(hidden_t)
    for i in range(last + 1):
        for n, (entry, _, _) in enumerate(entries):
            if i == entry + 3 * LAG_Z:
                finish(n)
        for n, (entry, _, _) in enumerate(entries):
            if i == entry + 2 * LAG_Z:
                join_middle(n)
        for n, (entry, _, _) in enumerate(entries):
            if i == entry + LAG_Z:
                join_pair(n)
        for entry, crosses, u in entries:
            if i == entry and not crosses:
                join_owned(u)
        for lag, stage in ((to_plane, join_plane), (LAG_CORE + LAG_A, join_diagonal), (LAG_CORE, join_cores), (0, produce)):
            if 0 <= i - lag < CROSSING:
                stage(i - lag)
        for piece in pieces.get(i, ()):
            piece()
    for u in range(UNITS):
        per_group(u, lambda at, side, first_row, count, by_row, matrix: total_copy(u, at, by_row, matrix).wait())


def backward(saved, shrink, weights):
    block = (UNIT, SPAN)
    low, f32 = jnp.bfloat16, jnp.float32
    dma = pltpu.SemaphoreType.DMA
    vmem = pl.BlockSpec(memory_space=pltpu.VMEM)
    hbm = pl.BlockSpec(memory_space=pl.ANY)
    shape = jax.ShapeDtypeStruct
    small = (32, 128)
    return pl.pallas_call(
        backward_kernel,
        out_shape=(
            shape((WORDS, WIDE), f32),
            shape((REGIONS, WIDE), f32),
            shape(small, f32),
            shape((3, UNIT, 3 * WIDE), low),
            shape((3, UNIT, WIDE), low),
            shape((2, UNIT, HIDDEN), low),
            shape((2, 4 * UNIT, WIDE), low),
        ),
        in_specs=[hbm] * (len(saved) + 1 + len(weights)),
        out_specs=[vmem] * 3 + [hbm] * 4,
        scratch_shapes=[pltpu.VMEM(array.shape, array.dtype) for array in saved]
        + [
            pltpu.VMEM((SLICE, WIDE), low),
            pltpu.VMEM((WINDOW, WIDE, WIDE), low),
            pltpu.VMEM((REGIONS, WIDE), low),
            pltpu.VMEM((ROWS, WIDE), low),
            pltpu.VMEM((ROWS, WIDE), low),
            pltpu.VMEM((ROWS, WIDE), f32),
            pltpu.VMEM((ROWS, WIDE), low),
            pltpu.VMEM((24, WIDE), f32),
            pltpu.VMEM((8, WIDE), f32),
            pltpu.VMEM((PLANE_WORDS, WIDE), low),
            pltpu.VMEM((8, SLICE), f32),
            pltpu.VMEM((SLICE, WIDE), f32),
            pltpu.VMEM((WIDE, SLICE), low),
            pltpu.VMEM((8, UNIT, SLICE), low),
            *row_sum_scratch(),
            dma((8,)),
            dma((8,)),
            dma((7,)),
            dma((7,)),
            pltpu.VMEM((UNITS,) + block, low),
            pltpu.VMEM((ACC_SLOTS, 4) + block, f32),
            pltpu.VMEM((SLOTS, 4) + block, low),
            pltpu.VMEM((SLOTS, 4) + block, low),
            pltpu.VMEM((SLOTS, 2, UNIT // 2, SPAN), low),
            pltpu.VMEM((SLOTS, 2, UNIT // 2, SPAN), low),
            pltpu.VMEM((SLOTS, 2) + block, low),
            pltpu.VMEM((SLOTS, 2) + block, low),
            pltpu.VMEM((Z_SLOTS,) + block, f32),
            pltpu.VMEM((Z_SLOTS,) + block, low),
            pltpu.VMEM((Z_SLOTS,) + block, low),
            pltpu.VMEM((Z_SLOTS,) + block, low),
            pltpu.VMEM((Z_SLOTS,) + block, low),
            pltpu.VMEM((8,) + small, f32),
            pltpu.VMEM((7,) + small, f32),
            pltpu.VMEM((4,) + small, f32),
            dma((23,)),
            dma((WINDOW,)),
            dma((UNITS,)),
            dma((SLOTS,)),
            dma((SLOTS,)),
            dma((SLOTS, 2)),
            dma((SLOTS, 2)),
            dma((SLOTS, 2)),
            dma((SLOTS, 2)),
            dma((2, Z_SLOTS)),
            dma((2, Z_SLOTS)),
            dma((UNITS,)),
            dma((UNITS,)),
            dma((10,)),
            dma((10,)),
            pltpu.SemaphoreType.REGULAR((7,)),
        ],
        compiler_params=pltpu.CompilerParams(
            collective_id=0, has_side_effects=True, vmem_limit_bytes=64 * 2**20 - 2**16
        ),
    )(*saved, shrink, *weights)


def deliver_kernel(*refs):
    moved, small, totals = refs[:4], refs[4], refs[5:9]
    moved_out, bias_out, gain_out, hidden_out, totals_out = refs[9:13], refs[13], refs[14], refs[15], refs[16:20]
    narrow, wide, held = refs[20:24], refs[24:28], refs[28:32]
    take_sems, give_sems, load_sems, store_sems = refs[32:]
    takes = [pltpu.make_async_copy(moved[i], held[i], take_sems.at[i]) for i in range(4)]
    gives = [pltpu.make_async_copy(held[i], moved_out[i], give_sems.at[i]) for i in range(4)]
    pieces = [(kind, index) for kind in range(4) for index in range(totals[kind].shape[0])]
    loads = [
        pltpu.make_async_copy(totals[kind].at[index], narrow[kind].at[index], load_sems.at[i])
        for i, (kind, index) in enumerate(pieces)
    ]
    stores = [
        pltpu.make_async_copy(wide[kind].at[index], totals_out[kind].at[index], store_sems.at[i])
        for i, (kind, index) in enumerate(pieces)
    ]
    for one in loads + takes:
        one.start()
    bias_out[...] = small[0:16, 0:UNIT]
    gain_out[...] = small[16:21, 0:UNIT]
    source = lax.broadcasted_iota(jnp.int32, (128, 4 * UNIT), 0)
    target = lax.broadcasted_iota(jnp.int32, (128, 4 * UNIT), 1)
    for f in range(2):
        row = jnp.zeros((1, 4 * UNIT), F32)
        for q in range(4):
            chosen = jnp.logical_and(source < UNIT, target == source + q * UNIT).astype(F32)
            line = 21 + 4 * f + q
            row = row + jnp.dot(
                small[line : line + 1, :], chosen, precision=lax.Precision.HIGHEST, preferred_element_type=F32
            )
        hidden_out[f : f + 1, :] = row
    for i, (kind, index) in enumerate(pieces):
        loads[i].wait()
        wide[kind][index] = narrow[kind][index].astype(F32)
        stores[i].start()
    for i in range(4):
        takes[i].wait()
        gives[i].start()
    for one in gives + stores:
        one.wait()


def deliver(moved, small, totals):
    vmem = pl.BlockSpec(memory_space=pltpu.VMEM)
    hbm = pl.BlockSpec(memory_space=pl.ANY)
    shape = jax.ShapeDtypeStruct
    widened = [shape(total.shape, F32) for total in totals]
    sem = pltpu.SemaphoreType.DMA((4,))
    piece_sem = pltpu.SemaphoreType.DMA((sum(total.shape[0] for total in totals),))
    return pl.pallas_call(
        deliver_kernel,
        out_shape=[shape(one.shape, one.dtype) for one in moved]
        + [shape((16, UNIT), F32), shape((5, UNIT), F32), shape((2, 4 * UNIT), F32)]
        + widened,
        in_specs=[hbm] * 4 + [vmem] + [hbm] * 4,
        out_specs=[hbm] * 4 + [vmem] * 3 + [hbm] * 4,
        scratch_shapes=[pltpu.VMEM(one.shape, one.dtype) for one in totals]
        + [pltpu.VMEM(one.shape, F32) for one in totals]
        + [pltpu.VMEM(one.shape, one.dtype) for one in moved]
        + [sem, sem, piece_sem, piece_sem],
        compiler_params=pltpu.CompilerParams(vmem_limit_bytes=64 * 2**20 - 2**16),
    )(*moved, small, *totals)


def paired(
    word_rows,
    region_rows,
    word_segment,
    region_segment,
    inward,
    outward,
    biases,
    norm_gain,
    expand_weight,
    shrink_weight,
    hidden_bias,
    word_cotangent,
    region_cotangent,
):
    results, saved, weights = forward(
        word_rows,
        region_rows,
        word_segment,
        region_segment,
        biases,
        norm_gain,
        hidden_bias,
        (inward, outward, expand_weight, shrink_weight),
    )
    word_gradient, region_gradient, small, *totals = backward(
        (saved[0], word_cotangent, region_cotangent, *saved[1:]), shrink_weight, weights
    )
    word_out, region_out, word_gradient, region_gradient, bias, gain, hidden, *totals = deliver(
        (*results, word_gradient, region_gradient), small, totals
    )
    inward_total, outward_total, expand_total, shrink_total = totals
    return (
        word_out,
        region_out,
        word_gradient,
        region_gradient,
        inward_total,
        outward_total,
        bias,
        gain,
        expand_total,
        shrink_total,
        hidden,
    )


def general(
    devices,
    word_rows,
    region_rows,
    word_segment,
    region_segment,
    inward,
    outward,
    biases,
    norm_gain,
    expand_weight,
    shrink_weight,
    hidden_bias,
    word_cotangent,
    region_cotangent,
):
    words_count = word_rows.shape[0]
    width = word_rows.shape[1]
    word_ids = word_segment[0]
    region_ids = region_segment[0]
    cross_mask = word_ids[:, None] == region_ids[None, :]
    word_mask = word_ids[:, None] == word_ids[None, :]
    region_mask = region_ids[:, None] == region_ids[None, :]
    shard = biases.shape[1]
    per_shard = hidden_bias.shape[1] // shard
    small_shard = jnp.concatenate([biases, norm_gain, hidden_bias.reshape(2 * per_shard, shard)], axis=0)
    small_all = lax.all_gather(small_shard, "fsdp", axis=0)
    bias_count = biases.shape[0]
    gain_count = norm_gain.shape[0]
    row_params = small_all[:, : bias_count + gain_count].transpose(1, 0, 2).reshape(bias_count + gain_count, width)
    hidden_all = (
        small_all[:, bias_count + gain_count :]
        .reshape(devices, 2, per_shard * shard)
        .transpose(1, 0, 2)
        .reshape(2, devices * per_shard * shard)
    )
    inward_all, outward_all = (
        lax.all_gather(inward, "fsdp", axis=1, tiled=True),
        lax.all_gather(outward, "fsdp", axis=1, tiled=True),
    )
    attend_set = (
        inward_all,
        outward_all,
        row_params[:bias_count].astype(jnp.float32),
        row_params[bias_count:].astype(jnp.float32),
    )
    crossed, cross_kept = cross_forward(word_rows, region_rows, attend_set, cross_mask)
    word_one, word_kept = self_forward(crossed[:words_count], attend_set, 1, word_mask)
    region_one, region_kept = self_forward(crossed[words_count:], attend_set, 2, region_mask)
    expand_all, shrink_all = (
        lax.all_gather(expand_weight, "fsdp", axis=1, tiled=True),
        lax.all_gather(shrink_weight, "fsdp", axis=1, tiled=True),
    )
    feed_set = (expand_all, shrink_all, hidden_all)
    word_two, word_feed = feed_forward(word_one, feed_set, 0, attend_set)
    region_two, region_feed = feed_forward(region_one, feed_set, 1, attend_set)
    word_back = feed_backward(word_cotangent.astype(jnp.float32), word_feed, feed_set, 0, attend_set[3])
    region_back = feed_backward(region_cotangent.astype(jnp.float32), region_feed, feed_set, 1, attend_set[3])
    word_self = self_backward(word_back[0], word_kept, attend_set, 1, word_mask)
    region_self = self_backward(region_back[0], region_kept, attend_set, 2, region_mask)
    grad_crossed = jnp.concatenate([word_self[0], region_self[0]], axis=0)
    cross_back = cross_backward(grad_crossed, cross_kept, attend_set, cross_mask, words_count)
    row_grads = jnp.stack(
        [
            cross_back[3][0],
            cross_back[3][1],
            cross_back[3][2],
            word_self[3][0],
            word_self[3][1],
            word_self[3][2],
            region_self[3][0],
            region_self[3][1],
            region_self[3][2],
            cross_back[5],
            word_self[5],
            region_self[5],
            word_back[6],
            region_back[6],
            word_back[4],
            region_back[4],
            cross_back[4],
            word_self[4],
            region_self[4],
            word_back[5],
            region_back[5],
        ]
    )
    hidden_grads = jnp.stack([word_back[3], region_back[3]])
    small_grads = jnp.concatenate(
        [
            row_grads.reshape(bias_count + gain_count, devices, shard).transpose(1, 0, 2),
            hidden_grads.reshape(2, devices, per_shard, shard)
            .transpose(1, 0, 2, 3)
            .reshape(devices, 2 * per_shard, shard),
        ],
        axis=1,
    )

    def reduced(products, axis):
        mine = lax.psum_scatter(jnp.stack(products), "fsdp", scatter_dimension=axis, tiled=True)
        return lax.psum(mine.astype(jnp.bfloat16), "rep").astype(jnp.float32)

    shrink_total = reduced([matmul_tn(*word_back[2]), matmul_tn(*region_back[2])], 1)
    expand_total = reduced([matmul_tn(*word_back[1]), matmul_tn(*region_back[1])], 1)
    outward_total = reduced([matmul_tn(*cross_back[2]), matmul_tn(*word_self[2]), matmul_tn(*region_self[2])], 1)
    inward_total = reduced([matmul_tn(*cross_back[1]), matmul_tn(*word_self[1]), matmul_tn(*region_self[1])], 1)
    small_total = lax.psum(lax.psum_scatter(small_grads, "fsdp", scatter_dimension=0, tiled=False), "rep")
    grad_rows = cross_back[0]
    return (
        word_two.astype(jnp.bfloat16),
        region_two.astype(jnp.bfloat16),
        grad_rows[:words_count],
        grad_rows[words_count:],
        inward_total,
        outward_total,
        small_total[:bias_count],
        small_total[bias_count : bias_count + gain_count],
        expand_total,
        shrink_total,
        small_total[bias_count + gain_count :].reshape(2, per_shard * shard),
    )


def solution(mesh):
    sizes = (mesh.shape["rep"], mesh.shape["fsdp"])
    return jax.shard_map(
        paired if sizes == (4, 8) else functools.partial(general, mesh.shape["fsdp"]),
        mesh=mesh,
        in_specs=(
            P(("rep", "fsdp"), None),
            P(("rep", "fsdp"), None),
            P(("rep", "fsdp"), None),
            P(("rep", "fsdp"), None),
            P(None, "fsdp", None),
            P(None, "fsdp", None),
            P(None, "fsdp"),
            P(None, "fsdp"),
            P(None, "fsdp", None),
            P(None, "fsdp", None),
            P(None, "fsdp"),
            P(("rep", "fsdp"), None),
            P(("rep", "fsdp"), None),
        ),
        out_specs=(
            P(("rep", "fsdp"), None),
            P(("rep", "fsdp"), None),
            P(("rep", "fsdp"), None),
            P(("rep", "fsdp"), None),
            P(None, "fsdp", None),
            P(None, "fsdp", None),
            P(None, "fsdp"),
            P(None, "fsdp"),
            P(None, "fsdp", None),
            P(None, "fsdp", None),
            P(None, "fsdp"),
        ),
        check_vma=False,
    )
```

```python
import functools

import jax
import jax.numpy as jnp
from jax import lax
from jax.experimental import pallas as pl
from jax.experimental.pallas import tpu as pltpu
from jax.sharding import PartitionSpec as P

MESH = pl.DeviceIdType.MESH

HEADS = 12
HEAD_DIM = 64


norm_epsilon = 1e-12
masked_score = -1e30


def matmul(left_op, right_op):
    return jnp.dot(left_op, right_op, preferred_element_type=jnp.float32)


def matmul_tn(left_op, right_op):
    return lax.dot_general(
        left_op, right_op, (((0,), (0,)), ((), ())), preferred_element_type=jnp.float32
    )


def matmul_nt(left_op, right_op):
    return lax.dot_general(
        left_op, right_op, (((1,), (1,)), ((), ())), preferred_element_type=jnp.float32
    )


def column_sums(values):
    return jnp.sum(values, axis=0, dtype=jnp.float32)


def heads_of(rows_in):
    return rows_in.reshape(rows_in.shape[0], HEADS, HEAD_DIM)


def merge_heads(head_rows):
    return head_rows.reshape(head_rows.shape[0], -1)


def normalize(summed, gain_row, shift_row):
    center = summed - jnp.mean(summed, axis=-1, keepdims=True)
    inverse = lax.rsqrt(jnp.mean(center * center, axis=-1, keepdims=True) + norm_epsilon)
    normed = center * inverse
    return (normed * gain_row + shift_row, (normed, inverse))


def normalize_back(grad_out, norm_stats, gain_row):
    normed, inverse = norm_stats
    grad_normed = grad_out * gain_row
    grad_sum = inverse * (
        grad_normed
        - jnp.mean(grad_normed, axis=-1, keepdims=True)
        - normed * jnp.mean(grad_normed * normed, axis=-1, keepdims=True)
    )
    return (grad_sum, column_sums(grad_out * normed), column_sums(grad_out))


def score_block(queries, key_rows, allowed):
    scores = jnp.einsum(
        "qhd,khd->hqk", heads_of(queries), heads_of(key_rows), preferred_element_type=jnp.float32
    ) * HEAD_DIM ** (-0.5)
    return jnp.where(allowed[None], scores, masked_score)


def attend(queries, key_rows, value_rows, allowed):
    scores = score_block(queries, key_rows, allowed)
    top_score = jnp.max(scores, axis=-1, keepdims=True)
    log_total = top_score + jnp.log(jnp.sum(jnp.exp(scores - top_score), axis=-1, keepdims=True))
    shares = jnp.exp(scores - log_total).astype(jnp.bfloat16)
    context = jnp.einsum(
        "hqk,khd->qhd", shares, heads_of(value_rows), preferred_element_type=jnp.float32
    )
    return (merge_heads(context).astype(jnp.bfloat16), log_total)


def attend_back(queries, key_rows, value_rows, allowed, log_total, grad_context):
    shares = jnp.exp(score_block(queries, key_rows, allowed) - log_total)
    grad_heads = heads_of(grad_context)
    grad_shares = jnp.einsum(
        "qhd,khd->hqk", grad_heads, heads_of(value_rows), preferred_element_type=jnp.float32
    )
    grad_values = jnp.einsum(
        "hqk,qhd->khd", shares.astype(jnp.bfloat16), grad_heads, preferred_element_type=jnp.float32
    )
    grad_scores = (
        shares * (grad_shares - jnp.sum(shares * grad_shares, axis=-1, keepdims=True))
    ).astype(jnp.bfloat16)
    score_scale = HEAD_DIM ** (-0.5)
    grad_queries = (
        jnp.einsum(
            "hqk,khd->qhd", grad_scores, heads_of(key_rows), preferred_element_type=jnp.float32
        )
        * score_scale
    )
    grad_keys = (
        jnp.einsum(
            "hqk,qhd->khd", grad_scores, heads_of(queries), preferred_element_type=jnp.float32
        )
        * score_scale
    )
    return (merge_heads(grad_queries), merge_heads(grad_keys), merge_heads(grad_values))


def project(rows_low, weight, bias_rows, module):
    width = weight.shape[0]
    bias_all = jnp.concatenate(
        [bias_rows[3 * module], jnp.zeros((width,), jnp.float32), bias_rows[3 * module + 1]]
    )
    return (matmul(rows_low, weight) + bias_all).astype(jnp.bfloat16)


def project_back(grad_sum, grad_parts, rows_low, weight):
    width = weight.shape[0]
    grad_mixed = jnp.concatenate(grad_parts, axis=1).astype(jnp.bfloat16)
    grad_weight = (rows_low, grad_mixed)
    grad_bias = column_sums(grad_mixed)
    grad_rows = grad_sum + matmul_nt(grad_mixed, weight)
    return (grad_rows, grad_weight, grad_bias[:width], grad_bias[2 * width :])


def branch_back(grad_out, context, norm_stats, gain_row, outward_one):
    grad_sum, grad_gain, grad_shift = normalize_back(grad_out, norm_stats, gain_row)
    grad_branch = grad_sum.astype(jnp.bfloat16)
    grad_outward = (context, grad_branch)
    grad_context = matmul_nt(grad_branch, outward_one).astype(jnp.bfloat16)
    return (grad_sum, grad_context, grad_outward, column_sums(grad_branch), grad_gain, grad_shift)


def self_forward(rows_in, weights, module, allowed):
    inward_all, outward_all, bias_rows, gain_rows = weights
    width = rows_in.shape[1]
    rows_low = rows_in.astype(jnp.bfloat16)
    mixed = project(rows_low, inward_all[module], bias_rows, module)
    context, log_total = attend(
        mixed[:, :width], mixed[:, width : 2 * width], mixed[:, 2 * width :], allowed
    )
    summed = rows_in + matmul(context, outward_all[module]) + bias_rows[3 * module + 2]
    result, norm_stats = normalize(summed, gain_rows[module], bias_rows[9 + module])
    return (result, (rows_low, mixed, context, log_total, norm_stats))


def self_backward(grad_out, kept, weights, module, allowed):
    inward_all, outward_all, bias_rows, gain_rows = weights
    rows_low, mixed, context, log_total, norm_stats = kept
    width = rows_low.shape[1]
    grad_sum, grad_context, grad_outward, grad_bias_out, grad_gain, grad_shift = branch_back(
        grad_out, context, norm_stats, gain_rows[module], outward_all[module]
    )
    grad_parts = attend_back(
        mixed[:, :width],
        mixed[:, width : 2 * width],
        mixed[:, 2 * width :],
        allowed,
        log_total,
        grad_context,
    )
    grad_rows, grad_inward, grad_bias_query, grad_bias_value = project_back(
        grad_sum, grad_parts, rows_low, inward_all[module]
    )
    return (
        grad_rows,
        grad_inward,
        grad_outward,
        (grad_bias_query, grad_bias_value, grad_bias_out),
        grad_gain,
        grad_shift,
    )


def cross_forward(word_rows, region_rows, weights, cross_mask):
    inward_all, outward_all, bias_rows, gain_rows = weights
    words_count = word_rows.shape[0]
    width = word_rows.shape[1]
    rows_low = jnp.concatenate([word_rows, region_rows], axis=0)
    mixed = project(rows_low, inward_all[0], bias_rows, 0)
    word_mix = mixed[:words_count]
    region_mix = mixed[words_count:]
    word_context, word_total = attend(
        word_mix[:, :width],
        region_mix[:, width : 2 * width],
        region_mix[:, 2 * width :],
        cross_mask,
    )
    region_context, region_total = attend(
        region_mix[:, :width],
        word_mix[:, width : 2 * width],
        word_mix[:, 2 * width :],
        cross_mask.T,
    )
    context = jnp.concatenate([word_context, region_context], axis=0)
    summed = rows_low.astype(jnp.float32) + matmul(context, outward_all[0]) + bias_rows[2]
    result, norm_stats = normalize(summed, gain_rows[0], bias_rows[9])
    return (result, (rows_low, mixed, context, word_total, region_total, norm_stats))


def cross_backward(grad_out, kept, weights, cross_mask, words_count):
    inward_all, outward_all, bias_rows, gain_rows = weights
    rows_low, mixed, context, word_total, region_total, norm_stats = kept
    width = rows_low.shape[1]
    grad_sum, grad_context, grad_outward, grad_bias_out, grad_gain, grad_shift = branch_back(
        grad_out, context, norm_stats, gain_rows[0], outward_all[0]
    )
    word_mix = mixed[:words_count]
    region_mix = mixed[words_count:]
    word_query_grad, region_key_grad, region_value_grad = attend_back(
        word_mix[:, :width],
        region_mix[:, width : 2 * width],
        region_mix[:, 2 * width :],
        cross_mask,
        word_total,
        grad_context[:words_count],
    )
    region_query_grad, word_key_grad, word_value_grad = attend_back(
        region_mix[:, :width],
        word_mix[:, width : 2 * width],
        word_mix[:, 2 * width :],
        cross_mask.T,
        region_total,
        grad_context[words_count:],
    )
    grad_parts = (
        jnp.concatenate([word_query_grad, region_query_grad], axis=0),
        jnp.concatenate([word_key_grad, region_key_grad], axis=0),
        jnp.concatenate([word_value_grad, region_value_grad], axis=0),
    )
    grad_rows, grad_inward, grad_bias_query, grad_bias_value = project_back(
        grad_sum, grad_parts, rows_low, inward_all[0]
    )
    return (
        grad_rows,
        grad_inward,
        grad_outward,
        (grad_bias_query, grad_bias_value, grad_bias_out),
        grad_gain,
        grad_shift,
    )


def gelu_exact(values):
    return jax.nn.gelu(values, approximate=False)


def feed_forward(rows_in, weights, feed_index, attend_set):
    expand_all, shrink_all, hidden_all = weights
    bias_rows, gain_rows = (attend_set[2], attend_set[3])
    rows_low = rows_in.astype(jnp.bfloat16)
    before = matmul(rows_low, expand_all[feed_index]) + hidden_all[feed_index].astype(jnp.float32)
    hidden = gelu_exact(before).astype(jnp.bfloat16)
    summed = rows_in + matmul(hidden, shrink_all[feed_index]) + bias_rows[14 + feed_index]
    result, norm_stats = normalize(summed, gain_rows[3 + feed_index], bias_rows[12 + feed_index])
    return (result, (rows_low, before, hidden, norm_stats))


def feed_backward(grad_out, kept, weights, feed_index, gain_rows):
    expand_all, shrink_all, hidden_all = weights
    rows_low, before, hidden, norm_stats = kept
    grad_sum, grad_gain, grad_shift = normalize_back(
        grad_out, norm_stats, gain_rows[3 + feed_index]
    )
    grad_branch = grad_sum.astype(jnp.bfloat16)
    grad_shrink = (hidden, grad_branch)
    grad_hidden = matmul_nt(grad_branch, shrink_all[feed_index])
    unused_value, slope_back = jax.vjp(gelu_exact, before)
    grad_before = slope_back(grad_hidden)[0].astype(jnp.bfloat16)
    grad_expand = (rows_low, grad_before)
    grad_rows = grad_sum + matmul_nt(grad_before, expand_all[feed_index])
    return (
        grad_rows,
        grad_expand,
        grad_shrink,
        column_sums(grad_before),
        column_sums(grad_branch),
        grad_gain,
        grad_shift,
    )


UNIT = 96
WIDE = 768
SLOTS = 6
ACC_SLOTS = 9
LAG_CORE = 2
LAG_A = 3
LAG_B = 3
LAG_Z = 3
SHRINK_QUARTERED = 256
OWNED_SHRINK_AT = 5
OWNED_EXPAND_AT = 10
WORDS = 128
REGIONS = 256
ROWS = 384
HIDDEN = 3072
SLICE = HIDDEN // 8
PLANE_WORDS = 8 * WORDS
PAIRS_OF_HEADS = 6
PAIR_WIDE = 128
LOW, F32 = jnp.bfloat16, jnp.float32

X, Y, DIAG_Y, DIAG_X, CORE_OWN, CORE_X, CORE_Y, CORE_DIAG = range(8)


def flip(position, bits):
    return lax.bitwise_xor(position, bits)


def remote(src, dst, send_sem, recv_sem, peer):
    return pltpu.make_async_remote_copy(
        src_ref=src, dst_ref=dst, send_sem=send_sem, recv_sem=recv_sem, device_id=peer, device_id_type=MESH
    )


def greet(me, z):
    barrier = pltpu.get_barrier_semaphore()
    for offset in range(1, 8):
        pl.semaphore_signal(barrier, inc=1, device_id={"fsdp": flip(me, offset)}, device_id_type=MESH)
    for offset in range(1, 4):
        pl.semaphore_signal(barrier, inc=1, device_id={"rep": (z + offset) % 4}, device_id_type=MESH)
    pl.semaphore_wait(barrier, 10)


def route(me, kind, arriving):
    owner, half, step = {
        X: (2 if arriving else 0, None, 2),
        Y: (4 if arriving else 0, None, 4),
        DIAG_Y: (6 if arriving else 2, 0, 4),
        DIAG_X: (6 if arriving else 4, 1, 2),
        CORE_OWN: (1 if arriving else 0, None, 1),
        CORE_X: (3 if arriving else 2, None, 1),
        CORE_Y: (5 if arriving else 4, None, 1),
        CORE_DIAG: (7 if arriving else 6, None, 1),
    }[kind]
    return flip(me, owner), half, {"fsdp": flip(me, step)}


class RowGather:
    def __init__(self, me, rows, sends, recvs):
        self.me, self.rows, self.sends, self.recvs = me, rows, sends, recvs

    def copy(self, kind, arriving=False):
        owner, half, peer = route(self.me, kind, arriving)
        first, count = (owner * WORDS, WORDS) if half is None else (owner * WORDS + half * (WORDS // 2), WORDS // 2)
        here = self.rows.at[pl.ds(pl.multiple_of(first, 16), count), :]
        return remote(here, here, self.sends.at[kind], self.recvs.at[kind], peer)

    def start(self):
        for kind in (X, Y, CORE_OWN):
            self.copy(kind).start()

    def first(self):
        self.copy(X, True).wait_recv()
        self.copy(DIAG_Y).start()
        self.copy(CORE_X).start()
        self.copy(Y, True).wait_recv()
        self.copy(DIAG_X).start()
        self.copy(CORE_Y).start()

    def second(self):
        self.copy(DIAG_Y, True).wait_recv()
        self.copy(DIAG_X, True).wait_recv()
        self.copy(CORE_DIAG).start()

    def complete(self):
        for kind in (CORE_OWN, CORE_X, CORE_Y, CORE_DIAG):
            self.copy(kind, True).wait_recv()

    def settle(self):
        for kind in range(8):
            self.copy(kind).wait_send()


class RowSum:
    def __init__(self, me, partial, core_out, core_in, half_out, half_in, full_out, full_in, sends, recvs):
        self.me, self.partial, self.sends, self.recvs = me, partial, sends, recvs
        self.core_out, self.core_in = core_out, core_in
        self.half_out, self.half_in, self.full_out, self.full_in = half_out, half_in, full_out, full_in
        self.chip, self.lane = me // 2, me % 2

    def copy(self, at):
        if at == 0:
            source, target, peer = self.core_out, self.core_in, 1
        elif at < 3:
            source, target, peer = self.half_out.at[at - 1], self.half_in.at[at - 1], (2, 4)[at - 1]
        else:
            source, target, peer = self.full_out.at[at - 3], self.full_in.at[at - 3], (2, 4)[at - 3]
        return remote(source, target, self.sends.at[at], self.recvs.at[at], {"fsdp": flip(self.me, peer)})

    def start(self):
        for block in range(4):
            self.core_out[block] = self.partial[2 * block + 1 - self.lane].astype(LOW)
        self.copy(0).start()

    def joined(self, block):
        return self.partial[2 * block + self.lane] + self.core_in[block].astype(F32)

    def cores(self):
        self.copy(0).wait()
        half = WORDS // 2
        summed = self.joined(flip(self.chip, 3))
        self.half_out[0] = summed[:half].astype(LOW)
        self.half_out[1] = summed[half:].astype(LOW)
        for way in range(2):
            self.copy(1 + way).start()

    def diagonal(self):
        half = WORDS // 2
        for way in range(2):
            self.copy(1 + way).wait()
        for way, side in ((1, 0), (0, 1)):
            summed = self.joined(flip(self.chip, 1 + way))
            at, other = (slice(0, half), slice(half, WORDS)) if side == 0 else (slice(half, WORDS), slice(0, half))
            self.full_out[way, at] = (summed[at] + self.half_in[side].astype(F32)).astype(LOW)
            self.full_out[way, other] = summed[other].astype(LOW)
            self.copy(3 + way).start()

    def total(self):
        for way in range(2):
            self.copy(3 + way).wait()
        return self.joined(self.chip) + (self.full_in[0].astype(F32) + self.full_in[1].astype(F32))


def row_sum_scratch():
    half, whole = (2, WORDS // 2, WIDE), (2, WORDS, WIDE)
    return [
        pltpu.VMEM((8, WORDS, WIDE), F32),
        pltpu.VMEM((4, WORDS, WIDE), LOW),
        pltpu.VMEM((4, WORDS, WIDE), LOW),
        pltpu.VMEM(half, LOW),
        pltpu.VMEM(half, LOW),
        pltpu.VMEM(whole, LOW),
        pltpu.VMEM(whole, LOW),
        pltpu.SemaphoreType.DMA((5,)),
        pltpu.SemaphoreType.DMA((5,)),
    ]


def dot_nt(left, right):
    return lax.dot_general(left, right, (((1,), (1,)), ((), ())), preferred_element_type=jnp.float32)


def dot_tn(left, right):
    return lax.dot_general(left, right, (((0,), (0,)), ((), ())), preferred_element_type=jnp.float32)


def spread(part):
    source = lax.broadcasted_iota(jnp.int32, (128, WIDE), 0)
    target = lax.broadcasted_iota(jnp.int32, (128, WIDE), 1)
    return jnp.logical_and(source < UNIT, target == source + part * UNIT)


def half_lanes():
    lane = lax.broadcasted_iota(jnp.int32, (1, PAIR_WIDE), 1)
    return (lane < HEAD_DIM, lane >= HEAD_DIM)


def only(values, chosen):
    return jnp.where(chosen, values, jnp.zeros_like(values))


ATTEND_CROSS_WORD = ((0, WORDS), (WORDS, REGIONS))
ATTEND_CROSS_REGION = ((WORDS, REGIONS), (0, WORDS))
ATTEND_WORD = ((0, WORDS), (0, WORDS))
ATTEND_REGION = ((WORDS, REGIONS), (WORDS, REGIONS))


def attend_into(rows_of, mixed, allowed, shares, context):
    (query_at, query_count), (key_at, key_count) = rows_of
    blocked = jnp.where(allowed, 0.0, masked_score)

    def pair(p, carry):
        at = pl.multiple_of(p * PAIR_WIDE, PAIR_WIDE)
        queries = mixed[pl.ds(query_at, query_count), pl.ds(at, PAIR_WIDE)]
        key_rows = mixed[pl.ds(key_at, key_count), pl.ds(WIDE + at, PAIR_WIDE)]
        value_rows = mixed[pl.ds(key_at, key_count), pl.ds(2 * WIDE + at, PAIR_WIDE)]
        total = jnp.zeros((query_count, PAIR_WIDE), jnp.float32)
        for side, chosen in enumerate(half_lanes()):
            scores = dot_nt(only(queries, chosen), key_rows) * HEAD_DIM ** (-0.5) + blocked
            lifted = jnp.exp(scores - jnp.max(scores, axis=-1, keepdims=True))
            share = (lifted / jnp.sum(lifted, axis=-1, keepdims=True)).astype(jnp.bfloat16)
            shares[2 * p + side] = share
            total = total + matmul(share, only(value_rows, chosen))
        context[pl.ds(query_at, query_count), pl.ds(at, PAIR_WIDE)] = total.astype(jnp.bfloat16)
        return carry

    lax.fori_loop(0, PAIRS_OF_HEADS, pair, 0)


def row_norm(summed):
    center = summed - jnp.mean(summed, axis=-1, keepdims=True)
    inverse = lax.rsqrt(jnp.mean(center * center, axis=-1, keepdims=True) + norm_epsilon)
    return (center * inverse, inverse)


def down(across):
    wide = jnp.broadcast_to(across.astype(jnp.float32), (128, across.shape[1]))
    return jnp.concatenate([wide[:, at : at + 128].T[:, :1] for at in range(0, across.shape[1], 128)], axis=0)


SAVED = (
    ((24, WIDE), F32),
    ((3, ROWS, WIDE), F32),
    ((3, ROWS, 128), F32),
    ((HIDDEN, REGIONS), LOW),
    ((REGIONS, HIDDEN), LOW),
    ((WIDE, REGIONS), LOW),
    ((PLANE_WORDS, SLICE), LOW),
    ((WIDE, SLICE), LOW),
    ((SLICE, PLANE_WORDS), LOW),
    ((WIDE, PLANE_WORDS), LOW),
    ((WIDE, ROWS), LOW),
    ((ROWS, 3 * WIDE), LOW),
    ((HEADS, WORDS, WORDS), LOW),
    ((HEADS, REGIONS, REGIONS), LOW),
    ((WIDE, ROWS), LOW),
    ((WIDE, ROWS), LOW),
    ((ROWS, 3 * WIDE), LOW),
    ((HEADS, WORDS, REGIONS), LOW),
    ((HEADS, REGIONS, WORDS), LOW),
    ((WIDE, ROWS), LOW),
)
WEIGHTS = (
    (3, WIDE, 3 * WIDE),
    (3, WIDE, WIDE),
    (1, WIDE, HIDDEN),
    (1, HIDDEN, WIDE),
)

INWARD, OUTWARD, EXPAND, SHRINK, BOTH = range(5)
GATHERED = ((2, WIDE, 3 * WIDE), (2, WIDE, WIDE), (1, WIDE, HIDDEN), (1, HIDDEN, WIDE), (1, WIDE, 4 * WIDE))

CHUNKS = (
    (BOTH, 0, (0, UNIT), True),
    (INWARD, 0, (0, UNIT), False),
    (OUTWARD, 0, (0, UNIT), False),
    (EXPAND, 0, (0, UNIT), True),
    (INWARD, 1, (0, UNIT), False),
    (OUTWARD, 1, (0, UNIT), False),
    (SHRINK, 0, (0, SHRINK_QUARTERED), True),
    (SHRINK, 0, (SHRINK_QUARTERED, 4 * UNIT - SHRINK_QUARTERED), False),
)
BOTH_2, INWARD_0, OUTWARD_0, EXPAND_1, INWARD_1, OUTWARD_1, SHRINK_1, SHRINK_REST = range(len(CHUNKS))


def forward_kernel(*refs):
    word_rows, region_rows, word_ids, region_ids, biases, gains, hidden_bias, *shards = refs[:11]
    word_result, region_result, *kept = refs[11:33]
    weights_kept = refs[33:37]
    (
        params,
        normed,
        inverse,
        hidden_t,
        slope,
        rows_two_t,
        slope_words,
        expand_words,
        hidden_words_t,
        rows_two_words_t,
        context_self_t,
        mixed_self,
        shares_w,
        shares_r,
        rows_one_t,
        context_cross_t,
        mixed_cross,
        shares_cw,
        shares_cr,
        rows_zero_t,
    ) = saved = refs[37:57]
    inward_all, outward_all, expand_all, shrink_all, both_all = gathered = refs[57:62]
    (
        small_own,
        small_all,
        hidden_rows,
        rows_low,
        stream,
        stream_low,
        context,
        hidden,
        words_two,
        hidden_words,
        shrink_words,
        partial,
        core_out,
        core_in,
        half_out,
        half_in,
        full_out,
        full_in,
        sum_sends,
        sum_recvs,
        gather_sends,
        gather_recvs,
        slice_sends,
        slice_recvs,
        sends,
        recvs,
        z_sends,
        z_recvs,
        foreign_sends,
        foreign_recvs,
        small_sends,
        small_recvs,
        local_sems,
        keep_sems,
    ) = refs[62:]
    me = lax.axis_index("fsdp")
    z = lax.axis_index("rep")
    above, below = {"rep": (z + 1) % 4}, {"rep": (z + 3) % 4}
    gather_words = RowGather(me, words_two, gather_sends, gather_recvs)
    sum_words = RowSum(
        me, partial, core_out, core_in, half_out, half_in, full_out, full_in, sum_sends, sum_recvs
    )
    def small_copy(offset, owner):
        return remote(
            small_all.at[owner],
            small_all.at[owner],
            small_sends.at[offset - 1],
            small_recvs.at[offset - 1],
            {"fsdp": flip(me, offset)},
        )

    def place(k, owner, half=None, quarter=None):
        kind, _, (first, count), _ = CHUNKS[k]
        shard_rows = GATHERED[kind][1] // 8
        column, columns = 0, GATHERED[kind][2]
        if quarter is not None and kind == SHRINK:
            count = count // 4
            first = first + quarter * count
        elif quarter is not None:
            columns = columns // 4
            column = quarter * columns
        if half is not None:
            count = count // 2
            first = first + half * count
        if not isinstance(column, int):
            column = pl.multiple_of(column, WIDE)
        if not isinstance(first, int):
            first = pl.multiple_of(first, 16)
        whole = pl.multiple_of(owner * shard_rows + first, 16)
        return pl.ds(whole, count), pl.ds(first, count), pl.ds(column, columns)

    def own_part(k, quarter=None):
        kind, index, _, _ = CHUNKS[k]
        if kind == BOTH:
            return part(k, me, None, quarter)
        _, rows, columns = place(k, me, None, quarter)
        return shards[kind].at[index + (1 if kind in (EXPAND, SHRINK) else 0), rows, columns]

    def part(k, owner, half=None, quarter=None):
        kind, index, _, _ = CHUNKS[k]
        rows, _, columns = place(k, owner, half, quarter)
        return gathered[kind].at[index, rows, columns]

    def mine(k):
        return z if CHUNKS[k][3] else None

    def copy(k, kind, arriving=False):
        owner, half, peer = route(me, kind, arriving)
        quarter = None if kind == CORE_OWN else mine(k)
        target = part(k, owner, half, quarter)
        source = own_part(k, quarter) if kind in (X, Y, CORE_OWN) and not arriving else target
        return remote(source, target, sends.at[k, kind], recvs.at[k, kind], peer)

    z_chunks = [k for k in range(len(CHUNKS)) if CHUNKS[k][3]]
    owners = (flip(me, 2), flip(me, 4), flip(me, 6))
    core_owners = (flip(me, 3), flip(me, 5), flip(me, 7))

    def z_copy(k, way, hop, which, arriving=False):
        steps = hop + 1 if arriving else hop
        quarter = z - steps if way == 0 else z + steps
        here = part(k, owners[which], None, quarter)
        at = (z_chunks.index(k), way, hop, which)
        return remote(here, here, z_sends.at[at], z_recvs.at[at], (above, below)[way])

    def foreign_copy(k, way, hop, which, arriving=False):
        quarter = z - hop - 1 if way == 0 else z + hop + 1
        here = part(k, (core_owners if arriving else owners)[which], None, quarter)
        at = (z_chunks.index(k), way, hop, which)
        return remote(here, here, foreign_sends.at[at], foreign_recvs.at[at], {"fsdp": flip(me, 1)})

    def goes(way, hop):
        return jnp.logical_and(z >= hop, z < 3) if way == 0 else jnp.logical_and(z <= 3 - hop, z > 0)

    def comes(way, hop):
        return z >= hop + 1 if way == 0 else z <= 2 - hop

    def send_z(k, hop, which):
        for way in range(2):

            @pl.when(goes(way, hop))
            def _(way=way):
                for one in which:
                    z_copy(k, way, hop, one).start()

    def own_local(k):
        return pltpu.make_async_copy(own_part(k), part(k, me), local_sems.at[k])

    def own_both(kind):
        rows, columns = pl.ds(pl.multiple_of(me * UNIT, UNIT), UNIT), pl.ds(3 * WIDE * kind, (3 * WIDE, WIDE)[kind])
        return pltpu.make_async_copy(
            shards[kind].at[2], both_all.at[0, rows, columns], local_sems.at[len(CHUNKS) + 2 + kind]
        )

    def own(k):
        for kind in (X, Y):
            copy(k, kind).start()
        if CHUNKS[k][0] != BOTH:
            own_local(k).start()
        copy(k, CORE_OWN).start()

    def pass_first(k):
        copy(k, X, True).wait_recv()
        copy(k, DIAG_Y).start()
        copy(k, Y, True).wait_recv()
        copy(k, DIAG_X).start()
        if k in z_chunks:
            send_z(k, 0, (0, 1))
        copy(k, CORE_X).start()
        copy(k, CORE_Y).start()

    def pass_second(k):
        copy(k, DIAG_Y, True).wait_recv()
        copy(k, DIAG_X, True).wait_recv()
        if k in z_chunks:
            send_z(k, 0, (2,))
        copy(k, CORE_DIAG).start()

    def pass_quarter(k, hop):
        for way in range(2):

            @pl.when(comes(way, hop))
            def _(way=way):
                for which in range(3):
                    z_copy(k, way, hop, which, True).wait_recv()

        if hop < 2:
            send_z(k, hop + 1, (0, 1, 2))
        for way in range(2):

            @pl.when(comes(way, hop))
            def _(way=way):
                for which in range(3):
                    foreign_copy(k, way, hop, which).start()

    def complete(k):
        if CHUNKS[k][0] != BOTH:
            own_local(k).wait()
        for kind in (CORE_OWN, CORE_X, CORE_Y, CORE_DIAG):
            copy(k, kind, True).wait_recv()
        if k in z_chunks:
            for hop in range(3):
                for way in range(2):

                    @pl.when(comes(way, hop))
                    def _(way=way, hop=hop):
                        for which in range(3):
                            foreign_copy(k, way, hop, which, True).wait_recv()

    def slice_copy(offset, arriving=False):
        peer = flip(me, offset)
        rows = pl.ds(pl.multiple_of((peer if arriving else me) * UNIT, UNIT), UNIT)
        target = expand_words.at[rows, :]
        source = shards[2].at[0, :, pl.ds(pl.multiple_of(peer * SLICE, SLICE), SLICE)]
        return remote(source, target, slice_sends.at[offset - 1], slice_recvs.at[offset - 1], {"fsdp": peer})

    own_slice = pltpu.make_async_copy(
        shards[2].at[0, :, pl.ds(pl.multiple_of(me * SLICE, SLICE), SLICE)],
        expand_words.at[pl.ds(pl.multiple_of(me * UNIT, UNIT), UNIT), :],
        local_sems.at[len(CHUNKS)],
    )
    own_shrink = pltpu.make_async_copy(shards[3].at[0], shrink_words, local_sems.at[len(CHUNKS) + 1])

    def start_slices():
        own_slice.start()
        own_shrink.start()
        for offset in range(1, 8):
            slice_copy(offset).start()

    def wait_slices():
        own_slice.wait()
        own_shrink.wait()
        for offset in range(1, 8):
            slice_copy(offset, True).wait_recv()

    keeps = []

    def keep(source, target):
        copied = pltpu.make_async_copy(source, target, keep_sems.at[len(keeps)])
        copied.start()
        keeps.append(copied)

    def keep_weights(kind, index):
        keep(gathered[kind].at[index], weights_kept[kind].at[index])

    def keep_both():
        keep(both_all.at[0, :, 0 : 3 * WIDE], weights_kept[INWARD].at[2])
        keep(both_all.at[0, :, 3 * WIDE : 4 * WIDE], weights_kept[OUTWARD].at[2])

    def keep_saved(*refs_done):
        for done in refs_done:
            index = [ref is done for ref in saved].index(True)
            keep(saved[index], kept[index])

    def give_small():
        small_own[...] = jnp.zeros_like(small_own)
        small_own[0:16, 0:UNIT] = biases[...].astype(F32)
        small_own[16:21, 0:UNIT] = gains[...].astype(F32)
        source = lax.broadcasted_iota(jnp.int32, (4 * UNIT, 128), 0)
        target = lax.broadcasted_iota(jnp.int32, (4 * UNIT, 128), 1)
        for q in range(4):
            chosen = jnp.logical_and(target < UNIT, source == target + q * UNIT).astype(LOW)
            placed = matmul(hidden_bias[...], chosen)
            for f in range(2):
                row = 21 + 4 * f + q
                small_own[row : row + 1, :] = placed[f : f + 1]
        small_all[me] = small_own[...].astype(LOW)
        for offset in range(1, 8):
            small_copy(offset, me).start()

    def read_small():
        for offset in range(1, 8):
            small_copy(offset, flip(me, offset)).wait_recv()
        totals = jnp.zeros((21, WIDE), jnp.float32)
        hidden_parts = [jnp.zeros((1, WIDE), jnp.float32) for _ in range(4)]
        for owner in range(8):
            one = small_all[owner]
            totals = totals + matmul(one, spread(owner).astype(LOW))[:21]
            for q in range(4):
                placed = matmul(one, spread((owner % 2) * 4 + q).astype(LOW))
                row = 25 + q
                hidden_parts[owner // 2] = hidden_parts[owner // 2] + placed[row : row + 1]
        params[...] = jnp.zeros_like(params)
        params[0:21, :] = totals
        for block in range(4):
            hidden_rows[:, block * WIDE : (block + 1) * WIDE] = hidden_parts[block]
        keep_saved(params)

    def read_rows():
        rows_low[0:WORDS, :] = word_rows[...]
        rows_low[WORDS:ROWS, :] = region_rows[...]
        for at in range(0, ROWS, 128):
            transposed_into(rows_zero_t, rows_low[at : at + 128, :], at, 128)
        keep_saved(rows_zero_t)

    def transposed_into(target, values, at, count):
        target[:, pl.ds(at, count)] = values.T

    def project_into(source, at, count, module, mixed, weights):
        for third, bias_row in enumerate((3 * module, None, 3 * module + 1)):
            product = matmul(source[pl.ds(at, count), :], weights[:, third * WIDE : (third + 1) * WIDE])
            if bias_row is not None:
                product = product + params[bias_row : bias_row + 1, :]
            mixed[pl.ds(at, count), third * WIDE : (third + 1) * WIDE] = product.astype(jnp.bfloat16)

    def join(at, product, residual, bias_row, norm_at, norm_index):
        rows = pl.ds(at, 128)
        unit, scale = row_norm(residual + product + params[bias_row : bias_row + 1, :])
        normed[norm_at, rows, :] = unit
        inverse[norm_at, rows, :] = jnp.broadcast_to(scale, (128, 128))
        return unit * params[16 + norm_index : 17 + norm_index, :] + params[9 + norm_index : 10 + norm_index, :]

    def cross_in():
        project_into(rows_low, 0, ROWS, 0, mixed_cross, inward_all.at[0])
        keep_saved(mixed_cross)
        keep_weights(0, 0)

    def cross_words():
        allowed = down(word_ids[...]) == region_ids[...].astype(F32)
        attend_into(ATTEND_CROSS_WORD, mixed_cross, allowed, shares_cw, context)
        keep_saved(shares_cw)

    def cross_regions():
        allowed = down(region_ids[...]) == word_ids[...].astype(F32)
        attend_into(ATTEND_CROSS_REGION, mixed_cross, allowed, shares_cr, context)
        keep_saved(shares_cr)

    def cross_out():
        for at in range(0, ROWS, 128):
            product = matmul(context[at : at + 128, :], outward_all[0])
            one = join(at, product, rows_low[at : at + 128, :].astype(F32), 2, 0, 0)
            stream[at : at + 128, :] = one
            one_low = one.astype(LOW)
            stream_low[at : at + 128, :] = one_low
            transposed_into(rows_one_t, one_low, at, 128)
            transposed_into(context_cross_t, context[at : at + 128, :], at, 128)
        keep_saved(rows_one_t, context_cross_t)
        keep_weights(1, 0)

    def word_in():
        project_into(stream_low, 0, WORDS, 1, mixed_self, inward_all.at[1])
        keep_weights(0, 1)
        allowed = down(word_ids[...]) == word_ids[...].astype(F32)
        attend_into(ATTEND_WORD, mixed_self, allowed, shares_w, context)
        transposed_into(context_self_t, context[0:WORDS, :], 0, WORDS)
        keep_saved(shares_w)

    def region_in():
        project_into(stream_low, WORDS, REGIONS, 2, mixed_self, both_all.at[0])
        keep_both()

    def region_attend():
        allowed = down(region_ids[...]) == region_ids[...].astype(F32)
        attend_into(ATTEND_REGION, mixed_self, allowed, shares_r, context)
        for at in range(WORDS, ROWS, 128):
            transposed_into(context_self_t, context[at : at + 128, :], at, 128)
        keep_saved(shares_r)

    def self_out(module, first, last):
        for at in range(first, last, 128):
            weights = outward_all[1] if module == 1 else both_all[0, :, 3 * WIDE : 4 * WIDE]
            product = matmul(context[at : at + 128, :], weights)
            two = join(at, product, stream[at : at + 128, :], 3 * module + 2, 1, module)
            stream[at : at + 128, :] = two
            two_low = two.astype(LOW)
            stream_low[at : at + 128, :] = two_low
            if module == 1:
                words_two[pl.ds(pl.multiple_of(me * WORDS, WORDS), WORDS), :] = two_low
            else:
                transposed_into(rows_two_t, two_low, at - WORDS, 128)
        if module == 1:
            keep_weights(OUTWARD, 1)

    def activate(before, hidden_to, hidden_t_to, slope_to):
        below = 0.5 * (1.0 + lax.erf(before * 0.5**0.5))
        density = jnp.exp(-0.5 * before * before) * 0.3989422804014327
        value = (before * below).astype(LOW)
        hidden_to[...] = value
        hidden_t_to[...] = value.T
        slope_to[...] = (below + before * density).astype(LOW)

    def feed_in(column, columns):
        step = 256

        def tile(t, carry):
            at = pl.ds(pl.multiple_of(column + t * step, step), step)
            for row in range(0, REGIONS, 128):
                rows = slice(row, row + 128)
                before = matmul(stream_low[WORDS + row : WORDS + row + 128, :], expand_all[0, :, at])
                activate(before + hidden_rows[:, at], hidden.at[rows, at], hidden_t.at[at, rows], slope.at[rows, at])
            return carry

        lax.fori_loop(0, columns // step, tile, 0)

    def feed_out():
        for at in range(WORDS, ROWS, 128):
            product = matmul(hidden[at - WORDS : at - WORDS + 128, :], shrink_all[0])
            last_rows = join(at, product, stream[at : at + 128, :], 15, 2, 4)
            region_result[at - WORDS : at - WORDS + 128, :] = last_rows.astype(LOW)

    def words_in():
        for at in range(0, PLANE_WORDS, 128):
            rows = slice(at, at + 128)
            before = matmul(words_two[rows, :], expand_words[...]) + hidden_bias[0:1, :].astype(F32)
            activate(before, hidden_words.at[rows, :], hidden_words_t.at[:, rows], slope_words.at[rows, :])
            rows_two_words_t[:, rows] = words_two[rows, :].T
        keep_saved(slope_words, expand_words, hidden_words_t, rows_two_words_t)

    def words_out():
        for at in range(0, PLANE_WORDS, 128):
            partial[at // 128] = matmul(hidden_words[at : at + 128, :], shrink_words[...])
        sum_words.start()

    def words_last():
        last_rows = join(0, sum_words.total(), stream[0:WORDS, :], 14, 2, 3)
        word_result[...] = last_rows.astype(LOW)

    for kind in range(2):
        own_both(kind).start()
    greet(me, z)
    for kind in range(2):
        own_both(kind).wait()
    own(BOTH_2)
    give_small()
    read_rows()
    pass_first(BOTH_2)
    own(INWARD_0)
    own(OUTWARD_0)
    read_small()
    pass_second(BOTH_2)
    pass_first(INWARD_0)
    own(EXPAND_1)
    pass_quarter(BOTH_2, 0)
    pass_first(OUTWARD_0)
    own(INWARD_1)
    pass_second(INWARD_0)
    pass_quarter(BOTH_2, 1)
    complete(INWARD_0)
    cross_in()
    pass_second(OUTWARD_0)
    pass_first(EXPAND_1)
    own(OUTWARD_1)
    cross_words()
    pass_second(EXPAND_1)
    cross_regions()
    pass_quarter(BOTH_2, 2)
    complete(OUTWARD_0)
    cross_out()
    pass_first(INWARD_1)
    own(SHRINK_1)
    complete(BOTH_2)
    region_in()
    pass_quarter(EXPAND_1, 0)
    region_attend()
    pass_second(INWARD_1)
    pass_first(OUTWARD_1)
    start_slices()
    complete(INWARD_1)
    word_in()
    keep_saved(mixed_self, context_self_t)
    pass_second(OUTWARD_1)
    pass_first(SHRINK_1)
    complete(OUTWARD_1)
    self_out(1, 0, WORDS)
    gather_words.start()
    own(SHRINK_REST)
    pass_quarter(EXPAND_1, 1)
    pass_second(SHRINK_1)
    self_out(2, WORDS, ROWS)
    keep_saved(rows_two_t)
    gather_words.first()
    pass_quarter(EXPAND_1, 2)
    gather_words.second()
    wait_slices()
    pass_first(SHRINK_REST)
    gather_words.complete()
    words_in()
    words_out()
    complete(EXPAND_1)
    keep_weights(2, 0)
    pass_quarter(SHRINK_1, 0)
    feed_in(0, 2 * WIDE)
    pass_second(SHRINK_REST)
    sum_words.cores()
    pass_quarter(SHRINK_1, 1)
    feed_in(2 * WIDE, WIDE)
    sum_words.diagonal()
    feed_in(3 * WIDE, WIDE)
    keep_saved(hidden_t, slope)
    pass_quarter(SHRINK_1, 2)
    words_last()
    complete(SHRINK_REST)
    complete(SHRINK_1)
    keep_weights(3, 0)
    feed_out()
    keep_saved(normed, inverse)
    for copied in keeps:
        copied.wait()
    for offset in range(1, 8):
        small_copy(offset, me).wait_send()
        slice_copy(offset).wait_send()
    gather_words.settle()
    for k in range(len(CHUNKS)):
        for kind in range(8):
            copy(k, kind).wait_send()
    for k in z_chunks:
        for way in range(2):
            for hop in range(3):

                @pl.when(goes(way, hop))
                def _(k=k, way=way, hop=hop):
                    for which in range(3):
                        z_copy(k, way, hop, which).wait_send()

                @pl.when(comes(way, hop))
                def _(k=k, way=way, hop=hop):
                    for which in range(3):
                        foreign_copy(k, way, hop, which).wait_send()


def forward(word_rows, region_rows, word_ids, region_ids, biases, gains, hidden_bias, shards):
    dma = pltpu.SemaphoreType.DMA
    vmem = pl.BlockSpec(memory_space=pltpu.VMEM)
    hbm = pl.BlockSpec(memory_space=pl.ANY)
    saved = [jax.ShapeDtypeStruct(*one) for one in SAVED]
    weights = [jax.ShapeDtypeStruct(one, LOW) for one in WEIGHTS]
    quarters = (sum(chunk[3] for chunk in CHUNKS), 2, 3, 3)
    outs = pl.pallas_call(
        forward_kernel,
        out_shape=[jax.ShapeDtypeStruct((WORDS, WIDE), LOW), jax.ShapeDtypeStruct((REGIONS, WIDE), LOW)] + saved + weights,
        in_specs=[vmem] * 7 + [hbm] * 4,
        out_specs=[vmem] * 2 + [hbm] * (len(saved) + len(weights)),
        scratch_shapes=[pltpu.VMEM(one.shape, one.dtype) for one in saved]
        + [pltpu.VMEM(one, LOW) for one in GATHERED]
        + [
            pltpu.VMEM((32, 128), F32),
            pltpu.VMEM((8, 32, 128), LOW),
            pltpu.VMEM((1, HIDDEN), F32),
            pltpu.VMEM((ROWS, WIDE), LOW),
            pltpu.VMEM((ROWS, WIDE), F32),
            pltpu.VMEM((ROWS, WIDE), LOW),
            pltpu.VMEM((ROWS, WIDE), LOW),
            pltpu.VMEM((REGIONS, HIDDEN), LOW),
            pltpu.VMEM((PLANE_WORDS, WIDE), LOW),
            pltpu.VMEM((PLANE_WORDS, SLICE), LOW),
            pltpu.VMEM((SLICE, WIDE), LOW),
            *row_sum_scratch(),
            dma((8,)),
            dma((8,)),
            dma((7,)),
            dma((7,)),
            dma((len(CHUNKS), 8)),
            dma((len(CHUNKS), 8)),
            dma(quarters),
            dma(quarters),
            dma(quarters),
            dma(quarters),
            dma((7,)),
            dma((7,)),
            dma((len(CHUNKS) + 4,)),
            dma((len(saved) + 8,)),
        ],
        compiler_params=pltpu.CompilerParams(
            collective_id=1, has_side_effects=True, vmem_limit_bytes=64 * 2**20 - 2**16
        ),
    )(word_rows, region_rows, word_ids, region_ids, biases, gains, hidden_bias, *shards)
    return outs[:2], outs[2 : 2 + len(saved)], outs[2 + len(saved) :]


WINDOW = 6
SPAN = WIDE // 2
Z_SLOTS = 10

GROUPS = (
    (8, None, 0, 0, True, (3, 0)),
    (8, None, 0, 0, False, (2, 0)),
    (8, 0, 0, REGIONS, True, (3, 1)),
    (8, 1, 0, REGIONS, False, (2, 1)),
    (2, 2, 0, WORDS, False, (1, 1)),
    (2, 2, WORDS, REGIONS, False, (1, 2)),
    (6, 3, 0, WORDS, False, (0, 1)),
    (6, 3, WORDS, REGIONS, False, (0, 2)),
    (2, 4, 0, ROWS, False, (1, 0)),
    (6, 5, 0, ROWS, False, (0, 0)),
)
UNITS = sum(group[0] for group in GROUPS)
OWNED = sum(group[0] for group in GROUPS if group[1] is None)
CROSSING = UNITS - OWNED

BLOCKS = (
    [(kind, 0, c) for c in range(4) for kind in (3, 2)]
    + [(1, 1, 0), (1, 2, 0)]
    + [(0, m, c) for m in (1, 2) for c in range(3)]
    + [(1, 0, 0)]
    + [(0, 0, c) for c in range(3)]
)


def attend_back_into(rows_of, mixed, shares, grad_context, grad_mixed, first_pair, last_pair):
    (query_at, query_count), (key_at, key_count) = rows_of
    query_rows, key_rows = pl.ds(query_at, query_count), pl.ds(key_at, key_count)

    def pair(p, carry):
        at = pl.multiple_of(p * PAIR_WIDE, PAIR_WIDE)
        at_query, at_key, at_value = (pl.ds(third * WIDE + at, PAIR_WIDE) for third in range(3))
        queries = mixed[query_rows, at_query]
        keys = mixed[key_rows, at_key]
        values = mixed[key_rows, at_value]
        grads = grad_context[query_rows, at_query]
        grad_queries = jnp.zeros((query_count, PAIR_WIDE), jnp.float32)
        grad_keys = jnp.zeros((key_count, PAIR_WIDE), jnp.float32)
        grad_values = jnp.zeros((key_count, PAIR_WIDE), jnp.float32)
        for side, chosen in enumerate(half_lanes()):
            share = shares[2 * p + side]
            grad_head = only(grads, chosen)
            wide = share.astype(jnp.float32)
            weighted = wide * dot_nt(grad_head, values)
            grad_scores = (weighted - wide * jnp.sum(weighted, axis=-1, keepdims=True)).astype(jnp.bfloat16)
            grad_values = grad_values + dot_tn(share, grad_head)
            grad_queries = grad_queries + matmul(grad_scores, only(keys, chosen))
            grad_keys = grad_keys + dot_tn(grad_scores, only(queries, chosen))
        score_scale = HEAD_DIM ** (-0.5)
        grad_mixed[query_rows, at_query] = (grad_queries * score_scale).astype(jnp.bfloat16)
        grad_mixed[key_rows, at_key] = (grad_keys * score_scale).astype(jnp.bfloat16)
        grad_mixed[key_rows, at_value] = grad_values.astype(jnp.bfloat16)
        return carry

    lax.fori_loop(first_pair, last_pair, pair, 0)


def backward_kernel(*refs):
    saved_hbm, weights = refs[:23], refs[23:27]
    word_gradient, region_gradient, small_out, *totals = refs[27:34]
    (
        params,
        word_cotangent,
        region_cotangent,
        normed,
        inverse,
        hidden_t,
        slope,
        rows_two_t,
        slope_words,
        expand_words,
        hidden_words_t,
        rows_two_words_t,
        context_self_t,
        mixed_self,
        shares_w,
        shares_r,
        rows_one_t,
        context_cross_t,
        mixed_cross,
        shares_cw,
        shares_cr,
        rows_zero_t,
        shrink_words,
    ) = saved = refs[34:57]
    (
        window,
        end_feed,
        end_self,
        end_cross,
        stream,
        grad_context,
        row_sums,
        hidden_sums,
        end_words,
        hidden_sums_words,
        owned_shrink,
        owned_out,
        owned_expand,
        partial,
        sum_core_out,
        sum_core_in,
        sum_half_out,
        sum_half_in,
        sum_full_out,
        sum_full_in,
        sum_sends,
        sum_recvs,
        gather_sends,
        gather_recvs,
        slice_sends,
        slice_recvs,
        out,
        acc,
        core_out,
        core_in,
        half_out,
        half_in,
        full_out,
        full_in,
        plane,
        end_out,
        end_in,
        mid_out,
        mid_in,
        small_in,
        small_in_plane,
        small_planes,
        saved_sems,
        window_sems,
        total_sems,
        core_send,
        core_recv,
        half_send,
        half_recv,
        full_send,
        full_recv,
        z_send,
        z_recv,
        back_send,
        back_recv,
        small_send,
        small_recv,
        free,
    ) = refs[57:]
    grad_before, before_words, grad_mixed_self, grad_mixed_cross = slope, slope_words, mixed_self, mixed_cross
    lefts = (hidden_t, rows_two_t, context_self_t, rows_one_t, context_cross_t, rows_zero_t)
    rights = (end_feed, grad_before, end_self, grad_mixed_self, end_cross, grad_mixed_cross)
    me = lax.axis_index("fsdp")
    z = lax.axis_index("rep")
    chip = me // 2
    lane = me % 2
    is_end = jnp.logical_or(z == 0, z == 3)
    is_mid = jnp.logical_or(z == 1, z == 2)
    core_peer = {"fsdp": flip(me, 1)}
    links = ({"fsdp": flip(me, 2)}, {"fsdp": flip(me, 4)})
    link_chip = (flip(chip, 1), flip(chip, 2))
    diagonal = flip(chip, 3)
    pair_peer = {"rep": flip(z, 1)}
    mid_peer = {"rep": 3 - z}
    low = LOW
    gather_words = RowGather(me, end_words, gather_sends, gather_recvs)
    sum_words = RowSum(
        me,
        partial,
        sum_core_out,
        sum_core_in,
        sum_half_out,
        sum_half_in,
        sum_full_out,
        sum_full_in,
        sum_sends,
        sum_recvs,
    )

    def load_saved(index):
        source = saved_hbm[index].at[0] if saved[index] is shrink_words else saved_hbm[index]
        return pltpu.make_async_copy(source, saved[index], saved_sems.at[index])

    def load_block(n):
        kind, index, c = BLOCKS[n]
        part = slice(c * WIDE, (c + 1) * WIDE)
        source = weights[kind].at[index, part, :] if kind == 3 else weights[kind].at[index, :, part]
        return pltpu.make_async_copy(source, window.at[n % WINDOW], window_sems.at[n % WINDOW])

    def wait_saved(*names):
        for name in names:
            load_saved([ref is name for ref in saved].index(True)).wait()

    first_saved = [0, 1, 2, 3, 4, 5]
    for index in first_saved:
        load_saved(index).start()
    for n in range(WINDOW):
        load_block(n).start()
    for index in [22, 8, 9, 10, 11, 6, 7] + list(range(12, 22)):
        load_saved(index).start()
    greet(me, z)

    def small_copy(offset):
        peer = flip(me, offset)
        return remote(
            small_in.at[peer],
            small_in_plane.at[offset - 1],
            small_send.at[offset - 1],
            small_recv.at[offset - 1],
            {"fsdp": peer},
        )

    def small_plane_copy(offset, source):
        peer = (z + offset) % 4 if source is z else source
        return remote(
            small_planes.at[source],
            small_planes.at[source],
            small_send.at[6 + offset],
            small_recv.at[6 + offset],
            {"rep": peer},
        )

    def core_copy(u):
        slot = u % SLOTS
        return remote(core_out.at[slot], core_in.at[slot], core_send.at[slot], core_recv.at[slot], core_peer)

    def half_copy(u, way):
        slot = u % SLOTS
        return remote(
            half_out.at[slot, way], half_in.at[slot, way], half_send.at[slot, way], half_recv.at[slot, way], links[way]
        )

    def full_copy(u, way):
        slot = u % SLOTS
        return remote(
            full_out.at[slot, way], full_in.at[slot, way], full_send.at[slot, way], full_recv.at[slot, way], links[way]
        )

    def end_copy(n):
        slot = n % Z_SLOTS
        return remote(end_out.at[slot], end_in.at[slot], z_send.at[0, slot], z_recv.at[0, slot], pair_peer)

    def mid_copy(n):
        slot = n % Z_SLOTS
        return remote(mid_out.at[slot], mid_in.at[slot], z_send.at[1, slot], z_recv.at[1, slot], mid_peer)

    def back_copy(n):
        u = z_order[n]
        return remote(out.at[u], out.at[u], back_send.at[u], back_recv.at[u], pair_peer)

    def credit(u, channel, peer, slots=SLOTS, count=CROSSING):
        if u + slots < count:
            pl.semaphore_signal(free.at[channel], inc=1, device_id=peer, device_id_type=MESH)

    def spend(u, channel, slots=SLOTS):
        if u >= slots:
            pl.semaphore_wait(free.at[channel], 1)

    def per_group(u, function):
        for group in GROUPS:
            if u < group[0]:
                return function(u, *group[1:])
            u = u - group[0]

    def produce(u):
        slot = u % SLOTS
        keep = u % ACC_SLOTS
        spend(u, 0)

        def products(at, side, first_row, count, by_row, matrix):
            rows = pl.ds(first_row, count)
            column = (at % 2 if by_row else at) * SPAN
            right = rights[side][rows, pl.ds(column, SPAN)]

            def product(core):
                blocks = []
                for block in range(4):
                    owner = 2 * block + core
                    row = owner * (4 * UNIT) + (at // 2) * UNIT if by_row else owner * UNIT
                    blocks.append(lefts[side][pl.ds(pl.multiple_of(row, 16), UNIT), rows])
                return matmul(jnp.concatenate(blocks, axis=0), right)

            other = product(1 - lane).astype(low)
            for block in range(4):
                core_out[slot, block] = other[block * UNIT : (block + 1) * UNIT]
            core_copy(u).start()
            own = product(lane)
            for block in range(4):
                acc[keep, block] = own[block * UNIT : (block + 1) * UNIT]

        per_group(crossing[u], products)

    def join_cores(u):
        slot = u % SLOTS
        keep = u % ACC_SLOTS
        core_copy(u).wait()
        for way in range(2):
            spend(u, 1 + way)
        summed = acc[keep, diagonal] + core_in[slot, diagonal].astype(jnp.float32)
        half_out[slot, 0] = summed[: UNIT // 2].astype(low)
        half_out[slot, 1] = summed[UNIT // 2 :].astype(low)
        for way in range(2):
            half_copy(u, way).start()
        for block in (link_chip[0], link_chip[1], chip):
            acc[keep, block] = acc[keep, block] + core_in[slot, block].astype(jnp.float32)
        credit(u, 0, core_peer)

    def join_diagonal(u):
        slot = u % SLOTS
        keep = u % ACC_SLOTS
        for way in range(2):
            half_copy(u, way).wait()
            spend(u, 3 + way)
        half = UNIT // 2
        full_out[slot, 1, :half] = (acc[keep, link_chip[1], :half] + half_in[slot, 0].astype(jnp.float32)).astype(low)
        full_out[slot, 1, half:] = acc[keep, link_chip[1], half:].astype(low)
        full_copy(u, 1).start()
        full_out[slot, 0, half:] = (acc[keep, link_chip[0], half:] + half_in[slot, 1].astype(jnp.float32)).astype(low)
        full_out[slot, 0, :half] = acc[keep, link_chip[0], :half].astype(low)
        full_copy(u, 0).start()
        for way in range(2):
            credit(u, 1 + way, links[way])

    def join_plane(u):
        slot = u % SLOTS
        keep = u % ACC_SLOTS
        for way in range(2):
            full_copy(u, way).wait()
        summed = acc[keep, chip] + (full_in[slot, 0].astype(F32) + full_in[slot, 1].astype(F32))
        for way in range(2):
            credit(u, 3 + way, links[way])
        enter(z_order.index(crossing[u]), summed)

    def join_owned(u):
        half = slice(u % 2 * SPAN, u % 2 * SPAN + SPAN)
        if u < 8:
            summed = owned_shrink[u // 2 * UNIT : (u // 2 + 1) * UNIT, half]
        else:
            summed = owned_expand[u - 8].astype(F32)
        enter(z_order.index(u), summed)

    def enter(n, summed):
        slot = n % Z_SLOTS

        @pl.when(is_end)
        def _():
            spend(n, 5, Z_SLOTS)
            end_out[slot] = summed.astype(low)
            end_copy(n).start()

        @pl.when(is_mid)
        def _():
            plane[slot] = summed

    def join_pair(n):
        slot = n % Z_SLOTS

        @pl.when(is_end)
        def _():
            end_copy(n).wait_send()

        @pl.when(is_mid)
        def _():
            end_copy(n).wait_recv()
            spend(n, 6, Z_SLOTS)
            mid_out[slot] = (plane[slot] + end_in[slot].astype(F32)).astype(low)
            mid_copy(n).start()
            credit(n, 5, pair_peer, Z_SLOTS, UNITS)

    def join_middle(n):
        slot = n % Z_SLOTS

        @pl.when(is_mid)
        def _():
            mid_copy(n).wait()
            out[z_order[n]] = (mid_out[slot].astype(F32) + mid_in[slot].astype(F32)).astype(low)
            back_copy(n).start()
            credit(n, 6, mid_peer, Z_SLOTS, UNITS)

    def total_copy(u, at, by_row, matrix):
        kind, index = matrix
        if by_row:
            row, column = (at // 2) * UNIT, (at % 2) * SPAN
        else:
            row, column = 0, at * SPAN
        place = totals[kind].at[index, pl.ds(row, UNIT), pl.ds(column, SPAN)]
        return pltpu.make_async_copy(out.at[u], place, total_sems.at[u])

    def finish(n):
        @pl.when(is_mid)
        def _():
            back_copy(n).wait_send()

        @pl.when(is_end)
        def _():
            back_copy(n).wait_recv()

        u = z_order[n]
        per_group(u, lambda at, side, first_row, count, by_row, matrix: total_copy(u, at, by_row, matrix).start())

    crossing = [u for u in range(UNITS) if u >= OWNED]
    to_plane = LAG_CORE + LAG_A + LAG_B
    entries = [(i + to_plane, 1, u) for i, u in enumerate(crossing)]
    entries += [(OWNED_SHRINK_AT + u * 3 // 8, 0, u) for u in range(8)]
    entries += [(OWNED_EXPAND_AT + 2 * (u - 8), 0, u) for u in range(8, OWNED)]
    entries.sort()
    z_order = [u for _, _, u in entries]
    for n in range(UNITS - Z_SLOTS):
        assert entries[n + Z_SLOTS][0] >= entries[n][0] + LAG_Z
    last = entries[-1][0] + 3 * LAG_Z

    row_tiles = ((0, 0), (1, 128), (1, 256))

    def add_row(index, values):
        row_sums[index : index + 1, :] += jnp.sum(values, axis=0, keepdims=True)

    def norm_back(grad, kind, norm_index, at, ends, end_bias, end_at=None):
        rows = slice(at, at + 128)
        unit = normed[kind, rows, :]
        grad_unit = grad * params[16 + norm_index : 17 + norm_index, :]
        summed = inverse[kind, rows, :1] * (
            grad_unit
            - jnp.mean(grad_unit, axis=-1, keepdims=True)
            - unit * jnp.mean(grad_unit * unit, axis=-1, keepdims=True)
        )
        add_row(16 + norm_index, grad * unit)
        add_row(9 + norm_index, grad)
        stream[rows, :] = summed
        summed_low = summed.astype(low)
        if end_at is None:
            ends[rows, :] = summed_low
        else:
            ends[pl.ds(end_at, 128), :] = summed_low
        add_row(end_bias, summed_low.astype(jnp.float32))

    def feed_norm():
        wait_saved(params, word_cotangent, region_cotangent, normed, inverse)
        row_sums[...] = jnp.zeros_like(row_sums)
        hidden_sums[...] = jnp.zeros_like(hidden_sums)
        hidden_sums_words[...] = jnp.zeros_like(hidden_sums_words)
        own_rows = pl.multiple_of(me * WORDS, WORDS)
        norm_back(word_cotangent[...].astype(F32), 2, 3, 0, end_words, 14, own_rows)
        gather_words.start()
        for at in range(0, REGIONS, 128):
            cotangent = region_cotangent[at : at + 128, :].astype(F32)
            norm_back(cotangent, 2, 4, WORDS + at, end_feed, 15, at)

    def slice_copy(offset, arriving=False):
        peer = flip(me, offset)
        rows = pl.ds(pl.multiple_of(peer * UNIT, UNIT), UNIT)
        target = owned_expand.at[peer if arriving else me]
        return remote(
            owned_out.at[rows, :], target, slice_sends.at[offset - 1], slice_recvs.at[offset - 1], {"fsdp": peer}
        )

    def words_back():
        wait_saved(shrink_words, slope_words, expand_words)
        for at in range(0, PLANE_WORDS, 128):
            rows = slice(at, at + 128)
            before = (dot_nt(end_words[rows, :], shrink_words[...]) * slope_words[rows, :].astype(F32)).astype(low)
            before_words[rows, :] = before
            hidden_sums_words[0:1, :] += jnp.sum(before.astype(F32), axis=0, keepdims=True)
            partial[at // 128] = dot_nt(before, expand_words[...])
        sum_words.start()

    def words_shrink():
        wait_saved(hidden_words_t)
        owned_shrink[...] = matmul(hidden_words_t[...], end_words[...])

    def words_expand():
        wait_saved(rows_two_words_t)
        owned_out[...] = matmul(rows_two_words_t[...], before_words[...]).astype(low)
        for offset in range(1, 8):
            slice_copy(offset).start()
        owned_expand[me] = owned_out[pl.ds(pl.multiple_of(me * UNIT, UNIT), UNIT), :]

    def words_expanded():
        for offset in range(1, 8):
            slice_copy(offset).wait_send()
            slice_copy(offset, True).wait_recv()

    def words_rows():
        stream[0:WORDS, :] += sum_words.total()

    def next_block(n):
        if n + WINDOW < len(BLOCKS):
            load_block(n + WINDOW).start()

    def feed_back(c):
        n = 2 * c
        load_block(n).wait()
        load_block(n + 1).wait()
        columns = slice(c * WIDE, (c + 1) * WIDE)
        for at in range(0, REGIONS, 128):
            rows = slice(at, at + 128)
            grad_hidden = dot_nt(end_feed[rows, :], window[n % WINDOW])
            before = (grad_hidden * slope[rows, columns].astype(F32)).astype(low)
            grad_before[rows, columns] = before
            hidden_sums[c : c + 1, :] += jnp.sum(before.astype(F32), axis=0, keepdims=True)
            stream[WORDS + at : WORDS + at + 128, :] += dot_nt(before, window[(n + 1) % WINDOW])
        next_block(n)
        next_block(n + 1)

    def self_norm():
        for f, at in row_tiles:
            norm_back(stream[at : at + 128, :], 1, 1 + f, at, end_self, 5 + 3 * f)

    def self_context():
        for f in range(2):
            n = 8 + f
            load_block(n).wait()
            for which, at in row_tiles:
                if which == f:
                    grad_context[at : at + 128, :] = dot_nt(end_self[at : at + 128, :], window[n % WINDOW]).astype(low)
            next_block(n)

    def project_back(n, module, grad_mixed, tiles):
        for c in range(3):
            load_block(n + c).wait()
            columns = slice(c * WIDE, (c + 1) * WIDE)
            for at in tiles:
                part = grad_mixed[at : at + 128, columns]
                if c != 1:
                    add_row(3 * module + c // 2, part.astype(jnp.float32))
                stream[at : at + 128, :] += dot_nt(part, window[(n + c) % WINDOW])
            next_block(n + c)

    def cross_norm():
        for _, at in row_tiles:
            norm_back(stream[at : at + 128, :], 0, 0, at, end_cross, 2)

    def cross_context():
        n = 16
        load_block(n).wait()
        for _, at in row_tiles:
            grad_context[at : at + 128, :] = dot_nt(end_cross[at : at + 128, :], window[n % WINDOW]).astype(low)
        next_block(n)

    def give_rows():
        word_gradient[...] = stream[0:WORDS, :]
        region_gradient[...] = stream[WORDS:ROWS, :]

    def exact_nt(left, right):
        return lax.dot_general(
            left,
            right.astype(jnp.float32),
            (((1,), (1,)), ((), ())),
            precision=lax.Precision.HIGHEST,
            preferred_element_type=jnp.float32,
        )

    def give_small():
        small_in[...] = jnp.zeros_like(small_in)
        for owner in range(8):
            small_in[owner, 0:21, :] = exact_nt(row_sums[...], spread(owner))[:21]
        for place in range(8):
            placed = exact_nt(hidden_sums[...], spread(place))
            for c in range(4):
                row = 25 + place % 4
                small_in[2 * c + place // 4, row : row + 1, :] = placed[c : c + 1]
        source = lax.broadcasted_iota(jnp.int32, (128, SLICE), 0)
        target = lax.broadcasted_iota(jnp.int32, (128, SLICE), 1)
        for q in range(4):
            chosen = jnp.logical_and(source < UNIT, target == source + q * UNIT)
            small_in[me, 21 + q : 22 + q, :] = exact_nt(hidden_sums_words[...], chosen)[0:1]
        for offset in range(1, 8):
            small_copy(offset).start()

    def join_small():
        summed = small_in[me]
        for offset in range(1, 8):
            small_copy(offset).wait()
            summed = summed + small_in_plane[offset - 1]
        small_planes[z] = summed
        for offset in range(1, 4):
            small_plane_copy(offset, z).start()

    def finish_small():
        for offset in range(1, 4):
            small_plane_copy(offset, z).wait_send()
            small_plane_copy(offset, (z + 4 - offset) % 4).wait_recv()
        small_out[...] = small_planes[0] + small_planes[1] + (small_planes[2] + small_planes[3])

    def self_back(rows_of, shares, first, last):
        attend_back_into(rows_of, mixed_self, shares, grad_context, grad_mixed_self, first, last)

    def cross_back(rows_of, shares, first, last):
        attend_back_into(rows_of, mixed_cross, shares, grad_context, grad_mixed_cross, first, last)

    pieces = {
        0: (gather_words.first, lambda: wait_saved(slope)),
        1: (gather_words.second, functools.partial(feed_back, 0)),
        2: (gather_words.complete, words_back),
        3: (functools.partial(feed_back, 1),),
        4: (sum_words.cores, words_shrink),
        5: (functools.partial(feed_back, 2), words_expand),
        6: (sum_words.diagonal,),
        7: (functools.partial(feed_back, 3), lambda: wait_saved(rows_two_t)),
        8: (words_rows, gather_words.settle),
        9: (words_expanded,),
        10: (self_norm,),
        11: (self_context, lambda: wait_saved(context_self_t, mixed_self, shares_w)),
        12: (lambda: self_back(ATTEND_WORD, shares_w, 0, 3),),
        13: (lambda: self_back(ATTEND_WORD, shares_w, 3, 6), lambda: wait_saved(shares_r, rows_one_t)),
        **{14 + p: (functools.partial(self_back, ATTEND_REGION, shares_r, p, p + 1),) for p in range(6)},
        20: (lambda: project_back(10, 1, grad_mixed_self, (0,)),),
        21: (lambda: project_back(13, 2, grad_mixed_self, (128, 256)),),
        23: (cross_norm, lambda: wait_saved(context_cross_t, mixed_cross, shares_cw, shares_cr, rows_zero_t)),
        24: (cross_context,),
        **{25 + p: (functools.partial(cross_back, ATTEND_CROSS_WORD, shares_cw, 2 * p, 2 * p + 2),) for p in range(3)},
        **{28 + p: (functools.partial(cross_back, ATTEND_CROSS_REGION, shares_cr, 2 * p, 2 * p + 2),) for p in range(3)},
        32: (lambda: project_back(17, 0, grad_mixed_cross, (0, 128, 256)),),
        33: (give_rows,),
        34: (give_small,),
        37: (join_small,),
        40: (finish_small,),
    }

    feed_norm()
    wait_saved(hidden_t)
    for i in range(last + 1):
        for n, (entry, _, _) in enumerate(entries):
            if i == entry + 3 * LAG_Z:
                finish(n)
        for n, (entry, _, _) in enumerate(entries):
            if i == entry + 2 * LAG_Z:
                join_middle(n)
        for n, (entry, _, _) in enumerate(entries):
            if i == entry + LAG_Z:
                join_pair(n)
        for entry, crosses, u in entries:
            if i == entry and not crosses:
                join_owned(u)
        for lag, stage in ((to_plane, join_plane), (LAG_CORE + LAG_A, join_diagonal), (LAG_CORE, join_cores), (0, produce)):
            if 0 <= i - lag < CROSSING:
                stage(i - lag)
        for piece in pieces.get(i, ()):
            piece()
    for u in range(UNITS):
        per_group(u, lambda at, side, first_row, count, by_row, matrix: total_copy(u, at, by_row, matrix).wait())


def backward(saved, shrink, weights):
    block = (UNIT, SPAN)
    low, f32 = jnp.bfloat16, jnp.float32
    dma = pltpu.SemaphoreType.DMA
    vmem = pl.BlockSpec(memory_space=pltpu.VMEM)
    hbm = pl.BlockSpec(memory_space=pl.ANY)
    shape = jax.ShapeDtypeStruct
    small = (32, 128)
    return pl.pallas_call(
        backward_kernel,
        out_shape=(
            shape((WORDS, WIDE), f32),
            shape((REGIONS, WIDE), f32),
            shape(small, f32),
            shape((3, UNIT, 3 * WIDE), low),
            shape((3, UNIT, WIDE), low),
            shape((2, UNIT, HIDDEN), low),
            shape((2, 4 * UNIT, WIDE), low),
        ),
        in_specs=[hbm] * (len(saved) + 1 + len(weights)),
        out_specs=[vmem] * 3 + [hbm] * 4,
        scratch_shapes=[pltpu.VMEM(array.shape, array.dtype) for array in saved]
        + [
            pltpu.VMEM((SLICE, WIDE), low),
            pltpu.VMEM((WINDOW, WIDE, WIDE), low),
            pltpu.VMEM((REGIONS, WIDE), low),
            pltpu.VMEM((ROWS, WIDE), low),
            pltpu.VMEM((ROWS, WIDE), low),
            pltpu.VMEM((ROWS, WIDE), f32),
            pltpu.VMEM((ROWS, WIDE), low),
            pltpu.VMEM((24, WIDE), f32),
            pltpu.VMEM((8, WIDE), f32),
            pltpu.VMEM((PLANE_WORDS, WIDE), low),
            pltpu.VMEM((8, SLICE), f32),
            pltpu.VMEM((SLICE, WIDE), f32),
            pltpu.VMEM((WIDE, SLICE), low),
            pltpu.VMEM((8, UNIT, SLICE), low),
            *row_sum_scratch(),
            dma((8,)),
            dma((8,)),
            dma((7,)),
            dma((7,)),
            pltpu.VMEM((UNITS,) + block, low),
            pltpu.VMEM((ACC_SLOTS, 4) + block, f32),
            pltpu.VMEM((SLOTS, 4) + block, low),
            pltpu.VMEM((SLOTS, 4) + block, low),
            pltpu.VMEM((SLOTS, 2, UNIT // 2, SPAN), low),
            pltpu.VMEM((SLOTS, 2, UNIT // 2, SPAN), low),
            pltpu.VMEM((SLOTS, 2) + block, low),
            pltpu.VMEM((SLOTS, 2) + block, low),
            pltpu.VMEM((Z_SLOTS,) + block, f32),
            pltpu.VMEM((Z_SLOTS,) + block, low),
            pltpu.VMEM((Z_SLOTS,) + block, low),
            pltpu.VMEM((Z_SLOTS,) + block, low),
            pltpu.VMEM((Z_SLOTS,) + block, low),
            pltpu.VMEM((8,) + small, f32),
            pltpu.VMEM((7,) + small, f32),
            pltpu.VMEM((4,) + small, f32),
            dma((23,)),
            dma((WINDOW,)),
            dma((UNITS,)),
            dma((SLOTS,)),
            dma((SLOTS,)),
            dma((SLOTS, 2)),
            dma((SLOTS, 2)),
            dma((SLOTS, 2)),
            dma((SLOTS, 2)),
            dma((2, Z_SLOTS)),
            dma((2, Z_SLOTS)),
            dma((UNITS,)),
            dma((UNITS,)),
            dma((10,)),
            dma((10,)),
            pltpu.SemaphoreType.REGULAR((7,)),
        ],
        compiler_params=pltpu.CompilerParams(
            collective_id=0, has_side_effects=True, vmem_limit_bytes=64 * 2**20 - 2**16
        ),
    )(*saved, shrink, *weights)


def deliver_kernel(*refs):
    moved, small, totals = refs[:4], refs[4], refs[5:9]
    moved_out, bias_out, gain_out, hidden_out, totals_out = refs[9:13], refs[13], refs[14], refs[15], refs[16:20]
    narrow, wide, held = refs[20:24], refs[24:28], refs[28:32]
    take_sems, give_sems, load_sems, store_sems = refs[32:]
    takes = [pltpu.make_async_copy(moved[i], held[i], take_sems.at[i]) for i in range(4)]
    gives = [pltpu.make_async_copy(held[i], moved_out[i], give_sems.at[i]) for i in range(4)]
    pieces = [(kind, index) for kind in range(4) for index in range(totals[kind].shape[0])]
    loads = [
        pltpu.make_async_copy(totals[kind].at[index], narrow[kind].at[index], load_sems.at[i])
        for i, (kind, index) in enumerate(pieces)
    ]
    stores = [
        pltpu.make_async_copy(wide[kind].at[index], totals_out[kind].at[index], store_sems.at[i])
        for i, (kind, index) in enumerate(pieces)
    ]
    for one in loads + takes:
        one.start()
    bias_out[...] = small[0:16, 0:UNIT]
    gain_out[...] = small[16:21, 0:UNIT]
    source = lax.broadcasted_iota(jnp.int32, (128, 4 * UNIT), 0)
    target = lax.broadcasted_iota(jnp.int32, (128, 4 * UNIT), 1)
    for f in range(2):
        row = jnp.zeros((1, 4 * UNIT), F32)
        for q in range(4):
            chosen = jnp.logical_and(source < UNIT, target == source + q * UNIT).astype(F32)
            line = 21 + 4 * f + q
            row = row + jnp.dot(
                small[line : line + 1, :], chosen, precision=lax.Precision.HIGHEST, preferred_element_type=F32
            )
        hidden_out[f : f + 1, :] = row
    for i, (kind, index) in enumerate(pieces):
        loads[i].wait()
        wide[kind][index] = narrow[kind][index].astype(F32)
        stores[i].start()
    for i in range(4):
        takes[i].wait()
        gives[i].start()
    for one in gives + stores:
        one.wait()


def deliver(moved, small, totals):
    vmem = pl.BlockSpec(memory_space=pltpu.VMEM)
    hbm = pl.BlockSpec(memory_space=pl.ANY)
    shape = jax.ShapeDtypeStruct
    widened = [shape(total.shape, F32) for total in totals]
    sem = pltpu.SemaphoreType.DMA((4,))
    piece_sem = pltpu.SemaphoreType.DMA((sum(total.shape[0] for total in totals),))
    return pl.pallas_call(
        deliver_kernel,
        out_shape=[shape(one.shape, one.dtype) for one in moved]
        + [shape((16, UNIT), F32), shape((5, UNIT), F32), shape((2, 4 * UNIT), F32)]
        + widened,
        in_specs=[hbm] * 4 + [vmem] + [hbm] * 4,
        out_specs=[hbm] * 4 + [vmem] * 3 + [hbm] * 4,
        scratch_shapes=[pltpu.VMEM(one.shape, one.dtype) for one in totals]
        + [pltpu.VMEM(one.shape, F32) for one in totals]
        + [pltpu.VMEM(one.shape, one.dtype) for one in moved]
        + [sem, sem, piece_sem, piece_sem],
        compiler_params=pltpu.CompilerParams(vmem_limit_bytes=64 * 2**20 - 2**16),
    )(*moved, small, *totals)


def paired(
    word_rows,
    region_rows,
    word_segment,
    region_segment,
    inward,
    outward,
    biases,
    norm_gain,
    expand_weight,
    shrink_weight,
    hidden_bias,
    word_cotangent,
    region_cotangent,
):
    results, saved, weights = forward(
        word_rows,
        region_rows,
        word_segment,
        region_segment,
        biases,
        norm_gain,
        hidden_bias,
        (inward, outward, expand_weight, shrink_weight),
    )
    word_gradient, region_gradient, small, *totals = backward(
        (saved[0], word_cotangent, region_cotangent, *saved[1:]), shrink_weight, weights
    )
    word_out, region_out, word_gradient, region_gradient, bias, gain, hidden, *totals = deliver(
        (*results, word_gradient, region_gradient), small, totals
    )
    inward_total, outward_total, expand_total, shrink_total = totals
    return (
        word_out,
        region_out,
        word_gradient,
        region_gradient,
        inward_total,
        outward_total,
        bias,
        gain,
        expand_total,
        shrink_total,
        hidden,
    )


def general(
    devices,
    word_rows,
    region_rows,
    word_segment,
    region_segment,
    inward,
    outward,
    biases,
    norm_gain,
    expand_weight,
    shrink_weight,
    hidden_bias,
    word_cotangent,
    region_cotangent,
):
    words_count = word_rows.shape[0]
    width = word_rows.shape[1]
    word_ids = word_segment[0]
    region_ids = region_segment[0]
    cross_mask = word_ids[:, None] == region_ids[None, :]
    word_mask = word_ids[:, None] == word_ids[None, :]
    region_mask = region_ids[:, None] == region_ids[None, :]
    shard = biases.shape[1]
    per_shard = hidden_bias.shape[1] // shard
    small_shard = jnp.concatenate([biases, norm_gain, hidden_bias.reshape(2 * per_shard, shard)], axis=0)
    small_all = lax.all_gather(small_shard, "fsdp", axis=0)
    bias_count = biases.shape[0]
    gain_count = norm_gain.shape[0]
    row_params = small_all[:, : bias_count + gain_count].transpose(1, 0, 2).reshape(bias_count + gain_count, width)
    hidden_all = (
        small_all[:, bias_count + gain_count :]
        .reshape(devices, 2, per_shard * shard)
        .transpose(1, 0, 2)
        .reshape(2, devices * per_shard * shard)
    )
    inward_all, outward_all = (
        lax.all_gather(inward, "fsdp", axis=1, tiled=True),
        lax.all_gather(outward, "fsdp", axis=1, tiled=True),
    )
    attend_set = (
        inward_all,
        outward_all,
        row_params[:bias_count].astype(jnp.float32),
        row_params[bias_count:].astype(jnp.float32),
    )
    crossed, cross_kept = cross_forward(word_rows, region_rows, attend_set, cross_mask)
    word_one, word_kept = self_forward(crossed[:words_count], attend_set, 1, word_mask)
    region_one, region_kept = self_forward(crossed[words_count:], attend_set, 2, region_mask)
    expand_all, shrink_all = (
        lax.all_gather(expand_weight, "fsdp", axis=1, tiled=True),
        lax.all_gather(shrink_weight, "fsdp", axis=1, tiled=True),
    )
    feed_set = (expand_all, shrink_all, hidden_all)
    word_two, word_feed = feed_forward(word_one, feed_set, 0, attend_set)
    region_two, region_feed = feed_forward(region_one, feed_set, 1, attend_set)
    word_back = feed_backward(word_cotangent.astype(jnp.float32), word_feed, feed_set, 0, attend_set[3])
    region_back = feed_backward(region_cotangent.astype(jnp.float32), region_feed, feed_set, 1, attend_set[3])
    word_self = self_backward(word_back[0], word_kept, attend_set, 1, word_mask)
    region_self = self_backward(region_back[0], region_kept, attend_set, 2, region_mask)
    grad_crossed = jnp.concatenate([word_self[0], region_self[0]], axis=0)
    cross_back = cross_backward(grad_crossed, cross_kept, attend_set, cross_mask, words_count)
    row_grads = jnp.stack(
        [
            cross_back[3][0],
            cross_back[3][1],
            cross_back[3][2],
            word_self[3][0],
            word_self[3][1],
            word_self[3][2],
            region_self[3][0],
            region_self[3][1],
            region_self[3][2],
            cross_back[5],
            word_self[5],
            region_self[5],
            word_back[6],
            region_back[6],
            word_back[4],
            region_back[4],
            cross_back[4],
            word_self[4],
            region_self[4],
            word_back[5],
            region_back[5],
        ]
    )
    hidden_grads = jnp.stack([word_back[3], region_back[3]])
    small_grads = jnp.concatenate(
        [
            row_grads.reshape(bias_count + gain_count, devices, shard).transpose(1, 0, 2),
            hidden_grads.reshape(2, devices, per_shard, shard)
            .transpose(1, 0, 2, 3)
            .reshape(devices, 2 * per_shard, shard),
        ],
        axis=1,
    )

    def reduced(products, axis):
        mine = lax.psum_scatter(jnp.stack(products), "fsdp", scatter_dimension=axis, tiled=True)
        return lax.psum(mine.astype(jnp.bfloat16), "rep").astype(jnp.float32)

    shrink_total = reduced([matmul_tn(*word_back[2]), matmul_tn(*region_back[2])], 1)
    expand_total = reduced([matmul_tn(*word_back[1]), matmul_tn(*region_back[1])], 1)
    outward_total = reduced([matmul_tn(*cross_back[2]), matmul_tn(*word_self[2]), matmul_tn(*region_self[2])], 1)
    inward_total = reduced([matmul_tn(*cross_back[1]), matmul_tn(*word_self[1]), matmul_tn(*region_self[1])], 1)
    small_total = lax.psum(lax.psum_scatter(small_grads, "fsdp", scatter_dimension=0, tiled=False), "rep")
    grad_rows = cross_back[0]
    return (
        word_two.astype(jnp.bfloat16),
        region_two.astype(jnp.bfloat16),
        grad_rows[:words_count],
        grad_rows[words_count:],
        inward_total,
        outward_total,
        small_total[:bias_count],
        small_total[bias_count : bias_count + gain_count],
        expand_total,
        shrink_total,
        small_total[bias_count + gain_count :].reshape(2, per_shard * shard),
    )


def solution(mesh):
    sizes = (mesh.shape["rep"], mesh.shape["fsdp"])
    return jax.shard_map(
        paired if sizes == (4, 8) else functools.partial(general, mesh.shape["fsdp"]),
        mesh=mesh,
        in_specs=(
            P(("rep", "fsdp"), None),
            P(("rep", "fsdp"), None),
            P(("rep", "fsdp"), None),
            P(("rep", "fsdp"), None),
            P(None, "fsdp", None),
            P(None, "fsdp", None),
            P(None, "fsdp"),
            P(None, "fsdp"),
            P(None, "fsdp", None),
            P(None, "fsdp", None),
            P(None, "fsdp"),
            P(("rep", "fsdp"), None),
            P(("rep", "fsdp"), None),
        ),
        out_specs=(
            P(("rep", "fsdp"), None),
            P(("rep", "fsdp"), None),
            P(("rep", "fsdp"), None),
            P(("rep", "fsdp"), None),
            P(None, "fsdp", None),
            P(None, "fsdp", None),
            P(None, "fsdp"),
            P(None, "fsdp"),
            P(None, "fsdp", None),
            P(None, "fsdp", None),
            P(None, "fsdp"),
        ),
        check_vma=False,
    )
```

```python
import functools

import jax
import jax.numpy as jnp
from jax import lax
from jax.experimental import pallas as pl
from jax.experimental.pallas import tpu as pltpu
from jax.sharding import PartitionSpec as P

MESH = pl.DeviceIdType.MESH

HEADS = 12
HEAD_DIM = 64


norm_epsilon = 1e-12
masked_score = -1e30


def matmul(left_op, right_op):
    return jnp.dot(left_op, right_op, preferred_element_type=jnp.float32)


def matmul_tn(left_op, right_op):
    return lax.dot_general(
        left_op, right_op, (((0,), (0,)), ((), ())), preferred_element_type=jnp.float32
    )


def matmul_nt(left_op, right_op):
    return lax.dot_general(
        left_op, right_op, (((1,), (1,)), ((), ())), preferred_element_type=jnp.float32
    )


def column_sums(values):
    return jnp.sum(values, axis=0, dtype=jnp.float32)


def heads_of(rows_in):
    return rows_in.reshape(rows_in.shape[0], HEADS, HEAD_DIM)


def merge_heads(head_rows):
    return head_rows.reshape(head_rows.shape[0], -1)


def normalize(summed, gain_row, shift_row):
    center = summed - jnp.mean(summed, axis=-1, keepdims=True)
    inverse = lax.rsqrt(jnp.mean(center * center, axis=-1, keepdims=True) + norm_epsilon)
    normed = center * inverse
    return (normed * gain_row + shift_row, (normed, inverse))


def normalize_back(grad_out, norm_stats, gain_row):
    normed, inverse = norm_stats
    grad_normed = grad_out * gain_row
    grad_sum = inverse * (
        grad_normed
        - jnp.mean(grad_normed, axis=-1, keepdims=True)
        - normed * jnp.mean(grad_normed * normed, axis=-1, keepdims=True)
    )
    return (grad_sum, column_sums(grad_out * normed), column_sums(grad_out))


def score_block(queries, key_rows, allowed):
    scores = jnp.einsum(
        "qhd,khd->hqk", heads_of(queries), heads_of(key_rows), preferred_element_type=jnp.float32
    ) * HEAD_DIM ** (-0.5)
    return jnp.where(allowed[None], scores, masked_score)


def attend(queries, key_rows, value_rows, allowed):
    scores = score_block(queries, key_rows, allowed)
    top_score = jnp.max(scores, axis=-1, keepdims=True)
    log_total = top_score + jnp.log(jnp.sum(jnp.exp(scores - top_score), axis=-1, keepdims=True))
    shares = jnp.exp(scores - log_total).astype(jnp.bfloat16)
    context = jnp.einsum(
        "hqk,khd->qhd", shares, heads_of(value_rows), preferred_element_type=jnp.float32
    )
    return (merge_heads(context).astype(jnp.bfloat16), log_total)


def attend_back(queries, key_rows, value_rows, allowed, log_total, grad_context):
    shares = jnp.exp(score_block(queries, key_rows, allowed) - log_total)
    grad_heads = heads_of(grad_context)
    grad_shares = jnp.einsum(
        "qhd,khd->hqk", grad_heads, heads_of(value_rows), preferred_element_type=jnp.float32
    )
    grad_values = jnp.einsum(
        "hqk,qhd->khd", shares.astype(jnp.bfloat16), grad_heads, preferred_element_type=jnp.float32
    )
    grad_scores = (
        shares * (grad_shares - jnp.sum(shares * grad_shares, axis=-1, keepdims=True))
    ).astype(jnp.bfloat16)
    score_scale = HEAD_DIM ** (-0.5)
    grad_queries = (
        jnp.einsum(
            "hqk,khd->qhd", grad_scores, heads_of(key_rows), preferred_element_type=jnp.float32
        )
        * score_scale
    )
    grad_keys = (
        jnp.einsum(
            "hqk,qhd->khd", grad_scores, heads_of(queries), preferred_element_type=jnp.float32
        )
        * score_scale
    )
    return (merge_heads(grad_queries), merge_heads(grad_keys), merge_heads(grad_values))


def project(rows_low, weight, bias_rows, module):
    width = weight.shape[0]
    bias_all = jnp.concatenate(
        [bias_rows[3 * module], jnp.zeros((width,), jnp.float32), bias_rows[3 * module + 1]]
    )
    return (matmul(rows_low, weight) + bias_all).astype(jnp.bfloat16)


def project_back(grad_sum, grad_parts, rows_low, weight):
    width = weight.shape[0]
    grad_mixed = jnp.concatenate(grad_parts, axis=1).astype(jnp.bfloat16)
    grad_weight = (rows_low, grad_mixed)
    grad_bias = column_sums(grad_mixed)
    grad_rows = grad_sum + matmul_nt(grad_mixed, weight)
    return (grad_rows, grad_weight, grad_bias[:width], grad_bias[2 * width :])


def branch_back(grad_out, context, norm_stats, gain_row, outward_one):
    grad_sum, grad_gain, grad_shift = normalize_back(grad_out, norm_stats, gain_row)
    grad_branch = grad_sum.astype(jnp.bfloat16)
    grad_outward = (context, grad_branch)
    grad_context = matmul_nt(grad_branch, outward_one).astype(jnp.bfloat16)
    return (grad_sum, grad_context, grad_outward, column_sums(grad_branch), grad_gain, grad_shift)


def self_forward(rows_in, weights, module, allowed):
    inward_all, outward_all, bias_rows, gain_rows = weights
    width = rows_in.shape[1]
    rows_low = rows_in.astype(jnp.bfloat16)
    mixed = project(rows_low, inward_all[module], bias_rows, module)
    context, log_total = attend(
        mixed[:, :width], mixed[:, width : 2 * width], mixed[:, 2 * width :], allowed
    )
    summed = rows_in + matmul(context, outward_all[module]) + bias_rows[3 * module + 2]
    result, norm_stats = normalize(summed, gain_rows[module], bias_rows[9 + module])
    return (result, (rows_low, mixed, context, log_total, norm_stats))


def self_backward(grad_out, kept, weights, module, allowed):
    inward_all, outward_all, bias_rows, gain_rows = weights
    rows_low, mixed, context, log_total, norm_stats = kept
    width = rows_low.shape[1]
    grad_sum, grad_context, grad_outward, grad_bias_out, grad_gain, grad_shift = branch_back(
        grad_out, context, norm_stats, gain_rows[module], outward_all[module]
    )
    grad_parts = attend_back(
        mixed[:, :width],
        mixed[:, width : 2 * width],
        mixed[:, 2 * width :],
        allowed,
        log_total,
        grad_context,
    )
    grad_rows, grad_inward, grad_bias_query, grad_bias_value = project_back(
        grad_sum, grad_parts, rows_low, inward_all[module]
    )
    return (
        grad_rows,
        grad_inward,
        grad_outward,
        (grad_bias_query, grad_bias_value, grad_bias_out),
        grad_gain,
        grad_shift,
    )


def cross_forward(word_rows, region_rows, weights, cross_mask):
    inward_all, outward_all, bias_rows, gain_rows = weights
    words_count = word_rows.shape[0]
    width = word_rows.shape[1]
    rows_low = jnp.concatenate([word_rows, region_rows], axis=0)
    mixed = project(rows_low, inward_all[0], bias_rows, 0)
    word_mix = mixed[:words_count]
    region_mix = mixed[words_count:]
    word_context, word_total = attend(
        word_mix[:, :width],
        region_mix[:, width : 2 * width],
        region_mix[:, 2 * width :],
        cross_mask,
    )
    region_context, region_total = attend(
        region_mix[:, :width],
        word_mix[:, width : 2 * width],
        word_mix[:, 2 * width :],
        cross_mask.T,
    )
    context = jnp.concatenate([word_context, region_context], axis=0)
    summed = rows_low.astype(jnp.float32) + matmul(context, outward_all[0]) + bias_rows[2]
    result, norm_stats = normalize(summed, gain_rows[0], bias_rows[9])
    return (result, (rows_low, mixed, context, word_total, region_total, norm_stats))


def cross_backward(grad_out, kept, weights, cross_mask, words_count):
    inward_all, outward_all, bias_rows, gain_rows = weights
    rows_low, mixed, context, word_total, region_total, norm_stats = kept
    width = rows_low.shape[1]
    grad_sum, grad_context, grad_outward, grad_bias_out, grad_gain, grad_shift = branch_back(
        grad_out, context, norm_stats, gain_rows[0], outward_all[0]
    )
    word_mix = mixed[:words_count]
    region_mix = mixed[words_count:]
    word_query_grad, region_key_grad, region_value_grad = attend_back(
        word_mix[:, :width],
        region_mix[:, width : 2 * width],
        region_mix[:, 2 * width :],
        cross_mask,
        word_total,
        grad_context[:words_count],
    )
    region_query_grad, word_key_grad, word_value_grad = attend_back(
        region_mix[:, :width],
        word_mix[:, width : 2 * width],
        word_mix[:, 2 * width :],
        cross_mask.T,
        region_total,
        grad_context[words_count:],
    )
    grad_parts = (
        jnp.concatenate([word_query_grad, region_query_grad], axis=0),
        jnp.concatenate([word_key_grad, region_key_grad], axis=0),
        jnp.concatenate([word_value_grad, region_value_grad], axis=0),
    )
    grad_rows, grad_inward, grad_bias_query, grad_bias_value = project_back(
        grad_sum, grad_parts, rows_low, inward_all[0]
    )
    return (
        grad_rows,
        grad_inward,
        grad_outward,
        (grad_bias_query, grad_bias_value, grad_bias_out),
        grad_gain,
        grad_shift,
    )


def gelu_exact(values):
    return jax.nn.gelu(values, approximate=False)


def feed_forward(rows_in, weights, feed_index, attend_set):
    expand_all, shrink_all, hidden_all = weights
    bias_rows, gain_rows = (attend_set[2], attend_set[3])
    rows_low = rows_in.astype(jnp.bfloat16)
    before = matmul(rows_low, expand_all[feed_index]) + hidden_all[feed_index].astype(jnp.float32)
    hidden = gelu_exact(before).astype(jnp.bfloat16)
    summed = rows_in + matmul(hidden, shrink_all[feed_index]) + bias_rows[14 + feed_index]
    result, norm_stats = normalize(summed, gain_rows[3 + feed_index], bias_rows[12 + feed_index])
    return (result, (rows_low, before, hidden, norm_stats))


def feed_backward(grad_out, kept, weights, feed_index, gain_rows):
    expand_all, shrink_all, hidden_all = weights
    rows_low, before, hidden, norm_stats = kept
    grad_sum, grad_gain, grad_shift = normalize_back(
        grad_out, norm_stats, gain_rows[3 + feed_index]
    )
    grad_branch = grad_sum.astype(jnp.bfloat16)
    grad_shrink = (hidden, grad_branch)
    grad_hidden = matmul_nt(grad_branch, shrink_all[feed_index])
    unused_value, slope_back = jax.vjp(gelu_exact, before)
    grad_before = slope_back(grad_hidden)[0].astype(jnp.bfloat16)
    grad_expand = (rows_low, grad_before)
    grad_rows = grad_sum + matmul_nt(grad_before, expand_all[feed_index])
    return (
        grad_rows,
        grad_expand,
        grad_shrink,
        column_sums(grad_before),
        column_sums(grad_branch),
        grad_gain,
        grad_shift,
    )


UNIT = 96
WIDE = 768
SLOTS = 6
ACC_SLOTS = 9
LAG_CORE = 2
LAG_A = 3
LAG_B = 3
LAG_Z = 3
SHRINK_QUARTERED = 256
OWNED_SHRINK_AT = 5
OWNED_EXPAND_AT = 10
WORDS = 128
REGIONS = 256
ROWS = 384
HIDDEN = 3072
SLICE = HIDDEN // 8
PLANE_WORDS = 8 * WORDS
PAIRS_OF_HEADS = 6
PAIR_WIDE = 128
LOW, F32 = jnp.bfloat16, jnp.float32

X, Y, DIAG_Y, DIAG_X, CORE_OWN, CORE_X, CORE_Y, CORE_DIAG = range(8)


def flip(position, bits):
    return lax.bitwise_xor(position, bits)


def remote(src, dst, send_sem, recv_sem, peer):
    return pltpu.make_async_remote_copy(
        src_ref=src, dst_ref=dst, send_sem=send_sem, recv_sem=recv_sem, device_id=peer, device_id_type=MESH
    )


def greet(me, z):
    barrier = pltpu.get_barrier_semaphore()
    for offset in range(1, 8):
        pl.semaphore_signal(barrier, inc=1, device_id={"fsdp": flip(me, offset)}, device_id_type=MESH)
    for offset in range(1, 4):
        pl.semaphore_signal(barrier, inc=1, device_id={"rep": (z + offset) % 4}, device_id_type=MESH)
    pl.semaphore_wait(barrier, 10)


def route(me, kind, arriving):
    owner, half, step = {
        X: (2 if arriving else 0, None, 2),
        Y: (4 if arriving else 0, None, 4),
        DIAG_Y: (6 if arriving else 2, 0, 4),
        DIAG_X: (6 if arriving else 4, 1, 2),
        CORE_OWN: (1 if arriving else 0, None, 1),
        CORE_X: (3 if arriving else 2, None, 1),
        CORE_Y: (5 if arriving else 4, None, 1),
        CORE_DIAG: (7 if arriving else 6, None, 1),
    }[kind]
    return flip(me, owner), half, {"fsdp": flip(me, step)}


class RowGather:
    def __init__(self, me, rows, sends, recvs):
        self.me, self.rows, self.sends, self.recvs = me, rows, sends, recvs

    def copy(self, kind, arriving=False):
        owner, half, peer = route(self.me, kind, arriving)
        first, count = (owner * WORDS, WORDS) if half is None else (owner * WORDS + half * (WORDS // 2), WORDS // 2)
        here = self.rows.at[pl.ds(pl.multiple_of(first, 16), count), :]
        return remote(here, here, self.sends.at[kind], self.recvs.at[kind], peer)

    def start(self):
        for kind in (X, Y, CORE_OWN):
            self.copy(kind).start()

    def first(self):
        self.copy(X, True).wait_recv()
        self.copy(DIAG_Y).start()
        self.copy(CORE_X).start()
        self.copy(Y, True).wait_recv()
        self.copy(DIAG_X).start()
        self.copy(CORE_Y).start()

    def second(self):
        self.copy(DIAG_Y, True).wait_recv()
        self.copy(DIAG_X, True).wait_recv()
        self.copy(CORE_DIAG).start()

    def complete(self):
        for kind in (CORE_OWN, CORE_X, CORE_Y, CORE_DIAG):
            self.copy(kind, True).wait_recv()

    def settle(self):
        for kind in range(8):
            self.copy(kind).wait_send()


class RowSum:
    def __init__(self, me, partial, core_out, core_in, half_out, half_in, full_out, full_in, sends, recvs):
        self.me, self.partial, self.sends, self.recvs = me, partial, sends, recvs
        self.core_out, self.core_in = core_out, core_in
        self.half_out, self.half_in, self.full_out, self.full_in = half_out, half_in, full_out, full_in
        self.chip, self.lane = me // 2, me % 2

    def copy(self, at):
        if at == 0:
            source, target, peer = self.core_out, self.core_in, 1
        elif at < 3:
            source, target, peer = self.half_out.at[at - 1], self.half_in.at[at - 1], (2, 4)[at - 1]
        else:
            source, target, peer = self.full_out.at[at - 3], self.full_in.at[at - 3], (2, 4)[at - 3]
        return remote(source, target, self.sends.at[at], self.recvs.at[at], {"fsdp": flip(self.me, peer)})

    def start(self):
        for block in range(4):
            self.core_out[block] = self.partial[2 * block + 1 - self.lane].astype(LOW)
        self.copy(0).start()

    def joined(self, block):
        return self.partial[2 * block + self.lane] + self.core_in[block].astype(F32)

    def cores(self):
        self.copy(0).wait()
        half = WORDS // 2
        summed = self.joined(flip(self.chip, 3))
        self.half_out[0] = summed[:half].astype(LOW)
        self.half_out[1] = summed[half:].astype(LOW)
        for way in range(2):
            self.copy(1 + way).start()

    def diagonal(self):
        half = WORDS // 2
        for way in range(2):
            self.copy(1 + way).wait()
        for way, side in ((1, 0), (0, 1)):
            summed = self.joined(flip(self.chip, 1 + way))
            at, other = (slice(0, half), slice(half, WORDS)) if side == 0 else (slice(half, WORDS), slice(0, half))
            self.full_out[way, at] = (summed[at] + self.half_in[side].astype(F32)).astype(LOW)
            self.full_out[way, other] = summed[other].astype(LOW)
            self.copy(3 + way).start()

    def total(self):
        for way in range(2):
            self.copy(3 + way).wait()
        return self.joined(self.chip) + (self.full_in[0].astype(F32) + self.full_in[1].astype(F32))


def row_sum_scratch():
    half, whole = (2, WORDS // 2, WIDE), (2, WORDS, WIDE)
    return [
        pltpu.VMEM((8, WORDS, WIDE), F32),
        pltpu.VMEM((4, WORDS, WIDE), LOW),
        pltpu.VMEM((4, WORDS, WIDE), LOW),
        pltpu.VMEM(half, LOW),
        pltpu.VMEM(half, LOW),
        pltpu.VMEM(whole, LOW),
        pltpu.VMEM(whole, LOW),
        pltpu.SemaphoreType.DMA((5,)),
        pltpu.SemaphoreType.DMA((5,)),
    ]


def dot_nt(left, right):
    return lax.dot_general(left, right, (((1,), (1,)), ((), ())), preferred_element_type=jnp.float32)


def dot_tn(left, right):
    return lax.dot_general(left, right, (((0,), (0,)), ((), ())), preferred_element_type=jnp.float32)


def spread(part):
    source = lax.broadcasted_iota(jnp.int32, (128, WIDE), 0)
    target = lax.broadcasted_iota(jnp.int32, (128, WIDE), 1)
    return jnp.logical_and(source < UNIT, target == source + part * UNIT)


def half_lanes():
    lane = lax.broadcasted_iota(jnp.int32, (1, PAIR_WIDE), 1)
    return (lane < HEAD_DIM, lane >= HEAD_DIM)


def only(values, chosen):
    return jnp.where(chosen, values, jnp.zeros_like(values))


ATTEND_CROSS_WORD = ((0, WORDS), (WORDS, REGIONS))
ATTEND_CROSS_REGION = ((WORDS, REGIONS), (0, WORDS))
ATTEND_WORD = ((0, WORDS), (0, WORDS))
ATTEND_REGION = ((WORDS, REGIONS), (WORDS, REGIONS))


def attend_into(rows_of, mixed, allowed, shares, context):
    (query_at, query_count), (key_at, key_count) = rows_of
    blocked = jnp.where(allowed, 0.0, masked_score)

    def pair(p, carry):
        at = pl.multiple_of(p * PAIR_WIDE, PAIR_WIDE)
        queries = mixed[pl.ds(query_at, query_count), pl.ds(at, PAIR_WIDE)]
        key_rows = mixed[pl.ds(key_at, key_count), pl.ds(WIDE + at, PAIR_WIDE)]
        value_rows = mixed[pl.ds(key_at, key_count), pl.ds(2 * WIDE + at, PAIR_WIDE)]
        total = jnp.zeros((query_count, PAIR_WIDE), jnp.float32)
        for side, chosen in enumerate(half_lanes()):
            scores = dot_nt(only(queries, chosen), key_rows) * HEAD_DIM ** (-0.5) + blocked
            lifted = jnp.exp(scores - jnp.max(scores, axis=-1, keepdims=True))
            share = (lifted / jnp.sum(lifted, axis=-1, keepdims=True)).astype(jnp.bfloat16)
            shares[2 * p + side] = share
            total = total + matmul(share, only(value_rows, chosen))
        context[pl.ds(query_at, query_count), pl.ds(at, PAIR_WIDE)] = total.astype(jnp.bfloat16)
        return carry

    lax.fori_loop(0, PAIRS_OF_HEADS, pair, 0)


def row_norm(summed):
    center = summed - jnp.mean(summed, axis=-1, keepdims=True)
    inverse = lax.rsqrt(jnp.mean(center * center, axis=-1, keepdims=True) + norm_epsilon)
    return (center * inverse, inverse)


def down(across):
    wide = jnp.broadcast_to(across.astype(jnp.float32), (128, across.shape[1]))
    return jnp.concatenate([wide[:, at : at + 128].T[:, :1] for at in range(0, across.shape[1], 128)], axis=0)


SAVED = (
    ((24, WIDE), F32),
    ((3, ROWS, WIDE), F32),
    ((3, ROWS, 128), F32),
    ((HIDDEN, REGIONS), LOW),
    ((REGIONS, HIDDEN), LOW),
    ((WIDE, REGIONS), LOW),
    ((PLANE_WORDS, SLICE), LOW),
    ((WIDE, SLICE), LOW),
    ((SLICE, PLANE_WORDS), LOW),
    ((WIDE, PLANE_WORDS), LOW),
    ((WIDE, ROWS), LOW),
    ((ROWS, 3 * WIDE), LOW),
    ((HEADS, WORDS, WORDS), LOW),
    ((HEADS, REGIONS, REGIONS), LOW),
    ((WIDE, ROWS), LOW),
    ((WIDE, ROWS), LOW),
    ((ROWS, 3 * WIDE), LOW),
    ((HEADS, WORDS, REGIONS), LOW),
    ((HEADS, REGIONS, WORDS), LOW),
    ((WIDE, ROWS), LOW),
)
WEIGHTS = (
    (3, WIDE, 3 * WIDE),
    (3, WIDE, WIDE),
    (1, WIDE, HIDDEN),
    (1, HIDDEN, WIDE),
)

INWARD, OUTWARD, EXPAND, SHRINK, BOTH = range(5)
GATHERED = ((2, WIDE, 3 * WIDE), (2, WIDE, WIDE), (1, WIDE, HIDDEN), (1, HIDDEN, WIDE), (1, WIDE, 4 * WIDE))

CHUNKS = (
    (BOTH, 0, (0, UNIT), True),
    (INWARD, 0, (0, UNIT), False),
    (OUTWARD, 0, (0, UNIT), False),
    (EXPAND, 0, (0, UNIT), True),
    (INWARD, 1, (0, UNIT), False),
    (OUTWARD, 1, (0, UNIT), False),
    (SHRINK, 0, (0, SHRINK_QUARTERED), True),
    (SHRINK, 0, (SHRINK_QUARTERED, 4 * UNIT - SHRINK_QUARTERED), False),
)
BOTH_2, INWARD_0, OUTWARD_0, EXPAND_1, INWARD_1, OUTWARD_1, SHRINK_1, SHRINK_REST = range(len(CHUNKS))


def forward_kernel(*refs):
    word_rows, region_rows, word_ids, region_ids, biases, gains, hidden_bias, *shards = refs[:11]
    word_result, region_result, *kept = refs[11:33]
    weights_kept = refs[33:37]
    (
        params,
        normed,
        inverse,
        hidden_t,
        slope,
        rows_two_t,
        slope_words,
        expand_words,
        hidden_words_t,
        rows_two_words_t,
        context_self_t,
        mixed_self,
        shares_w,
        shares_r,
        rows_one_t,
        context_cross_t,
        mixed_cross,
        shares_cw,
        shares_cr,
        rows_zero_t,
    ) = saved = refs[37:57]
    inward_all, outward_all, expand_all, shrink_all, both_all = gathered = refs[57:62]
    (
        small_own,
        small_all,
        hidden_rows,
        rows_low,
        stream,
        stream_low,
        context,
        hidden,
        words_two,
        hidden_words,
        shrink_words,
        partial,
        core_out,
        core_in,
        half_out,
        half_in,
        full_out,
        full_in,
        sum_sends,
        sum_recvs,
        gather_sends,
        gather_recvs,
        slice_sends,
        slice_recvs,
        sends,
        recvs,
        z_sends,
        z_recvs,
        foreign_sends,
        foreign_recvs,
        small_sends,
        small_recvs,
        local_sems,
        keep_sems,
    ) = refs[62:]
    me = lax.axis_index("fsdp")
    z = lax.axis_index("rep")
    above, below = {"rep": (z + 1) % 4}, {"rep": (z + 3) % 4}
    gather_words = RowGather(me, words_two, gather_sends, gather_recvs)
    sum_words = RowSum(
        me, partial, core_out, core_in, half_out, half_in, full_out, full_in, sum_sends, sum_recvs
    )
    def small_copy(offset, owner):
        return remote(
            small_all.at[owner],
            small_all.at[owner],
            small_sends.at[offset - 1],
            small_recvs.at[offset - 1],
            {"fsdp": flip(me, offset)},
        )

    def place(k, owner, half=None, quarter=None):
        kind, _, (first, count), _ = CHUNKS[k]
        shard_rows = GATHERED[kind][1] // 8
        column, columns = 0, GATHERED[kind][2]
        if quarter is not None and kind == SHRINK:
            count = count // 4
            first = first + quarter * count
        elif quarter is not None:
            columns = columns // 4
            column = quarter * columns
        if half is not None:
            count = count // 2
            first = first + half * count
        if not isinstance(column, int):
            column = pl.multiple_of(column, WIDE)
        if not isinstance(first, int):
            first = pl.multiple_of(first, 16)
        whole = pl.multiple_of(owner * shard_rows + first, 16)
        return pl.ds(whole, count), pl.ds(first, count), pl.ds(column, columns)

    def own_part(k, quarter=None):
        kind, index, _, _ = CHUNKS[k]
        if kind == BOTH:
            return part(k, me, None, quarter)
        _, rows, columns = place(k, me, None, quarter)
        return shards[kind].at[index + (1 if kind in (EXPAND, SHRINK) else 0), rows, columns]

    def part(k, owner, half=None, quarter=None):
        kind, index, _, _ = CHUNKS[k]
        rows, _, columns = place(k, owner, half, quarter)
        return gathered[kind].at[index, rows, columns]

    def mine(k):
        return z if CHUNKS[k][3] else None

    def copy(k, kind, arriving=False):
        owner, half, peer = route(me, kind, arriving)
        quarter = None if kind == CORE_OWN else mine(k)
        target = part(k, owner, half, quarter)
        source = own_part(k, quarter) if kind in (X, Y, CORE_OWN) and not arriving else target
        return remote(source, target, sends.at[k, kind], recvs.at[k, kind], peer)

    z_chunks = [k for k in range(len(CHUNKS)) if CHUNKS[k][3]]
    owners = (flip(me, 2), flip(me, 4), flip(me, 6))
    core_owners = (flip(me, 3), flip(me, 5), flip(me, 7))

    def z_copy(k, way, hop, which, arriving=False):
        steps = hop + 1 if arriving else hop
        quarter = z - steps if way == 0 else z + steps
        here = part(k, owners[which], None, quarter)
        at = (z_chunks.index(k), way, hop, which)
        return remote(here, here, z_sends.at[at], z_recvs.at[at], (above, below)[way])

    def foreign_copy(k, way, hop, which, arriving=False):
        quarter = z - hop - 1 if way == 0 else z + hop + 1
        here = part(k, (core_owners if arriving else owners)[which], None, quarter)
        at = (z_chunks.index(k), way, hop, which)
        return remote(here, here, foreign_sends.at[at], foreign_recvs.at[at], {"fsdp": flip(me, 1)})

    def goes(way, hop):
        return jnp.logical_and(z >= hop, z < 3) if way == 0 else jnp.logical_and(z <= 3 - hop, z > 0)

    def comes(way, hop):
        return z >= hop + 1 if way == 0 else z <= 2 - hop

    def send_z(k, hop, which):
        for way in range(2):

            @pl.when(goes(way, hop))
            def _(way=way):
                for one in which:
                    z_copy(k, way, hop, one).start()

    def own_local(k):
        return pltpu.make_async_copy(own_part(k), part(k, me), local_sems.at[k])

    def own_both(kind):
        rows, columns = pl.ds(pl.multiple_of(me * UNIT, UNIT), UNIT), pl.ds(3 * WIDE * kind, (3 * WIDE, WIDE)[kind])
        return pltpu.make_async_copy(
            shards[kind].at[2], both_all.at[0, rows, columns], local_sems.at[len(CHUNKS) + 2 + kind]
        )

    def own(k):
        for kind in (X, Y):
            copy(k, kind).start()
        if CHUNKS[k][0] != BOTH:
            own_local(k).start()
        copy(k, CORE_OWN).start()

    def pass_first(k):
        copy(k, X, True).wait_recv()
        copy(k, DIAG_Y).start()
        copy(k, Y, True).wait_recv()
        copy(k, DIAG_X).start()
        if k in z_chunks:
            send_z(k, 0, (0, 1))
        copy(k, CORE_X).start()
        copy(k, CORE_Y).start()

    def pass_second(k):
        copy(k, DIAG_Y, True).wait_recv()
        copy(k, DIAG_X, True).wait_recv()
        if k in z_chunks:
            send_z(k, 0, (2,))
        copy(k, CORE_DIAG).start()

    def pass_quarter(k, hop):
        for way in range(2):

            @pl.when(comes(way, hop))
            def _(way=way):
                for which in range(3):
                    z_copy(k, way, hop, which, True).wait_recv()

        if hop < 2:
            send_z(k, hop + 1, (0, 1, 2))
        for way in range(2):

            @pl.when(comes(way, hop))
            def _(way=way):
                for which in range(3):
                    foreign_copy(k, way, hop, which).start()

    def complete(k):
        if CHUNKS[k][0] != BOTH:
            own_local(k).wait()
        for kind in (CORE_OWN, CORE_X, CORE_Y, CORE_DIAG):
            copy(k, kind, True).wait_recv()
        if k in z_chunks:
            for hop in range(3):
                for way in range(2):

                    @pl.when(comes(way, hop))
                    def _(way=way, hop=hop):
                        for which in range(3):
                            foreign_copy(k, way, hop, which, True).wait_recv()

    def slice_copy(offset, arriving=False):
        peer = flip(me, offset)
        rows = pl.ds(pl.multiple_of((peer if arriving else me) * UNIT, UNIT), UNIT)
        target = expand_words.at[rows, :]
        source = shards[2].at[0, :, pl.ds(pl.multiple_of(peer * SLICE, SLICE), SLICE)]
        return remote(source, target, slice_sends.at[offset - 1], slice_recvs.at[offset - 1], {"fsdp": peer})

    own_slice = pltpu.make_async_copy(
        shards[2].at[0, :, pl.ds(pl.multiple_of(me * SLICE, SLICE), SLICE)],
        expand_words.at[pl.ds(pl.multiple_of(me * UNIT, UNIT), UNIT), :],
        local_sems.at[len(CHUNKS)],
    )
    own_shrink = pltpu.make_async_copy(shards[3].at[0], shrink_words, local_sems.at[len(CHUNKS) + 1])

    def start_slices():
        own_slice.start()
        own_shrink.start()
        for offset in range(1, 8):
            slice_copy(offset).start()

    def wait_slices():
        own_slice.wait()
        own_shrink.wait()
        for offset in range(1, 8):
            slice_copy(offset, True).wait_recv()

    keeps = []

    def keep_norm(kind):
        for source in (normed, inverse):
            index = [ref is source for ref in saved].index(True)
            keep(source.at[kind], kept[index].at[kind])

    def keep(source, target):
        copied = pltpu.make_async_copy(source, target, keep_sems.at[len(keeps)])
        copied.start()
        keeps.append(copied)

    def keep_weights(kind, index):
        keep(gathered[kind].at[index], weights_kept[kind].at[index])

    def keep_both():
        keep(both_all.at[0, :, 0 : 3 * WIDE], weights_kept[INWARD].at[2])
        keep(both_all.at[0, :, 3 * WIDE : 4 * WIDE], weights_kept[OUTWARD].at[2])

    def keep_saved(*refs_done):
        for done in refs_done:
            index = [ref is done for ref in saved].index(True)
            keep(saved[index], kept[index])

    def give_small():
        small_own[...] = jnp.zeros_like(small_own)
        small_own[0:16, 0:UNIT] = biases[...].astype(F32)
        small_own[16:21, 0:UNIT] = gains[...].astype(F32)
        source = lax.broadcasted_iota(jnp.int32, (4 * UNIT, 128), 0)
        target = lax.broadcasted_iota(jnp.int32, (4 * UNIT, 128), 1)
        for q in range(4):
            chosen = jnp.logical_and(target < UNIT, source == target + q * UNIT).astype(LOW)
            placed = matmul(hidden_bias[...], chosen)
            for f in range(2):
                row = 21 + 4 * f + q
                small_own[row : row + 1, :] = placed[f : f + 1]
        small_all[me] = small_own[...].astype(LOW)
        for offset in range(1, 8):
            small_copy(offset, me).start()

    def read_small():
        for offset in range(1, 8):
            small_copy(offset, flip(me, offset)).wait_recv()
        totals = jnp.zeros((21, WIDE), jnp.float32)
        hidden_parts = [jnp.zeros((1, WIDE), jnp.float32) for _ in range(4)]
        for owner in range(8):
            one = small_all[owner]
            totals = totals + matmul(one, spread(owner).astype(LOW))[:21]
            for q in range(4):
                placed = matmul(one, spread((owner % 2) * 4 + q).astype(LOW))
                row = 25 + q
                hidden_parts[owner // 2] = hidden_parts[owner // 2] + placed[row : row + 1]
        params[...] = jnp.zeros_like(params)
        params[0:21, :] = totals
        for block in range(4):
            hidden_rows[:, block * WIDE : (block + 1) * WIDE] = hidden_parts[block]
        keep_saved(params)

    def read_rows():
        rows_low[0:WORDS, :] = word_rows[...]
        rows_low[WORDS:ROWS, :] = region_rows[...]
        for at in range(0, ROWS, 128):
            transposed_into(rows_zero_t, rows_low[at : at + 128, :], at, 128)
        keep_saved(rows_zero_t)

    def transposed_into(target, values, at, count):
        target[:, pl.ds(at, count)] = values.T

    def project_into(source, at, count, module, mixed, weights):
        for third, bias_row in enumerate((3 * module, None, 3 * module + 1)):
            product = matmul(source[pl.ds(at, count), :], weights[:, third * WIDE : (third + 1) * WIDE])
            if bias_row is not None:
                product = product + params[bias_row : bias_row + 1, :]
            mixed[pl.ds(at, count), third * WIDE : (third + 1) * WIDE] = product.astype(jnp.bfloat16)

    def join(at, product, residual, bias_row, norm_at, norm_index):
        rows = pl.ds(at, 128)
        unit, scale = row_norm(residual + product + params[bias_row : bias_row + 1, :])
        normed[norm_at, rows, :] = unit
        inverse[norm_at, rows, :] = jnp.broadcast_to(scale, (128, 128))
        return unit * params[16 + norm_index : 17 + norm_index, :] + params[9 + norm_index : 10 + norm_index, :]

    def cross_in():
        project_into(rows_low, 0, ROWS, 0, mixed_cross, inward_all.at[0])
        keep_saved(mixed_cross)
        keep_weights(0, 0)

    def cross_words():
        allowed = down(word_ids[...]) == region_ids[...].astype(F32)
        attend_into(ATTEND_CROSS_WORD, mixed_cross, allowed, shares_cw, context)
        keep_saved(shares_cw)

    def cross_regions():
        allowed = down(region_ids[...]) == word_ids[...].astype(F32)
        attend_into(ATTEND_CROSS_REGION, mixed_cross, allowed, shares_cr, context)
        keep_saved(shares_cr)

    def cross_out():
        for at in range(0, ROWS, 128):
            product = matmul(context[at : at + 128, :], outward_all[0])
            one = join(at, product, rows_low[at : at + 128, :].astype(F32), 2, 0, 0)
            stream[at : at + 128, :] = one
            one_low = one.astype(LOW)
            stream_low[at : at + 128, :] = one_low
            transposed_into(rows_one_t, one_low, at, 128)
            transposed_into(context_cross_t, context[at : at + 128, :], at, 128)
        keep_saved(rows_one_t, context_cross_t)
        keep_norm(0)
        keep_weights(1, 0)

    def word_in():
        project_into(stream_low, 0, WORDS, 1, mixed_self, inward_all.at[1])
        keep_weights(0, 1)
        allowed = down(word_ids[...]) == word_ids[...].astype(F32)
        attend_into(ATTEND_WORD, mixed_self, allowed, shares_w, context)
        transposed_into(context_self_t, context[0:WORDS, :], 0, WORDS)
        keep_saved(shares_w)

    def region_in():
        project_into(stream_low, WORDS, REGIONS, 2, mixed_self, both_all.at[0])
        keep_both()

    def region_attend():
        allowed = down(region_ids[...]) == region_ids[...].astype(F32)
        attend_into(ATTEND_REGION, mixed_self, allowed, shares_r, context)
        for at in range(WORDS, ROWS, 128):
            transposed_into(context_self_t, context[at : at + 128, :], at, 128)
        keep_saved(shares_r)

    def self_out(module, first, last):
        for at in range(first, last, 128):
            weights = outward_all[1] if module == 1 else both_all[0, :, 3 * WIDE : 4 * WIDE]
            product = matmul(context[at : at + 128, :], weights)
            two = join(at, product, stream[at : at + 128, :], 3 * module + 2, 1, module)
            stream[at : at + 128, :] = two
            two_low = two.astype(LOW)
            stream_low[at : at + 128, :] = two_low
            if module == 1:
                words_two[pl.ds(pl.multiple_of(me * WORDS, WORDS), WORDS), :] = two_low
            else:
                transposed_into(rows_two_t, two_low, at - WORDS, 128)
        if module == 1:
            keep_weights(OUTWARD, 1)

    def activate(before, hidden_to, hidden_t_to, slope_to):
        below = 0.5 * (1.0 + lax.erf(before * 0.5**0.5))
        density = jnp.exp(-0.5 * before * before) * 0.3989422804014327
        value = (before * below).astype(LOW)
        hidden_to[...] = value
        hidden_t_to[...] = value.T
        slope_to[...] = (below + before * density).astype(LOW)

    def feed_in(column, columns):
        step = 256

        def tile(t, carry):
            at = pl.ds(pl.multiple_of(column + t * step, step), step)
            for row in range(0, REGIONS, 128):
                rows = slice(row, row + 128)
                before = matmul(stream_low[WORDS + row : WORDS + row + 128, :], expand_all[0, :, at])
                activate(before + hidden_rows[:, at], hidden.at[rows, at], hidden_t.at[at, rows], slope.at[rows, at])
            return carry

        lax.fori_loop(0, columns // step, tile, 0)

    def feed_out():
        for at in range(WORDS, ROWS, 128):
            product = matmul(hidden[at - WORDS : at - WORDS + 128, :], shrink_all[0])
            last_rows = join(at, product, stream[at : at + 128, :], 15, 2, 4)
            region_result[at - WORDS : at - WORDS + 128, :] = last_rows.astype(LOW)

    def words_in():
        for at in range(0, PLANE_WORDS, 128):
            rows = slice(at, at + 128)
            before = matmul(words_two[rows, :], expand_words[...]) + hidden_bias[0:1, :].astype(F32)
            activate(before, hidden_words.at[rows, :], hidden_words_t.at[:, rows], slope_words.at[rows, :])
            rows_two_words_t[:, rows] = words_two[rows, :].T
        keep_saved(slope_words, expand_words, hidden_words_t, rows_two_words_t)

    def words_out():
        for at in range(0, PLANE_WORDS, 128):
            partial[at // 128] = matmul(hidden_words[at : at + 128, :], shrink_words[...])
        sum_words.start()

    def words_last():
        last_rows = join(0, sum_words.total(), stream[0:WORDS, :], 14, 2, 3)
        word_result[...] = last_rows.astype(LOW)

    for kind in range(2):
        own_both(kind).start()
    greet(me, z)
    for kind in range(2):
        own_both(kind).wait()
    own(BOTH_2)
    give_small()
    read_rows()
    pass_first(BOTH_2)
    own(INWARD_0)
    own(OUTWARD_0)
    read_small()
    pass_second(BOTH_2)
    pass_first(INWARD_0)
    own(EXPAND_1)
    pass_quarter(BOTH_2, 0)
    pass_first(OUTWARD_0)
    own(INWARD_1)
    pass_second(INWARD_0)
    pass_quarter(BOTH_2, 1)
    complete(INWARD_0)
    cross_in()
    pass_second(OUTWARD_0)
    pass_first(EXPAND_1)
    own(OUTWARD_1)
    cross_words()
    pass_second(EXPAND_1)
    cross_regions()
    pass_quarter(BOTH_2, 2)
    complete(OUTWARD_0)
    cross_out()
    pass_first(INWARD_1)
    own(SHRINK_1)
    complete(BOTH_2)
    region_in()
    pass_quarter(EXPAND_1, 0)
    region_attend()
    pass_second(INWARD_1)
    pass_first(OUTWARD_1)
    start_slices()
    complete(INWARD_1)
    word_in()
    keep_saved(mixed_self, context_self_t)
    pass_second(OUTWARD_1)
    pass_first(SHRINK_1)
    complete(OUTWARD_1)
    self_out(1, 0, WORDS)
    gather_words.start()
    pass_second(SHRINK_1)
    pass_quarter(EXPAND_1, 1)
    self_out(2, WORDS, ROWS)
    keep_saved(rows_two_t)
    keep_norm(1)
    gather_words.first()
    own(SHRINK_REST)
    gather_words.second()
    pass_quarter(EXPAND_1, 2)
    wait_slices()
    pass_first(SHRINK_REST)
    gather_words.complete()
    words_in()
    words_out()
    complete(EXPAND_1)
    keep_weights(2, 0)
    pass_quarter(SHRINK_1, 0)
    feed_in(0, 2 * WIDE)
    pass_second(SHRINK_REST)
    sum_words.cores()
    pass_quarter(SHRINK_1, 1)
    feed_in(2 * WIDE, WIDE)
    sum_words.diagonal()
    feed_in(3 * WIDE, WIDE)
    keep_saved(hidden_t, slope)
    pass_quarter(SHRINK_1, 2)
    words_last()
    complete(SHRINK_REST)
    complete(SHRINK_1)
    keep_weights(3, 0)
    feed_out()
    keep_norm(2)
    for copied in keeps:
        copied.wait()
    for offset in range(1, 8):
        small_copy(offset, me).wait_send()
        slice_copy(offset).wait_send()
    gather_words.settle()
    for k in range(len(CHUNKS)):
        for kind in range(8):
            copy(k, kind).wait_send()
    for k in z_chunks:
        for way in range(2):
            for hop in range(3):

                @pl.when(goes(way, hop))
                def _(k=k, way=way, hop=hop):
                    for which in range(3):
                        z_copy(k, way, hop, which).wait_send()

                @pl.when(comes(way, hop))
                def _(k=k, way=way, hop=hop):
                    for which in range(3):
                        foreign_copy(k, way, hop, which).wait_send()


def forward(word_rows, region_rows, word_ids, region_ids, biases, gains, hidden_bias, shards):
    dma = pltpu.SemaphoreType.DMA
    vmem = pl.BlockSpec(memory_space=pltpu.VMEM)
    hbm = pl.BlockSpec(memory_space=pl.ANY)
    saved = [jax.ShapeDtypeStruct(*one) for one in SAVED]
    weights = [jax.ShapeDtypeStruct(one, LOW) for one in WEIGHTS]
    quarters = (sum(chunk[3] for chunk in CHUNKS), 2, 3, 3)
    outs = pl.pallas_call(
        forward_kernel,
        out_shape=[jax.ShapeDtypeStruct((WORDS, WIDE), LOW), jax.ShapeDtypeStruct((REGIONS, WIDE), LOW)] + saved + weights,
        in_specs=[vmem] * 7 + [hbm] * 4,
        out_specs=[vmem] * 2 + [hbm] * (len(saved) + len(weights)),
        scratch_shapes=[pltpu.VMEM(one.shape, one.dtype) for one in saved]
        + [pltpu.VMEM(one, LOW) for one in GATHERED]
        + [
            pltpu.VMEM((32, 128), F32),
            pltpu.VMEM((8, 32, 128), LOW),
            pltpu.VMEM((1, HIDDEN), F32),
            pltpu.VMEM((ROWS, WIDE), LOW),
            pltpu.VMEM((ROWS, WIDE), F32),
            pltpu.VMEM((ROWS, WIDE), LOW),
            pltpu.VMEM((ROWS, WIDE), LOW),
            pltpu.VMEM((REGIONS, HIDDEN), LOW),
            pltpu.VMEM((PLANE_WORDS, WIDE), LOW),
            pltpu.VMEM((PLANE_WORDS, SLICE), LOW),
            pltpu.VMEM((SLICE, WIDE), LOW),
            *row_sum_scratch(),
            dma((8,)),
            dma((8,)),
            dma((7,)),
            dma((7,)),
            dma((len(CHUNKS), 8)),
            dma((len(CHUNKS), 8)),
            dma(quarters),
            dma(quarters),
            dma(quarters),
            dma(quarters),
            dma((7,)),
            dma((7,)),
            dma((len(CHUNKS) + 4,)),
            dma((len(saved) + 12,)),
        ],
        compiler_params=pltpu.CompilerParams(
            collective_id=1, has_side_effects=True, vmem_limit_bytes=64 * 2**20 - 2**16
        ),
    )(word_rows, region_rows, word_ids, region_ids, biases, gains, hidden_bias, *shards)
    return outs[:2], outs[2 : 2 + len(saved)], outs[2 + len(saved) :]


WINDOW = 6
EARLIER_NORMS = 23
SPAN = WIDE // 2
Z_SLOTS = 10

GROUPS = (
    (8, None, 0, 0, True, (3, 0)),
    (8, None, 0, 0, False, (2, 0)),
    (8, 0, 0, REGIONS, True, (3, 1)),
    (8, 1, 0, REGIONS, False, (2, 1)),
    (2, 2, 0, WORDS, False, (1, 1)),
    (2, 2, WORDS, REGIONS, False, (1, 2)),
    (6, 3, 0, WORDS, False, (0, 1)),
    (6, 3, WORDS, REGIONS, False, (0, 2)),
    (2, 4, 0, ROWS, False, (1, 0)),
    (6, 5, 0, ROWS, False, (0, 0)),
)
UNITS = sum(group[0] for group in GROUPS)
OWNED = sum(group[0] for group in GROUPS if group[1] is None)
CROSSING = UNITS - OWNED

BLOCKS = (
    [(kind, 0, c) for c in range(4) for kind in (3, 2)]
    + [(1, 1, 0), (1, 2, 0)]
    + [(0, m, c) for m in (1, 2) for c in range(3)]
    + [(1, 0, 0)]
    + [(0, 0, c) for c in range(3)]
)


def attend_back_into(rows_of, mixed, shares, grad_context, grad_mixed, first_pair, last_pair):
    (query_at, query_count), (key_at, key_count) = rows_of
    query_rows, key_rows = pl.ds(query_at, query_count), pl.ds(key_at, key_count)

    def pair(p, carry):
        at = pl.multiple_of(p * PAIR_WIDE, PAIR_WIDE)
        at_query, at_key, at_value = (pl.ds(third * WIDE + at, PAIR_WIDE) for third in range(3))
        queries = mixed[query_rows, at_query]
        keys = mixed[key_rows, at_key]
        values = mixed[key_rows, at_value]
        grads = grad_context[query_rows, at_query]
        grad_queries = jnp.zeros((query_count, PAIR_WIDE), jnp.float32)
        grad_keys = jnp.zeros((key_count, PAIR_WIDE), jnp.float32)
        grad_values = jnp.zeros((key_count, PAIR_WIDE), jnp.float32)
        for side, chosen in enumerate(half_lanes()):
            share = shares[2 * p + side]
            grad_head = only(grads, chosen)
            wide = share.astype(jnp.float32)
            weighted = wide * dot_nt(grad_head, values)
            grad_scores = (weighted - wide * jnp.sum(weighted, axis=-1, keepdims=True)).astype(jnp.bfloat16)
            grad_values = grad_values + dot_tn(share, grad_head)
            grad_queries = grad_queries + matmul(grad_scores, only(keys, chosen))
            grad_keys = grad_keys + dot_tn(grad_scores, only(queries, chosen))
        score_scale = HEAD_DIM ** (-0.5)
        grad_mixed[query_rows, at_query] = (grad_queries * score_scale).astype(jnp.bfloat16)
        grad_mixed[key_rows, at_key] = (grad_keys * score_scale).astype(jnp.bfloat16)
        grad_mixed[key_rows, at_value] = grad_values.astype(jnp.bfloat16)
        return carry

    lax.fori_loop(first_pair, last_pair, pair, 0)


def backward_kernel(*refs):
    saved_hbm, weights = refs[:23], refs[23:27]
    word_gradient, region_gradient, small_out, *totals = refs[27:34]
    (
        params,
        word_cotangent,
        region_cotangent,
        normed,
        inverse,
        hidden_t,
        slope,
        rows_two_t,
        slope_words,
        expand_words,
        hidden_words_t,
        rows_two_words_t,
        context_self_t,
        mixed_self,
        shares_w,
        shares_r,
        rows_one_t,
        context_cross_t,
        mixed_cross,
        shares_cw,
        shares_cr,
        rows_zero_t,
        shrink_words,
    ) = saved = refs[34:57]
    (
        window,
        end_feed,
        end_self,
        end_cross,
        stream,
        grad_context,
        row_sums,
        hidden_sums,
        end_words,
        hidden_sums_words,
        owned_shrink,
        owned_out,
        owned_expand,
        partial,
        sum_core_out,
        sum_core_in,
        sum_half_out,
        sum_half_in,
        sum_full_out,
        sum_full_in,
        sum_sends,
        sum_recvs,
        gather_sends,
        gather_recvs,
        slice_sends,
        slice_recvs,
        out,
        acc,
        core_out,
        core_in,
        half_out,
        half_in,
        full_out,
        full_in,
        plane,
        end_out,
        end_in,
        mid_out,
        mid_in,
        small_in,
        small_in_plane,
        small_planes,
        saved_sems,
        window_sems,
        total_sems,
        core_send,
        core_recv,
        half_send,
        half_recv,
        full_send,
        full_recv,
        z_send,
        z_recv,
        back_send,
        back_recv,
        small_send,
        small_recv,
        free,
    ) = refs[57:]
    grad_before, before_words, grad_mixed_self, grad_mixed_cross = slope, slope_words, mixed_self, mixed_cross
    lefts = (hidden_t, rows_two_t, context_self_t, rows_one_t, context_cross_t, rows_zero_t)
    rights = (end_feed, grad_before, end_self, grad_mixed_self, end_cross, grad_mixed_cross)
    me = lax.axis_index("fsdp")
    z = lax.axis_index("rep")
    chip = me // 2
    lane = me % 2
    is_end = jnp.logical_or(z == 0, z == 3)
    is_mid = jnp.logical_or(z == 1, z == 2)
    core_peer = {"fsdp": flip(me, 1)}
    links = ({"fsdp": flip(me, 2)}, {"fsdp": flip(me, 4)})
    link_chip = (flip(chip, 1), flip(chip, 2))
    diagonal = flip(chip, 3)
    pair_peer = {"rep": flip(z, 1)}
    mid_peer = {"rep": 3 - z}
    low = LOW
    gather_words = RowGather(me, end_words, gather_sends, gather_recvs)
    sum_words = RowSum(
        me,
        partial,
        sum_core_out,
        sum_core_in,
        sum_half_out,
        sum_half_in,
        sum_full_out,
        sum_full_in,
        sum_sends,
        sum_recvs,
    )

    def load_saved(index):
        if index == EARLIER_NORMS:
            return pltpu.make_async_copy(saved_hbm[3].at[0:2], normed.at[0:2], saved_sems.at[index])
        source, target = saved_hbm[index], saved[index]
        if target is shrink_words:
            source = source.at[0]
        if target is normed:
            source, target = source.at[2], target.at[2]
        return pltpu.make_async_copy(source, target, saved_sems.at[index])

    def load_block(n):
        kind, index, c = BLOCKS[n]
        part = slice(c * WIDE, (c + 1) * WIDE)
        source = weights[kind].at[index, part, :] if kind == 3 else weights[kind].at[index, :, part]
        return pltpu.make_async_copy(source, window.at[n % WINDOW], window_sems.at[n % WINDOW])

    def wait_saved(*names):
        for name in names:
            load_saved([ref is name for ref in saved].index(True)).wait()

    first_saved = [0, 1, 2, 3, 4, 5]
    for index in first_saved:
        load_saved(index).start()
    for n in range(WINDOW):
        load_block(n).start()
    for index in [22, 8, 9, 10, 11, 6, 7, EARLIER_NORMS] + list(range(12, 22)):
        load_saved(index).start()
    greet(me, z)

    def small_copy(offset):
        peer = flip(me, offset)
        return remote(
            small_in.at[peer],
            small_in_plane.at[offset - 1],
            small_send.at[offset - 1],
            small_recv.at[offset - 1],
            {"fsdp": peer},
        )

    def small_plane_copy(offset, source):
        peer = (z + offset) % 4 if source is z else source
        return remote(
            small_planes.at[source],
            small_planes.at[source],
            small_send.at[6 + offset],
            small_recv.at[6 + offset],
            {"rep": peer},
        )

    def core_copy(u):
        slot = u % SLOTS
        return remote(core_out.at[slot], core_in.at[slot], core_send.at[slot], core_recv.at[slot], core_peer)

    def half_copy(u, way):
        slot = u % SLOTS
        return remote(
            half_out.at[slot, way], half_in.at[slot, way], half_send.at[slot, way], half_recv.at[slot, way], links[way]
        )

    def full_copy(u, way):
        slot = u % SLOTS
        return remote(
            full_out.at[slot, way], full_in.at[slot, way], full_send.at[slot, way], full_recv.at[slot, way], links[way]
        )

    def end_copy(n):
        slot = n % Z_SLOTS
        return remote(end_out.at[slot], end_in.at[slot], z_send.at[0, slot], z_recv.at[0, slot], pair_peer)

    def mid_copy(n):
        slot = n % Z_SLOTS
        return remote(mid_out.at[slot], mid_in.at[slot], z_send.at[1, slot], z_recv.at[1, slot], mid_peer)

    def back_copy(n):
        u = z_order[n]
        return remote(out.at[u], out.at[u], back_send.at[u], back_recv.at[u], pair_peer)

    def credit(u, channel, peer, slots=SLOTS, count=CROSSING):
        if u + slots < count:
            pl.semaphore_signal(free.at[channel], inc=1, device_id=peer, device_id_type=MESH)

    def spend(u, channel, slots=SLOTS):
        if u >= slots:
            pl.semaphore_wait(free.at[channel], 1)

    def per_group(u, function):
        for group in GROUPS:
            if u < group[0]:
                return function(u, *group[1:])
            u = u - group[0]

    def produce(u):
        slot = u % SLOTS
        keep = u % ACC_SLOTS
        spend(u, 0)

        def products(at, side, first_row, count, by_row, matrix):
            rows = pl.ds(first_row, count)
            column = (at % 2 if by_row else at) * SPAN
            right = rights[side][rows, pl.ds(column, SPAN)]

            def product(core):
                blocks = []
                for block in range(4):
                    owner = 2 * block + core
                    row = owner * (4 * UNIT) + (at // 2) * UNIT if by_row else owner * UNIT
                    blocks.append(lefts[side][pl.ds(pl.multiple_of(row, 16), UNIT), rows])
                return matmul(jnp.concatenate(blocks, axis=0), right)

            other = product(1 - lane).astype(low)
            for block in range(4):
                core_out[slot, block] = other[block * UNIT : (block + 1) * UNIT]
            core_copy(u).start()
            own = product(lane)
            for block in range(4):
                acc[keep, block] = own[block * UNIT : (block + 1) * UNIT]

        per_group(crossing[u], products)

    def join_cores(u):
        slot = u % SLOTS
        keep = u % ACC_SLOTS
        core_copy(u).wait()
        for way in range(2):
            spend(u, 1 + way)
        summed = acc[keep, diagonal] + core_in[slot, diagonal].astype(jnp.float32)
        half_out[slot, 0] = summed[: UNIT // 2].astype(low)
        half_out[slot, 1] = summed[UNIT // 2 :].astype(low)
        for way in range(2):
            half_copy(u, way).start()
        for block in (link_chip[0], link_chip[1], chip):
            acc[keep, block] = acc[keep, block] + core_in[slot, block].astype(jnp.float32)
        credit(u, 0, core_peer)

    def join_diagonal(u):
        slot = u % SLOTS
        keep = u % ACC_SLOTS
        for way in range(2):
            half_copy(u, way).wait()
            spend(u, 3 + way)
        half = UNIT // 2
        full_out[slot, 1, :half] = (acc[keep, link_chip[1], :half] + half_in[slot, 0].astype(jnp.float32)).astype(low)
        full_out[slot, 1, half:] = acc[keep, link_chip[1], half:].astype(low)
        full_copy(u, 1).start()
        full_out[slot, 0, half:] = (acc[keep, link_chip[0], half:] + half_in[slot, 1].astype(jnp.float32)).astype(low)
        full_out[slot, 0, :half] = acc[keep, link_chip[0], :half].astype(low)
        full_copy(u, 0).start()
        for way in range(2):
            credit(u, 1 + way, links[way])

    def join_plane(u):
        slot = u % SLOTS
        keep = u % ACC_SLOTS
        for way in range(2):
            full_copy(u, way).wait()
        summed = acc[keep, chip] + (full_in[slot, 0].astype(F32) + full_in[slot, 1].astype(F32))
        for way in range(2):
            credit(u, 3 + way, links[way])
        enter(z_order.index(crossing[u]), summed)

    def join_owned(u):
        half = slice(u % 2 * SPAN, u % 2 * SPAN + SPAN)
        if u < 8:
            summed = owned_shrink[u // 2 * UNIT : (u // 2 + 1) * UNIT, half]
        else:
            summed = owned_expand[u - 8].astype(F32)
        enter(z_order.index(u), summed)

    def enter(n, summed):
        slot = n % Z_SLOTS

        @pl.when(is_end)
        def _():
            spend(n, 5, Z_SLOTS)
            end_out[slot] = summed.astype(low)
            end_copy(n).start()

        @pl.when(is_mid)
        def _():
            plane[slot] = summed

    def join_pair(n):
        slot = n % Z_SLOTS

        @pl.when(is_end)
        def _():
            end_copy(n).wait_send()

        @pl.when(is_mid)
        def _():
            end_copy(n).wait_recv()
            spend(n, 6, Z_SLOTS)
            mid_out[slot] = (plane[slot] + end_in[slot].astype(F32)).astype(low)
            mid_copy(n).start()
            credit(n, 5, pair_peer, Z_SLOTS, UNITS)

    def join_middle(n):
        slot = n % Z_SLOTS

        @pl.when(is_mid)
        def _():
            mid_copy(n).wait()
            out[z_order[n]] = (mid_out[slot].astype(F32) + mid_in[slot].astype(F32)).astype(low)
            back_copy(n).start()
            credit(n, 6, mid_peer, Z_SLOTS, UNITS)

    def total_copy(u, at, by_row, matrix):
        kind, index = matrix
        if by_row:
            row, column = (at // 2) * UNIT, (at % 2) * SPAN
        else:
            row, column = 0, at * SPAN
        place = totals[kind].at[index, pl.ds(row, UNIT), pl.ds(column, SPAN)]
        return pltpu.make_async_copy(out.at[u], place, total_sems.at[u])

    def finish(n):
        @pl.when(is_mid)
        def _():
            back_copy(n).wait_send()

        @pl.when(is_end)
        def _():
            back_copy(n).wait_recv()

        u = z_order[n]
        per_group(u, lambda at, side, first_row, count, by_row, matrix: total_copy(u, at, by_row, matrix).start())

    crossing = [u for u in range(UNITS) if u >= OWNED]
    to_plane = LAG_CORE + LAG_A + LAG_B
    entries = [(i + to_plane, 1, u) for i, u in enumerate(crossing)]
    entries += [(OWNED_SHRINK_AT + u * 3 // 8, 0, u) for u in range(8)]
    entries += [(OWNED_EXPAND_AT + 2 * (u - 8), 0, u) for u in range(8, OWNED)]
    entries.sort()
    z_order = [u for _, _, u in entries]
    for n in range(UNITS - Z_SLOTS):
        assert entries[n + Z_SLOTS][0] >= entries[n][0] + LAG_Z
    last = entries[-1][0] + 3 * LAG_Z

    row_tiles = ((0, 0), (1, 128), (1, 256))

    def add_row(index, values):
        row_sums[index : index + 1, :] += jnp.sum(values, axis=0, keepdims=True)

    def norm_back(grad, kind, norm_index, at, ends, end_bias, end_at=None):
        rows = slice(at, at + 128)
        unit = normed[kind, rows, :]
        grad_unit = grad * params[16 + norm_index : 17 + norm_index, :]
        summed = inverse[kind, rows, :1] * (
            grad_unit
            - jnp.mean(grad_unit, axis=-1, keepdims=True)
            - unit * jnp.mean(grad_unit * unit, axis=-1, keepdims=True)
        )
        add_row(16 + norm_index, grad * unit)
        add_row(9 + norm_index, grad)
        stream[rows, :] = summed
        summed_low = summed.astype(low)
        if end_at is None:
            ends[rows, :] = summed_low
        else:
            ends[pl.ds(end_at, 128), :] = summed_low
        add_row(end_bias, summed_low.astype(jnp.float32))

    def feed_norm():
        wait_saved(params, word_cotangent, region_cotangent, normed, inverse)
        row_sums[...] = jnp.zeros_like(row_sums)
        hidden_sums[...] = jnp.zeros_like(hidden_sums)
        hidden_sums_words[...] = jnp.zeros_like(hidden_sums_words)
        own_rows = pl.multiple_of(me * WORDS, WORDS)
        norm_back(word_cotangent[...].astype(F32), 2, 3, 0, end_words, 14, own_rows)
        gather_words.start()
        for at in range(0, REGIONS, 128):
            cotangent = region_cotangent[at : at + 128, :].astype(F32)
            norm_back(cotangent, 2, 4, WORDS + at, end_feed, 15, at)

    def slice_copy(offset, arriving=False):
        peer = flip(me, offset)
        rows = pl.ds(pl.multiple_of(peer * UNIT, UNIT), UNIT)
        target = owned_expand.at[peer if arriving else me]
        return remote(
            owned_out.at[rows, :], target, slice_sends.at[offset - 1], slice_recvs.at[offset - 1], {"fsdp": peer}
        )

    def words_back():
        wait_saved(shrink_words, slope_words, expand_words)
        for at in range(0, PLANE_WORDS, 128):
            rows = slice(at, at + 128)
            before = (dot_nt(end_words[rows, :], shrink_words[...]) * slope_words[rows, :].astype(F32)).astype(low)
            before_words[rows, :] = before
            hidden_sums_words[0:1, :] += jnp.sum(before.astype(F32), axis=0, keepdims=True)
            partial[at // 128] = dot_nt(before, expand_words[...])
        sum_words.start()

    def words_shrink():
        wait_saved(hidden_words_t)
        owned_shrink[...] = matmul(hidden_words_t[...], end_words[...])

    def words_expand():
        wait_saved(rows_two_words_t)
        owned_out[...] = matmul(rows_two_words_t[...], before_words[...]).astype(low)
        for offset in range(1, 8):
            slice_copy(offset).start()
        owned_expand[me] = owned_out[pl.ds(pl.multiple_of(me * UNIT, UNIT), UNIT), :]

    def words_expanded():
        for offset in range(1, 8):
            slice_copy(offset).wait_send()
            slice_copy(offset, True).wait_recv()

    def words_rows():
        stream[0:WORDS, :] += sum_words.total()

    def next_block(n):
        if n + WINDOW < len(BLOCKS):
            load_block(n + WINDOW).start()

    def feed_back(c):
        n = 2 * c
        load_block(n).wait()
        load_block(n + 1).wait()
        columns = slice(c * WIDE, (c + 1) * WIDE)
        for at in range(0, REGIONS, 128):
            rows = slice(at, at + 128)
            grad_hidden = dot_nt(end_feed[rows, :], window[n % WINDOW])
            before = (grad_hidden * slope[rows, columns].astype(F32)).astype(low)
            grad_before[rows, columns] = before
            hidden_sums[c : c + 1, :] += jnp.sum(before.astype(F32), axis=0, keepdims=True)
            stream[WORDS + at : WORDS + at + 128, :] += dot_nt(before, window[(n + 1) % WINDOW])
        next_block(n)
        next_block(n + 1)

    def self_norm():
        for f, at in row_tiles:
            norm_back(stream[at : at + 128, :], 1, 1 + f, at, end_self, 5 + 3 * f)

    def self_context():
        for f in range(2):
            n = 8 + f
            load_block(n).wait()
            for which, at in row_tiles:
                if which == f:
                    grad_context[at : at + 128, :] = dot_nt(end_self[at : at + 128, :], window[n % WINDOW]).astype(low)
            next_block(n)

    def project_back(n, module, grad_mixed, tiles):
        for c in range(3):
            load_block(n + c).wait()
            columns = slice(c * WIDE, (c + 1) * WIDE)
            for at in tiles:
                part = grad_mixed[at : at + 128, columns]
                if c != 1:
                    add_row(3 * module + c // 2, part.astype(jnp.float32))
                stream[at : at + 128, :] += dot_nt(part, window[(n + c) % WINDOW])
            next_block(n + c)

    def cross_norm():
        for _, at in row_tiles:
            norm_back(stream[at : at + 128, :], 0, 0, at, end_cross, 2)

    def cross_context():
        n = 16
        load_block(n).wait()
        for _, at in row_tiles:
            grad_context[at : at + 128, :] = dot_nt(end_cross[at : at + 128, :], window[n % WINDOW]).astype(low)
        next_block(n)

    def give_rows():
        word_gradient[...] = stream[0:WORDS, :]
        region_gradient[...] = stream[WORDS:ROWS, :]

    def exact_nt(left, right):
        return lax.dot_general(
            left,
            right.astype(jnp.float32),
            (((1,), (1,)), ((), ())),
            precision=lax.Precision.HIGHEST,
            preferred_element_type=jnp.float32,
        )

    def give_small():
        small_in[...] = jnp.zeros_like(small_in)
        for owner in range(8):
            small_in[owner, 0:21, :] = exact_nt(row_sums[...], spread(owner))[:21]
        for place in range(8):
            placed = exact_nt(hidden_sums[...], spread(place))
            for c in range(4):
                row = 25 + place % 4
                small_in[2 * c + place // 4, row : row + 1, :] = placed[c : c + 1]
        source = lax.broadcasted_iota(jnp.int32, (128, SLICE), 0)
        target = lax.broadcasted_iota(jnp.int32, (128, SLICE), 1)
        for q in range(4):
            chosen = jnp.logical_and(source < UNIT, target == source + q * UNIT)
            small_in[me, 21 + q : 22 + q, :] = exact_nt(hidden_sums_words[...], chosen)[0:1]
        for offset in range(1, 8):
            small_copy(offset).start()

    def join_small():
        summed = small_in[me]
        for offset in range(1, 8):
            small_copy(offset).wait()
            summed = summed + small_in_plane[offset - 1]
        small_planes[z] = summed
        for offset in range(1, 4):
            small_plane_copy(offset, z).start()

    def finish_small():
        for offset in range(1, 4):
            small_plane_copy(offset, z).wait_send()
            small_plane_copy(offset, (z + 4 - offset) % 4).wait_recv()
        small_out[...] = small_planes[0] + small_planes[1] + (small_planes[2] + small_planes[3])

    def self_back(rows_of, shares, first, last):
        attend_back_into(rows_of, mixed_self, shares, grad_context, grad_mixed_self, first, last)

    def cross_back(rows_of, shares, first, last):
        attend_back_into(rows_of, mixed_cross, shares, grad_context, grad_mixed_cross, first, last)

    pieces = {
        0: (gather_words.first, lambda: wait_saved(slope)),
        1: (gather_words.second, functools.partial(feed_back, 0)),
        2: (gather_words.complete, words_back),
        3: (functools.partial(feed_back, 1),),
        4: (sum_words.cores, words_shrink),
        5: (functools.partial(feed_back, 2), words_expand),
        6: (sum_words.diagonal,),
        7: (functools.partial(feed_back, 3), lambda: wait_saved(rows_two_t)),
        8: (words_rows, gather_words.settle),
        9: (words_expanded,),
        10: (lambda: load_saved(EARLIER_NORMS).wait(), self_norm),
        11: (self_context, lambda: wait_saved(context_self_t, mixed_self, shares_w)),
        12: (lambda: self_back(ATTEND_WORD, shares_w, 0, 3),),
        13: (lambda: self_back(ATTEND_WORD, shares_w, 3, 6), lambda: wait_saved(shares_r, rows_one_t)),
        **{14 + p: (functools.partial(self_back, ATTEND_REGION, shares_r, p, p + 1),) for p in range(6)},
        20: (lambda: project_back(10, 1, grad_mixed_self, (0,)),),
        21: (lambda: project_back(13, 2, grad_mixed_self, (128, 256)),),
        23: (cross_norm, lambda: wait_saved(context_cross_t, mixed_cross, shares_cw, shares_cr, rows_zero_t)),
        24: (cross_context,),
        **{25 + p: (functools.partial(cross_back, ATTEND_CROSS_WORD, shares_cw, 2 * p, 2 * p + 2),) for p in range(3)},
        **{28 + p: (functools.partial(cross_back, ATTEND_CROSS_REGION, shares_cr, 2 * p, 2 * p + 2),) for p in range(3)},
        32: (lambda: project_back(17, 0, grad_mixed_cross, (0, 128, 256)),),
        33: (give_rows,),
        34: (give_small,),
        37: (join_small,),
        40: (finish_small,),
    }

    feed_norm()
    wait_saved(hidden_t)
    for i in range(last + 1):
        for n, (entry, _, _) in enumerate(entries):
            if i == entry + 3 * LAG_Z:
                finish(n)
        for n, (entry, _, _) in enumerate(entries):
            if i == entry + 2 * LAG_Z:
                join_middle(n)
        for n, (entry, _, _) in enumerate(entries):
            if i == entry + LAG_Z:
                join_pair(n)
        for entry, crosses, u in entries:
            if i == entry and not crosses:
                join_owned(u)
        for lag, stage in ((to_plane, join_plane), (LAG_CORE + LAG_A, join_diagonal), (LAG_CORE, join_cores), (0, produce)):
            if 0 <= i - lag < CROSSING:
                stage(i - lag)
        for piece in pieces.get(i, ()):
            piece()
    for u in range(UNITS):
        per_group(u, lambda at, side, first_row, count, by_row, matrix: total_copy(u, at, by_row, matrix).wait())


def backward(saved, shrink, weights):
    block = (UNIT, SPAN)
    low, f32 = jnp.bfloat16, jnp.float32
    dma = pltpu.SemaphoreType.DMA
    vmem = pl.BlockSpec(memory_space=pltpu.VMEM)
    hbm = pl.BlockSpec(memory_space=pl.ANY)
    shape = jax.ShapeDtypeStruct
    small = (32, 128)
    return pl.pallas_call(
        backward_kernel,
        out_shape=(
            shape((WORDS, WIDE), f32),
            shape((REGIONS, WIDE), f32),
            shape(small, f32),
            shape((3, UNIT, 3 * WIDE), low),
            shape((3, UNIT, WIDE), low),
            shape((2, UNIT, HIDDEN), low),
            shape((2, 4 * UNIT, WIDE), low),
        ),
        in_specs=[hbm] * (len(saved) + 1 + len(weights)),
        out_specs=[vmem] * 3 + [hbm] * 4,
        scratch_shapes=[pltpu.VMEM(array.shape, array.dtype) for array in saved]
        + [
            pltpu.VMEM((SLICE, WIDE), low),
            pltpu.VMEM((WINDOW, WIDE, WIDE), low),
            pltpu.VMEM((REGIONS, WIDE), low),
            pltpu.VMEM((ROWS, WIDE), low),
            pltpu.VMEM((ROWS, WIDE), low),
            pltpu.VMEM((ROWS, WIDE), f32),
            pltpu.VMEM((ROWS, WIDE), low),
            pltpu.VMEM((24, WIDE), f32),
            pltpu.VMEM((8, WIDE), f32),
            pltpu.VMEM((PLANE_WORDS, WIDE), low),
            pltpu.VMEM((8, SLICE), f32),
            pltpu.VMEM((SLICE, WIDE), f32),
            pltpu.VMEM((WIDE, SLICE), low),
            pltpu.VMEM((8, UNIT, SLICE), low),
            *row_sum_scratch(),
            dma((8,)),
            dma((8,)),
            dma((7,)),
            dma((7,)),
            pltpu.VMEM((UNITS,) + block, low),
            pltpu.VMEM((ACC_SLOTS, 4) + block, f32),
            pltpu.VMEM((SLOTS, 4) + block, low),
            pltpu.VMEM((SLOTS, 4) + block, low),
            pltpu.VMEM((SLOTS, 2, UNIT // 2, SPAN), low),
            pltpu.VMEM((SLOTS, 2, UNIT // 2, SPAN), low),
            pltpu.VMEM((SLOTS, 2) + block, low),
            pltpu.VMEM((SLOTS, 2) + block, low),
            pltpu.VMEM((Z_SLOTS,) + block, f32),
            pltpu.VMEM((Z_SLOTS,) + block, low),
            pltpu.VMEM((Z_SLOTS,) + block, low),
            pltpu.VMEM((Z_SLOTS,) + block, low),
            pltpu.VMEM((Z_SLOTS,) + block, low),
            pltpu.VMEM((8,) + small, f32),
            pltpu.VMEM((7,) + small, f32),
            pltpu.VMEM((4,) + small, f32),
            dma((24,)),
            dma((WINDOW,)),
            dma((UNITS,)),
            dma((SLOTS,)),
            dma((SLOTS,)),
            dma((SLOTS, 2)),
            dma((SLOTS, 2)),
            dma((SLOTS, 2)),
            dma((SLOTS, 2)),
            dma((2, Z_SLOTS)),
            dma((2, Z_SLOTS)),
            dma((UNITS,)),
            dma((UNITS,)),
            dma((10,)),
            dma((10,)),
            pltpu.SemaphoreType.REGULAR((7,)),
        ],
        compiler_params=pltpu.CompilerParams(
            collective_id=0, has_side_effects=True, vmem_limit_bytes=64 * 2**20 - 2**16
        ),
    )(*saved, shrink, *weights)


def deliver_kernel(*refs):
    moved, small, totals = refs[:4], refs[4], refs[5:9]
    moved_out, bias_out, gain_out, hidden_out, totals_out = refs[9:13], refs[13], refs[14], refs[15], refs[16:20]
    narrow, wide, held = refs[20:24], refs[24:28], refs[28:32]
    take_sems, give_sems, load_sems, store_sems = refs[32:]
    takes = [pltpu.make_async_copy(moved[i], held[i], take_sems.at[i]) for i in range(4)]
    gives = [pltpu.make_async_copy(held[i], moved_out[i], give_sems.at[i]) for i in range(4)]
    pieces = [(kind, index) for kind in range(4) for index in range(totals[kind].shape[0])]
    loads = [
        pltpu.make_async_copy(totals[kind].at[index], narrow[kind].at[index], load_sems.at[i])
        for i, (kind, index) in enumerate(pieces)
    ]
    stores = [
        pltpu.make_async_copy(wide[kind].at[index], totals_out[kind].at[index], store_sems.at[i])
        for i, (kind, index) in enumerate(pieces)
    ]
    for one in loads + takes:
        one.start()
    bias_out[...] = small[0:16, 0:UNIT]
    gain_out[...] = small[16:21, 0:UNIT]
    source = lax.broadcasted_iota(jnp.int32, (128, 4 * UNIT), 0)
    target = lax.broadcasted_iota(jnp.int32, (128, 4 * UNIT), 1)
    for f in range(2):
        row = jnp.zeros((1, 4 * UNIT), F32)
        for q in range(4):
            chosen = jnp.logical_and(source < UNIT, target == source + q * UNIT).astype(F32)
            line = 21 + 4 * f + q
            row = row + jnp.dot(
                small[line : line + 1, :], chosen, precision=lax.Precision.HIGHEST, preferred_element_type=F32
            )
        hidden_out[f : f + 1, :] = row
    for i, (kind, index) in enumerate(pieces):
        loads[i].wait()
        wide[kind][index] = narrow[kind][index].astype(F32)
        stores[i].start()
    for i in range(4):
        takes[i].wait()
        gives[i].start()
    for one in gives + stores:
        one.wait()


def deliver(moved, small, totals):
    vmem = pl.BlockSpec(memory_space=pltpu.VMEM)
    hbm = pl.BlockSpec(memory_space=pl.ANY)
    shape = jax.ShapeDtypeStruct
    widened = [shape(total.shape, F32) for total in totals]
    sem = pltpu.SemaphoreType.DMA((4,))
    piece_sem = pltpu.SemaphoreType.DMA((sum(total.shape[0] for total in totals),))
    return pl.pallas_call(
        deliver_kernel,
        out_shape=[shape(one.shape, one.dtype) for one in moved]
        + [shape((16, UNIT), F32), shape((5, UNIT), F32), shape((2, 4 * UNIT), F32)]
        + widened,
        in_specs=[hbm] * 4 + [vmem] + [hbm] * 4,
        out_specs=[hbm] * 4 + [vmem] * 3 + [hbm] * 4,
        scratch_shapes=[pltpu.VMEM(one.shape, one.dtype) for one in totals]
        + [pltpu.VMEM(one.shape, F32) for one in totals]
        + [pltpu.VMEM(one.shape, one.dtype) for one in moved]
        + [sem, sem, piece_sem, piece_sem],
        compiler_params=pltpu.CompilerParams(vmem_limit_bytes=64 * 2**20 - 2**16),
    )(*moved, small, *totals)


def paired(
    word_rows,
    region_rows,
    word_segment,
    region_segment,
    inward,
    outward,
    biases,
    norm_gain,
    expand_weight,
    shrink_weight,
    hidden_bias,
    word_cotangent,
    region_cotangent,
):
    results, saved, weights = forward(
        word_rows,
        region_rows,
        word_segment,
        region_segment,
        biases,
        norm_gain,
        hidden_bias,
        (inward, outward, expand_weight, shrink_weight),
    )
    word_gradient, region_gradient, small, *totals = backward(
        (saved[0], word_cotangent, region_cotangent, *saved[1:]), shrink_weight, weights
    )
    word_out, region_out, word_gradient, region_gradient, bias, gain, hidden, *totals = deliver(
        (*results, word_gradient, region_gradient), small, totals
    )
    inward_total, outward_total, expand_total, shrink_total = totals
    return (
        word_out,
        region_out,
        word_gradient,
        region_gradient,
        inward_total,
        outward_total,
        bias,
        gain,
        expand_total,
        shrink_total,
        hidden,
    )


def general(
    devices,
    word_rows,
    region_rows,
    word_segment,
    region_segment,
    inward,
    outward,
    biases,
    norm_gain,
    expand_weight,
    shrink_weight,
    hidden_bias,
    word_cotangent,
    region_cotangent,
):
    words_count = word_rows.shape[0]
    width = word_rows.shape[1]
    word_ids = word_segment[0]
    region_ids = region_segment[0]
    cross_mask = word_ids[:, None] == region_ids[None, :]
    word_mask = word_ids[:, None] == word_ids[None, :]
    region_mask = region_ids[:, None] == region_ids[None, :]
    shard = biases.shape[1]
    per_shard = hidden_bias.shape[1] // shard
    small_shard = jnp.concatenate([biases, norm_gain, hidden_bias.reshape(2 * per_shard, shard)], axis=0)
    small_all = lax.all_gather(small_shard, "fsdp", axis=0)
    bias_count = biases.shape[0]
    gain_count = norm_gain.shape[0]
    row_params = small_all[:, : bias_count + gain_count].transpose(1, 0, 2).reshape(bias_count + gain_count, width)
    hidden_all = (
        small_all[:, bias_count + gain_count :]
        .reshape(devices, 2, per_shard * shard)
        .transpose(1, 0, 2)
        .reshape(2, devices * per_shard * shard)
    )
    inward_all, outward_all = (
        lax.all_gather(inward, "fsdp", axis=1, tiled=True),
        lax.all_gather(outward, "fsdp", axis=1, tiled=True),
    )
    attend_set = (
        inward_all,
        outward_all,
        row_params[:bias_count].astype(jnp.float32),
        row_params[bias_count:].astype(jnp.float32),
    )
    crossed, cross_kept = cross_forward(word_rows, region_rows, attend_set, cross_mask)
    word_one, word_kept = self_forward(crossed[:words_count], attend_set, 1, word_mask)
    region_one, region_kept = self_forward(crossed[words_count:], attend_set, 2, region_mask)
    expand_all, shrink_all = (
        lax.all_gather(expand_weight, "fsdp", axis=1, tiled=True),
        lax.all_gather(shrink_weight, "fsdp", axis=1, tiled=True),
    )
    feed_set = (expand_all, shrink_all, hidden_all)
    word_two, word_feed = feed_forward(word_one, feed_set, 0, attend_set)
    region_two, region_feed = feed_forward(region_one, feed_set, 1, attend_set)
    word_back = feed_backward(word_cotangent.astype(jnp.float32), word_feed, feed_set, 0, attend_set[3])
    region_back = feed_backward(region_cotangent.astype(jnp.float32), region_feed, feed_set, 1, attend_set[3])
    word_self = self_backward(word_back[0], word_kept, attend_set, 1, word_mask)
    region_self = self_backward(region_back[0], region_kept, attend_set, 2, region_mask)
    grad_crossed = jnp.concatenate([word_self[0], region_self[0]], axis=0)
    cross_back = cross_backward(grad_crossed, cross_kept, attend_set, cross_mask, words_count)
    row_grads = jnp.stack(
        [
            cross_back[3][0],
            cross_back[3][1],
            cross_back[3][2],
            word_self[3][0],
            word_self[3][1],
            word_self[3][2],
            region_self[3][0],
            region_self[3][1],
            region_self[3][2],
            cross_back[5],
            word_self[5],
            region_self[5],
            word_back[6],
            region_back[6],
            word_back[4],
            region_back[4],
            cross_back[4],
            word_self[4],
            region_self[4],
            word_back[5],
            region_back[5],
        ]
    )
    hidden_grads = jnp.stack([word_back[3], region_back[3]])
    small_grads = jnp.concatenate(
        [
            row_grads.reshape(bias_count + gain_count, devices, shard).transpose(1, 0, 2),
            hidden_grads.reshape(2, devices, per_shard, shard)
            .transpose(1, 0, 2, 3)
            .reshape(devices, 2 * per_shard, shard),
        ],
        axis=1,
    )

    def reduced(products, axis):
        mine = lax.psum_scatter(jnp.stack(products), "fsdp", scatter_dimension=axis, tiled=True)
        return lax.psum(mine.astype(jnp.bfloat16), "rep").astype(jnp.float32)

    shrink_total = reduced([matmul_tn(*word_back[2]), matmul_tn(*region_back[2])], 1)
    expand_total = reduced([matmul_tn(*word_back[1]), matmul_tn(*region_back[1])], 1)
    outward_total = reduced([matmul_tn(*cross_back[2]), matmul_tn(*word_self[2]), matmul_tn(*region_self[2])], 1)
    inward_total = reduced([matmul_tn(*cross_back[1]), matmul_tn(*word_self[1]), matmul_tn(*region_self[1])], 1)
    small_total = lax.psum(lax.psum_scatter(small_grads, "fsdp", scatter_dimension=0, tiled=False), "rep")
    grad_rows = cross_back[0]
    return (
        word_two.astype(jnp.bfloat16),
        region_two.astype(jnp.bfloat16),
        grad_rows[:words_count],
        grad_rows[words_count:],
        inward_total,
        outward_total,
        small_total[:bias_count],
        small_total[bias_count : bias_count + gain_count],
        expand_total,
        shrink_total,
        small_total[bias_count + gain_count :].reshape(2, per_shard * shard),
    )


def solution(mesh):
    sizes = (mesh.shape["rep"], mesh.shape["fsdp"])
    return jax.shard_map(
        paired if sizes == (4, 8) else functools.partial(general, mesh.shape["fsdp"]),
        mesh=mesh,
        in_specs=(
            P(("rep", "fsdp"), None),
            P(("rep", "fsdp"), None),
            P(("rep", "fsdp"), None),
            P(("rep", "fsdp"), None),
            P(None, "fsdp", None),
            P(None, "fsdp", None),
            P(None, "fsdp"),
            P(None, "fsdp"),
            P(None, "fsdp", None),
            P(None, "fsdp", None),
            P(None, "fsdp"),
            P(("rep", "fsdp"), None),
            P(("rep", "fsdp"), None),
        ),
        out_specs=(
            P(("rep", "fsdp"), None),
            P(("rep", "fsdp"), None),
            P(("rep", "fsdp"), None),
            P(("rep", "fsdp"), None),
            P(None, "fsdp", None),
            P(None, "fsdp", None),
            P(None, "fsdp"),
            P(None, "fsdp"),
            P(None, "fsdp", None),
            P(None, "fsdp", None),
            P(None, "fsdp"),
        ),
        check_vma=False,
    )
```

```python
import functools

import jax
import jax.numpy as jnp
from jax import lax
from jax.experimental import pallas as pl
from jax.experimental.pallas import tpu as pltpu
from jax.sharding import PartitionSpec as P

MESH = pl.DeviceIdType.MESH

HEADS = 12
HEAD_DIM = 64


norm_epsilon = 1e-12
masked_score = -1e30


def matmul(left_op, right_op):
    return jnp.dot(left_op, right_op, preferred_element_type=jnp.float32)


def matmul_tn(left_op, right_op):
    return lax.dot_general(
        left_op, right_op, (((0,), (0,)), ((), ())), preferred_element_type=jnp.float32
    )


def matmul_nt(left_op, right_op):
    return lax.dot_general(
        left_op, right_op, (((1,), (1,)), ((), ())), preferred_element_type=jnp.float32
    )


def column_sums(values):
    return jnp.sum(values, axis=0, dtype=jnp.float32)


def heads_of(rows_in):
    return rows_in.reshape(rows_in.shape[0], HEADS, HEAD_DIM)


def merge_heads(head_rows):
    return head_rows.reshape(head_rows.shape[0], -1)


def normalize(summed, gain_row, shift_row):
    center = summed - jnp.mean(summed, axis=-1, keepdims=True)
    inverse = lax.rsqrt(jnp.mean(center * center, axis=-1, keepdims=True) + norm_epsilon)
    normed = center * inverse
    return (normed * gain_row + shift_row, (normed, inverse))


def normalize_back(grad_out, norm_stats, gain_row):
    normed, inverse = norm_stats
    grad_normed = grad_out * gain_row
    grad_sum = inverse * (
        grad_normed
        - jnp.mean(grad_normed, axis=-1, keepdims=True)
        - normed * jnp.mean(grad_normed * normed, axis=-1, keepdims=True)
    )
    return (grad_sum, column_sums(grad_out * normed), column_sums(grad_out))


def score_block(queries, key_rows, allowed):
    scores = jnp.einsum(
        "qhd,khd->hqk", heads_of(queries), heads_of(key_rows), preferred_element_type=jnp.float32
    ) * HEAD_DIM ** (-0.5)
    return jnp.where(allowed[None], scores, masked_score)


def attend(queries, key_rows, value_rows, allowed):
    scores = score_block(queries, key_rows, allowed)
    top_score = jnp.max(scores, axis=-1, keepdims=True)
    log_total = top_score + jnp.log(jnp.sum(jnp.exp(scores - top_score), axis=-1, keepdims=True))
    shares = jnp.exp(scores - log_total).astype(jnp.bfloat16)
    context = jnp.einsum(
        "hqk,khd->qhd", shares, heads_of(value_rows), preferred_element_type=jnp.float32
    )
    return (merge_heads(context).astype(jnp.bfloat16), log_total)


def attend_back(queries, key_rows, value_rows, allowed, log_total, grad_context):
    shares = jnp.exp(score_block(queries, key_rows, allowed) - log_total)
    grad_heads = heads_of(grad_context)
    grad_shares = jnp.einsum(
        "qhd,khd->hqk", grad_heads, heads_of(value_rows), preferred_element_type=jnp.float32
    )
    grad_values = jnp.einsum(
        "hqk,qhd->khd", shares.astype(jnp.bfloat16), grad_heads, preferred_element_type=jnp.float32
    )
    grad_scores = (
        shares * (grad_shares - jnp.sum(shares * grad_shares, axis=-1, keepdims=True))
    ).astype(jnp.bfloat16)
    score_scale = HEAD_DIM ** (-0.5)
    grad_queries = (
        jnp.einsum(
            "hqk,khd->qhd", grad_scores, heads_of(key_rows), preferred_element_type=jnp.float32
        )
        * score_scale
    )
    grad_keys = (
        jnp.einsum(
            "hqk,qhd->khd", grad_scores, heads_of(queries), preferred_element_type=jnp.float32
        )
        * score_scale
    )
    return (merge_heads(grad_queries), merge_heads(grad_keys), merge_heads(grad_values))


def project(rows_low, weight, bias_rows, module):
    width = weight.shape[0]
    bias_all = jnp.concatenate(
        [bias_rows[3 * module], jnp.zeros((width,), jnp.float32), bias_rows[3 * module + 1]]
    )
    return (matmul(rows_low, weight) + bias_all).astype(jnp.bfloat16)


def project_back(grad_sum, grad_parts, rows_low, weight):
    width = weight.shape[0]
    grad_mixed = jnp.concatenate(grad_parts, axis=1).astype(jnp.bfloat16)
    grad_weight = (rows_low, grad_mixed)
    grad_bias = column_sums(grad_mixed)
    grad_rows = grad_sum + matmul_nt(grad_mixed, weight)
    return (grad_rows, grad_weight, grad_bias[:width], grad_bias[2 * width :])


def branch_back(grad_out, context, norm_stats, gain_row, outward_one):
    grad_sum, grad_gain, grad_shift = normalize_back(grad_out, norm_stats, gain_row)
    grad_branch = grad_sum.astype(jnp.bfloat16)
    grad_outward = (context, grad_branch)
    grad_context = matmul_nt(grad_branch, outward_one).astype(jnp.bfloat16)
    return (grad_sum, grad_context, grad_outward, column_sums(grad_branch), grad_gain, grad_shift)


def self_forward(rows_in, weights, module, allowed):
    inward_all, outward_all, bias_rows, gain_rows = weights
    width = rows_in.shape[1]
    rows_low = rows_in.astype(jnp.bfloat16)
    mixed = project(rows_low, inward_all[module], bias_rows, module)
    context, log_total = attend(
        mixed[:, :width], mixed[:, width : 2 * width], mixed[:, 2 * width :], allowed
    )
    summed = rows_in + matmul(context, outward_all[module]) + bias_rows[3 * module + 2]
    result, norm_stats = normalize(summed, gain_rows[module], bias_rows[9 + module])
    return (result, (rows_low, mixed, context, log_total, norm_stats))


def self_backward(grad_out, kept, weights, module, allowed):
    inward_all, outward_all, bias_rows, gain_rows = weights
    rows_low, mixed, context, log_total, norm_stats = kept
    width = rows_low.shape[1]
    grad_sum, grad_context, grad_outward, grad_bias_out, grad_gain, grad_shift = branch_back(
        grad_out, context, norm_stats, gain_rows[module], outward_all[module]
    )
    grad_parts = attend_back(
        mixed[:, :width],
        mixed[:, width : 2 * width],
        mixed[:, 2 * width :],
        allowed,
        log_total,
        grad_context,
    )
    grad_rows, grad_inward, grad_bias_query, grad_bias_value = project_back(
        grad_sum, grad_parts, rows_low, inward_all[module]
    )
    return (
        grad_rows,
        grad_inward,
        grad_outward,
        (grad_bias_query, grad_bias_value, grad_bias_out),
        grad_gain,
        grad_shift,
    )


def cross_forward(word_rows, region_rows, weights, cross_mask):
    inward_all, outward_all, bias_rows, gain_rows = weights
    words_count = word_rows.shape[0]
    width = word_rows.shape[1]
    rows_low = jnp.concatenate([word_rows, region_rows], axis=0)
    mixed = project(rows_low, inward_all[0], bias_rows, 0)
    word_mix = mixed[:words_count]
    region_mix = mixed[words_count:]
    word_context, word_total = attend(
        word_mix[:, :width],
        region_mix[:, width : 2 * width],
        region_mix[:, 2 * width :],
        cross_mask,
    )
    region_context, region_total = attend(
        region_mix[:, :width],
        word_mix[:, width : 2 * width],
        word_mix[:, 2 * width :],
        cross_mask.T,
    )
    context = jnp.concatenate([word_context, region_context], axis=0)
    summed = rows_low.astype(jnp.float32) + matmul(context, outward_all[0]) + bias_rows[2]
    result, norm_stats = normalize(summed, gain_rows[0], bias_rows[9])
    return (result, (rows_low, mixed, context, word_total, region_total, norm_stats))


def cross_backward(grad_out, kept, weights, cross_mask, words_count):
    inward_all, outward_all, bias_rows, gain_rows = weights
    rows_low, mixed, context, word_total, region_total, norm_stats = kept
    width = rows_low.shape[1]
    grad_sum, grad_context, grad_outward, grad_bias_out, grad_gain, grad_shift = branch_back(
        grad_out, context, norm_stats, gain_rows[0], outward_all[0]
    )
    word_mix = mixed[:words_count]
    region_mix = mixed[words_count:]
    word_query_grad, region_key_grad, region_value_grad = attend_back(
        word_mix[:, :width],
        region_mix[:, width : 2 * width],
        region_mix[:, 2 * width :],
        cross_mask,
        word_total,
        grad_context[:words_count],
    )
    region_query_grad, word_key_grad, word_value_grad = attend_back(
        region_mix[:, :width],
        word_mix[:, width : 2 * width],
        word_mix[:, 2 * width :],
        cross_mask.T,
        region_total,
        grad_context[words_count:],
    )
    grad_parts = (
        jnp.concatenate([word_query_grad, region_query_grad], axis=0),
        jnp.concatenate([word_key_grad, region_key_grad], axis=0),
        jnp.concatenate([word_value_grad, region_value_grad], axis=0),
    )
    grad_rows, grad_inward, grad_bias_query, grad_bias_value = project_back(
        grad_sum, grad_parts, rows_low, inward_all[0]
    )
    return (
        grad_rows,
        grad_inward,
        grad_outward,
        (grad_bias_query, grad_bias_value, grad_bias_out),
        grad_gain,
        grad_shift,
    )


def gelu_exact(values):
    return jax.nn.gelu(values, approximate=False)


def feed_forward(rows_in, weights, feed_index, attend_set):
    expand_all, shrink_all, hidden_all = weights
    bias_rows, gain_rows = (attend_set[2], attend_set[3])
    rows_low = rows_in.astype(jnp.bfloat16)
    before = matmul(rows_low, expand_all[feed_index]) + hidden_all[feed_index].astype(jnp.float32)
    hidden = gelu_exact(before).astype(jnp.bfloat16)
    summed = rows_in + matmul(hidden, shrink_all[feed_index]) + bias_rows[14 + feed_index]
    result, norm_stats = normalize(summed, gain_rows[3 + feed_index], bias_rows[12 + feed_index])
    return (result, (rows_low, before, hidden, norm_stats))


def feed_backward(grad_out, kept, weights, feed_index, gain_rows):
    expand_all, shrink_all, hidden_all = weights
    rows_low, before, hidden, norm_stats = kept
    grad_sum, grad_gain, grad_shift = normalize_back(
        grad_out, norm_stats, gain_rows[3 + feed_index]
    )
    grad_branch = grad_sum.astype(jnp.bfloat16)
    grad_shrink = (hidden, grad_branch)
    grad_hidden = matmul_nt(grad_branch, shrink_all[feed_index])
    unused_value, slope_back = jax.vjp(gelu_exact, before)
    grad_before = slope_back(grad_hidden)[0].astype(jnp.bfloat16)
    grad_expand = (rows_low, grad_before)
    grad_rows = grad_sum + matmul_nt(grad_before, expand_all[feed_index])
    return (
        grad_rows,
        grad_expand,
        grad_shrink,
        column_sums(grad_before),
        column_sums(grad_branch),
        grad_gain,
        grad_shift,
    )


UNIT = 96
WIDE = 768
SLOTS = 6
ACC_SLOTS = 9
LAG_CORE = 2
LAG_A = 3
LAG_B = 3
LAG_Z = 3
SHRINK_QUARTERED = 256
OWNED_SHRINK_AT = 5
OWNED_EXPAND_AT = 10
WORDS = 128
REGIONS = 256
ROWS = 384
HIDDEN = 3072
SLICE = HIDDEN // 8
PLANE_WORDS = 8 * WORDS
PAIRS_OF_HEADS = 6
PAIR_WIDE = 128
LOW, F32 = jnp.bfloat16, jnp.float32

X, Y, DIAG_Y, DIAG_X, CORE_OWN, CORE_X, CORE_Y, CORE_DIAG = range(8)


def flip(position, bits):
    return lax.bitwise_xor(position, bits)


def remote(src, dst, send_sem, recv_sem, peer):
    return pltpu.make_async_remote_copy(
        src_ref=src, dst_ref=dst, send_sem=send_sem, recv_sem=recv_sem, device_id=peer, device_id_type=MESH
    )


def greet(me, z):
    barrier = pltpu.get_barrier_semaphore()
    for offset in range(1, 8):
        pl.semaphore_signal(barrier, inc=1, device_id={"fsdp": flip(me, offset)}, device_id_type=MESH)
    for offset in range(1, 4):
        pl.semaphore_signal(barrier, inc=1, device_id={"rep": (z + offset) % 4}, device_id_type=MESH)
    pl.semaphore_wait(barrier, 10)


def route(me, kind, arriving):
    owner, half, step = {
        X: (2 if arriving else 0, None, 2),
        Y: (4 if arriving else 0, None, 4),
        DIAG_Y: (6 if arriving else 2, 0, 4),
        DIAG_X: (6 if arriving else 4, 1, 2),
        CORE_OWN: (1 if arriving else 0, None, 1),
        CORE_X: (3 if arriving else 2, None, 1),
        CORE_Y: (5 if arriving else 4, None, 1),
        CORE_DIAG: (7 if arriving else 6, None, 1),
    }[kind]
    return flip(me, owner), half, {"fsdp": flip(me, step)}


class RowGather:
    def __init__(self, me, rows, sends, recvs):
        self.me, self.rows, self.sends, self.recvs = me, rows, sends, recvs

    def copy(self, kind, arriving=False):
        owner, half, peer = route(self.me, kind, arriving)
        first, count = (owner * WORDS, WORDS) if half is None else (owner * WORDS + half * (WORDS // 2), WORDS // 2)
        here = self.rows.at[pl.ds(pl.multiple_of(first, 16), count), :]
        return remote(here, here, self.sends.at[kind], self.recvs.at[kind], peer)

    def start(self):
        for kind in (X, Y, CORE_OWN):
            self.copy(kind).start()

    def first(self):
        self.copy(X, True).wait_recv()
        self.copy(DIAG_Y).start()
        self.copy(CORE_X).start()
        self.copy(Y, True).wait_recv()
        self.copy(DIAG_X).start()
        self.copy(CORE_Y).start()

    def second(self):
        self.copy(DIAG_Y, True).wait_recv()
        self.copy(DIAG_X, True).wait_recv()
        self.copy(CORE_DIAG).start()

    def complete(self):
        for kind in (CORE_OWN, CORE_X, CORE_Y, CORE_DIAG):
            self.copy(kind, True).wait_recv()

    def settle(self):
        for kind in range(8):
            self.copy(kind).wait_send()


class RowSum:
    def __init__(self, me, partial, core_out, core_in, half_out, half_in, full_out, full_in, sends, recvs):
        self.me, self.partial, self.sends, self.recvs = me, partial, sends, recvs
        self.core_out, self.core_in = core_out, core_in
        self.half_out, self.half_in, self.full_out, self.full_in = half_out, half_in, full_out, full_in
        self.chip, self.lane = me // 2, me % 2

    def copy(self, at):
        if at == 0:
            source, target, peer = self.core_out, self.core_in, 1
        elif at < 3:
            source, target, peer = self.half_out.at[at - 1], self.half_in.at[at - 1], (2, 4)[at - 1]
        else:
            source, target, peer = self.full_out.at[at - 3], self.full_in.at[at - 3], (2, 4)[at - 3]
        return remote(source, target, self.sends.at[at], self.recvs.at[at], {"fsdp": flip(self.me, peer)})

    def start(self):
        for block in range(4):
            self.core_out[block] = self.partial[2 * block + 1 - self.lane].astype(LOW)
        self.copy(0).start()

    def joined(self, block):
        return self.partial[2 * block + self.lane] + self.core_in[block].astype(F32)

    def cores(self):
        self.copy(0).wait()
        half = WORDS // 2
        summed = self.joined(flip(self.chip, 3))
        self.half_out[0] = summed[:half].astype(LOW)
        self.half_out[1] = summed[half:].astype(LOW)
        for way in range(2):
            self.copy(1 + way).start()

    def diagonal(self):
        half = WORDS // 2
        for way in range(2):
            self.copy(1 + way).wait()
        for way, side in ((1, 0), (0, 1)):
            summed = self.joined(flip(self.chip, 1 + way))
            at, other = (slice(0, half), slice(half, WORDS)) if side == 0 else (slice(half, WORDS), slice(0, half))
            self.full_out[way, at] = (summed[at] + self.half_in[side].astype(F32)).astype(LOW)
            self.full_out[way, other] = summed[other].astype(LOW)
            self.copy(3 + way).start()

    def total(self):
        for way in range(2):
            self.copy(3 + way).wait()
        return self.joined(self.chip) + (self.full_in[0].astype(F32) + self.full_in[1].astype(F32))


def row_sum_scratch():
    half, whole = (2, WORDS // 2, WIDE), (2, WORDS, WIDE)
    return [
        pltpu.VMEM((8, WORDS, WIDE), F32),
        pltpu.VMEM((4, WORDS, WIDE), LOW),
        pltpu.VMEM((4, WORDS, WIDE), LOW),
        pltpu.VMEM(half, LOW),
        pltpu.VMEM(half, LOW),
        pltpu.VMEM(whole, LOW),
        pltpu.VMEM(whole, LOW),
        pltpu.SemaphoreType.DMA((5,)),
        pltpu.SemaphoreType.DMA((5,)),
    ]


def dot_nt(left, right):
    return lax.dot_general(left, right, (((1,), (1,)), ((), ())), preferred_element_type=jnp.float32)


def dot_tn(left, right):
    return lax.dot_general(left, right, (((0,), (0,)), ((), ())), preferred_element_type=jnp.float32)


def spread(part):
    source = lax.broadcasted_iota(jnp.int32, (128, WIDE), 0)
    target = lax.broadcasted_iota(jnp.int32, (128, WIDE), 1)
    return jnp.logical_and(source < UNIT, target == source + part * UNIT)


def half_lanes():
    lane = lax.broadcasted_iota(jnp.int32, (1, PAIR_WIDE), 1)
    return (lane < HEAD_DIM, lane >= HEAD_DIM)


def only(values, chosen):
    return jnp.where(chosen, values, jnp.zeros_like(values))


ATTEND_CROSS_WORD = ((0, WORDS), (WORDS, REGIONS))
ATTEND_CROSS_REGION = ((WORDS, REGIONS), (0, WORDS))
ATTEND_WORD = ((0, WORDS), (0, WORDS))
ATTEND_REGION = ((WORDS, REGIONS), (WORDS, REGIONS))


def attend_into(rows_of, mixed, allowed, shares, context):
    (query_at, query_count), (key_at, key_count) = rows_of
    blocked = jnp.where(allowed, 0.0, masked_score)

    def pair(p, carry):
        at = pl.multiple_of(p * PAIR_WIDE, PAIR_WIDE)
        queries = mixed[pl.ds(query_at, query_count), pl.ds(at, PAIR_WIDE)]
        key_rows = mixed[pl.ds(key_at, key_count), pl.ds(WIDE + at, PAIR_WIDE)]
        value_rows = mixed[pl.ds(key_at, key_count), pl.ds(2 * WIDE + at, PAIR_WIDE)]
        total = jnp.zeros((query_count, PAIR_WIDE), jnp.float32)
        for side, chosen in enumerate(half_lanes()):
            scores = dot_nt(only(queries, chosen), key_rows) * HEAD_DIM ** (-0.5) + blocked
            lifted = jnp.exp(scores - jnp.max(scores, axis=-1, keepdims=True))
            share = (lifted / jnp.sum(lifted, axis=-1, keepdims=True)).astype(jnp.bfloat16)
            shares[2 * p + side] = share
            total = total + matmul(share, only(value_rows, chosen))
        context[pl.ds(query_at, query_count), pl.ds(at, PAIR_WIDE)] = total.astype(jnp.bfloat16)
        return carry

    lax.fori_loop(0, PAIRS_OF_HEADS, pair, 0)


def row_norm(summed):
    center = summed - jnp.mean(summed, axis=-1, keepdims=True)
    inverse = lax.rsqrt(jnp.mean(center * center, axis=-1, keepdims=True) + norm_epsilon)
    return (center * inverse, inverse)


def down(across):
    wide = jnp.broadcast_to(across.astype(jnp.float32), (128, across.shape[1]))
    return jnp.concatenate([wide[:, at : at + 128].T[:, :1] for at in range(0, across.shape[1], 128)], axis=0)


SAVED = (
    ((24, WIDE), F32),
    ((3, ROWS, WIDE), F32),
    ((3, ROWS, 128), F32),
    ((HIDDEN, REGIONS), LOW),
    ((REGIONS, HIDDEN), LOW),
    ((WIDE, REGIONS), LOW),
    ((PLANE_WORDS, SLICE), LOW),
    ((WIDE, SLICE), LOW),
    ((SLICE, PLANE_WORDS), LOW),
    ((WIDE, PLANE_WORDS), LOW),
    ((WIDE, ROWS), LOW),
    ((ROWS, 3 * WIDE), LOW),
    ((HEADS, WORDS, WORDS), LOW),
    ((HEADS, REGIONS, REGIONS), LOW),
    ((WIDE, ROWS), LOW),
    ((WIDE, ROWS), LOW),
    ((ROWS, 3 * WIDE), LOW),
    ((HEADS, WORDS, REGIONS), LOW),
    ((HEADS, REGIONS, WORDS), LOW),
    ((WIDE, ROWS), LOW),
)
WEIGHTS = (
    (3, WIDE, 3 * WIDE),
    (3, WIDE, WIDE),
    (1, WIDE, HIDDEN),
    (1, HIDDEN, WIDE),
)

INWARD, OUTWARD, EXPAND, SHRINK, BOTH = range(5)
GATHERED = ((2, WIDE, 3 * WIDE), (2, WIDE, WIDE), (1, WIDE, HIDDEN), (1, HIDDEN, WIDE), (1, WIDE, 4 * WIDE))

CHUNKS = (
    (BOTH, 0, (0, UNIT), True),
    (INWARD, 0, (0, UNIT), False),
    (OUTWARD, 0, (0, UNIT), False),
    (EXPAND, 0, (0, UNIT), True),
    (INWARD, 1, (0, UNIT), False),
    (OUTWARD, 1, (0, UNIT), False),
    (SHRINK, 0, (0, SHRINK_QUARTERED), True),
    (SHRINK, 0, (SHRINK_QUARTERED, 4 * UNIT - SHRINK_QUARTERED), False),
)
BOTH_2, INWARD_0, OUTWARD_0, EXPAND_1, INWARD_1, OUTWARD_1, SHRINK_1, SHRINK_REST = range(len(CHUNKS))


def forward_kernel(*refs):
    word_rows, region_rows, word_ids, region_ids, biases, gains, hidden_bias, *shards = refs[:11]
    word_result, region_result, *kept = refs[11:33]
    weights_kept = refs[33:37]
    (
        params,
        normed,
        inverse,
        hidden_t,
        slope,
        rows_two_t,
        slope_words,
        expand_words,
        hidden_words_t,
        rows_two_words_t,
        context_self_t,
        mixed_self,
        shares_w,
        shares_r,
        rows_one_t,
        context_cross_t,
        mixed_cross,
        shares_cw,
        shares_cr,
        rows_zero_t,
    ) = saved = refs[37:57]
    inward_all, outward_all, expand_all, shrink_all, both_all = gathered = refs[57:62]
    (
        small_own,
        small_all,
        hidden_rows,
        rows_low,
        result,
        row_sems,
        stream,
        stream_low,
        context,
        hidden,
        words_two,
        hidden_words,
        shrink_words,
        partial,
        core_out,
        core_in,
        half_out,
        half_in,
        full_out,
        full_in,
        sum_sends,
        sum_recvs,
        gather_sends,
        gather_recvs,
        slice_sends,
        slice_recvs,
        sends,
        recvs,
        z_sends,
        z_recvs,
        foreign_sends,
        foreign_recvs,
        small_sends,
        small_recvs,
        local_sems,
        keep_sems,
    ) = refs[62:]
    me = lax.axis_index("fsdp")
    z = lax.axis_index("rep")
    above, below = {"rep": (z + 1) % 4}, {"rep": (z + 3) % 4}
    gather_words = RowGather(me, words_two, gather_sends, gather_recvs)
    sum_words = RowSum(
        me, partial, core_out, core_in, half_out, half_in, full_out, full_in, sum_sends, sum_recvs
    )
    def small_copy(offset, owner):
        return remote(
            small_all.at[owner],
            small_all.at[owner],
            small_sends.at[offset - 1],
            small_recvs.at[offset - 1],
            {"fsdp": flip(me, offset)},
        )

    def place(k, owner, half=None, quarter=None):
        kind, _, (first, count), _ = CHUNKS[k]
        shard_rows = GATHERED[kind][1] // 8
        column, columns = 0, GATHERED[kind][2]
        if quarter is not None and kind == SHRINK:
            count = count // 4
            first = first + quarter * count
        elif quarter is not None:
            columns = columns // 4
            column = quarter * columns
        if half is not None:
            count = count // 2
            first = first + half * count
        if not isinstance(column, int):
            column = pl.multiple_of(column, WIDE)
        if not isinstance(first, int):
            first = pl.multiple_of(first, 16)
        whole = pl.multiple_of(owner * shard_rows + first, 16)
        return pl.ds(whole, count), pl.ds(first, count), pl.ds(column, columns)

    def own_part(k, quarter=None):
        kind, index, _, _ = CHUNKS[k]
        if kind == BOTH:
            return part(k, me, None, quarter)
        _, rows, columns = place(k, me, None, quarter)
        return shards[kind].at[index + (1 if kind in (EXPAND, SHRINK) else 0), rows, columns]

    def part(k, owner, half=None, quarter=None):
        kind, index, _, _ = CHUNKS[k]
        rows, _, columns = place(k, owner, half, quarter)
        return gathered[kind].at[index, rows, columns]

    def mine(k):
        return z if CHUNKS[k][3] else None

    def copy(k, kind, arriving=False):
        owner, half, peer = route(me, kind, arriving)
        quarter = None if kind == CORE_OWN else mine(k)
        target = part(k, owner, half, quarter)
        source = own_part(k, quarter) if kind in (X, Y, CORE_OWN) and not arriving else target
        return remote(source, target, sends.at[k, kind], recvs.at[k, kind], peer)

    z_chunks = [k for k in range(len(CHUNKS)) if CHUNKS[k][3]]
    owners = (flip(me, 2), flip(me, 4), flip(me, 6))
    core_owners = (flip(me, 3), flip(me, 5), flip(me, 7))

    def z_copy(k, way, hop, which, arriving=False):
        steps = hop + 1 if arriving else hop
        quarter = z - steps if way == 0 else z + steps
        here = part(k, owners[which], None, quarter)
        at = (z_chunks.index(k), way, hop, which)
        return remote(here, here, z_sends.at[at], z_recvs.at[at], (above, below)[way])

    def foreign_copy(k, way, hop, which, arriving=False):
        quarter = z - hop - 1 if way == 0 else z + hop + 1
        here = part(k, (core_owners if arriving else owners)[which], None, quarter)
        at = (z_chunks.index(k), way, hop, which)
        return remote(here, here, foreign_sends.at[at], foreign_recvs.at[at], {"fsdp": flip(me, 1)})

    def goes(way, hop):
        return jnp.logical_and(z >= hop, z < 3) if way == 0 else jnp.logical_and(z <= 3 - hop, z > 0)

    def comes(way, hop):
        return z >= hop + 1 if way == 0 else z <= 2 - hop

    def send_z(k, hop, which):
        for way in range(2):

            @pl.when(goes(way, hop))
            def _(way=way):
                for one in which:
                    z_copy(k, way, hop, one).start()

    def own_local(k):
        return pltpu.make_async_copy(own_part(k), part(k, me), local_sems.at[k])

    def own_both(kind):
        rows, columns = pl.ds(pl.multiple_of(me * UNIT, UNIT), UNIT), pl.ds(3 * WIDE * kind, (3 * WIDE, WIDE)[kind])
        return pltpu.make_async_copy(
            shards[kind].at[2], both_all.at[0, rows, columns], local_sems.at[len(CHUNKS) + 2 + kind]
        )

    def own(k):
        for kind in (X, Y):
            copy(k, kind).start()
        if CHUNKS[k][0] != BOTH:
            own_local(k).start()
        copy(k, CORE_OWN).start()

    def pass_first(k):
        copy(k, X, True).wait_recv()
        copy(k, DIAG_Y).start()
        copy(k, Y, True).wait_recv()
        copy(k, DIAG_X).start()
        if k in z_chunks:
            send_z(k, 0, (0, 1))
        copy(k, CORE_X).start()
        copy(k, CORE_Y).start()

    def pass_second(k):
        copy(k, DIAG_Y, True).wait_recv()
        copy(k, DIAG_X, True).wait_recv()
        if k in z_chunks:
            send_z(k, 0, (2,))
        copy(k, CORE_DIAG).start()

    def pass_quarter(k, hop):
        for way in range(2):

            @pl.when(comes(way, hop))
            def _(way=way):
                for which in range(3):
                    z_copy(k, way, hop, which, True).wait_recv()

        if hop < 2:
            send_z(k, hop + 1, (0, 1, 2))
        for way in range(2):

            @pl.when(comes(way, hop))
            def _(way=way):
                for which in range(3):
                    foreign_copy(k, way, hop, which).start()

    def complete(k):
        if CHUNKS[k][0] != BOTH:
            own_local(k).wait()
        for kind in (CORE_OWN, CORE_X, CORE_Y, CORE_DIAG):
            copy(k, kind, True).wait_recv()
        if k in z_chunks:
            for hop in range(3):
                for way in range(2):

                    @pl.when(comes(way, hop))
                    def _(way=way, hop=hop):
                        for which in range(3):
                            foreign_copy(k, way, hop, which, True).wait_recv()

    def slice_copy(offset, arriving=False):
        peer = flip(me, offset)
        rows = pl.ds(pl.multiple_of((peer if arriving else me) * UNIT, UNIT), UNIT)
        target = expand_words.at[rows, :]
        source = shards[2].at[0, :, pl.ds(pl.multiple_of(peer * SLICE, SLICE), SLICE)]
        return remote(source, target, slice_sends.at[offset - 1], slice_recvs.at[offset - 1], {"fsdp": peer})

    own_slice = pltpu.make_async_copy(
        shards[2].at[0, :, pl.ds(pl.multiple_of(me * SLICE, SLICE), SLICE)],
        expand_words.at[pl.ds(pl.multiple_of(me * UNIT, UNIT), UNIT), :],
        local_sems.at[len(CHUNKS)],
    )
    own_shrink = pltpu.make_async_copy(shards[3].at[0], shrink_words, local_sems.at[len(CHUNKS) + 1])

    def start_slices():
        own_slice.start()
        own_shrink.start()
        for offset in range(1, 8):
            slice_copy(offset).start()

    def wait_slices():
        own_slice.wait()
        own_shrink.wait()
        for offset in range(1, 8):
            slice_copy(offset, True).wait_recv()

    keeps = []

    def keep_norm(kind):
        for source in (normed, inverse):
            index = [ref is source for ref in saved].index(True)
            keep(source.at[kind], kept[index].at[kind])

    def keep(source, target):
        copied = pltpu.make_async_copy(source, target, keep_sems.at[len(keeps)])
        copied.start()
        keeps.append(copied)

    def keep_weights(kind, index):
        keep(gathered[kind].at[index], weights_kept[kind].at[index])

    def keep_both():
        keep(both_all.at[0, :, 0 : 3 * WIDE], weights_kept[INWARD].at[2])
        keep(both_all.at[0, :, 3 * WIDE : 4 * WIDE], weights_kept[OUTWARD].at[2])

    def keep_saved(*refs_done):
        for done in refs_done:
            index = [ref is done for ref in saved].index(True)
            keep(saved[index], kept[index])

    def give_small():
        small_own[...] = jnp.zeros_like(small_own)
        small_own[0:16, 0:UNIT] = biases[...].astype(F32)
        small_own[16:21, 0:UNIT] = gains[...].astype(F32)
        source = lax.broadcasted_iota(jnp.int32, (4 * UNIT, 128), 0)
        target = lax.broadcasted_iota(jnp.int32, (4 * UNIT, 128), 1)
        for q in range(4):
            chosen = jnp.logical_and(target < UNIT, source == target + q * UNIT).astype(LOW)
            placed = matmul(hidden_bias[...], chosen)
            for f in range(2):
                row = 21 + 4 * f + q
                small_own[row : row + 1, :] = placed[f : f + 1]
        small_all[me] = small_own[...].astype(LOW)
        for offset in range(1, 8):
            small_copy(offset, me).start()

    def read_small():
        for offset in range(1, 8):
            small_copy(offset, flip(me, offset)).wait_recv()
        totals = jnp.zeros((21, WIDE), jnp.float32)
        hidden_parts = [jnp.zeros((1, WIDE), jnp.float32) for _ in range(4)]
        for owner in range(8):
            one = small_all[owner]
            totals = totals + matmul(one, spread(owner).astype(LOW))[:21]
            for q in range(4):
                placed = matmul(one, spread((owner % 2) * 4 + q).astype(LOW))
                row = 25 + q
                hidden_parts[owner // 2] = hidden_parts[owner // 2] + placed[row : row + 1]
        params[...] = jnp.zeros_like(params)
        params[0:21, :] = totals
        for block in range(4):
            hidden_rows[:, block * WIDE : (block + 1) * WIDE] = hidden_parts[block]
        keep_saved(params)

    def read_rows():
        for copied in rows_come:
            copied.wait()
        for at in range(0, ROWS, 128):
            transposed_into(rows_zero_t, rows_low[at : at + 128, :], at, 128)
        keep_saved(rows_zero_t)

    def transposed_into(target, values, at, count):
        target[:, pl.ds(at, count)] = values.T

    def project_into(source, at, count, module, mixed, weights):
        for third, bias_row in enumerate((3 * module, None, 3 * module + 1)):
            product = matmul(source[pl.ds(at, count), :], weights[:, third * WIDE : (third + 1) * WIDE])
            if bias_row is not None:
                product = product + params[bias_row : bias_row + 1, :]
            mixed[pl.ds(at, count), third * WIDE : (third + 1) * WIDE] = product.astype(jnp.bfloat16)

    def join(at, product, residual, bias_row, norm_at, norm_index):
        rows = pl.ds(at, 128)
        unit, scale = row_norm(residual + product + params[bias_row : bias_row + 1, :])
        normed[norm_at, rows, :] = unit
        inverse[norm_at, rows, :] = jnp.broadcast_to(scale, (128, 128))
        return unit * params[16 + norm_index : 17 + norm_index, :] + params[9 + norm_index : 10 + norm_index, :]

    def cross_in():
        project_into(rows_low, 0, ROWS, 0, mixed_cross, inward_all.at[0])
        keep_saved(mixed_cross)
        keep_weights(0, 0)

    def cross_words():
        allowed = down(word_ids[...]) == region_ids[...].astype(F32)
        attend_into(ATTEND_CROSS_WORD, mixed_cross, allowed, shares_cw, context)
        keep_saved(shares_cw)

    def cross_regions():
        allowed = down(region_ids[...]) == word_ids[...].astype(F32)
        attend_into(ATTEND_CROSS_REGION, mixed_cross, allowed, shares_cr, context)
        keep_saved(shares_cr)

    def cross_out():
        for at in range(0, ROWS, 128):
            product = matmul(context[at : at + 128, :], outward_all[0])
            one = join(at, product, rows_low[at : at + 128, :].astype(F32), 2, 0, 0)
            stream[at : at + 128, :] = one
            one_low = one.astype(LOW)
            stream_low[at : at + 128, :] = one_low
            transposed_into(rows_one_t, one_low, at, 128)
            transposed_into(context_cross_t, context[at : at + 128, :], at, 128)
        keep_saved(rows_one_t, context_cross_t)
        keep_norm(0)
        keep_weights(1, 0)

    def word_in():
        project_into(stream_low, 0, WORDS, 1, mixed_self, inward_all.at[1])
        keep_weights(0, 1)
        allowed = down(word_ids[...]) == word_ids[...].astype(F32)
        attend_into(ATTEND_WORD, mixed_self, allowed, shares_w, context)
        transposed_into(context_self_t, context[0:WORDS, :], 0, WORDS)
        keep_saved(shares_w)

    def region_in():
        project_into(stream_low, WORDS, REGIONS, 2, mixed_self, both_all.at[0])
        keep_both()

    def region_attend():
        allowed = down(region_ids[...]) == region_ids[...].astype(F32)
        attend_into(ATTEND_REGION, mixed_self, allowed, shares_r, context)
        for at in range(WORDS, ROWS, 128):
            transposed_into(context_self_t, context[at : at + 128, :], at, 128)
        keep_saved(shares_r)

    def self_out(module, first, last):
        for at in range(first, last, 128):
            weights = outward_all[1] if module == 1 else both_all[0, :, 3 * WIDE : 4 * WIDE]
            product = matmul(context[at : at + 128, :], weights)
            two = join(at, product, stream[at : at + 128, :], 3 * module + 2, 1, module)
            stream[at : at + 128, :] = two
            two_low = two.astype(LOW)
            stream_low[at : at + 128, :] = two_low
            if module == 1:
                words_two[pl.ds(pl.multiple_of(me * WORDS, WORDS), WORDS), :] = two_low
            else:
                transposed_into(rows_two_t, two_low, at - WORDS, 128)
        if module == 1:
            keep_weights(OUTWARD, 1)

    def activate(before, hidden_to, hidden_t_to, slope_to):
        below = 0.5 * (1.0 + lax.erf(before * 0.5**0.5))
        density = jnp.exp(-0.5 * before * before) * 0.3989422804014327
        value = (before * below).astype(LOW)
        hidden_to[...] = value
        hidden_t_to[...] = value.T
        slope_to[...] = (below + before * density).astype(LOW)

    def feed_in(column, columns):
        step = 256

        def tile(t, carry):
            at = pl.ds(pl.multiple_of(column + t * step, step), step)
            for row in range(0, REGIONS, 128):
                rows = slice(row, row + 128)
                before = matmul(stream_low[WORDS + row : WORDS + row + 128, :], expand_all[0, :, at])
                activate(before + hidden_rows[:, at], hidden.at[rows, at], hidden_t.at[at, rows], slope.at[rows, at])
            return carry

        lax.fori_loop(0, columns // step, tile, 0)

    def feed_out():
        for at in range(WORDS, ROWS, 128):
            product = matmul(hidden[at - WORDS : at - WORDS + 128, :], shrink_all[0])
            last_rows = join(at, product, stream[at : at + 128, :], 15, 2, 4)
            result[at : at + 128, :] = last_rows.astype(LOW)
        keep(result.at[WORDS:ROWS, :], region_result)

    def words_in():
        for at in range(0, PLANE_WORDS, 128):
            rows = slice(at, at + 128)
            before = matmul(words_two[rows, :], expand_words[...]) + hidden_bias[0:1, :].astype(F32)
            activate(before, hidden_words.at[rows, :], hidden_words_t.at[:, rows], slope_words.at[rows, :])
            rows_two_words_t[:, rows] = words_two[rows, :].T
        keep_saved(slope_words, expand_words, hidden_words_t, rows_two_words_t)

    def words_out():
        for at in range(0, PLANE_WORDS, 128):
            partial[at // 128] = matmul(hidden_words[at : at + 128, :], shrink_words[...])
        sum_words.start()

    def words_last():
        last_rows = join(0, sum_words.total(), stream[0:WORDS, :], 14, 2, 3)
        result[0:WORDS, :] = last_rows.astype(LOW)
        keep(result.at[0:WORDS, :], word_result)

    rows_come = [
        pltpu.make_async_copy(word_rows, rows_low.at[0:WORDS, :], row_sems.at[0]),
        pltpu.make_async_copy(region_rows, rows_low.at[WORDS:ROWS, :], row_sems.at[1]),
    ]
    for copied in rows_come:
        copied.start()
    for kind in range(2):
        own_both(kind).start()
    greet(me, z)
    for kind in range(2):
        own_both(kind).wait()
    own(BOTH_2)
    give_small()
    read_rows()
    pass_first(BOTH_2)
    own(INWARD_0)
    own(OUTWARD_0)
    read_small()
    pass_second(BOTH_2)
    pass_first(INWARD_0)
    own(EXPAND_1)
    pass_quarter(BOTH_2, 0)
    pass_first(OUTWARD_0)
    own(INWARD_1)
    pass_second(INWARD_0)
    pass_quarter(BOTH_2, 1)
    complete(INWARD_0)
    cross_in()
    pass_second(OUTWARD_0)
    pass_first(EXPAND_1)
    own(OUTWARD_1)
    cross_words()
    pass_second(EXPAND_1)
    cross_regions()
    pass_quarter(BOTH_2, 2)
    complete(OUTWARD_0)
    cross_out()
    pass_first(INWARD_1)
    own(SHRINK_1)
    complete(BOTH_2)
    region_in()
    pass_quarter(EXPAND_1, 0)
    region_attend()
    pass_second(INWARD_1)
    pass_first(OUTWARD_1)
    start_slices()
    complete(INWARD_1)
    word_in()
    keep_saved(mixed_self, context_self_t)
    pass_second(OUTWARD_1)
    pass_first(SHRINK_1)
    complete(OUTWARD_1)
    self_out(1, 0, WORDS)
    gather_words.start()
    pass_second(SHRINK_1)
    pass_quarter(EXPAND_1, 1)
    self_out(2, WORDS, ROWS)
    keep_saved(rows_two_t)
    keep_norm(1)
    gather_words.first()
    own(SHRINK_REST)
    gather_words.second()
    pass_quarter(EXPAND_1, 2)
    wait_slices()
    pass_first(SHRINK_REST)
    gather_words.complete()
    words_in()
    words_out()
    complete(EXPAND_1)
    keep_weights(2, 0)
    pass_quarter(SHRINK_1, 0)
    feed_in(0, 2 * WIDE)
    pass_second(SHRINK_REST)
    sum_words.cores()
    pass_quarter(SHRINK_1, 1)
    feed_in(2 * WIDE, WIDE)
    sum_words.diagonal()
    feed_in(3 * WIDE, WIDE)
    keep_saved(hidden_t, slope)
    pass_quarter(SHRINK_1, 2)
    words_last()
    complete(SHRINK_REST)
    complete(SHRINK_1)
    keep_weights(3, 0)
    feed_out()
    keep_norm(2)
    for copied in keeps:
        copied.wait()
    for offset in range(1, 8):
        small_copy(offset, me).wait_send()
        slice_copy(offset).wait_send()
    gather_words.settle()
    for k in range(len(CHUNKS)):
        for kind in range(8):
            copy(k, kind).wait_send()
    for k in z_chunks:
        for way in range(2):
            for hop in range(3):

                @pl.when(goes(way, hop))
                def _(k=k, way=way, hop=hop):
                    for which in range(3):
                        z_copy(k, way, hop, which).wait_send()

                @pl.when(comes(way, hop))
                def _(k=k, way=way, hop=hop):
                    for which in range(3):
                        foreign_copy(k, way, hop, which).wait_send()


def forward(word_rows, region_rows, word_ids, region_ids, biases, gains, hidden_bias, shards):
    dma = pltpu.SemaphoreType.DMA
    vmem = pl.BlockSpec(memory_space=pltpu.VMEM)
    hbm = pl.BlockSpec(memory_space=pl.ANY)
    saved = [jax.ShapeDtypeStruct(*one) for one in SAVED]
    weights = [jax.ShapeDtypeStruct(one, LOW) for one in WEIGHTS]
    quarters = (sum(chunk[3] for chunk in CHUNKS), 2, 3, 3)
    outs = pl.pallas_call(
        forward_kernel,
        out_shape=[jax.ShapeDtypeStruct((WORDS, WIDE), LOW), jax.ShapeDtypeStruct((REGIONS, WIDE), LOW)] + saved + weights,
        in_specs=[hbm] * 2 + [vmem] * 5 + [hbm] * 4,
        out_specs=[hbm] * (2 + len(saved) + len(weights)),
        scratch_shapes=[pltpu.VMEM(one.shape, one.dtype) for one in saved]
        + [pltpu.VMEM(one, LOW) for one in GATHERED]
        + [
            pltpu.VMEM((32, 128), F32),
            pltpu.VMEM((8, 32, 128), LOW),
            pltpu.VMEM((1, HIDDEN), F32),
            pltpu.VMEM((ROWS, WIDE), LOW),
            pltpu.VMEM((ROWS, WIDE), LOW),
            dma((2,)),
            pltpu.VMEM((ROWS, WIDE), F32),
            pltpu.VMEM((ROWS, WIDE), LOW),
            pltpu.VMEM((ROWS, WIDE), LOW),
            pltpu.VMEM((REGIONS, HIDDEN), LOW),
            pltpu.VMEM((PLANE_WORDS, WIDE), LOW),
            pltpu.VMEM((PLANE_WORDS, SLICE), LOW),
            pltpu.VMEM((SLICE, WIDE), LOW),
            *row_sum_scratch(),
            dma((8,)),
            dma((8,)),
            dma((7,)),
            dma((7,)),
            dma((len(CHUNKS), 8)),
            dma((len(CHUNKS), 8)),
            dma(quarters),
            dma(quarters),
            dma(quarters),
            dma(quarters),
            dma((7,)),
            dma((7,)),
            dma((len(CHUNKS) + 4,)),
            dma((len(saved) + 14,)),
        ],
        compiler_params=pltpu.CompilerParams(
            collective_id=1, has_side_effects=True, vmem_limit_bytes=64 * 2**20 - 2**16
        ),
    )(word_rows, region_rows, word_ids, region_ids, biases, gains, hidden_bias, *shards)
    return outs[:2], outs[2 : 2 + len(saved)], outs[2 + len(saved) :]


WINDOW = 6
EARLIER_NORMS = 23
SPAN = WIDE // 2
Z_SLOTS = 10

GROUPS = (
    (8, None, 0, 0, True, (3, 0)),
    (8, None, 0, 0, False, (2, 0)),
    (8, 0, 0, REGIONS, True, (3, 1)),
    (8, 1, 0, REGIONS, False, (2, 1)),
    (2, 2, 0, WORDS, False, (1, 1)),
    (2, 2, WORDS, REGIONS, False, (1, 2)),
    (6, 3, 0, WORDS, False, (0, 1)),
    (6, 3, WORDS, REGIONS, False, (0, 2)),
    (2, 4, 0, ROWS, False, (1, 0)),
    (6, 5, 0, ROWS, False, (0, 0)),
)
UNITS = sum(group[0] for group in GROUPS)
OWNED = sum(group[0] for group in GROUPS if group[1] is None)
CROSSING = UNITS - OWNED

BLOCKS = (
    [(kind, 0, c) for c in range(4) for kind in (3, 2)]
    + [(1, 1, 0), (1, 2, 0)]
    + [(0, m, c) for m in (1, 2) for c in range(3)]
    + [(1, 0, 0)]
    + [(0, 0, c) for c in range(3)]
)


def attend_back_into(rows_of, mixed, shares, grad_context, grad_mixed, first_pair, last_pair):
    (query_at, query_count), (key_at, key_count) = rows_of
    query_rows, key_rows = pl.ds(query_at, query_count), pl.ds(key_at, key_count)

    def pair(p, carry):
        at = pl.multiple_of(p * PAIR_WIDE, PAIR_WIDE)
        at_query, at_key, at_value = (pl.ds(third * WIDE + at, PAIR_WIDE) for third in range(3))
        queries = mixed[query_rows, at_query]
        keys = mixed[key_rows, at_key]
        values = mixed[key_rows, at_value]
        grads = grad_context[query_rows, at_query]
        grad_queries = jnp.zeros((query_count, PAIR_WIDE), jnp.float32)
        grad_keys = jnp.zeros((key_count, PAIR_WIDE), jnp.float32)
        grad_values = jnp.zeros((key_count, PAIR_WIDE), jnp.float32)
        for side, chosen in enumerate(half_lanes()):
            share = shares[2 * p + side]
            grad_head = only(grads, chosen)
            wide = share.astype(jnp.float32)
            weighted = wide * dot_nt(grad_head, values)
            grad_scores = (weighted - wide * jnp.sum(weighted, axis=-1, keepdims=True)).astype(jnp.bfloat16)
            grad_values = grad_values + dot_tn(share, grad_head)
            grad_queries = grad_queries + matmul(grad_scores, only(keys, chosen))
            grad_keys = grad_keys + dot_tn(grad_scores, only(queries, chosen))
        score_scale = HEAD_DIM ** (-0.5)
        grad_mixed[query_rows, at_query] = (grad_queries * score_scale).astype(jnp.bfloat16)
        grad_mixed[key_rows, at_key] = (grad_keys * score_scale).astype(jnp.bfloat16)
        grad_mixed[key_rows, at_value] = grad_values.astype(jnp.bfloat16)
        return carry

    lax.fori_loop(first_pair, last_pair, pair, 0)


def backward_kernel(*refs):
    saved_hbm, weights = refs[:23], refs[23:27]
    word_gradient, region_gradient, small_out, *totals = refs[27:34]
    (
        params,
        word_cotangent,
        region_cotangent,
        normed,
        inverse,
        hidden_t,
        slope,
        rows_two_t,
        slope_words,
        expand_words,
        hidden_words_t,
        rows_two_words_t,
        context_self_t,
        mixed_self,
        shares_w,
        shares_r,
        rows_one_t,
        context_cross_t,
        mixed_cross,
        shares_cw,
        shares_cr,
        rows_zero_t,
        shrink_words,
    ) = saved = refs[34:57]
    (
        window,
        end_feed,
        end_self,
        end_cross,
        stream,
        grad_context,
        row_sums,
        hidden_sums,
        end_words,
        hidden_sums_words,
        owned_shrink,
        owned_out,
        owned_expand,
        partial,
        sum_core_out,
        sum_core_in,
        sum_half_out,
        sum_half_in,
        sum_full_out,
        sum_full_in,
        sum_sends,
        sum_recvs,
        gather_sends,
        gather_recvs,
        slice_sends,
        slice_recvs,
        out,
        acc,
        core_out,
        core_in,
        half_out,
        half_in,
        full_out,
        full_in,
        plane,
        end_out,
        end_in,
        mid_out,
        mid_in,
        small_in,
        small_in_plane,
        small_planes,
        small_total,
        row_sems,
        saved_sems,
        window_sems,
        total_sems,
        core_send,
        core_recv,
        half_send,
        half_recv,
        full_send,
        full_recv,
        z_send,
        z_recv,
        back_send,
        back_recv,
        small_send,
        small_recv,
        free,
    ) = refs[57:]
    grad_before, before_words, grad_mixed_self, grad_mixed_cross = slope, slope_words, mixed_self, mixed_cross
    lefts = (hidden_t, rows_two_t, context_self_t, rows_one_t, context_cross_t, rows_zero_t)
    rights = (end_feed, grad_before, end_self, grad_mixed_self, end_cross, grad_mixed_cross)
    me = lax.axis_index("fsdp")
    z = lax.axis_index("rep")
    chip = me // 2
    lane = me % 2
    is_end = jnp.logical_or(z == 0, z == 3)
    is_mid = jnp.logical_or(z == 1, z == 2)
    core_peer = {"fsdp": flip(me, 1)}
    links = ({"fsdp": flip(me, 2)}, {"fsdp": flip(me, 4)})
    link_chip = (flip(chip, 1), flip(chip, 2))
    diagonal = flip(chip, 3)
    pair_peer = {"rep": flip(z, 1)}
    mid_peer = {"rep": 3 - z}
    low = LOW
    gather_words = RowGather(me, end_words, gather_sends, gather_recvs)
    sum_words = RowSum(
        me,
        partial,
        sum_core_out,
        sum_core_in,
        sum_half_out,
        sum_half_in,
        sum_full_out,
        sum_full_in,
        sum_sends,
        sum_recvs,
    )

    def load_saved(index):
        if index == EARLIER_NORMS:
            return pltpu.make_async_copy(saved_hbm[3].at[0:2], normed.at[0:2], saved_sems.at[index])
        source, target = saved_hbm[index], saved[index]
        if target is shrink_words:
            source = source.at[0]
        if target is normed:
            source, target = source.at[2], target.at[2]
        return pltpu.make_async_copy(source, target, saved_sems.at[index])

    def load_block(n):
        kind, index, c = BLOCKS[n]
        part = slice(c * WIDE, (c + 1) * WIDE)
        source = weights[kind].at[index, part, :] if kind == 3 else weights[kind].at[index, :, part]
        return pltpu.make_async_copy(source, window.at[n % WINDOW], window_sems.at[n % WINDOW])

    def wait_saved(*names):
        for name in names:
            load_saved([ref is name for ref in saved].index(True)).wait()

    first_saved = [0, 1, 2, 3, 4, 5]
    for index in first_saved:
        load_saved(index).start()
    for n in range(WINDOW):
        load_block(n).start()
    for index in [22, 8, 9, 10, 11, 6, 7, EARLIER_NORMS] + list(range(12, 22)):
        load_saved(index).start()
    greet(me, z)

    def small_copy(offset):
        peer = flip(me, offset)
        return remote(
            small_in.at[peer],
            small_in_plane.at[offset - 1],
            small_send.at[offset - 1],
            small_recv.at[offset - 1],
            {"fsdp": peer},
        )

    def small_plane_copy(offset, source):
        peer = (z + offset) % 4 if source is z else source
        return remote(
            small_planes.at[source],
            small_planes.at[source],
            small_send.at[6 + offset],
            small_recv.at[6 + offset],
            {"rep": peer},
        )

    def core_copy(u):
        slot = u % SLOTS
        return remote(core_out.at[slot], core_in.at[slot], core_send.at[slot], core_recv.at[slot], core_peer)

    def half_copy(u, way):
        slot = u % SLOTS
        return remote(
            half_out.at[slot, way], half_in.at[slot, way], half_send.at[slot, way], half_recv.at[slot, way], links[way]
        )

    def full_copy(u, way):
        slot = u % SLOTS
        return remote(
            full_out.at[slot, way], full_in.at[slot, way], full_send.at[slot, way], full_recv.at[slot, way], links[way]
        )

    def end_copy(n):
        slot = n % Z_SLOTS
        return remote(end_out.at[slot], end_in.at[slot], z_send.at[0, slot], z_recv.at[0, slot], pair_peer)

    def mid_copy(n):
        slot = n % Z_SLOTS
        return remote(mid_out.at[slot], mid_in.at[slot], z_send.at[1, slot], z_recv.at[1, slot], mid_peer)

    def back_copy(n):
        u = z_order[n]
        return remote(out.at[u], out.at[u], back_send.at[u], back_recv.at[u], pair_peer)

    def credit(u, channel, peer, slots=SLOTS, count=CROSSING):
        if u + slots < count:
            pl.semaphore_signal(free.at[channel], inc=1, device_id=peer, device_id_type=MESH)

    def spend(u, channel, slots=SLOTS):
        if u >= slots:
            pl.semaphore_wait(free.at[channel], 1)

    def per_group(u, function):
        for group in GROUPS:
            if u < group[0]:
                return function(u, *group[1:])
            u = u - group[0]

    def produce(u):
        slot = u % SLOTS
        keep = u % ACC_SLOTS
        spend(u, 0)

        def products(at, side, first_row, count, by_row, matrix):
            rows = pl.ds(first_row, count)
            column = (at % 2 if by_row else at) * SPAN
            right = rights[side][rows, pl.ds(column, SPAN)]

            def product(core):
                blocks = []
                for block in range(4):
                    owner = 2 * block + core
                    row = owner * (4 * UNIT) + (at // 2) * UNIT if by_row else owner * UNIT
                    blocks.append(lefts[side][pl.ds(pl.multiple_of(row, 16), UNIT), rows])
                return matmul(jnp.concatenate(blocks, axis=0), right)

            other = product(1 - lane).astype(low)
            for block in range(4):
                core_out[slot, block] = other[block * UNIT : (block + 1) * UNIT]
            core_copy(u).start()
            own = product(lane)
            for block in range(4):
                acc[keep, block] = own[block * UNIT : (block + 1) * UNIT]

        per_group(crossing[u], products)

    def join_cores(u):
        slot = u % SLOTS
        keep = u % ACC_SLOTS
        core_copy(u).wait()
        for way in range(2):
            spend(u, 1 + way)
        summed = acc[keep, diagonal] + core_in[slot, diagonal].astype(jnp.float32)
        half_out[slot, 0] = summed[: UNIT // 2].astype(low)
        half_out[slot, 1] = summed[UNIT // 2 :].astype(low)
        for way in range(2):
            half_copy(u, way).start()
        for block in (link_chip[0], link_chip[1], chip):
            acc[keep, block] = acc[keep, block] + core_in[slot, block].astype(jnp.float32)
        credit(u, 0, core_peer)

    def join_diagonal(u):
        slot = u % SLOTS
        keep = u % ACC_SLOTS
        for way in range(2):
            half_copy(u, way).wait()
            spend(u, 3 + way)
        half = UNIT // 2
        full_out[slot, 1, :half] = (acc[keep, link_chip[1], :half] + half_in[slot, 0].astype(jnp.float32)).astype(low)
        full_out[slot, 1, half:] = acc[keep, link_chip[1], half:].astype(low)
        full_copy(u, 1).start()
        full_out[slot, 0, half:] = (acc[keep, link_chip[0], half:] + half_in[slot, 1].astype(jnp.float32)).astype(low)
        full_out[slot, 0, :half] = acc[keep, link_chip[0], :half].astype(low)
        full_copy(u, 0).start()
        for way in range(2):
            credit(u, 1 + way, links[way])

    def join_plane(u):
        slot = u % SLOTS
        keep = u % ACC_SLOTS
        for way in range(2):
            full_copy(u, way).wait()
        summed = acc[keep, chip] + (full_in[slot, 0].astype(F32) + full_in[slot, 1].astype(F32))
        for way in range(2):
            credit(u, 3 + way, links[way])
        enter(z_order.index(crossing[u]), summed)

    def join_owned(u):
        half = slice(u % 2 * SPAN, u % 2 * SPAN + SPAN)
        if u < 8:
            summed = owned_shrink[u // 2 * UNIT : (u // 2 + 1) * UNIT, half]
        else:
            summed = owned_expand[u - 8].astype(F32)
        enter(z_order.index(u), summed)

    def enter(n, summed):
        slot = n % Z_SLOTS

        @pl.when(is_end)
        def _():
            spend(n, 5, Z_SLOTS)
            end_out[slot] = summed.astype(low)
            end_copy(n).start()

        @pl.when(is_mid)
        def _():
            plane[slot] = summed

    def join_pair(n):
        slot = n % Z_SLOTS

        @pl.when(is_end)
        def _():
            end_copy(n).wait_send()

        @pl.when(is_mid)
        def _():
            end_copy(n).wait_recv()
            spend(n, 6, Z_SLOTS)
            mid_out[slot] = (plane[slot] + end_in[slot].astype(F32)).astype(low)
            mid_copy(n).start()
            credit(n, 5, pair_peer, Z_SLOTS, UNITS)

    def join_middle(n):
        slot = n % Z_SLOTS

        @pl.when(is_mid)
        def _():
            mid_copy(n).wait()
            out[z_order[n]] = (mid_out[slot].astype(F32) + mid_in[slot].astype(F32)).astype(low)
            back_copy(n).start()
            credit(n, 6, mid_peer, Z_SLOTS, UNITS)

    def total_copy(u, at, by_row, matrix):
        kind, index = matrix
        if by_row:
            row, column = (at // 2) * UNIT, (at % 2) * SPAN
        else:
            row, column = 0, at * SPAN
        place = totals[kind].at[index, pl.ds(row, UNIT), pl.ds(column, SPAN)]
        return pltpu.make_async_copy(out.at[u], place, total_sems.at[u])

    def finish(n):
        @pl.when(is_mid)
        def _():
            back_copy(n).wait_send()

        @pl.when(is_end)
        def _():
            back_copy(n).wait_recv()

        u = z_order[n]
        per_group(u, lambda at, side, first_row, count, by_row, matrix: total_copy(u, at, by_row, matrix).start())

    crossing = [u for u in range(UNITS) if u >= OWNED]
    to_plane = LAG_CORE + LAG_A + LAG_B
    entries = [(i + to_plane, 1, u) for i, u in enumerate(crossing)]
    entries += [(OWNED_SHRINK_AT + u * 3 // 8, 0, u) for u in range(8)]
    entries += [(OWNED_EXPAND_AT + 2 * (u - 8), 0, u) for u in range(8, OWNED)]
    entries.sort()
    z_order = [u for _, _, u in entries]
    for n in range(UNITS - Z_SLOTS):
        assert entries[n + Z_SLOTS][0] >= entries[n][0] + LAG_Z
    last = entries[-1][0] + 3 * LAG_Z

    row_tiles = ((0, 0), (1, 128), (1, 256))

    def add_row(index, values):
        row_sums[index : index + 1, :] += jnp.sum(values, axis=0, keepdims=True)

    def norm_back(grad, kind, norm_index, at, ends, end_bias, end_at=None):
        rows = slice(at, at + 128)
        unit = normed[kind, rows, :]
        grad_unit = grad * params[16 + norm_index : 17 + norm_index, :]
        summed = inverse[kind, rows, :1] * (
            grad_unit
            - jnp.mean(grad_unit, axis=-1, keepdims=True)
            - unit * jnp.mean(grad_unit * unit, axis=-1, keepdims=True)
        )
        add_row(16 + norm_index, grad * unit)
        add_row(9 + norm_index, grad)
        stream[rows, :] = summed
        summed_low = summed.astype(low)
        if end_at is None:
            ends[rows, :] = summed_low
        else:
            ends[pl.ds(end_at, 128), :] = summed_low
        add_row(end_bias, summed_low.astype(jnp.float32))

    def feed_norm():
        wait_saved(params, word_cotangent, region_cotangent, normed, inverse)
        row_sums[...] = jnp.zeros_like(row_sums)
        hidden_sums[...] = jnp.zeros_like(hidden_sums)
        hidden_sums_words[...] = jnp.zeros_like(hidden_sums_words)
        own_rows = pl.multiple_of(me * WORDS, WORDS)
        norm_back(word_cotangent[...].astype(F32), 2, 3, 0, end_words, 14, own_rows)
        gather_words.start()
        for at in range(0, REGIONS, 128):
            cotangent = region_cotangent[at : at + 128, :].astype(F32)
            norm_back(cotangent, 2, 4, WORDS + at, end_feed, 15, at)

    def slice_copy(offset, arriving=False):
        peer = flip(me, offset)
        rows = pl.ds(pl.multiple_of(peer * UNIT, UNIT), UNIT)
        target = owned_expand.at[peer if arriving else me]
        return remote(
            owned_out.at[rows, :], target, slice_sends.at[offset - 1], slice_recvs.at[offset - 1], {"fsdp": peer}
        )

    def words_back():
        wait_saved(shrink_words, slope_words, expand_words)
        for at in range(0, PLANE_WORDS, 128):
            rows = slice(at, at + 128)
            before = (dot_nt(end_words[rows, :], shrink_words[...]) * slope_words[rows, :].astype(F32)).astype(low)
            before_words[rows, :] = before
            hidden_sums_words[0:1, :] += jnp.sum(before.astype(F32), axis=0, keepdims=True)
            partial[at // 128] = dot_nt(before, expand_words[...])
        sum_words.start()

    def words_shrink():
        wait_saved(hidden_words_t)
        owned_shrink[...] = matmul(hidden_words_t[...], end_words[...])

    def words_expand():
        wait_saved(rows_two_words_t)
        owned_out[...] = matmul(rows_two_words_t[...], before_words[...]).astype(low)
        for offset in range(1, 8):
            slice_copy(offset).start()
        owned_expand[me] = owned_out[pl.ds(pl.multiple_of(me * UNIT, UNIT), UNIT), :]

    def words_expanded():
        for offset in range(1, 8):
            slice_copy(offset).wait_send()
            slice_copy(offset, True).wait_recv()

    def words_rows():
        stream[0:WORDS, :] += sum_words.total()

    def next_block(n):
        if n + WINDOW < len(BLOCKS):
            load_block(n + WINDOW).start()

    def feed_back(c):
        n = 2 * c
        load_block(n).wait()
        load_block(n + 1).wait()
        columns = slice(c * WIDE, (c + 1) * WIDE)
        for at in range(0, REGIONS, 128):
            rows = slice(at, at + 128)
            grad_hidden = dot_nt(end_feed[rows, :], window[n % WINDOW])
            before = (grad_hidden * slope[rows, columns].astype(F32)).astype(low)
            grad_before[rows, columns] = before
            hidden_sums[c : c + 1, :] += jnp.sum(before.astype(F32), axis=0, keepdims=True)
            stream[WORDS + at : WORDS + at + 128, :] += dot_nt(before, window[(n + 1) % WINDOW])
        next_block(n)
        next_block(n + 1)

    def self_norm():
        for f, at in row_tiles:
            norm_back(stream[at : at + 128, :], 1, 1 + f, at, end_self, 5 + 3 * f)

    def self_context():
        for f in range(2):
            n = 8 + f
            load_block(n).wait()
            for which, at in row_tiles:
                if which == f:
                    grad_context[at : at + 128, :] = dot_nt(end_self[at : at + 128, :], window[n % WINDOW]).astype(low)
            next_block(n)

    def project_back(n, module, grad_mixed, tiles):
        for c in range(3):
            load_block(n + c).wait()
            columns = slice(c * WIDE, (c + 1) * WIDE)
            for at in tiles:
                part = grad_mixed[at : at + 128, columns]
                if c != 1:
                    add_row(3 * module + c // 2, part.astype(jnp.float32))
                stream[at : at + 128, :] += dot_nt(part, window[(n + c) % WINDOW])
            next_block(n + c)

    def cross_norm():
        for _, at in row_tiles:
            norm_back(stream[at : at + 128, :], 0, 0, at, end_cross, 2)

    def cross_context():
        n = 16
        load_block(n).wait()
        for _, at in row_tiles:
            grad_context[at : at + 128, :] = dot_nt(end_cross[at : at + 128, :], window[n % WINDOW]).astype(low)
        next_block(n)

    def give_rows():
        for copied in row_copies:
            copied.start()

    row_copies = [
        pltpu.make_async_copy(stream.at[0:WORDS, :], word_gradient, row_sems.at[0]),
        pltpu.make_async_copy(stream.at[WORDS:ROWS, :], region_gradient, row_sems.at[1]),
    ]
    small_leaves = pltpu.make_async_copy(small_total, small_out, row_sems.at[2])

    def exact_nt(left, right):
        return lax.dot_general(
            left,
            right.astype(jnp.float32),
            (((1,), (1,)), ((), ())),
            precision=lax.Precision.HIGHEST,
            preferred_element_type=jnp.float32,
        )

    def give_small():
        small_in[...] = jnp.zeros_like(small_in)
        for owner in range(8):
            small_in[owner, 0:21, :] = exact_nt(row_sums[...], spread(owner))[:21]
        for place in range(8):
            placed = exact_nt(hidden_sums[...], spread(place))
            for c in range(4):
                row = 25 + place % 4
                small_in[2 * c + place // 4, row : row + 1, :] = placed[c : c + 1]
        source = lax.broadcasted_iota(jnp.int32, (128, SLICE), 0)
        target = lax.broadcasted_iota(jnp.int32, (128, SLICE), 1)
        for q in range(4):
            chosen = jnp.logical_and(source < UNIT, target == source + q * UNIT)
            small_in[me, 21 + q : 22 + q, :] = exact_nt(hidden_sums_words[...], chosen)[0:1]
        for offset in range(1, 8):
            small_copy(offset).start()

    def join_small():
        summed = small_in[me]
        for offset in range(1, 8):
            small_copy(offset).wait()
            summed = summed + small_in_plane[offset - 1]
        small_planes[z] = summed
        for offset in range(1, 4):
            small_plane_copy(offset, z).start()

    def finish_small():
        for offset in range(1, 4):
            small_plane_copy(offset, z).wait_send()
            small_plane_copy(offset, (z + 4 - offset) % 4).wait_recv()
        small_total[...] = small_planes[0] + small_planes[1] + (small_planes[2] + small_planes[3])
        small_leaves.start()

    def self_back(rows_of, shares, first, last):
        attend_back_into(rows_of, mixed_self, shares, grad_context, grad_mixed_self, first, last)

    def cross_back(rows_of, shares, first, last):
        attend_back_into(rows_of, mixed_cross, shares, grad_context, grad_mixed_cross, first, last)

    pieces = {
        0: (gather_words.first, lambda: wait_saved(slope)),
        1: (gather_words.second, functools.partial(feed_back, 0)),
        2: (gather_words.complete, words_back),
        3: (functools.partial(feed_back, 1),),
        4: (sum_words.cores, words_shrink),
        5: (functools.partial(feed_back, 2), words_expand),
        6: (sum_words.diagonal,),
        7: (functools.partial(feed_back, 3), lambda: wait_saved(rows_two_t)),
        8: (words_rows, gather_words.settle),
        9: (words_expanded,),
        10: (lambda: load_saved(EARLIER_NORMS).wait(), self_norm),
        11: (self_context, lambda: wait_saved(context_self_t, mixed_self, shares_w)),
        12: (lambda: self_back(ATTEND_WORD, shares_w, 0, 3),),
        13: (lambda: self_back(ATTEND_WORD, shares_w, 3, 6), lambda: wait_saved(shares_r, rows_one_t)),
        **{14 + p: (functools.partial(self_back, ATTEND_REGION, shares_r, p, p + 1),) for p in range(6)},
        20: (lambda: project_back(10, 1, grad_mixed_self, (0,)),),
        21: (lambda: project_back(13, 2, grad_mixed_self, (128, 256)),),
        23: (cross_norm, lambda: wait_saved(context_cross_t, mixed_cross, shares_cw, shares_cr, rows_zero_t)),
        24: (cross_context,),
        **{25 + p: (functools.partial(cross_back, ATTEND_CROSS_WORD, shares_cw, 2 * p, 2 * p + 2),) for p in range(3)},
        **{28 + p: (functools.partial(cross_back, ATTEND_CROSS_REGION, shares_cr, 2 * p, 2 * p + 2),) for p in range(3)},
        32: (lambda: project_back(17, 0, grad_mixed_cross, (0, 128, 256)),),
        33: (give_rows,),
        34: (give_small,),
        37: (join_small,),
        40: (finish_small,),
    }

    feed_norm()
    wait_saved(hidden_t)
    for i in range(last + 1):
        for n, (entry, _, _) in enumerate(entries):
            if i == entry + 3 * LAG_Z:
                finish(n)
        for n, (entry, _, _) in enumerate(entries):
            if i == entry + 2 * LAG_Z:
                join_middle(n)
        for n, (entry, _, _) in enumerate(entries):
            if i == entry + LAG_Z:
                join_pair(n)
        for entry, crosses, u in entries:
            if i == entry and not crosses:
                join_owned(u)
        for lag, stage in ((to_plane, join_plane), (LAG_CORE + LAG_A, join_diagonal), (LAG_CORE, join_cores), (0, produce)):
            if 0 <= i - lag < CROSSING:
                stage(i - lag)
        for piece in pieces.get(i, ()):
            piece()
    for u in range(UNITS):
        per_group(u, lambda at, side, first_row, count, by_row, matrix: total_copy(u, at, by_row, matrix).wait())
    for copied in row_copies + [small_leaves]:
        copied.wait()


def backward(saved, shrink, weights):
    block = (UNIT, SPAN)
    low, f32 = jnp.bfloat16, jnp.float32
    dma = pltpu.SemaphoreType.DMA
    vmem = pl.BlockSpec(memory_space=pltpu.VMEM)
    hbm = pl.BlockSpec(memory_space=pl.ANY)
    shape = jax.ShapeDtypeStruct
    small = (32, 128)
    return pl.pallas_call(
        backward_kernel,
        out_shape=(
            shape((WORDS, WIDE), f32),
            shape((REGIONS, WIDE), f32),
            shape(small, f32),
            shape((3, UNIT, 3 * WIDE), low),
            shape((3, UNIT, WIDE), low),
            shape((2, UNIT, HIDDEN), low),
            shape((2, 4 * UNIT, WIDE), low),
        ),
        in_specs=[hbm] * (len(saved) + 1 + len(weights)),
        out_specs=[hbm] * 7,
        scratch_shapes=[pltpu.VMEM(array.shape, array.dtype) for array in saved]
        + [
            pltpu.VMEM((SLICE, WIDE), low),
            pltpu.VMEM((WINDOW, WIDE, WIDE), low),
            pltpu.VMEM((REGIONS, WIDE), low),
            pltpu.VMEM((ROWS, WIDE), low),
            pltpu.VMEM((ROWS, WIDE), low),
            pltpu.VMEM((ROWS, WIDE), f32),
            pltpu.VMEM((ROWS, WIDE), low),
            pltpu.VMEM((24, WIDE), f32),
            pltpu.VMEM((8, WIDE), f32),
            pltpu.VMEM((PLANE_WORDS, WIDE), low),
            pltpu.VMEM((8, SLICE), f32),
            pltpu.VMEM((SLICE, WIDE), f32),
            pltpu.VMEM((WIDE, SLICE), low),
            pltpu.VMEM((8, UNIT, SLICE), low),
            *row_sum_scratch(),
            dma((8,)),
            dma((8,)),
            dma((7,)),
            dma((7,)),
            pltpu.VMEM((UNITS,) + block, low),
            pltpu.VMEM((ACC_SLOTS, 4) + block, f32),
            pltpu.VMEM((SLOTS, 4) + block, low),
            pltpu.VMEM((SLOTS, 4) + block, low),
            pltpu.VMEM((SLOTS, 2, UNIT // 2, SPAN), low),
            pltpu.VMEM((SLOTS, 2, UNIT // 2, SPAN), low),
            pltpu.VMEM((SLOTS, 2) + block, low),
            pltpu.VMEM((SLOTS, 2) + block, low),
            pltpu.VMEM((Z_SLOTS,) + block, f32),
            pltpu.VMEM((Z_SLOTS,) + block, low),
            pltpu.VMEM((Z_SLOTS,) + block, low),
            pltpu.VMEM((Z_SLOTS,) + block, low),
            pltpu.VMEM((Z_SLOTS,) + block, low),
            pltpu.VMEM((8,) + small, f32),
            pltpu.VMEM((7,) + small, f32),
            pltpu.VMEM((4,) + small, f32),
            pltpu.VMEM(small, f32),
            dma((3,)),
            dma((24,)),
            dma((WINDOW,)),
            dma((UNITS,)),
            dma((SLOTS,)),
            dma((SLOTS,)),
            dma((SLOTS, 2)),
            dma((SLOTS, 2)),
            dma((SLOTS, 2)),
            dma((SLOTS, 2)),
            dma((2, Z_SLOTS)),
            dma((2, Z_SLOTS)),
            dma((UNITS,)),
            dma((UNITS,)),
            dma((10,)),
            dma((10,)),
            pltpu.SemaphoreType.REGULAR((7,)),
        ],
        compiler_params=pltpu.CompilerParams(
            collective_id=0, has_side_effects=True, vmem_limit_bytes=64 * 2**20 - 2**16
        ),
    )(*saved, shrink, *weights)


def deliver_kernel(*refs):
    moved, small, totals = refs[:4], refs[4], refs[5:9]
    moved_out, bias_out, gain_out, hidden_out, totals_out = refs[9:13], refs[13], refs[14], refs[15], refs[16:20]
    narrow, wide, held = refs[20:24], refs[24:28], refs[28:32]
    take_sems, give_sems, load_sems, store_sems = refs[32:]
    takes = [pltpu.make_async_copy(moved[i], held[i], take_sems.at[i]) for i in range(4)]
    gives = [pltpu.make_async_copy(held[i], moved_out[i], give_sems.at[i]) for i in range(4)]
    pieces = [(kind, index) for kind in range(4) for index in range(totals[kind].shape[0])]
    loads = [
        pltpu.make_async_copy(totals[kind].at[index], narrow[kind].at[index], load_sems.at[i])
        for i, (kind, index) in enumerate(pieces)
    ]
    stores = [
        pltpu.make_async_copy(wide[kind].at[index], totals_out[kind].at[index], store_sems.at[i])
        for i, (kind, index) in enumerate(pieces)
    ]
    for one in loads + takes:
        one.start()
    bias_out[...] = small[0:16, 0:UNIT]
    gain_out[...] = small[16:21, 0:UNIT]
    source = lax.broadcasted_iota(jnp.int32, (128, 4 * UNIT), 0)
    target = lax.broadcasted_iota(jnp.int32, (128, 4 * UNIT), 1)
    for f in range(2):
        row = jnp.zeros((1, 4 * UNIT), F32)
        for q in range(4):
            chosen = jnp.logical_and(source < UNIT, target == source + q * UNIT).astype(F32)
            line = 21 + 4 * f + q
            row = row + jnp.dot(
                small[line : line + 1, :], chosen, precision=lax.Precision.HIGHEST, preferred_element_type=F32
            )
        hidden_out[f : f + 1, :] = row
    for i, (kind, index) in enumerate(pieces):
        loads[i].wait()
        wide[kind][index] = narrow[kind][index].astype(F32)
        stores[i].start()
    for i in range(4):
        takes[i].wait()
        gives[i].start()
    for one in gives + stores:
        one.wait()


def deliver(moved, small, totals):
    vmem = pl.BlockSpec(memory_space=pltpu.VMEM)
    hbm = pl.BlockSpec(memory_space=pl.ANY)
    shape = jax.ShapeDtypeStruct
    widened = [shape(total.shape, F32) for total in totals]
    sem = pltpu.SemaphoreType.DMA((4,))
    piece_sem = pltpu.SemaphoreType.DMA((sum(total.shape[0] for total in totals),))
    return pl.pallas_call(
        deliver_kernel,
        out_shape=[shape(one.shape, one.dtype) for one in moved]
        + [shape((16, UNIT), F32), shape((5, UNIT), F32), shape((2, 4 * UNIT), F32)]
        + widened,
        in_specs=[hbm] * 4 + [vmem] + [hbm] * 4,
        out_specs=[hbm] * 4 + [vmem] * 3 + [hbm] * 4,
        scratch_shapes=[pltpu.VMEM(one.shape, one.dtype) for one in totals]
        + [pltpu.VMEM(one.shape, F32) for one in totals]
        + [pltpu.VMEM(one.shape, one.dtype) for one in moved]
        + [sem, sem, piece_sem, piece_sem],
        compiler_params=pltpu.CompilerParams(vmem_limit_bytes=64 * 2**20 - 2**16),
    )(*moved, small, *totals)


def paired(
    word_rows,
    region_rows,
    word_segment,
    region_segment,
    inward,
    outward,
    biases,
    norm_gain,
    expand_weight,
    shrink_weight,
    hidden_bias,
    word_cotangent,
    region_cotangent,
):
    results, saved, weights = forward(
        word_rows,
        region_rows,
        word_segment,
        region_segment,
        biases,
        norm_gain,
        hidden_bias,
        (inward, outward, expand_weight, shrink_weight),
    )
    word_gradient, region_gradient, small, *totals = backward(
        (saved[0], word_cotangent, region_cotangent, *saved[1:]), shrink_weight, weights
    )
    word_out, region_out, word_gradient, region_gradient, bias, gain, hidden, *totals = deliver(
        (*results, word_gradient, region_gradient), small, totals
    )
    inward_total, outward_total, expand_total, shrink_total = totals
    return (
        word_out,
        region_out,
        word_gradient,
        region_gradient,
        inward_total,
        outward_total,
        bias,
        gain,
        expand_total,
        shrink_total,
        hidden,
    )


def general(
    devices,
    word_rows,
    region_rows,
    word_segment,
    region_segment,
    inward,
    outward,
    biases,
    norm_gain,
    expand_weight,
    shrink_weight,
    hidden_bias,
    word_cotangent,
    region_cotangent,
):
    words_count = word_rows.shape[0]
    width = word_rows.shape[1]
    word_ids = word_segment[0]
    region_ids = region_segment[0]
    cross_mask = word_ids[:, None] == region_ids[None, :]
    word_mask = word_ids[:, None] == word_ids[None, :]
    region_mask = region_ids[:, None] == region_ids[None, :]
    shard = biases.shape[1]
    per_shard = hidden_bias.shape[1] // shard
    small_shard = jnp.concatenate([biases, norm_gain, hidden_bias.reshape(2 * per_shard, shard)], axis=0)
    small_all = lax.all_gather(small_shard, "fsdp", axis=0)
    bias_count = biases.shape[0]
    gain_count = norm_gain.shape[0]
    row_params = small_all[:, : bias_count + gain_count].transpose(1, 0, 2).reshape(bias_count + gain_count, width)
    hidden_all = (
        small_all[:, bias_count + gain_count :]
        .reshape(devices, 2, per_shard * shard)
        .transpose(1, 0, 2)
        .reshape(2, devices * per_shard * shard)
    )
    inward_all, outward_all = (
        lax.all_gather(inward, "fsdp", axis=1, tiled=True),
        lax.all_gather(outward, "fsdp", axis=1, tiled=True),
    )
    attend_set = (
        inward_all,
        outward_all,
        row_params[:bias_count].astype(jnp.float32),
        row_params[bias_count:].astype(jnp.float32),
    )
    crossed, cross_kept = cross_forward(word_rows, region_rows, attend_set, cross_mask)
    word_one, word_kept = self_forward(crossed[:words_count], attend_set, 1, word_mask)
    region_one, region_kept = self_forward(crossed[words_count:], attend_set, 2, region_mask)
    expand_all, shrink_all = (
        lax.all_gather(expand_weight, "fsdp", axis=1, tiled=True),
        lax.all_gather(shrink_weight, "fsdp", axis=1, tiled=True),
    )
    feed_set = (expand_all, shrink_all, hidden_all)
    word_two, word_feed = feed_forward(word_one, feed_set, 0, attend_set)
    region_two, region_feed = feed_forward(region_one, feed_set, 1, attend_set)
    word_back = feed_backward(word_cotangent.astype(jnp.float32), word_feed, feed_set, 0, attend_set[3])
    region_back = feed_backward(region_cotangent.astype(jnp.float32), region_feed, feed_set, 1, attend_set[3])
    word_self = self_backward(word_back[0], word_kept, attend_set, 1, word_mask)
    region_self = self_backward(region_back[0], region_kept, attend_set, 2, region_mask)
    grad_crossed = jnp.concatenate([word_self[0], region_self[0]], axis=0)
    cross_back = cross_backward(grad_crossed, cross_kept, attend_set, cross_mask, words_count)
    row_grads = jnp.stack(
        [
            cross_back[3][0],
            cross_back[3][1],
            cross_back[3][2],
            word_self[3][0],
            word_self[3][1],
            word_self[3][2],
            region_self[3][0],
            region_self[3][1],
            region_self[3][2],
            cross_back[5],
            word_self[5],
            region_self[5],
            word_back[6],
            region_back[6],
            word_back[4],
            region_back[4],
            cross_back[4],
            word_self[4],
            region_self[4],
            word_back[5],
            region_back[5],
        ]
    )
    hidden_grads = jnp.stack([word_back[3], region_back[3]])
    small_grads = jnp.concatenate(
        [
            row_grads.reshape(bias_count + gain_count, devices, shard).transpose(1, 0, 2),
            hidden_grads.reshape(2, devices, per_shard, shard)
            .transpose(1, 0, 2, 3)
            .reshape(devices, 2 * per_shard, shard),
        ],
        axis=1,
    )

    def reduced(products, axis):
        mine = lax.psum_scatter(jnp.stack(products), "fsdp", scatter_dimension=axis, tiled=True)
        return lax.psum(mine.astype(jnp.bfloat16), "rep").astype(jnp.float32)

    shrink_total = reduced([matmul_tn(*word_back[2]), matmul_tn(*region_back[2])], 1)
    expand_total = reduced([matmul_tn(*word_back[1]), matmul_tn(*region_back[1])], 1)
    outward_total = reduced([matmul_tn(*cross_back[2]), matmul_tn(*word_self[2]), matmul_tn(*region_self[2])], 1)
    inward_total = reduced([matmul_tn(*cross_back[1]), matmul_tn(*word_self[1]), matmul_tn(*region_self[1])], 1)
    small_total = lax.psum(lax.psum_scatter(small_grads, "fsdp", scatter_dimension=0, tiled=False), "rep")
    grad_rows = cross_back[0]
    return (
        word_two.astype(jnp.bfloat16),
        region_two.astype(jnp.bfloat16),
        grad_rows[:words_count],
        grad_rows[words_count:],
        inward_total,
        outward_total,
        small_total[:bias_count],
        small_total[bias_count : bias_count + gain_count],
        expand_total,
        shrink_total,
        small_total[bias_count + gain_count :].reshape(2, per_shard * shard),
    )


def solution(mesh):
    sizes = (mesh.shape["rep"], mesh.shape["fsdp"])
    return jax.shard_map(
        paired if sizes == (4, 8) else functools.partial(general, mesh.shape["fsdp"]),
        mesh=mesh,
        in_specs=(
            P(("rep", "fsdp"), None),
            P(("rep", "fsdp"), None),
            P(("rep", "fsdp"), None),
            P(("rep", "fsdp"), None),
            P(None, "fsdp", None),
            P(None, "fsdp", None),
            P(None, "fsdp"),
            P(None, "fsdp"),
            P(None, "fsdp", None),
            P(None, "fsdp", None),
            P(None, "fsdp"),
            P(("rep", "fsdp"), None),
            P(("rep", "fsdp"), None),
        ),
        out_specs=(
            P(("rep", "fsdp"), None),
            P(("rep", "fsdp"), None),
            P(("rep", "fsdp"), None),
            P(("rep", "fsdp"), None),
            P(None, "fsdp", None),
            P(None, "fsdp", None),
            P(None, "fsdp"),
            P(None, "fsdp"),
            P(None, "fsdp", None),
            P(None, "fsdp", None),
            P(None, "fsdp"),
        ),
        check_vma=False,
    )
```
